256 devices in a mesh: row: 8 (over x, core), col: 32 (over z, y).
Axes of the slice: x: 4, y: 4, z: 8, core: 2. Of those that a mesh axis runs over, the one named last changes fastest.
Arguments:
- positions: int32 [3, 8192], P(None, ('row', 'col')), may hold values from 0 to 31, as said below
- start_vector: float32 [3, 8192, 128], P(None, ('row', 'col')), may hold values from -6 to 6
Outputs:
- displacement: float32 [3, 8192, 128], P(None, ('row', 'col'))
The draws below stay inside these ranges and needn't reach their ends.
Inputs may be any that keep to these rules, and one draw needn't show every extreme that they name: `positions`: for each bead: x and y coordinates in 0 to 31, z coordinate in 0 to 31; no two beads share a lattice site.
All inputs are finite; a program needn't handle non-finite values.
Results may differ from the reference program's by a relative error of at most 0.0003.
Values sent between devices are 32-bit elements; how exact they have to be, the bound alone decides.
A program may use at most 64 MiB of HBM per device.

```python
import jax
import jax.numpy as jnp
from jax import lax

BEADS = 8192
SAMPLES = 128
ITERS = 3


def draw_positions(key, part):
    key = jax.random.fold_in(key, 11)
    sites = jax.random.permutation(key, 4 * BEADS)[:BEADS].astype(jnp.int32)
    return jnp.stack([sites % 32, sites // 32 % 32, sites // 1024]).astype(jnp.int32)


def steps_of(own_key, shape, pieces, smallest, largest):
    def one(axis_at, blocks):
        steps = jax.random.uniform(jax.random.fold_in(jax.random.fold_in(own_key, 6), axis_at), (blocks,), jnp.float32, smallest / len(pieces), largest / len(pieces))
        return jnp.repeat(jnp.exp(steps), shape[axis_at] // blocks).reshape((-1,) + (1,) * (len(shape) - axis_at - 1))

    factor_of = one(*pieces[0])
    for cut in pieces[1:]:
        factor_of = factor_of * one(*cut)
    return factor_of


def bell_draw(stream_key, dims, spread, most, cuts=(), kind=jnp.bfloat16):
    result = jax.random.normal(stream_key, dims, jnp.float32) * spread
    if len(cuts) > 0:
        result = steps_of(stream_key, dims, cuts, -0.22, 0.18) * result
    return jnp.clip(result, min=-most, max=most).astype(kind)


def setup_inputs(seed: int = 0) -> dict:
    seeds = jax.random.split(jax.random.key(seed), 3)
    positions = draw_positions(jax.random.fold_in(seeds[2], 71), 0)
    start_vector = bell_draw(seeds[1], (3, BEADS, SAMPLES), 1.0, 6.0, ((1, 256),), jnp.float32)
    return {"positions": positions, "start_vector": start_vector}


RADIUS = 0.4
PAIRS = ((0, 0), (0, 1), (0, 2), (1, 1), (1, 2), (2, 2))
PAIR_SLOT = ((0, 1, 2), (1, 3, 4), (2, 4, 5))

def pair_tensors(row_pos, col_pos):
    offset = row_pos[:, :, None] - col_pos[:, None, :]
    squared = lax.optimization_barrier(jnp.sum(offset * offset, axis=0))
    distant = squared > 0.5
    inverse = 1.0 / jnp.where(distant, squared, 1.0)
    prefactor = 0.75 * RADIUS * jnp.sqrt(inverse)
    isotropic = jnp.where(distant, prefactor * (1.0 + 2.0 / 3.0 * RADIUS * RADIUS * inverse), 1.0)
    along_axis = jnp.where(distant, prefactor * (1.0 - 2.0 * RADIUS * RADIUS * inverse) * inverse, 0.0)
    components = []
    for left_axis, right_axis in PAIRS:
        tensor_part = along_axis * offset[left_axis] * offset[right_axis]
        if left_axis == right_axis:
            tensor_part = tensor_part + isotropic
        components.append(tensor_part)
    return components

def apply_tensors(components, col_vec):
    outputs = []
    for left_axis in range(3):
        summed = jnp.dot(components[PAIR_SLOT[left_axis][0]], col_vec[0], precision=lax.Precision.HIGHEST)
        for right_axis in range(1, 3):
            summed = summed + jnp.dot(components[PAIR_SLOT[left_axis][right_axis]], col_vec[right_axis], precision=lax.Precision.HIGHEST)
        outputs.append(summed)
    return jnp.stack(outputs)

def inverse_three(matrix):

    def entry(row_index, col_index):
        return matrix[row_index, col_index]
    cofactor = [[None] * 3 for _ in range(3)]
    for row_index in range(3):
        for col_index in range(3):
            rows_left = [k for k in range(3) if k != row_index]
            cols_left = [k for k in range(3) if k != col_index]
            minor = entry(rows_left[0], cols_left[0]) * entry(rows_left[1], cols_left[1]) - entry(rows_left[0], cols_left[1]) * entry(rows_left[1], cols_left[0])
            cofactor[row_index][col_index] = minor if (row_index + col_index) % 2 == 0 else -minor
    determinant = entry(0, 0) * cofactor[0][0] + entry(0, 1) * cofactor[0][1] + entry(0, 2) * cofactor[0][2]
    return jnp.stack([jnp.stack([cofactor[col_index][row_index] / determinant for col_index in range(3)]) for row_index in range(3)])

def square_root(tri):
    scale = (tri[0, 0] + tri[1, 1] + tri[2, 2]) / ITERS
    current = tri / scale
    partner = jnp.eye(3, dtype=jnp.float32)[:, :, None] * jnp.ones((1, 1, tri.shape[2]), jnp.float32)
    for newton_step in range(20):
        current, partner = (0.5 * (current + inverse_three(partner)), 0.5 * (partner + inverse_three(current)))
    return current * jnp.sqrt(scale)

def tridiagonal(alphas, betas):
    zero = jnp.zeros_like(alphas[0])
    return jnp.stack([jnp.stack([alphas[0], betas[0], zero]), jnp.stack([betas[0], alphas[1], betas[1]]), jnp.stack([zero, betas[1], alphas[2]])])

def reference(positions, start_vector):
    coords = positions.astype(jnp.float32)
    block_rows = min(512, BEADS)
    row_stack = coords.reshape(3, BEADS // block_rows, block_rows).transpose(1, 0, 2)

    def mobility_apply(vector):

        def one_block(block_pos):
            return apply_tensors(pair_tensors(block_pos, coords), vector)
        stacked = lax.map(one_block, row_stack)
        return stacked.transpose(1, 0, 2, 3).reshape(3, BEADS, SAMPLES)
    beta_start = jnp.sqrt(lax.optimization_barrier(jnp.sum(start_vector * start_vector, axis=(0, 1))))
    current = start_vector / beta_start
    previous = jnp.zeros_like(start_vector)
    beta = jnp.zeros((SAMPLES,), jnp.float32)
    basis, alphas, betas = ([], [], [])
    for step in range(ITERS):
        basis.append(current)
        work = mobility_apply(current) - beta * previous
        alpha = lax.optimization_barrier(jnp.sum(current * work, axis=(0, 1)))
        work = work - alpha * current
        alphas.append(alpha)
        if step + 1 < ITERS:
            beta = jnp.sqrt(lax.optimization_barrier(jnp.sum(work * work, axis=(0, 1))))
            betas.append(beta)
            previous = current
            current = work / beta
    root = square_root(tridiagonal(alphas, betas))
    displacement = jnp.zeros_like(start_vector)
    for step in range(ITERS):
        displacement = displacement + beta_start * root[step, 0] * basis[step]
    return displacement
```

```python
import jax
import jax.numpy as jnp
from jax import lax
from jax.experimental import pallas as pl
from jax.experimental.pallas import tpu as pltpu
from jax.sharding import PartitionSpec as P

ITERS = 3
RADIUS = 0.4
MESH = pl.DeviceIdType.MESH
F32 = jnp.float32
BF16 = jnp.bfloat16

PLANE, LINE = 32, 16
HALF = 64
BLOCK = 512


def kernel(pos_ref, z_ref, out_ref, posbuf, colbc, lanevec, mob, wide, ag, rs, rs_send, packed, acc, part,
           red_src, red_one, red_two, moments, pos_sem, line_sem, plane_sem, ag_send, rs_recv, rs_sent, red_sem):
    row, col = lax.axis_index("row"), lax.axis_index("col")
    x, core = lax.div(row, 2), lax.rem(row, 2)
    z, y = lax.div(col, 4), lax.rem(col, 4)
    chip = x * 4 + y
    my_p, my_l = chip * 2 + core, z * 2 + core

    def plane_dev(p):
        return (lax.div(p, 8) * 2 + lax.rem(p, 2), z * 4 + lax.rem(lax.div(p, 2), 4))

    def line_dev(l):
        return (x * 2 + lax.rem(l, 2), lax.div(l, 2) * 4 + y)

    def remote(src, dst, send, recv, device):
        return pltpu.make_async_remote_copy(
            src_ref=src, dst_ref=dst, send_sem=send, recv_sem=recv, device_id=device, device_id_type=MESH)

    def wait_recv(ref, sem):
        remote(ref, ref, sem, sem, (row, col)).wait_recv()

    def wait_send(ref, sem):
        remote(ref, ref, sem, sem, (row, col)).wait_send()

    first = lax.broadcasted_iota(jnp.int32, (16, 128), 1) < HALF

    def turn(value):
        return pltpu.roll(value, HALF, 1)

    barrier = pltpu.get_barrier_semaphore()

    @pl.loop(0, PLANE)
    def _(p):
        @pl.when(p != my_p)
        def _():
            pl.semaphore_signal(barrier, inc=1, device_id=plane_dev(p), device_id_type=MESH)

    @pl.loop(0, LINE)
    def _(l):
        @pl.when(lax.div(l, 2) != z)
        def _():
            pl.semaphore_signal(barrier, inc=1, device_id=line_dev(l), device_id_type=MESH)

    posbuf[my_p] = pos_ref[...]
    posbuf[PLANE + my_l] = pos_ref[...]
    for axis in range(3):
        low, high = z_ref[axis, :16, :], z_ref[axis, 16:, :]
        packed[0, 0, axis] = jnp.where(first, low, turn(high))
        packed[0, 1, axis] = jnp.where(first, turn(low), high)
    pl.semaphore_wait(barrier, 45)

    @pl.loop(0, PLANE)
    def _(p):
        @pl.when(p != my_p)
        def _():
            remote(pos_ref, posbuf.at[my_p], pos_sem.at[1], pos_sem.at[0], plane_dev(p)).start()

    @pl.loop(0, LINE)
    def _(l):
        @pl.when(l != my_l)
        def _():
            remote(pos_ref, posbuf.at[PLANE + my_l], pos_sem.at[1], pos_sem.at[0], line_dev(l)).start()

    def gather(step):
        last = step == 2

        @pl.loop(0, LINE)
        def _(l):
            half = lax.rem(l, 2)

            @pl.when((l != my_l) & (last | (half == 0)))
            def _():
                remote(packed.at[step, half], ag.at[step, PLANE + my_l], ag_send.at[step],
                       line_sem.at[step], line_dev(l)).start()

        @pl.loop(0, PLANE)
        def _(p):
            half = lax.rem(p, 2)

            @pl.when((p != my_p) & (last | (half == 1)))
            def _():
                remote(packed.at[step, half], ag.at[step, my_p], ag_send.at[step],
                       plane_sem.at[step], plane_dev(p)).start()

        ag[step, my_p] = packed[step, core]
        ag[step, PLANE + my_l] = packed[step, core]

    gather(0)
    acc[...] = jnp.zeros_like(acc)
    part[...] = jnp.zeros_like(part)
    wait_recv(posbuf.at[pl.ds(0, 46)], pos_sem.at[0])

    lane_of = lax.broadcasted_iota(jnp.int32, (BLOCK, 128), 1)
    bead_of = lax.rem(lax.broadcasted_iota(jnp.int32, (BLOCK, 128), 0), 32)
    entry_of = lax.broadcasted_iota(jnp.int32, (128, BLOCK), 0)
    column_of = lax.rem(lax.broadcasted_iota(jnp.int32, (128, BLOCK), 1), 32)
    owner_of = lax.div(lax.broadcasted_iota(jnp.int32, (16, BLOCK), 1), 32)
    source_of = lax.broadcasted_iota(jnp.int32, (16, BLOCK), 0)
    ones = jnp.ones((128, 128), BF16)

    @pl.loop(0, 2)
    def _(h):
        rows_at = jnp.where(core == 0, h, 2) * 16
        lanes_at = jnp.where(core == 0, 2, h) * 16
        spread = jnp.concatenate([jnp.broadcast_to(posbuf[rows_at + d], (32, 128)) for d in range(16)], axis=0)
        flat = jnp.concatenate([posbuf[lanes_at + d] for d in range(16)], axis=0).astype(BF16)
        for axis in range(3):
            own = jnp.where(lane_of == axis * 32 + bead_of, spread, 0.0).astype(BF16)
            colbc[h, axis] = jnp.dot(own, ones, preferred_element_type=F32)
            pick = jnp.where(entry_of == axis * 32 + column_of, 1.0, 0.0).astype(BF16)
            moved = jnp.dot(flat, pick, preferred_element_type=F32)
            lanevec[h, axis:axis + 1, :] = jnp.sum(jnp.where(owner_of == source_of, moved, 0.0), axis=0, keepdims=True)

    @pl.loop(0, 2)
    def _(h):
        @pl.loop(0, BLOCK // 16)
        def _(t):
            rows = pl.ds(pl.multiple_of(t * 16, 16), 16)
            mine = [colbc[h, axis, rows, :] for axis in range(3)]
            for tile in range(4):
                lanes = slice(tile * 128, tile * 128 + 128)
                d = [mine[axis] - lanevec[h, axis:axis + 1, lanes] for axis in range(3)]
                squared = d[0] * d[0] + d[1] * d[1] + d[2] * d[2]
                squared = jnp.where(squared > 0.5, squared, 1e30)
                root = lax.rsqrt(squared)
                root = root * (1.5 - 0.5 * squared * (root * root))
                inverse = root * root
                prefactor = (0.75 * RADIUS) * root
                iso = prefactor * (1.0 + (2.0 / 3.0 * RADIUS * RADIUS) * inverse)
                along = (prefactor * inverse) * (1.0 - (2.0 * RADIUS * RADIUS) * inverse)
                s = [along * d[axis] for axis in range(3)]
                parts = (s[0] * d[0] + iso, s[0] * d[1], s[0] * d[2], s[1] * d[1] + iso, s[1] * d[2],
                         s[2] * d[2] + iso)
                for k, value in enumerate(parts):
                    high = value.astype(BF16)
                    mob[h, k, rows, lanes] = high
                    mob[h, k, rows, slice(BLOCK + tile * 128, BLOCK + tile * 128 + 128)] = (
                        value - high.astype(F32)).astype(BF16)

    def widen(step, h):
        base = jnp.where(core == 0, PLANE, h * 16)

        @pl.loop(0, 16)
        def _(s):
            for axis in range(3):
                value = ag[step, base + s, axis]
                other = turn(value)
                for j, both in enumerate((jnp.where(first, value, other), jnp.where(first, other, value))):
                    high = both.astype(BF16).astype(F32)
                    tile = jnp.where(first, high, both - high).astype(BF16)
                    for copy in range(2):
                        at = pl.ds(pl.multiple_of(copy * BLOCK + s * 32 + j * 16, 16), 16)
                        wide[h, at, axis * 128:axis * 128 + 128] = tile
                        if axis == 0:
                            wide[h, at, 384:512] = tile

    def product(t):
        h = jnp.where(core == 0, lax.div(t, 2), lax.rem(t, 2))
        rt = jnp.where(core == 0, lax.rem(t, 2), lax.div(t, 2))
        w = jnp.where(core == 0, 0, h)
        rows = pl.ds(pl.multiple_of(rt * 256, 256), 256)

        def dot(k, lo, hi):
            return jnp.dot(mob[h, k, rows, :], wide[w, :, lo:hi], preferred_element_type=F32)

        xy, yz, zx = dot(1, 0, 256), dot(4, 128, 384), dot(2, 256, 512)
        return (dot(0, 0, 128) + xy[:, 128:] + zx[:, :128],
                dot(3, 128, 256) + xy[:, :128] + yz[:, 128:],
                dot(5, 256, 384) + zx[:, 128:] + yz[:, :128])

    def pack(i, axis):
        low, high = acc[axis, i * 32:i * 32 + 16, :], acc[axis, i * 32 + 16:i * 32 + 32, :]
        return jnp.where(first, low + turn(low), high + turn(high))

    @pl.loop(0, ITERS)
    def _(step):
        last = step == 2

        @pl.when((core == 0) | last)
        def _():
            wait_recv(ag.at[step, pl.ds(0, LINE - 1)], line_sem.at[step])

        @pl.when((core == 1) | last)
        def _():
            wait_recv(ag.at[step, pl.ds(0, PLANE - 1)], plane_sem.at[step])

        widen(step, 0)

        @pl.when(core == 1)
        def _():
            widen(step, 1)

        @pl.loop(0, 4)
        def _(t):
            more = (core == 1) & (lax.rem(t, 2) == 1) & (step < 2)
            for axis, value in enumerate(product(t)):
                acc[axis] = jnp.where(more, acc[axis], 0.0) + value
            group = jnp.where(core == 0, t, lax.div(t, 2))

            @pl.when((step < 2) & ((core == 0) | (lax.rem(t, 2) == 1)))
            def _():
                for i in range(8):
                    for axis in range(3):
                        rs_send[step, group * 8 + i, axis] = pack(i, axis)
                slot = jnp.where(core == 0, chip, 16 + z)
                mine = jnp.where(core == 0, my_p, my_l)

                @pl.loop(0, 8)
                def _(i):
                    q = group * 8 + i
                    p_row, p_col = plane_dev(q)
                    l_row, l_col = line_dev(q)
                    device = (jnp.where(core == 0, p_row, l_row), jnp.where(core == 0, p_col, l_col))

                    @pl.when(q != mine)
                    def _():
                        remote(rs_send.at[step, q], rs.at[step, slot], rs_sent.at[step], rs_recv.at[step],
                               device).start()

                    @pl.when(q == mine)
                    def _():
                        rs[step, slot] = rs_send[step, q]

            @pl.when(last)
            def _():
                at = jnp.where(core == 0, 0, PLANE) + group * 8
                total = part[...]
                for i in range(8):
                    for axis in range(3):
                        total = total + pack(i, axis) * ag[2, at + i, axis]
                part[...] = total

        @pl.when(step < 2)
        def _():
            wait_recv(rs.at[step, pl.ds(0, 23)], rs_recv.at[step])
            for axis in range(3):
                total = rs[step, 0, axis]
                for s in range(1, 16):
                    total = total + rs[step, s, axis]
                packed[step + 1, 0, axis] = total
                total = rs[step, 16, axis]
                for s in range(17, 24):
                    total = total + rs[step, s, axis]
                packed[step + 1, 1, axis] = total
            gather(step + 1)

    front = lax.broadcasted_iota(jnp.int32, (1, 128), 1) < HALF

    def fold(value):
        line = jnp.sum(value, axis=0, keepdims=True)
        return line + turn(line)

    def inner(left, right):
        sums = [sum(packed[left, half, axis] * packed[right, half, axis] for axis in range(3)) for half in range(2)]
        return jnp.where(front, fold(sums[0]), fold(sums[1]))

    for at, (left, right) in enumerate(((0, 0), (0, 1), (1, 1), (1, 2), (2, 2))):
        red_src[0, at:at + 1, :] = inner(left, right)
    red_src[0, 5:6, :] = jnp.where(front == (core == 0), fold(part[...]), 0.0)
    red_src[0, 6:8, :] = jnp.zeros((2, 128), F32)

    @pl.loop(0, 16)
    def _(c):
        @pl.when(c != chip)
        def _():
            remote(red_src.at[0], red_one.at[chip], red_sem.at[0], red_sem.at[1], plane_dev(c * 2 + core)).start()

    red_one[chip] = red_src[0]
    wait_recv(red_one.at[pl.ds(0, 15)], red_sem.at[1])
    total = red_one[0]
    for s in range(1, 16):
        total = total + red_one[s]
    red_src[1] = total

    @pl.loop(0, LINE)
    def _(l):
        @pl.when(l != my_l)
        def _():
            remote(red_src.at[1], red_two.at[my_l], red_sem.at[2], red_sem.at[3], line_dev(l)).start()

    red_two[my_l] = red_src[1]
    wait_recv(red_two.at[pl.ds(0, 15)], red_sem.at[3])
    total = red_two[0]
    for s in range(1, 16):
        total = total + red_two[s]
    for k in range(6):
        moments[k] = jnp.broadcast_to(total[k:k + 1, :], (8, 128))
    moments[6] = jnp.zeros((8, 128), F32)
    moments[7] = jnp.ones((8, 128), F32)
    m0, m1, m2, m3, m4, m5, zero, one = (moments[k] for k in range(8))

    a1 = m1 / m0
    e1 = m2 - a1 * m1
    bb2 = e1 / m0
    a2 = (m3 - 2.0 * a1 * m2 + a1 * a1 * m1) / e1
    p, q = a1 + a2, a1 * a2 - bb2
    e2 = m4 - p * m3 + q * m2
    bb3 = e2 / e1
    a3 = (m5 - 2.0 * p * m4 + (p * p + 2.0 * q) * m3 - 2.0 * p * q * m2 + q * q * m1) / e2
    a1, a2, a3 = 1.0 + a1, 1.0 + a2, 1.0 + a3
    scale = (a1 + a2 + a3) / ITERS
    current = (a1 / scale, jnp.sqrt(bb2) / scale, zero, a2 / scale, jnp.sqrt(bb3) / scale, a3 / scale)
    partner = (one, zero, zero, one, zero, one)

    def inverse_three(m):
        c00, c01, c02 = m[3] * m[5] - m[4] * m[4], m[2] * m[4] - m[1] * m[5], m[1] * m[4] - m[2] * m[3]
        c11, c12, c22 = m[0] * m[5] - m[2] * m[2], m[1] * m[2] - m[0] * m[4], m[0] * m[3] - m[1] * m[1]
        over = 1.0 / (m[0] * c00 + m[1] * c01 + m[2] * c02)
        return tuple(c * over for c in (c00, c01, c02, c11, c12, c22))

    def newton(_, state):
        now, other = state
        return (tuple(0.5 * (u + v) for u, v in zip(now, inverse_three(other))),
                tuple(0.5 * (u + v) for u, v in zip(other, inverse_three(now))))

    current, partner = lax.fori_loop(0, 20, newton, (current, partner))
    size = jnp.sqrt(scale)
    beta = jnp.sqrt(m0)
    r1, r2, r3 = (current[k] * size for k in range(3))
    f2, f3 = beta * r2 / jnp.sqrt(e1), beta * r3 / jnp.sqrt(e2)
    c0 = r1 - f2 * (a1 - 1.0) + f3 * q
    c1 = f2 - f3 * p
    c0, c1, f3 = (jnp.concatenate([c, c], axis=0) for c in (c0, c1, f3))
    for axis in range(3):
        one_a, one_b = packed[1, 0, axis], packed[1, 1, axis]
        two_a, two_b = packed[2, 0, axis], packed[2, 1, axis]
        out_ref[axis, :16, :] = (c0 * z_ref[axis, :16, :] + c1 * jnp.where(first, one_a, turn(one_b))
                                 + f3 * jnp.where(first, two_a, turn(two_b)))
        out_ref[axis, 16:, :] = (c0 * z_ref[axis, 16:, :] + c1 * jnp.where(first, turn(one_a), one_b)
                                 + f3 * jnp.where(first, turn(two_a), two_b))

    wait_send(posbuf.at[pl.ds(0, 46)], pos_sem.at[1])
    wait_send(ag.at[0, pl.ds(0, 23)], ag_send.at[0])
    wait_send(ag.at[1, pl.ds(0, 23)], ag_send.at[1])
    wait_send(ag.at[2, pl.ds(0, 46)], ag_send.at[2])
    wait_send(red_one.at[pl.ds(0, 15)], red_sem.at[0])
    wait_send(red_two.at[pl.ds(0, 15)], red_sem.at[2])
    for step in range(2):
        @pl.when(core == 0)
        def _():
            wait_send(rs_send.at[step, pl.ds(0, PLANE - 1)], rs_sent.at[step])

        @pl.when(core == 1)
        def _():
            wait_send(rs_send.at[step, pl.ds(0, LINE - 1)], rs_sent.at[step])


def shards(positions, start_vector):
    place = jnp.pad(positions.astype(F32).reshape(1, 96), ((0, 0), (0, 32)))
    chunk = (3, 16, 128)
    vmem = pl.BlockSpec(memory_space=pltpu.VMEM)
    return pl.pallas_call(
        kernel,
        out_shape=jax.ShapeDtypeStruct(start_vector.shape, F32),
        in_specs=[vmem, vmem],
        out_specs=vmem,
        scratch_shapes=[
            pltpu.VMEM((PLANE + LINE, 1, 128), F32),
            pltpu.VMEM((2, 3, BLOCK, 128), F32),
            pltpu.VMEM((2, 8, BLOCK), F32),
            pltpu.VMEM((2, 6, BLOCK, 2 * BLOCK), BF16),
            pltpu.VMEM((2, 2 * BLOCK, 512), BF16),
            pltpu.VMEM((3, PLANE + LINE) + chunk, F32),
            pltpu.VMEM((2, 24) + chunk, F32),
            pltpu.VMEM((2, PLANE) + chunk, F32),
            pltpu.VMEM((3, 2) + chunk, F32),
            pltpu.VMEM((3, 256, 128), F32),
            pltpu.VMEM((16, 128), F32),
            pltpu.VMEM((2, 8, 128), F32),
            pltpu.VMEM((16, 8, 128), F32),
            pltpu.VMEM((16, 8, 128), F32),
            pltpu.VMEM((8, 8, 128), F32),
            pltpu.SemaphoreType.DMA((2,)),
            pltpu.SemaphoreType.DMA((3,)),
            pltpu.SemaphoreType.DMA((3,)),
            pltpu.SemaphoreType.DMA((3,)),
            pltpu.SemaphoreType.DMA((2,)),
            pltpu.SemaphoreType.DMA((2,)),
            pltpu.SemaphoreType.DMA((4,)),
        ],
        compiler_params=pltpu.CompilerParams(
            collective_id=0, has_side_effects=True, vmem_limit_bytes=40 * 1024 * 1024),
    )(place, start_vector)


def solution(mesh):
    in_specs = (P(None, ("row", "col")), P(None, ("row", "col"), None))
    out_specs = P(None, ("row", "col"), None)
    return jax.shard_map(shards, mesh=mesh, in_specs=in_specs, out_specs=out_specs, check_vma=False)
```

```python
import jax
import jax.numpy as jnp
from jax import lax
from jax.experimental import pallas as pl
from jax.experimental.pallas import tpu as pltpu
from jax.sharding import PartitionSpec as P

ITERS = 3
RADIUS = 0.4
MESH = pl.DeviceIdType.MESH
F32 = jnp.float32
BF16 = jnp.bfloat16

PLANE, LINE = 32, 16
LINE_ORDER = (4, 3, 5, 2, 6, 1, 7)
PLANE_ORDER = ((2, 2), (1, 2), (2, 1), (3, 2), (2, 3), (1, 1), (3, 3), (1, 3), (3, 1), (2, 0), (0, 2),
               (1, 0), (0, 1), (3, 0), (0, 3))
ORDER = [item for n, spot in enumerate(PLANE_ORDER) for item in
         ([("line", LINE_ORDER[n // 2])] if n % 2 == 0 and n < 14 else []) + [("plane", spot)]]
HALF = 64
BLOCK = 512


def kernel(pos_ref, z_hbm, out_ref, posbuf, colbc, lanevec, mob, wide, ag, rs, rs_send, packed, acc, part,
           red_src, red_one, red_two, moments, flatten, z_ref, load_sem, pos_sem, ag_recv, ag_send, rs_recv, rs_sent, red_sem):
    row, col = lax.axis_index("row"), lax.axis_index("col")
    x, core = lax.div(row, 2), lax.rem(row, 2)
    z, y = lax.div(col, 4), lax.rem(col, 4)
    chip = x * 4 + y
    my_p, my_l = chip * 2 + core, z * 2 + core

    xs = [lax.rem(x + d, 4) for d in range(4)]
    ys = [lax.rem(y + d, 4) for d in range(4)]
    zs = [lax.rem(z + d, 8) for d in range(8)]

    def plane_at(dx, dy, c):
        return (xs[dx] * 2 + c, z * 4 + ys[dy])

    def line_at(dz, c):
        return (x * 2 + c, zs[dz] * 4 + y)

    sibling = (x * 2 + 1 - core, col)

    def remote(src, dst, send, recv, device):
        return pltpu.make_async_remote_copy(
            src_ref=src, dst_ref=dst, send_sem=send, recv_sem=recv, device_id=device, device_id_type=MESH)

    def wait_recv(ref, sem):
        remote(ref, ref, sem, sem, (row, col)).wait_recv()

    def wait_send(ref, sem):
        remote(ref, ref, sem, sem, (row, col)).wait_send()

    first = lax.broadcasted_iota(jnp.int32, (16, 128), 1) < HALF

    def turn(value):
        return pltpu.roll(value, HALF, 1)

    barrier = pltpu.get_barrier_semaphore()

    def signal(device):
        pl.semaphore_signal(barrier, inc=1, device_id=device, device_id_type=MESH)

    signal(sibling)
    for c in range(2):
        for dz in LINE_ORDER:
            signal(line_at(dz, c))
        for dx, dy in PLANE_ORDER:
            signal(plane_at(dx, dy, c))

    load_z = pltpu.make_async_copy(z_hbm, z_ref, load_sem)
    load_z.start()
    flatten[...] = jnp.zeros_like(flatten)
    flatten[0:3, 0:32] = pos_ref[...].astype(F32)
    rows3 = flatten[...]
    flatten[0:1, :] = rows3[0:1] + pltpu.roll(rows3[1:2], 32, 1) + pltpu.roll(rows3[2:3], 64, 1)
    posbuf[my_p] = flatten[0:1, :]
    posbuf[PLANE + my_l] = flatten[0:1, :]
    load_z.wait()
    for axis in range(3):
        low, high = z_ref[axis, :16, :], z_ref[axis, 16:, :]
        packed[0, 0, axis] = jnp.where(first, low, turn(high))
        packed[0, 1, axis] = jnp.where(first, turn(low), high)
    pl.semaphore_wait(barrier, 45)

    def send_place(slot, device):
        remote(posbuf.at[slot], posbuf.at[slot], pos_sem.at[1], pos_sem.at[0], device).start()

    for kind, offset in ORDER:
        for c in range(2):
            if kind == "line":
                send_place(PLANE + my_l, line_at(offset, c))
            else:
                send_place(my_p, plane_at(*offset, c))
    send_place(PLANE + my_l, sibling)
    send_place(my_p, sibling)

    def gather(step):
        def send(half, which, device):
            slot = PLANE + my_l if which == 0 else my_p
            remote(packed.at[step, half], ag.at[step, slot], ag_send.at[step], ag_recv.at[step, which],
                   device).start()

        def send_sibling(which):
            slot = jnp.where(which == 0, PLANE + my_l, my_p)
            remote(packed.at[step, 1 - core], ag.at[step, slot], ag_send.at[step], ag_recv.at[step, which],
                   sibling).start()

        for kind, offset in ORDER:
            if kind == "line":
                send(0, 0, line_at(offset, 0))
            else:
                send(1, 1, plane_at(*offset, 1))
        send_sibling(1 - core)
        ag[step, my_p] = packed[step, core]
        ag[step, PLANE + my_l] = packed[step, core]

        @pl.when(step == 2)
        def _():
            for kind, offset in ORDER:
                if kind == "line":
                    send(1, 0, line_at(offset, 1))
                else:
                    send(0, 1, plane_at(*offset, 0))
            send_sibling(core)

    gather(0)
    acc[...] = jnp.zeros_like(acc)
    part[...] = jnp.zeros_like(part)
    wait_recv(posbuf.at[pl.ds(0, 46)], pos_sem.at[0])

    lane_of = lax.broadcasted_iota(jnp.int32, (BLOCK, 128), 1)
    bead_of = lax.rem(lax.broadcasted_iota(jnp.int32, (BLOCK, 128), 0), 32)
    entry_of = lax.broadcasted_iota(jnp.int32, (128, BLOCK), 0)
    column_of = lax.rem(lax.broadcasted_iota(jnp.int32, (128, BLOCK), 1), 32)
    owner_of = lax.div(lax.broadcasted_iota(jnp.int32, (16, BLOCK), 1), 32)
    source_of = lax.broadcasted_iota(jnp.int32, (16, BLOCK), 0)
    ones = jnp.ones((128, 128), BF16)

    @pl.loop(0, 2)
    def _(h):
        rows_at = jnp.where(core == 0, h, 2) * 16
        lanes_at = jnp.where(core == 0, 2, h) * 16
        spread = jnp.concatenate([jnp.broadcast_to(posbuf[rows_at + d], (32, 128)) for d in range(16)], axis=0)
        flat = jnp.concatenate([posbuf[lanes_at + d] for d in range(16)], axis=0).astype(BF16)
        for axis in range(3):
            own = jnp.where(lane_of == axis * 32 + bead_of, spread, 0.0).astype(BF16)
            colbc[h, axis] = jnp.dot(own, ones, preferred_element_type=F32)
            pick = jnp.where(entry_of == axis * 32 + column_of, 1.0, 0.0).astype(BF16)
            moved = jnp.dot(flat, pick, preferred_element_type=F32)
            lanevec[h, axis:axis + 1, :] = jnp.sum(jnp.where(owner_of == source_of, moved, 0.0), axis=0, keepdims=True)

    @pl.loop(0, 2)
    def _(h):
        @pl.loop(0, BLOCK // 16)
        def _(t):
            rows = pl.ds(pl.multiple_of(t * 16, 16), 16)
            mine = [colbc[h, axis, rows, :] for axis in range(3)]
            for tile in range(4):
                lanes = slice(tile * 128, tile * 128 + 128)
                d = [mine[axis] - lanevec[h, axis:axis + 1, lanes] for axis in range(3)]
                squared = d[0] * d[0] + d[1] * d[1] + d[2] * d[2]
                squared = jnp.where(squared > 0.5, squared, 1e30)
                root = lax.rsqrt(squared)
                root = root * (1.5 - 0.5 * squared * (root * root))
                inverse = root * root
                prefactor = (0.75 * RADIUS) * root
                iso = prefactor * (1.0 + (2.0 / 3.0 * RADIUS * RADIUS) * inverse)
                along = (prefactor * inverse) * (1.0 - (2.0 * RADIUS * RADIUS) * inverse)
                s = [along * d[axis] for axis in range(3)]
                parts = (s[0] * d[0] + iso, s[0] * d[1], s[0] * d[2], s[1] * d[1] + iso, s[1] * d[2],
                         s[2] * d[2] + iso)
                for k, value in enumerate(parts):
                    high = value.astype(BF16)
                    mob[h, k, rows, lanes] = high
                    mob[h, k, rows, slice(BLOCK + tile * 128, BLOCK + tile * 128 + 128)] = (
                        value - high.astype(F32)).astype(BF16)

    def widen(step, h):
        base = jnp.where(core == 0, PLANE, h * 16)

        @pl.loop(0, 16)
        def _(s):
            for axis in range(3):
                value = ag[step, base + s, axis]
                other = turn(value)
                for j, both in enumerate((jnp.where(first, value, other), jnp.where(first, other, value))):
                    high = both.astype(BF16).astype(F32)
                    tile = jnp.where(first, high, both - high).astype(BF16)
                    for copy in range(2):
                        at = pl.ds(pl.multiple_of(copy * BLOCK + s * 32 + j * 16, 16), 16)
                        wide[h, at, axis * 128:axis * 128 + 128] = tile
                        if axis == 0:
                            wide[h, at, 384:512] = tile

    def group_of(t):
        d = jnp.where(t == 0, 2, jnp.where(t == 1, 1, jnp.where(t == 2, 3, 0)))
        return jnp.where(core == 0, lax.rem(x + d, 4), lax.rem(lax.div(z, 4) + 1 + lax.div(t, 2), 2))

    def product(t):
        group = group_of(t)
        h = jnp.where(core == 0, lax.div(group, 2), lax.rem(t, 2))
        rt = jnp.where(core == 0, lax.rem(group, 2), group)
        w = jnp.where(core == 0, 0, h)
        rows = pl.ds(pl.multiple_of(rt * 256, 256), 256)

        def dot(k, lo, hi):
            return jnp.dot(mob[h, k, rows, :], wide[w, :, lo:hi], preferred_element_type=F32)

        xy, yz, zx = dot(1, 0, 256), dot(4, 128, 384), dot(2, 256, 512)
        return (dot(0, 0, 128) + xy[:, 128:] + zx[:, :128],
                dot(3, 128, 256) + xy[:, :128] + yz[:, 128:],
                dot(5, 256, 384) + zx[:, 128:] + yz[:, :128])

    def pack(i, axis):
        low, high = acc[axis, i * 32:i * 32 + 16, :], acc[axis, i * 32 + 16:i * 32 + 32, :]
        return jnp.where(first, low + turn(low), high + turn(high))

    @pl.loop(0, ITERS)
    def _(step):
        last = step == 2

        @pl.when((core == 0) | last)
        def _():
            wait_recv(ag.at[step, pl.ds(0, LINE - 1)], ag_recv.at[step, 0])

        @pl.when((core == 1) | last)
        def _():
            wait_recv(ag.at[step, pl.ds(0, PLANE - 1)], ag_recv.at[step, 1])

        widen(step, 0)

        @pl.when(core == 1)
        def _():
            widen(step, 1)

        @pl.loop(0, 4)
        def _(t):
            more = (core == 1) & (lax.rem(t, 2) == 1) & (step < 2)
            for axis, value in enumerate(product(t)):
                acc[axis] = jnp.where(more, acc[axis], 0.0) + value
            group = group_of(t)

            @pl.when((step < 2) & ((core == 0) | (lax.rem(t, 2) == 1)))
            def _():
                for i in range(8):
                    for axis in range(3):
                        rs_send[step, group * 8 + i, axis] = pack(i, axis)
                slot = jnp.where(core == 0, chip, 16 + z)
                mine = jnp.where(core == 0, my_p, my_l)
                near = jnp.where(core == 0, y, lax.rem(z, 4))
                for d in (2, 1, 3, 0):
                    j = lax.rem(near + d, 4)
                    for c in range(2):
                        q = group * 8 + j * 2 + c
                        device = (jnp.where(core == 0, group, x) * 2 + c,
                                  jnp.where(core == 0, z * 4 + j, (group * 4 + j) * 4 + y))

                        def send(q=q, device=device):
                            remote(rs_send.at[step, q], rs.at[step, slot], rs_sent.at[step], rs_recv.at[step],
                                   device).start()

                        if d:
                            send()
                        else:
                            pl.when(q != mine)(send)

                            @pl.when(q == mine)
                            def _(q=q):
                                rs[step, slot] = rs_send[step, q]

            @pl.when(last)
            def _():
                at = jnp.where(core == 0, 0, PLANE) + group * 8
                total = part[...]
                for i in range(8):
                    for axis in range(3):
                        total = total + pack(i, axis) * ag[2, at + i, axis]
                part[...] = total

        @pl.when(step < 2)
        def _():
            wait_recv(rs.at[step, pl.ds(0, 23)], rs_recv.at[step])
            for axis in range(3):
                total = rs[step, 0, axis]
                for s in range(1, 16):
                    total = total + rs[step, s, axis]
                packed[step + 1, 0, axis] = total
                total = rs[step, 16, axis]
                for s in range(17, 24):
                    total = total + rs[step, s, axis]
                packed[step + 1, 1, axis] = total
            gather(step + 1)

    front = lax.broadcasted_iota(jnp.int32, (1, 128), 1) < HALF

    def fold(value):
        line = jnp.sum(value, axis=0, keepdims=True)
        return line + turn(line)

    def inner(left, right):
        sums = [sum(packed[left, half, axis] * packed[right, half, axis] for axis in range(3)) for half in range(2)]
        return jnp.where(front, fold(sums[0]), fold(sums[1]))

    for at, (left, right) in enumerate(((0, 0), (0, 1), (1, 1), (1, 2), (2, 2))):
        red_src[0, at:at + 1, :] = inner(left, right)
    red_src[0, 5:6, :] = jnp.where(front == (core == 0), fold(part[...]), 0.0)
    red_src[0, 6:8, :] = jnp.zeros((2, 128), F32)

    for dx, dy in PLANE_ORDER:
        remote(red_src.at[0], red_one.at[chip], red_sem.at[0], red_sem.at[1], plane_at(dx, dy, core)).start()
    red_one[chip] = red_src[0]
    wait_recv(red_one.at[pl.ds(0, 15)], red_sem.at[1])
    total = red_one[0]
    for s in range(1, 16):
        total = total + red_one[s]
    red_src[1] = total

    for dz in LINE_ORDER:
        for c in range(2):
            remote(red_src.at[1], red_two.at[my_l], red_sem.at[2], red_sem.at[3], line_at(dz, c)).start()
    remote(red_src.at[1], red_two.at[my_l], red_sem.at[2], red_sem.at[3], sibling).start()
    red_two[my_l] = red_src[1]
    wait_recv(red_two.at[pl.ds(0, 15)], red_sem.at[3])
    total = red_two[0]
    for s in range(1, 16):
        total = total + red_two[s]
    for k in range(6):
        moments[k] = jnp.broadcast_to(total[k:k + 1, :], (8, 128))
    moments[6] = jnp.zeros((8, 128), F32)
    moments[7] = jnp.ones((8, 128), F32)
    m0, m1, m2, m3, m4, m5, zero, one = (moments[k] for k in range(8))

    a1 = m1 / m0
    e1 = m2 - a1 * m1
    bb2 = e1 / m0
    a2 = (m3 - 2.0 * a1 * m2 + a1 * a1 * m1) / e1
    p, q = a1 + a2, a1 * a2 - bb2
    e2 = m4 - p * m3 + q * m2
    bb3 = e2 / e1
    a3 = (m5 - 2.0 * p * m4 + (p * p + 2.0 * q) * m3 - 2.0 * p * q * m2 + q * q * m1) / e2
    a1, a2, a3 = 1.0 + a1, 1.0 + a2, 1.0 + a3
    scale = (a1 + a2 + a3) / ITERS
    current = (a1 / scale, jnp.sqrt(bb2) / scale, zero, a2 / scale, jnp.sqrt(bb3) / scale, a3 / scale)
    partner = (one, zero, zero, one, zero, one)

    def inverse_three(m):
        c00, c01, c02 = m[3] * m[5] - m[4] * m[4], m[2] * m[4] - m[1] * m[5], m[1] * m[4] - m[2] * m[3]
        c11, c12, c22 = m[0] * m[5] - m[2] * m[2], m[1] * m[2] - m[0] * m[4], m[0] * m[3] - m[1] * m[1]
        over = 1.0 / (m[0] * c00 + m[1] * c01 + m[2] * c02)
        return tuple(c * over for c in (c00, c01, c02, c11, c12, c22))

    def newton(_, state):
        now, other = state
        return (tuple(0.5 * (u + v) for u, v in zip(now, inverse_three(other))),
                tuple(0.5 * (u + v) for u, v in zip(other, inverse_three(now))))

    current, partner = lax.fori_loop(0, 20, newton, (current, partner))
    size = jnp.sqrt(scale)
    beta = jnp.sqrt(m0)
    r1, r2, r3 = (current[k] * size for k in range(3))
    f2, f3 = beta * r2 / jnp.sqrt(e1), beta * r3 / jnp.sqrt(e2)
    c0 = r1 - f2 * (a1 - 1.0) + f3 * q
    c1 = f2 - f3 * p
    c0, c1, f3 = (jnp.concatenate([c, c], axis=0) for c in (c0, c1, f3))
    for axis in range(3):
        one_a, one_b = packed[1, 0, axis], packed[1, 1, axis]
        two_a, two_b = packed[2, 0, axis], packed[2, 1, axis]
        out_ref[axis, :16, :] = (c0 * z_ref[axis, :16, :] + c1 * jnp.where(first, one_a, turn(one_b))
                                 + f3 * jnp.where(first, two_a, turn(two_b)))
        out_ref[axis, 16:, :] = (c0 * z_ref[axis, 16:, :] + c1 * jnp.where(first, turn(one_a), one_b)
                                 + f3 * jnp.where(first, turn(two_a), two_b))

    wait_send(posbuf.at[pl.ds(0, 46)], pos_sem.at[1])
    wait_send(ag.at[0, pl.ds(0, 23)], ag_send.at[0])
    wait_send(ag.at[1, pl.ds(0, 23)], ag_send.at[1])
    wait_send(ag.at[2, pl.ds(0, 46)], ag_send.at[2])
    wait_send(red_one.at[pl.ds(0, 15)], red_sem.at[0])
    wait_send(red_two.at[pl.ds(0, 15)], red_sem.at[2])
    for step in range(2):
        @pl.when(core == 0)
        def _():
            wait_send(rs_send.at[step, pl.ds(0, PLANE - 1)], rs_sent.at[step])

        @pl.when(core == 1)
        def _():
            wait_send(rs_send.at[step, pl.ds(0, LINE - 1)], rs_sent.at[step])


def shards(positions, start_vector):
    chunk = (3, 16, 128)
    vmem = pl.BlockSpec(memory_space=pltpu.VMEM)
    return pl.pallas_call(
        kernel,
        out_shape=jax.ShapeDtypeStruct(start_vector.shape, F32),
        in_specs=[vmem, pl.BlockSpec(memory_space=pl.ANY)],
        out_specs=vmem,
        scratch_shapes=[
            pltpu.VMEM((PLANE + LINE, 1, 128), F32),
            pltpu.VMEM((2, 3, BLOCK, 128), F32),
            pltpu.VMEM((2, 8, BLOCK), F32),
            pltpu.VMEM((2, 6, BLOCK, 2 * BLOCK), BF16),
            pltpu.VMEM((2, 2 * BLOCK, 512), BF16),
            pltpu.VMEM((3, PLANE + LINE) + chunk, F32),
            pltpu.VMEM((2, 24) + chunk, F32),
            pltpu.VMEM((2, PLANE) + chunk, F32),
            pltpu.VMEM((3, 2) + chunk, F32),
            pltpu.VMEM((3, 256, 128), F32),
            pltpu.VMEM((16, 128), F32),
            pltpu.VMEM((2, 8, 128), F32),
            pltpu.VMEM((16, 8, 128), F32),
            pltpu.VMEM((16, 8, 128), F32),
            pltpu.VMEM((8, 8, 128), F32),
            pltpu.VMEM((8, 128), F32),
            pltpu.VMEM((3, 32, 128), F32),
            pltpu.SemaphoreType.DMA(()),
            pltpu.SemaphoreType.DMA((2,)),
            pltpu.SemaphoreType.DMA((3, 2)),
            pltpu.SemaphoreType.DMA((3,)),
            pltpu.SemaphoreType.DMA((2,)),
            pltpu.SemaphoreType.DMA((2,)),
            pltpu.SemaphoreType.DMA((4,)),
        ],
        compiler_params=pltpu.CompilerParams(
            collective_id=0, has_side_effects=True, vmem_limit_bytes=40 * 1024 * 1024),
    )(positions, start_vector)


def solution(mesh):
    in_specs = (P(None, ("row", "col")), P(None, ("row", "col"), None))
    out_specs = P(None, ("row", "col"), None)
    return jax.shard_map(shards, mesh=mesh, in_specs=in_specs, out_specs=out_specs, check_vma=False)
```

```python
import jax
import jax.numpy as jnp
from jax import lax
from jax.experimental import pallas as pl
from jax.experimental.pallas import tpu as pltpu
from jax.sharding import PartitionSpec as P

ITERS = 3
RADIUS = 0.4
MESH = pl.DeviceIdType.MESH
F32 = jnp.float32
BF16 = jnp.bfloat16

PLANE, LINE = 32, 16
LINE_ORDER = (4, 3, 5, 2, 6, 1, 7)
PLANE_ORDER = ((2, 2), (1, 2), (2, 1), (3, 2), (2, 3), (1, 1), (3, 3), (1, 3), (3, 1), (2, 0), (0, 2),
               (1, 0), (0, 1), (3, 0), (0, 3))
ORDER = [item for n, spot in enumerate(PLANE_ORDER) for item in
         ([("line", LINE_ORDER[n // 2])] if n % 2 == 0 and n < 14 else []) + [("plane", spot)]]
HALF = 64
BLOCK = 512


def kernel(pos_hbm, z_hbm, out_ref, posbuf, colbc, lanevec, mob_high, mob_low, wide, narrow, ag, rs, rs_send, packed,
           first_dir, acc, acc_wide, part, red_src, red_one, red_two, moments, pos_ref, flatten, z_ref, load_sem, pos_sem, ag_recv, ag_send, rs_recv, rs_sent, red_sem):
    row, col = lax.axis_index("row"), lax.axis_index("col")
    x, core = lax.div(row, 2), lax.rem(row, 2)
    z, y = lax.div(col, 4), lax.rem(col, 4)
    chip = x * 4 + y
    my_p, my_l = chip * 2 + core, z * 2 + core

    xs = [lax.rem(x + d, 4) for d in range(4)]
    ys = [lax.rem(y + d, 4) for d in range(4)]
    zs = [lax.rem(z + d, 8) for d in range(8)]

    def plane_at(dx, dy, c):
        return (xs[dx] * 2 + c, z * 4 + ys[dy])

    def line_at(dz, c):
        return (x * 2 + c, zs[dz] * 4 + y)

    sibling = (x * 2 + 1 - core, col)

    def remote(src, dst, send, recv, device):
        return pltpu.make_async_remote_copy(
            src_ref=src, dst_ref=dst, send_sem=send, recv_sem=recv, device_id=device, device_id_type=MESH)

    def wait_recv(ref, sem):
        remote(ref, ref, sem, sem, (row, col)).wait_recv()

    def wait_send(ref, sem):
        remote(ref, ref, sem, sem, (row, col)).wait_send()

    first = lax.broadcasted_iota(jnp.int32, (16, 128), 1) < HALF

    def turn(value):
        return pltpu.roll(value, HALF, 1)

    barrier = pltpu.get_barrier_semaphore()

    def signal(device):
        pl.semaphore_signal(barrier, inc=1, device_id=device, device_id_type=MESH)

    signal(sibling)
    for c in range(2):
        for dz in LINE_ORDER:
            signal(line_at(dz, c))
        for dx, dy in PLANE_ORDER:
            signal(plane_at(dx, dy, c))

    load_pos = pltpu.make_async_copy(pos_hbm, pos_ref, load_sem.at[0])
    load_pos.start()
    load_z = pltpu.make_async_copy(z_hbm, z_ref, load_sem.at[1])
    load_z.start()
    flatten[...] = jnp.zeros_like(flatten)
    narrow[...] = jnp.zeros_like(narrow)
    load_pos.wait()
    flatten[0:3, 0:32] = pos_ref[...].astype(F32)
    rows3 = flatten[...]
    flatten[0:1, :] = rows3[0:1] + pltpu.roll(rows3[1:2], 32, 1) + pltpu.roll(rows3[2:3], 64, 1)
    posbuf[my_p] = flatten[0:1, :]
    posbuf[PLANE + my_l] = flatten[0:1, :]
    load_z.wait()
    for axis in range(3):
        low, high = z_ref[axis, :16, :], z_ref[axis, 16:, :]
        packed[0, 0, axis] = jnp.where(first, low, turn(high))
        packed[0, 1, axis] = jnp.where(first, turn(low), high)
    pl.semaphore_wait(barrier, 45)

    def send_place(slot, device):
        remote(posbuf.at[slot], posbuf.at[slot], pos_sem.at[1], pos_sem.at[0], device).start()

    for kind, offset in ORDER:
        for c in range(2):
            if kind == "line":
                send_place(PLANE + my_l, line_at(offset, c))
            else:
                send_place(my_p, plane_at(*offset, c))
    send_place(PLANE + my_l, sibling)
    send_place(my_p, sibling)

    def gather(step):
        def send(half, which, device):
            slot = PLANE + my_l if which == 0 else my_p
            remote(packed.at[step, half], ag.at[step, slot], ag_send.at[step], ag_recv.at[step, which],
                   device).start()

        def send_sibling(which):
            slot = jnp.where(which == 0, PLANE + my_l, my_p)
            remote(packed.at[step, 1 - core], ag.at[step, slot], ag_send.at[step], ag_recv.at[step, which],
                   sibling).start()

        for kind, offset in ORDER:
            if kind == "line":
                send(0, 0, line_at(offset, 0))
            else:
                send(1, 1, plane_at(*offset, 1))
        send_sibling(1 - core)
        ag[step, my_p] = packed[step, core]
        ag[step, PLANE + my_l] = packed[step, core]

        @pl.when(step == 2)
        def _():
            for kind, offset in ORDER:
                if kind == "line":
                    send(1, 0, line_at(offset, 1))
                else:
                    send(0, 1, plane_at(*offset, 0))
            send_sibling(core)

    gather(0)
    acc[...] = jnp.zeros_like(acc)
    acc_wide[...] = jnp.zeros_like(acc_wide)
    for k in range(2):
        red_src[2 * k] = jnp.zeros((1, 512), F32)
    part[...] = jnp.zeros_like(part)
    wait_recv(posbuf.at[pl.ds(0, 46)], pos_sem.at[0])

    lane_of = lax.broadcasted_iota(jnp.int32, (BLOCK, 128), 1)
    bead_of = lax.broadcasted_iota(jnp.int32, (BLOCK, 128), 0) & 31
    entry_of = lax.broadcasted_iota(jnp.int32, (128, BLOCK), 0)
    column_of = lax.broadcasted_iota(jnp.int32, (128, BLOCK), 1) & 31
    owner_of = lax.broadcasted_iota(jnp.int32, (16, BLOCK), 1) >> 5
    source_of = lax.broadcasted_iota(jnp.int32, (16, BLOCK), 0)
    ones = jnp.ones((128, 128), BF16)

    @pl.loop(0, 2)
    def _(h):
        rows_at = jnp.where(core == 0, h, 2) * 16
        lanes_at = jnp.where(core == 0, 2, h) * 16
        spread = jnp.concatenate([jnp.broadcast_to(posbuf[rows_at + d], (32, 128)) for d in range(16)], axis=0)
        flat = jnp.concatenate([posbuf[lanes_at + d] for d in range(16)], axis=0).astype(BF16)
        for axis in range(3):
            own = jnp.where(lane_of == axis * 32 + bead_of, spread, 0.0).astype(BF16)
            colbc[h, axis] = jnp.dot(own, ones, preferred_element_type=F32)
            pick = jnp.where(entry_of == axis * 32 + column_of, 1.0, 0.0).astype(BF16)
            moved = jnp.dot(flat, pick, preferred_element_type=F32)
            lanevec[h, axis:axis + 1, :] = jnp.sum(jnp.where(owner_of == source_of, moved, 0.0), axis=0, keepdims=True)

    @pl.loop(0, 2)
    def _(h):
        @pl.loop(0, BLOCK // 16)
        def _(t):
            rows = pl.ds(pl.multiple_of(t * 16, 16), 16)
            mine = [colbc[h, axis, rows, :] for axis in range(3)]
            for tile in range(4):
                lanes = slice(tile * 128, tile * 128 + 128)
                d = [mine[axis] - lanevec[h, axis:axis + 1, lanes] for axis in range(3)]
                squared = d[0] * d[0] + d[1] * d[1] + d[2] * d[2]
                squared = jnp.where(squared > 0.5, squared, 1e30)
                root = lax.rsqrt(squared)
                root = root * (1.5 - 0.5 * squared * (root * root))
                inverse = root * root
                prefactor = (0.75 * RADIUS) * root
                iso = prefactor * (1.0 + (2.0 / 3.0 * RADIUS * RADIUS) * inverse)
                along = (prefactor * inverse) * (1.0 - (2.0 * RADIUS * RADIUS) * inverse)
                s = [along * d[axis] for axis in range(3)]
                parts = (s[0] * d[0] + iso, s[0] * d[1], s[0] * d[2], s[1] * d[1] + iso, s[1] * d[2],
                         s[2] * d[2] + iso)
                for k, value in enumerate(parts):
                    high = value.astype(BF16)
                    at = slice(k * BLOCK + tile * 128, k * BLOCK + tile * 128 + 128)
                    mob_high[h, rows, at] = high
                    mob_low[h, rows, at] = (value - high.astype(F32)).astype(BF16)

    def widen(h):
        base = jnp.where(core == 0, PLANE, h * 16)

        @pl.loop(0, 16, unroll=2)
        def _(s):
            for axis in range(3):
                value = ag[0, base + s, axis]
                other = turn(value)
                for j, both in enumerate((jnp.where(first, value, other), jnp.where(first, other, value))):
                    high = both.astype(BF16).astype(F32)
                    tile = jnp.where(first, high, both - high).astype(BF16)
                    at = pl.ds(pl.multiple_of(s * 32 + j * 16, 16), 16)
                    wide[h, at, axis * 128:axis * 128 + 128] = tile
                    if axis == 0:
                        wide[h, at, 384:512] = tile

    def arrange(step, h):
        base = jnp.where(core == 0, PLANE, h * 16)

        @pl.loop(0, 16, unroll=2)
        def _(s):
            values = [ag[step, base + s, axis] for axis in range(3)]
            others = [turn(value) for value in values]
            for j in range(2):
                left, right = (values, others) if j == 0 else (others, values)
                lx, ly, lz = (jnp.where(first, v, 0.0).astype(BF16) for v in left)
                ry, rz = (jnp.where(first, 0.0, v).astype(BF16) for v in right[1:])
                yx = jnp.where(first, left[1], right[0]).astype(BF16)
                for k, half, tile in ((0, 0, lx), (1, 0, yx), (2, 0, lz), (2, 1, lx), (3, 0, ry), (4, 0, rz),
                                      (4, 1, ly), (5, 1, lz)):
                    at = pl.ds(pl.multiple_of(k * BLOCK + s * 32 + j * 16, 16), 16)
                    narrow[h, at, half * 128:half * 128 + 128] = tile

    def group_of(t):
        d = jnp.where(t == 0, 2, jnp.where(t == 1, 1, jnp.where(t == 2, 3, 0)))
        return jnp.where(core == 0, lax.rem(x + d, 4), lax.rem(lax.div(z, 4) + 1 + lax.div(t, 2), 2))

    def places(t, group):
        h = jnp.where(core == 0, lax.div(group, 2), lax.rem(t, 2))
        rt = jnp.where(core == 0, lax.rem(group, 2), group)
        return h, jnp.where(core == 0, 0, h), pl.ds(pl.multiple_of(rt * 256, 256), 256)

    def dot(left, right):
        return jnp.dot(left, right, preferred_element_type=F32)

    def product(t, group):
        h, w, rows = places(t, group)

        def both(k, lo, hi):
            at = slice(k * BLOCK, k * BLOCK + BLOCK)
            return dot(mob_high[h, rows, at], wide[w, :, lo:hi]) + dot(mob_low[h, rows, at], wide[w, :, lo:hi])

        xy, yz, zx = both(1, 0, 256), both(4, 128, 384), both(2, 256, 512)
        return (both(0, 0, 128) + xy[:, 128:] + zx[:, :128],
                both(3, 128, 256) + xy[:, :128] + yz[:, 128:],
                both(5, 256, 384) + zx[:, 128:] + yz[:, :128])

    def pack(i):
        chunk = []
        for axis in range(3):
            low, high = acc[axis, i * 32:i * 32 + 16, :], acc[axis, i * 32 + 16:i * 32 + 32, :]
            chunk.append(jnp.where(first, low + turn(low), high + turn(high)))
        return chunk

    def pack_wide(i):
        low, high = slice(i * 32, i * 32 + 16), slice(i * 32 + 16, i * 32 + 32)
        xy_low, xy_high = acc_wide[low, :128], acc_wide[high, :128]
        z_low, z_high = acc_wide[low, 128:], acc_wide[high, 128:]
        return (jnp.where(first, xy_low, turn(xy_high)), jnp.where(first, turn(xy_low), xy_high),
                jnp.where(first, z_low, turn(z_high)))

    def scatter(step, group, packer):
        for i in range(8):
            for axis, value in enumerate(packer(i)):
                rs_send[step, group * 8 + i, axis] = value
        slot = jnp.where(core == 0, chip, 16 + z)
        mine = jnp.where(core == 0, my_p, my_l)
        near = jnp.where(core == 0, y, lax.rem(z, 4))
        for d in (2, 1, 3, 0):
            j = lax.rem(near + d, 4)
            for c in range(2):
                q = group * 8 + j * 2 + c
                device = (jnp.where(core == 0, group, x) * 2 + c,
                          jnp.where(core == 0, z * 4 + j, (group * 4 + j) * 4 + y))

                def send(q=q, device=device):
                    remote(rs_send.at[step, q], rs.at[step, slot], rs_sent.at[step], rs_recv.at[step], device).start()

                if d:
                    send()
                else:
                    pl.when(q != mine)(send)

                    @pl.when(q == mine)
                    def _(q=q):
                        rs[step, slot] = rs_send[step, q]

    def collect(step, half, axis):
        span = range(16) if half == 0 else range(16, 24)
        return sum((rs[step, s, axis] for s in span[1:]), rs[step, span[0], axis])

    def wait_vector(step):
        @pl.when(core == 0)
        def _():
            wait_recv(ag.at[step, pl.ds(0, LINE - 1)], ag_recv.at[step, 0])

        @pl.when(core == 1)
        def _():
            wait_recv(ag.at[step, pl.ds(0, PLANE - 1)], ag_recv.at[step, 1])

    front = lax.broadcasted_iota(jnp.int32, (1, 128), 1) < HALF

    def fold(value):
        line = jnp.sum(value, axis=0, keepdims=True)
        return line + turn(line)

    def inner(left, right):
        sums = [sum(left[half, axis] * right[half, axis] for axis in range(3)) for half in range(2)]
        return jnp.where(front, fold(sums[0]), fold(sums[1]))

    def reduce_plane(k, values):
        for n, value in enumerate(values):
            red_src[2 * k, :, n * 128:n * 128 + 128] = value
        for dx, dy in PLANE_ORDER:
            remote(red_src.at[2 * k], red_one.at[k, chip], red_sem.at[k, 0], red_sem.at[k, 1],
                   plane_at(dx, dy, core)).start()
        red_one[k, chip] = red_src[2 * k]

    def reduce_line(k):
        wait_recv(red_one.at[k, pl.ds(0, 15)], red_sem.at[k, 1])
        red_src[2 * k + 1] = sum((red_one[k, s] for s in range(1, 16)), red_one[k, 0])
        for dz in LINE_ORDER:
            for c in range(2):
                remote(red_src.at[2 * k + 1], red_two.at[k, my_l], red_sem.at[k, 2], red_sem.at[k, 3],
                       line_at(dz, c)).start()
        remote(red_src.at[2 * k + 1], red_two.at[k, my_l], red_sem.at[k, 2], red_sem.at[k, 3], sibling).start()
        red_two[k, my_l] = red_src[2 * k + 1]

    def reduced(k, count):
        wait_recv(red_two.at[k, pl.ds(0, 15)], red_sem.at[k, 3])
        total = sum((red_two[k, s] for s in range(1, 16)), red_two[k, 0])
        return [total[:, n * 128:n * 128 + 128] for n in range(count)]

    wait_vector(0)
    widen(0)

    @pl.when(core == 1)
    def _():
        widen(1)

    @pl.loop(0, 4)
    def _(t):
        group = group_of(t)
        more = (core == 1) & (lax.rem(t, 2) == 1)
        for axis, value in enumerate(product(t, group)):
            acc[axis] = jnp.where(more, acc[axis], 0.0) + value

        @pl.when((core == 0) | (lax.rem(t, 2) == 1))
        def _():
            scatter(0, group, pack)

    wait_recv(rs.at[0, pl.ds(0, 23)], rs_recv.at[0])
    for axis in range(3):
        for half in range(2):
            packed[1, half, axis] = collect(0, half, axis)
    gather(1)
    reduce_plane(0, (inner(packed.at[0], packed.at[0]), inner(packed.at[0], packed.at[1])))

    @pl.loop(1, ITERS)
    def _(step):
        wait_vector(step)
        arrange(step, 0)

        @pl.when(core == 1)
        def _():
            arrange(step, 1)

        @pl.loop(0, 4)
        def _(t):
            group = group_of(t)
            h, w, rows = places(t, group)
            more = (core == 1) & (lax.rem(t, 2) == 1) & (step == 1)
            acc_wide[...] = jnp.where(more, acc_wide[...], 0.0) + dot(mob_high[h, rows, :], narrow[w])

            @pl.when((step == 1) & ((core == 0) | (lax.rem(t, 2) == 1)))
            def _():
                scatter(1, group, pack_wide)

            @pl.when(step == 2)
            def _():
                @pl.when((t == 0) & (core == 0))
                def _():
                    wait_recv(ag.at[2, pl.ds(0, PLANE - 1)], ag_recv.at[2, 1])

                @pl.when((t == 0) & (core == 1))
                def _():
                    wait_recv(ag.at[2, pl.ds(0, LINE - 1)], ag_recv.at[2, 0])

                at = jnp.where(core == 0, 0, PLANE) + group * 8
                total = part[...]
                for i in range(8):
                    for axis, value in enumerate(pack_wide(i)):
                        total = total + value * ag[2, at + i, axis]
                part[...] = total

        @pl.when(step == 1)
        def _():
            reduce_line(0)
            wait_recv(rs.at[1, pl.ds(0, 23)], rs_recv.at[1])
            m0, m1 = reduced(0, 2)
            moments[0] = jnp.broadcast_to(m0, (8, 128))
            moments[1] = jnp.broadcast_to(m1, (8, 128))
            a1 = moments[1] / moments[0]
            a1 = jnp.concatenate([a1, a1], axis=0)
            for half, here in enumerate((jnp.where(first, a1, turn(a1)), jnp.where(first, turn(a1), a1))):
                for axis in range(3):
                    y1 = packed[1, half, axis]
                    packed[2, half, axis] = collect(1, half, axis) - here * y1
                    first_dir[half, axis] = y1 - here * packed[0, half, axis]
            gather(2)

    reduce_plane(1, (inner(first_dir, first_dir), inner(first_dir, packed.at[2]), inner(packed.at[2], packed.at[2]),
                     jnp.where(front == (core == 0), fold(part[...]), 0.0)))
    reduce_line(1)
    for k, value in enumerate(reduced(1, 4)):
        moments[2 + k] = jnp.broadcast_to(value, (8, 128))
    moments[6] = jnp.zeros((8, 128), F32)
    moments[7] = jnp.ones((8, 128), F32)
    m0, m1, e1, f1, g, third, zero, one = (moments[k] for k in range(8))

    a1, a2, bb2 = m1 / m0, f1 / e1, e1 / m0
    e2 = g - a2 * f1 - bb2 * e1
    bb3 = e2 / e1
    a3 = (third - a2 * g - bb2 * (f1 + a1 * e1)) / e2 - a2
    d1, d2, d3 = 1.0 + a1, 1.0 + a2, 1.0 + a3
    scale = (d1 + d2 + d3) / ITERS
    current = (d1 / scale, jnp.sqrt(bb2) / scale, zero, d2 / scale, jnp.sqrt(bb3) / scale, d3 / scale)
    partner = (one, zero, zero, one, zero, one)

    def inverse_three(m):
        c00, c01, c02 = m[3] * m[5] - m[4] * m[4], m[2] * m[4] - m[1] * m[5], m[1] * m[4] - m[2] * m[3]
        c11, c12, c22 = m[0] * m[5] - m[2] * m[2], m[1] * m[2] - m[0] * m[4], m[0] * m[3] - m[1] * m[1]
        over = 1.0 / (m[0] * c00 + m[1] * c01 + m[2] * c02)
        return tuple(c * over for c in (c00, c01, c02, c11, c12, c22))

    def newton(_, state):
        now, other = state
        return (tuple(0.5 * (u + v) for u, v in zip(now, inverse_three(other))),
                tuple(0.5 * (u + v) for u, v in zip(other, inverse_three(now))))

    current, partner = lax.fori_loop(0, 20, newton, (current, partner))
    size = jnp.sqrt(scale)
    beta = jnp.sqrt(m0)
    r1, r2, r3 = (current[k] * size for k in range(3))
    f2, f3 = beta * r2 / jnp.sqrt(e1), beta * r3 / jnp.sqrt(e2)
    c0, c1, c2 = (jnp.concatenate([c, c], axis=0) for c in (r1 - f3 * bb2, f2 - f3 * a2, f3))
    for axis in range(3):
        w_a, w_b, u_a, u_b = first_dir[0, axis], first_dir[1, axis], packed[2, 0, axis], packed[2, 1, axis]
        out_ref[axis, :16, :] = (c0 * z_ref[axis, :16, :] + c1 * jnp.where(first, w_a, turn(w_b))
                                 + c2 * jnp.where(first, u_a, turn(u_b)))
        out_ref[axis, 16:, :] = (c0 * z_ref[axis, 16:, :] + c1 * jnp.where(first, turn(w_a), w_b)
                                 + c2 * jnp.where(first, turn(u_a), u_b))

    wait_send(posbuf.at[pl.ds(0, 46)], pos_sem.at[1])
    wait_send(ag.at[0, pl.ds(0, 23)], ag_send.at[0])
    wait_send(ag.at[1, pl.ds(0, 23)], ag_send.at[1])
    wait_send(ag.at[2, pl.ds(0, 46)], ag_send.at[2])
    for k in range(2):
        wait_send(red_one.at[k, pl.ds(0, 15)], red_sem.at[k, 0])
        wait_send(red_two.at[k, pl.ds(0, 15)], red_sem.at[k, 2])
    for step in range(2):
        @pl.when(core == 0)
        def _():
            wait_send(rs_send.at[step, pl.ds(0, PLANE - 1)], rs_sent.at[step])

        @pl.when(core == 1)
        def _():
            wait_send(rs_send.at[step, pl.ds(0, LINE - 1)], rs_sent.at[step])


def shards(positions, start_vector):
    chunk = (3, 16, 128)
    return pl.pallas_call(
        kernel,
        out_shape=jax.ShapeDtypeStruct(start_vector.shape, F32),
        in_specs=[pl.BlockSpec(memory_space=pl.ANY)] * 2,
        out_specs=pl.BlockSpec(memory_space=pltpu.VMEM),
        scratch_shapes=[
            pltpu.VMEM((PLANE + LINE, 1, 128), F32),
            pltpu.VMEM((2, 3, BLOCK, 128), F32),
            pltpu.VMEM((2, 8, BLOCK), F32),
            pltpu.VMEM((2, BLOCK, 6 * BLOCK), BF16),
            pltpu.VMEM((2, BLOCK, 6 * BLOCK), BF16),
            pltpu.VMEM((2, BLOCK, 512), BF16),
            pltpu.VMEM((2, 6 * BLOCK, 256), BF16),
            pltpu.VMEM((3, PLANE + LINE) + chunk, F32),
            pltpu.VMEM((2, 24) + chunk, F32),
            pltpu.VMEM((2, PLANE) + chunk, F32),
            pltpu.VMEM((3, 2) + chunk, F32),
            pltpu.VMEM((2,) + chunk, F32),
            pltpu.VMEM((3, 256, 128), F32),
            pltpu.VMEM((256, 256), F32),
            pltpu.VMEM((16, 128), F32),
            pltpu.VMEM((4, 1, 512), F32),
            pltpu.VMEM((2, 16, 1, 512), F32),
            pltpu.VMEM((2, 16, 1, 512), F32),
            pltpu.VMEM((8, 8, 128), F32),
            pltpu.VMEM((3, 32), jnp.int32),
            pltpu.VMEM((8, 128), F32),
            pltpu.VMEM((3, 32, 128), F32),
            pltpu.SemaphoreType.DMA((2,)),
            pltpu.SemaphoreType.DMA((2,)),
            pltpu.SemaphoreType.DMA((3, 2)),
            pltpu.SemaphoreType.DMA((3,)),
            pltpu.SemaphoreType.DMA((2,)),
            pltpu.SemaphoreType.DMA((2,)),
            pltpu.SemaphoreType.DMA((2, 4)),
        ],
        compiler_params=pltpu.CompilerParams(
            collective_id=0, has_side_effects=True, vmem_limit_bytes=40 * 1024 * 1024),
    )(positions, start_vector)


def solution(mesh):
    in_specs = (P(None, ("row", "col")), P(None, ("row", "col"), None))
    out_specs = P(None, ("row", "col"), None)
    return jax.shard_map(shards, mesh=mesh, in_specs=in_specs, out_specs=out_specs, check_vma=False)
```

```python
import jax
import jax.numpy as jnp
from jax import lax
from jax.experimental import pallas as pl
from jax.experimental.pallas import tpu as pltpu
from jax.sharding import PartitionSpec as P

ITERS = 3
RADIUS = 0.4
MESH = pl.DeviceIdType.MESH
F32 = jnp.float32
BF16 = jnp.bfloat16

PLANE, LINE = 32, 16
LINE_ORDER = (4, 3, 5, 2, 6, 1, 7)
PLANE_ORDER = ((2, 2), (1, 2), (2, 1), (3, 2), (2, 3), (1, 1), (3, 3), (1, 3), (3, 1), (2, 0), (0, 2),
               (1, 0), (0, 1), (3, 0), (0, 3))
ORDER = [item for n, spot in enumerate(PLANE_ORDER) for item in
         ([("line", LINE_ORDER[n // 2])] if n % 2 == 0 and n < 14 else []) + [("plane", spot)]]
HALF = 64
BLOCK = 512


def kernel(pos_hbm, z_hbm, out_ref, posbuf, colbc, lanevec, mob_high, mob_low, wide, narrow, ag, rs, rs_send, packed,
           first_dir, acc, acc_wide, part, red_src, red_one, red_two, moments, pos_ref, flatten, z_ref, load_sem, pos_sem, ag_recv, ag_send, rs_recv, rs_sent, red_sem):
    row, col = lax.axis_index("row"), lax.axis_index("col")
    x, core = lax.div(row, 2), lax.rem(row, 2)
    z, y = lax.div(col, 4), lax.rem(col, 4)
    chip = x * 4 + y
    my_p, my_l = chip * 2 + core, z * 2 + core

    xs = [lax.rem(x + d, 4) for d in range(4)]
    ys = [lax.rem(y + d, 4) for d in range(4)]
    zs = [lax.rem(z + d, 8) for d in range(8)]

    def plane_at(dx, dy, c):
        return (xs[dx] * 2 + c, z * 4 + ys[dy])

    def line_at(dz, c):
        return (x * 2 + c, zs[dz] * 4 + y)

    sibling = (x * 2 + 1 - core, col)

    def remote(src, dst, send, recv, device):
        return pltpu.make_async_remote_copy(
            src_ref=src, dst_ref=dst, send_sem=send, recv_sem=recv, device_id=device, device_id_type=MESH)

    def wait_recv(ref, sem):
        remote(ref, ref, sem, sem, (row, col)).wait_recv()

    def wait_send(ref, sem):
        remote(ref, ref, sem, sem, (row, col)).wait_send()

    first = lax.broadcasted_iota(jnp.int32, (16, 128), 1) < HALF

    def turn(value):
        return pltpu.roll(value, HALF, 1)

    barrier = pltpu.get_barrier_semaphore()

    def signal(device):
        pl.semaphore_signal(barrier, inc=1, device_id=device, device_id_type=MESH)

    signal(sibling)
    for c in range(2):
        for dz in LINE_ORDER:
            signal(line_at(dz, c))
        for dx, dy in PLANE_ORDER:
            signal(plane_at(dx, dy, c))

    load_pos = pltpu.make_async_copy(pos_hbm, pos_ref, load_sem.at[0])
    load_pos.start()
    load_z = pltpu.make_async_copy(z_hbm, z_ref, load_sem.at[1])
    load_z.start()
    flatten[...] = jnp.zeros_like(flatten)
    narrow[...] = jnp.zeros_like(narrow)
    load_pos.wait()
    flatten[0:3, 0:32] = pos_ref[...].astype(F32)
    rows3 = flatten[...]
    flatten[0:1, :] = rows3[0:1] + pltpu.roll(rows3[1:2], 32, 1) + pltpu.roll(rows3[2:3], 64, 1)
    posbuf[my_p] = flatten[0:1, :]
    posbuf[PLANE + my_l] = flatten[0:1, :]
    load_z.wait()
    for axis in range(3):
        low, high = z_ref[axis, :16, :], z_ref[axis, 16:, :]
        packed[0, 0, axis] = jnp.where(first, low, turn(high))
        packed[0, 1, axis] = jnp.where(first, turn(low), high)
    pl.semaphore_wait(barrier, 45)

    def send_place(slot, device):
        remote(posbuf.at[slot], posbuf.at[slot], pos_sem.at[1], pos_sem.at[0], device).start()

    for kind, offset in ORDER:
        for c in range(2):
            if kind == "line":
                send_place(PLANE + my_l, line_at(offset, c))
            else:
                send_place(my_p, plane_at(*offset, c))
    send_place(PLANE + my_l, sibling)
    send_place(my_p, sibling)

    def gather(step):
        def send(half, which, device):
            slot = PLANE + my_l if which == 0 else my_p
            remote(packed.at[step, half], ag.at[step, slot], ag_send.at[step], ag_recv.at[step, which],
                   device).start()

        def send_sibling(which):
            slot = jnp.where(which == 0, PLANE + my_l, my_p)
            remote(packed.at[step, 1 - core], ag.at[step, slot], ag_send.at[step], ag_recv.at[step, which],
                   sibling).start()

        for kind, offset in ORDER:
            if kind == "line":
                send(0, 0, line_at(offset, 0))
            else:
                send(1, 1, plane_at(*offset, 1))
        send_sibling(1 - core)
        ag[step, my_p] = packed[step, core]
        ag[step, PLANE + my_l] = packed[step, core]

        @pl.when(step == 2)
        def _():
            for kind, offset in ORDER:
                if kind == "line":
                    send(1, 0, line_at(offset, 1))
                else:
                    send(0, 1, plane_at(*offset, 0))
            send_sibling(core)

    gather(0)
    acc[...] = jnp.zeros_like(acc)
    acc_wide[...] = jnp.zeros_like(acc_wide)
    for k in range(2):
        red_src[2 * k] = jnp.zeros((1, 512), F32)
    part[...] = jnp.zeros_like(part)
    wait_recv(posbuf.at[pl.ds(0, 46)], pos_sem.at[0])

    lane_of = lax.broadcasted_iota(jnp.int32, (BLOCK, 128), 1)
    bead_of = lax.broadcasted_iota(jnp.int32, (BLOCK, 128), 0) & 31
    entry_of = lax.broadcasted_iota(jnp.int32, (128, BLOCK), 0)
    column_of = lax.broadcasted_iota(jnp.int32, (128, BLOCK), 1) & 31
    owner_of = lax.broadcasted_iota(jnp.int32, (16, BLOCK), 1) >> 5
    source_of = lax.broadcasted_iota(jnp.int32, (16, BLOCK), 0)
    ones = jnp.ones((128, 128), BF16)

    @pl.loop(0, 2)
    def _(h):
        rows_at = jnp.where(core == 0, h, 2) * 16
        lanes_at = jnp.where(core == 0, 2, h) * 16
        spread = jnp.concatenate([jnp.broadcast_to(posbuf[rows_at + d], (32, 128)) for d in range(16)], axis=0)
        flat = jnp.concatenate([posbuf[lanes_at + d] for d in range(16)], axis=0).astype(BF16)
        for axis in range(3):
            own = jnp.where(lane_of == axis * 32 + bead_of, spread, 0.0).astype(BF16)
            colbc[h, axis] = jnp.dot(own, ones, preferred_element_type=F32)
            pick = jnp.where(entry_of == axis * 32 + column_of, 1.0, 0.0).astype(BF16)
            moved = jnp.dot(flat, pick, preferred_element_type=F32)
            lanevec[h, axis:axis + 1, :] = jnp.sum(jnp.where(owner_of == source_of, moved, 0.0), axis=0, keepdims=True)

    def group_of(t):
        d = jnp.where(t == 0, 2, jnp.where(t == 1, 1, jnp.where(t == 2, 3, 0)))
        return jnp.where(core == 0, lax.rem(x + d, 4), lax.rem(lax.div(z, 4) + 1 + lax.div(t, 2), 2))

    def places(t, group):
        h = jnp.where(core == 0, lax.div(group, 2), lax.rem(t, 2))
        rt = jnp.where(core == 0, lax.rem(group, 2), group)
        return h, jnp.where(core == 0, 0, h), pl.ds(pl.multiple_of(rt * 256, 256), 256)

    def build(t):
        h, _, span = places(t, group_of(t))

        @pl.loop(0, 16, unroll=2)
        def _(r):
            rows = pl.ds(pl.multiple_of(span.start + r * 16, 16), 16)
            mine = [colbc[h, axis, rows, :] for axis in range(3)]
            for tile in range(4):
                lanes = slice(tile * 128, tile * 128 + 128)
                d = [mine[axis] - lanevec[h, axis:axis + 1, lanes] for axis in range(3)]
                squared = d[0] * d[0] + d[1] * d[1] + d[2] * d[2]
                root = lax.rsqrt(jnp.where(squared > 0.5, squared, 1e30))
                inverse = root * root
                prefactor = (0.75 * RADIUS) * root
                iso = prefactor * (1.0 + (2.0 / 3.0 * RADIUS * RADIUS) * inverse)
                along = (prefactor * inverse) * (1.0 - (2.0 * RADIUS * RADIUS) * inverse)
                s = [along * d[axis] for axis in range(3)]
                parts = (s[0] * d[0] + iso, s[0] * d[1], s[0] * d[2], s[1] * d[1] + iso, s[1] * d[2],
                         s[2] * d[2] + iso)
                for k, value in enumerate(parts):
                    high = value.astype(BF16)
                    at = slice(k * BLOCK + tile * 128, k * BLOCK + tile * 128 + 128)
                    mob_high[h, rows, at] = high
                    mob_low[h, rows, at] = (value - high.astype(F32)).astype(BF16)

    def widen(h):
        base = jnp.where(core == 0, PLANE, h * 16)

        @pl.loop(0, 16, unroll=2)
        def _(s):
            for axis in range(3):
                value = ag[0, base + s, axis]
                other = turn(value)
                for j, both in enumerate((jnp.where(first, value, other), jnp.where(first, other, value))):
                    high = both.astype(BF16).astype(F32)
                    tile = jnp.where(first, high, both - high).astype(BF16)
                    at = pl.ds(pl.multiple_of(s * 32 + j * 16, 16), 16)
                    wide[h, at, axis * 128:axis * 128 + 128] = tile
                    if axis == 0:
                        wide[h, at, 384:512] = tile

    def arrange(step, h):
        base = jnp.where(core == 0, PLANE, h * 16)

        @pl.loop(0, 16, unroll=2)
        def _(s):
            values = [ag[step, base + s, axis] for axis in range(3)]
            others = [turn(value) for value in values]
            for j in range(2):
                left, right = (values, others) if j == 0 else (others, values)
                lx, ly, lz = (jnp.where(first, v, 0.0).astype(BF16) for v in left)
                ry, rz = (jnp.where(first, 0.0, v).astype(BF16) for v in right[1:])
                yx = jnp.where(first, left[1], right[0]).astype(BF16)
                for k, half, tile in ((0, 0, lx), (1, 0, yx), (2, 0, lz), (2, 1, lx), (3, 0, ry), (4, 0, rz),
                                      (4, 1, ly), (5, 1, lz)):
                    at = pl.ds(pl.multiple_of(k * BLOCK + s * 32 + j * 16, 16), 16)
                    narrow[h, at, half * 128:half * 128 + 128] = tile

    def dot(left, right):
        return jnp.dot(left, right, preferred_element_type=F32)

    def product(t, group):
        h, w, rows = places(t, group)

        def both(k, lo, hi):
            at = slice(k * BLOCK, k * BLOCK + BLOCK)
            return dot(mob_high[h, rows, at], wide[w, :, lo:hi]) + dot(mob_low[h, rows, at], wide[w, :, lo:hi])

        xy, yz, zx = both(1, 0, 256), both(4, 128, 384), both(2, 256, 512)
        return (both(0, 0, 128) + xy[:, 128:] + zx[:, :128],
                both(3, 128, 256) + xy[:, :128] + yz[:, 128:],
                both(5, 256, 384) + zx[:, 128:] + yz[:, :128])

    def halves(i, upper):
        return pl.ds(pl.multiple_of(i * 32 + upper * 16, 16), 16)

    def pack(i):
        chunk = []
        for axis in range(3):
            low, high = acc[axis, halves(i, 0), :], acc[axis, halves(i, 1), :]
            chunk.append(jnp.where(first, low + turn(low), high + turn(high)))
        return chunk

    def pack_wide(i):
        low, high = halves(i, 0), halves(i, 1)
        xy_low, xy_high = acc_wide[low, :128], acc_wide[high, :128]
        z_low, z_high = acc_wide[low, 128:], acc_wide[high, 128:]
        return (jnp.where(first, xy_low, turn(xy_high)), jnp.where(first, turn(xy_low), xy_high),
                jnp.where(first, z_low, turn(z_high)))

    def scatter(step, group, packer):
        slot = jnp.where(core == 0, chip, 16 + z)
        mine = jnp.where(core == 0, my_p, my_l)
        near = jnp.where(core == 0, y, lax.rem(z, 4))
        for d in (2, 1, 3, 0):
            j = lax.rem(near + d, 4)
            for c in range(2):
                i = j * 2 + c
                q = group * 8 + i
                for axis, value in enumerate(packer(i)):
                    rs_send[step, q, axis] = value
                device = (jnp.where(core == 0, group, x) * 2 + c,
                          jnp.where(core == 0, z * 4 + j, (group * 4 + j) * 4 + y))

                def send(q=q, device=device):
                    remote(rs_send.at[step, q], rs.at[step, slot], rs_sent.at[step], rs_recv.at[step], device).start()

                if d:
                    send()
                else:
                    pl.when(q != mine)(send)

                    @pl.when(q == mine)
                    def _(q=q):
                        rs[step, slot] = rs_send[step, q]

    def collect(step, half, axis):
        span = range(16) if half == 0 else range(16, 24)
        return sum((rs[step, s, axis] for s in span[1:]), rs[step, span[0], axis])

    def wait_vector(step):
        @pl.when(core == 0)
        def _():
            wait_recv(ag.at[step, pl.ds(0, LINE - 1)], ag_recv.at[step, 0])

        @pl.when(core == 1)
        def _():
            wait_recv(ag.at[step, pl.ds(0, PLANE - 1)], ag_recv.at[step, 1])

    front = lax.broadcasted_iota(jnp.int32, (1, 128), 1) < HALF

    def fold(value):
        line = jnp.sum(value, axis=0, keepdims=True)
        return line + turn(line)

    def inner(left, right):
        sums = [sum(left[half, axis] * right[half, axis] for axis in range(3)) for half in range(2)]
        return jnp.where(front, fold(sums[0]), fold(sums[1]))

    def reduce_plane(k, values):
        for n, value in enumerate(values):
            red_src[2 * k, :, n * 128:n * 128 + 128] = value
        for dx, dy in PLANE_ORDER:
            remote(red_src.at[2 * k], red_one.at[k, chip], red_sem.at[k, 0], red_sem.at[k, 1],
                   plane_at(dx, dy, core)).start()
        red_one[k, chip] = red_src[2 * k]

    def reduce_line(k):
        wait_recv(red_one.at[k, pl.ds(0, 15)], red_sem.at[k, 1])
        red_src[2 * k + 1] = sum((red_one[k, s] for s in range(1, 16)), red_one[k, 0])
        for dz in LINE_ORDER:
            for c in range(2):
                remote(red_src.at[2 * k + 1], red_two.at[k, my_l], red_sem.at[k, 2], red_sem.at[k, 3],
                       line_at(dz, c)).start()
        remote(red_src.at[2 * k + 1], red_two.at[k, my_l], red_sem.at[k, 2], red_sem.at[k, 3], sibling).start()
        red_two[k, my_l] = red_src[2 * k + 1]

    def reduced(k, count):
        wait_recv(red_two.at[k, pl.ds(0, 15)], red_sem.at[k, 3])
        total = sum((red_two[k, s] for s in range(1, 16)), red_two[k, 0])
        return [total[:, n * 128:n * 128 + 128] for n in range(count)]

    @pl.loop(0, 2)
    def _(t):
        build(t)

    wait_vector(0)
    widen(0)

    @pl.when(core == 1)
    def _():
        widen(1)

    @pl.loop(0, 4)
    def _(t):
        group = group_of(t)

        @pl.when(t >= 2)
        def _():
            build(t)

        more = (core == 1) & (lax.rem(t, 2) == 1)
        for axis, value in enumerate(product(t, group)):
            acc[axis] = jnp.where(more, acc[axis], 0.0) + value

        @pl.when((core == 0) | (lax.rem(t, 2) == 1))
        def _():
            scatter(0, group, pack)

    wait_recv(rs.at[0, pl.ds(0, 23)], rs_recv.at[0])
    for axis in range(3):
        for half in range(2):
            packed[1, half, axis] = collect(0, half, axis)
    gather(1)
    reduce_plane(0, (inner(packed.at[0], packed.at[0]), inner(packed.at[0], packed.at[1])))

    @pl.loop(1, ITERS)
    def _(step):
        wait_vector(step)
        arrange(step, 0)

        @pl.when(core == 1)
        def _():
            arrange(step, 1)

        @pl.loop(0, 4)
        def _(t):
            group = group_of(t)
            h, w, rows = places(t, group)
            more = (core == 1) & (lax.rem(t, 2) == 1) & (step == 1)
            acc_wide[...] = jnp.where(more, acc_wide[...], 0.0) + dot(mob_high[h, rows, :], narrow[w])

            @pl.when((step == 1) & ((core == 0) | (lax.rem(t, 2) == 1)))
            def _():
                scatter(1, group, pack_wide)

            @pl.when(step == 2)
            def _():
                @pl.when((t == 0) & (core == 0))
                def _():
                    wait_recv(ag.at[2, pl.ds(0, PLANE - 1)], ag_recv.at[2, 1])

                @pl.when((t == 0) & (core == 1))
                def _():
                    wait_recv(ag.at[2, pl.ds(0, LINE - 1)], ag_recv.at[2, 0])

                at = jnp.where(core == 0, 0, PLANE) + group * 8
                total = part[...]
                for i in range(8):
                    for axis, value in enumerate(pack_wide(i)):
                        total = total + value * ag[2, at + i, axis]
                part[...] = total

        @pl.when(step == 1)
        def _():
            reduce_line(0)
            wait_recv(rs.at[1, pl.ds(0, 23)], rs_recv.at[1])
            m0, m1 = reduced(0, 2)
            moments[0] = jnp.broadcast_to(m0, (8, 128))
            moments[1] = jnp.broadcast_to(m1, (8, 128))
            a1 = moments[1] / moments[0]
            a1 = jnp.concatenate([a1, a1], axis=0)
            for half, here in enumerate((jnp.where(first, a1, turn(a1)), jnp.where(first, turn(a1), a1))):
                for axis in range(3):
                    y1 = packed[1, half, axis]
                    packed[2, half, axis] = collect(1, half, axis) - here * y1
                    first_dir[half, axis] = y1 - here * packed[0, half, axis]
            gather(2)

    reduce_plane(1, (inner(first_dir, first_dir), inner(first_dir, packed.at[2]), inner(packed.at[2], packed.at[2]),
                     jnp.where(front == (core == 0), fold(part[...]), 0.0)))
    reduce_line(1)
    for k, value in enumerate(reduced(1, 4)):
        moments[2 + k] = jnp.broadcast_to(value, (8, 128))
    moments[6] = jnp.zeros((8, 128), F32)
    moments[7] = jnp.ones((8, 128), F32)
    m0, m1, e1, f1, g, third, zero, one = (moments[k] for k in range(8))

    a1, a2, bb2 = m1 / m0, f1 / e1, e1 / m0
    e2 = g - a2 * f1 - bb2 * e1
    bb3 = e2 / e1
    a3 = (third - a2 * g - bb2 * (f1 + a1 * e1)) / e2 - a2
    d1, d2, d3 = 1.0 + a1, 1.0 + a2, 1.0 + a3
    scale = (d1 + d2 + d3) / ITERS
    current = (d1 / scale, jnp.sqrt(bb2) / scale, zero, d2 / scale, jnp.sqrt(bb3) / scale, d3 / scale)
    partner = (one, zero, zero, one, zero, one)

    def inverse_three(m):
        c00, c01, c02 = m[3] * m[5] - m[4] * m[4], m[2] * m[4] - m[1] * m[5], m[1] * m[4] - m[2] * m[3]
        c11, c12, c22 = m[0] * m[5] - m[2] * m[2], m[1] * m[2] - m[0] * m[4], m[0] * m[3] - m[1] * m[1]
        over = 1.0 / (m[0] * c00 + m[1] * c01 + m[2] * c02)
        return tuple(c * over for c in (c00, c01, c02, c11, c12, c22))

    def newton(_, state):
        now, other = state
        return (tuple(0.5 * (u + v) for u, v in zip(now, inverse_three(other))),
                tuple(0.5 * (u + v) for u, v in zip(other, inverse_three(now))))

    current, partner = lax.fori_loop(0, 20, newton, (current, partner))
    size = jnp.sqrt(scale)
    beta = jnp.sqrt(m0)
    r1, r2, r3 = (current[k] * size for k in range(3))
    f2, f3 = beta * r2 / jnp.sqrt(e1), beta * r3 / jnp.sqrt(e2)
    c0, c1, c2 = (jnp.concatenate([c, c], axis=0) for c in (r1 - f3 * bb2, f2 - f3 * a2, f3))
    for axis in range(3):
        w_a, w_b, u_a, u_b = first_dir[0, axis], first_dir[1, axis], packed[2, 0, axis], packed[2, 1, axis]
        out_ref[axis, :16, :] = (c0 * z_ref[axis, :16, :] + c1 * jnp.where(first, w_a, turn(w_b))
                                 + c2 * jnp.where(first, u_a, turn(u_b)))
        out_ref[axis, 16:, :] = (c0 * z_ref[axis, 16:, :] + c1 * jnp.where(first, turn(w_a), w_b)
                                 + c2 * jnp.where(first, turn(u_a), u_b))

    wait_send(posbuf.at[pl.ds(0, 46)], pos_sem.at[1])
    wait_send(ag.at[0, pl.ds(0, 23)], ag_send.at[0])
    wait_send(ag.at[1, pl.ds(0, 23)], ag_send.at[1])
    wait_send(ag.at[2, pl.ds(0, 46)], ag_send.at[2])
    for k in range(2):
        wait_send(red_one.at[k, pl.ds(0, 15)], red_sem.at[k, 0])
        wait_send(red_two.at[k, pl.ds(0, 15)], red_sem.at[k, 2])
    for step in range(2):
        @pl.when(core == 0)
        def _():
            wait_send(rs_send.at[step, pl.ds(0, PLANE - 1)], rs_sent.at[step])

        @pl.when(core == 1)
        def _():
            wait_send(rs_send.at[step, pl.ds(0, LINE - 1)], rs_sent.at[step])


def shards(positions, start_vector):
    chunk = (3, 16, 128)
    return pl.pallas_call(
        kernel,
        out_shape=jax.ShapeDtypeStruct(start_vector.shape, F32),
        in_specs=[pl.BlockSpec(memory_space=pl.ANY)] * 2,
        out_specs=pl.BlockSpec(memory_space=pltpu.VMEM),
        scratch_shapes=[
            pltpu.VMEM((PLANE + LINE, 1, 128), F32),
            pltpu.VMEM((2, 3, BLOCK, 128), F32),
            pltpu.VMEM((2, 8, BLOCK), F32),
            pltpu.VMEM((2, BLOCK, 6 * BLOCK), BF16),
            pltpu.VMEM((2, BLOCK, 6 * BLOCK), BF16),
            pltpu.VMEM((2, BLOCK, 512), BF16),
            pltpu.VMEM((2, 6 * BLOCK, 256), BF16),
            pltpu.VMEM((3, PLANE + LINE) + chunk, F32),
            pltpu.VMEM((2, 24) + chunk, F32),
            pltpu.VMEM((2, PLANE) + chunk, F32),
            pltpu.VMEM((3, 2) + chunk, F32),
            pltpu.VMEM((2,) + chunk, F32),
            pltpu.VMEM((3, 256, 128), F32),
            pltpu.VMEM((256, 256), F32),
            pltpu.VMEM((16, 128), F32),
            pltpu.VMEM((4, 1, 512), F32),
            pltpu.VMEM((2, 16, 1, 512), F32),
            pltpu.VMEM((2, 16, 1, 512), F32),
            pltpu.VMEM((8, 8, 128), F32),
            pltpu.VMEM((3, 32), jnp.int32),
            pltpu.VMEM((8, 128), F32),
            pltpu.VMEM((3, 32, 128), F32),
            pltpu.SemaphoreType.DMA((2,)),
            pltpu.SemaphoreType.DMA((2,)),
            pltpu.SemaphoreType.DMA((3, 2)),
            pltpu.SemaphoreType.DMA((3,)),
            pltpu.SemaphoreType.DMA((2,)),
            pltpu.SemaphoreType.DMA((2,)),
            pltpu.SemaphoreType.DMA((2, 4)),
        ],
        compiler_params=pltpu.CompilerParams(
            collective_id=0, has_side_effects=True, vmem_limit_bytes=62 * 1024 * 1024),
    )(positions, start_vector)


def solution(mesh):
    in_specs = (P(None, ("row", "col")), P(None, ("row", "col"), None))
    out_specs = P(None, ("row", "col"), None)
    return jax.shard_map(shards, mesh=mesh, in_specs=in_specs, out_specs=out_specs, check_vma=False)
```

```python
import jax
import jax.numpy as jnp
from jax import lax
from jax.experimental import pallas as pl
from jax.experimental.pallas import tpu as pltpu
from jax.sharding import PartitionSpec as P

ITERS = 3
RADIUS = 0.4
MESH = pl.DeviceIdType.MESH
F32 = jnp.float32
BF16 = jnp.bfloat16

PLANE, LINE = 16, 8
LINE_ORDER = (4, 3, 5, 2, 6, 1, 7)
PLANE_ORDER = ((2, 2), (1, 2), (2, 1), (3, 2), (2, 3), (1, 1), (3, 3), (1, 3), (3, 1), (2, 0), (0, 2),
               (1, 0), (0, 1), (3, 0), (0, 3))
HALF = 64
BLOCK = 512
WIDTH = 768


def kernel(pos_hbm, z_hbm, out_ref, posrow, posbuf, colbc, lanevec, mob_high, mob_low, wide, narrow, ag, rs, rs_send,
           packed, first_dir, mate, acc, acc_wide, part, red_src, red_one, red_two, moments, pos_ref, flatten, z_ref,
           z_mate, load_sem, mate_sem, pos_sem, ag_recv, ag_send, rs_recv, rs_sent, red_sem):
    row, col = lax.axis_index("row"), lax.axis_index("col")
    x, core = lax.div(row, 2), lax.rem(row, 2)
    z, y = lax.div(col, 4), lax.rem(col, 4)
    chip = x * 4 + y
    my_line = PLANE + z

    xs = [lax.rem(x + d, 4) for d in range(4)]
    ys = [lax.rem(y + d, 4) for d in range(4)]
    zs = [lax.rem(z + d, 8) for d in range(8)]

    def plane_at(dx, dy):
        return (xs[dx] * 2 + core, z * 4 + ys[dy])

    def line_at(dz):
        return (row, zs[dz] * 4 + y)

    def line_mate(dz):
        return (x * 2 + 1 - core, zs[dz] * 4 + y)

    sibling = (x * 2 + 1 - core, col)

    def remote(src, dst, send, recv, device):
        return pltpu.make_async_remote_copy(
            src_ref=src, dst_ref=dst, send_sem=send, recv_sem=recv, device_id=device, device_id_type=MESH)

    def wait_recv(ref, sem):
        remote(ref, ref, sem, sem, (row, col)).wait_recv()

    def wait_send(ref, sem):
        remote(ref, ref, sem, sem, (row, col)).wait_send()

    first = lax.broadcasted_iota(jnp.int32, (32, 128), 1) < HALF
    keep = first == (core == 0)

    def turn(value):
        return pltpu.roll(value, HALF, 1)

    load_pos = pltpu.make_async_copy(pos_hbm, pos_ref, load_sem.at[0])
    load_pos.start()
    load_z = pltpu.make_async_copy(z_hbm, z_ref, load_sem.at[1])
    load_z.start()
    barrier = pltpu.get_barrier_semaphore()

    def signal(device):
        pl.semaphore_signal(barrier, inc=1, device_id=device, device_id_type=MESH)

    signal(sibling)
    for dx, dy in PLANE_ORDER:
        signal(plane_at(dx, dy))
    for dz in LINE_ORDER:
        signal(line_at(dz))
        signal(line_mate(dz))

    flatten[...] = jnp.zeros_like(flatten)
    acc[...] = jnp.zeros_like(acc)
    acc_wide[...] = jnp.zeros_like(acc_wide)
    part[...] = jnp.zeros_like(part)
    for k in range(2):
        red_src[2 * k] = jnp.zeros((1, WIDTH), F32)
    load_pos.wait()
    flatten[0:3, 0:32] = pos_ref[...].astype(F32)
    rows3 = flatten[...]
    posrow[core] = rows3[0:1] + pltpu.roll(rows3[1:2], 32, 1) + pltpu.roll(rows3[2:3], 64, 1)
    load_z.wait()
    pl.semaphore_wait(barrier, 30)

    remote(posrow.at[core], posrow.at[core], pos_sem.at[0], pos_sem.at[1], sibling).start()
    remote(z_ref, z_mate, mate_sem.at[0], mate_sem.at[1], sibling).start()
    wait_recv(posrow.at[0], pos_sem.at[1])
    both = jnp.concatenate([posrow[0], posrow[1]], axis=1)
    posbuf[chip] = both
    posbuf[my_line] = both
    for n, spot in enumerate(PLANE_ORDER):
        if n < 7:
            remote(posbuf.at[my_line], posbuf.at[my_line], pos_sem.at[2], pos_sem.at[3],
                   line_at(LINE_ORDER[n])).start()
        remote(posbuf.at[chip], posbuf.at[chip], pos_sem.at[2], pos_sem.at[3], plane_at(*spot)).start()
    wait_recv(z_mate, mate_sem.at[1])
    for axis in range(3):
        packed[0, axis] = jnp.where(keep, z_ref[axis], turn(z_mate[axis]))

    def gather(step):
        def to_line():
            for dz in LINE_ORDER:
                remote(packed.at[step], ag.at[step, my_line], ag_send.at[step], ag_recv.at[step, 0],
                       line_at(dz)).start()

        def to_plane():
            for spot in PLANE_ORDER:
                remote(packed.at[step], ag.at[step, chip], ag_send.at[step], ag_recv.at[step, 1],
                       plane_at(*spot)).start()

        last = step == 2
        pl.when(core == 0)(to_line)
        pl.when((core == 1) | last)(to_plane)
        pl.when((core == 1) & last)(to_line)
        ag[step, chip] = packed[step]
        ag[step, my_line] = packed[step]

    gather(0)
    narrow[...] = jnp.zeros_like(narrow)
    wait_recv(posbuf.at[pl.ds(0, 22)], pos_sem.at[3])

    lane_of = lax.broadcasted_iota(jnp.int32, (BLOCK, 128), 1)
    bead_of = lax.broadcasted_iota(jnp.int32, (BLOCK, 128), 0) & 31
    entry_of = lax.broadcasted_iota(jnp.int32, (128, BLOCK), 0)
    column_of = lax.broadcasted_iota(jnp.int32, (128, BLOCK), 1) & 31
    owner_of = lax.broadcasted_iota(jnp.int32, (16, BLOCK), 1) >> 5
    source_of = lax.broadcasted_iota(jnp.int32, (16, BLOCK), 0)
    ones = jnp.ones((128, 128), BF16)

    def place(at, d):
        return posbuf[at + d // 2][:, (d % 2) * 128:(d % 2) * 128 + 128]

    @pl.loop(0, 2)
    def _(h):
        rows_at = jnp.where(core == 0, h, 2) * 8
        lanes_at = jnp.where(core == 0, 2, h) * 8
        spread = jnp.concatenate([jnp.broadcast_to(place(rows_at, d), (32, 128)) for d in range(16)], axis=0)
        flat = jnp.concatenate([place(lanes_at, d) for d in range(16)], axis=0).astype(BF16)
        for axis in range(3):
            own = jnp.where(lane_of == axis * 32 + bead_of, spread, 0.0).astype(BF16)
            colbc[h, axis] = jnp.dot(own, ones, preferred_element_type=F32)
            pick = jnp.where(entry_of == axis * 32 + column_of, 1.0, 0.0).astype(BF16)
            moved = jnp.dot(flat, pick, preferred_element_type=F32)
            lanevec[h, axis:axis + 1, :] = jnp.sum(jnp.where(owner_of == source_of, moved, 0.0), axis=0, keepdims=True)

    def group_of(t):
        d = jnp.where(t == 0, 2, jnp.where(t == 1, 1, jnp.where(t == 2, 3, 0)))
        return jnp.where(core == 0, lax.rem(x + d, 4), lax.rem(lax.div(z, 4) + 1 + lax.div(t, 2), 2))

    def places(t, group):
        h = jnp.where(core == 0, lax.div(group, 2), lax.rem(t, 2))
        rt = jnp.where(core == 0, lax.rem(group, 2), group)
        return h, jnp.where(core == 0, 0, h), pl.ds(pl.multiple_of(rt * 256, 256), 256)

    def build(t):
        h, _, span = places(t, group_of(t))

        @pl.loop(0, 16, unroll=2)
        def _(r):
            rows = pl.ds(pl.multiple_of(span.start + r * 16, 16), 16)
            mine = [colbc[h, axis, rows, :] for axis in range(3)]
            for tile in range(4):
                lanes = slice(tile * 128, tile * 128 + 128)
                d = [mine[axis] - lanevec[h, axis:axis + 1, lanes] for axis in range(3)]
                squared = d[0] * d[0] + d[1] * d[1] + d[2] * d[2]
                root = lax.rsqrt(jnp.where(squared > 0.5, squared, 1e30))
                inverse = root * root
                prefactor = (0.75 * RADIUS) * root
                iso = prefactor * (1.0 + (2.0 / 3.0 * RADIUS * RADIUS) * inverse)
                along = (prefactor * inverse) * (1.0 - (2.0 * RADIUS * RADIUS) * inverse)
                s = [along * d[axis] for axis in range(3)]
                parts = (s[0] * d[0] + iso, s[0] * d[1], s[0] * d[2], s[1] * d[1] + iso, s[1] * d[2],
                         s[2] * d[2] + iso)
                for k, value in enumerate(parts):
                    high = value.astype(BF16)
                    at = slice(k * BLOCK + tile * 128, k * BLOCK + tile * 128 + 128)
                    mob_high[h, rows, at] = high
                    mob_low[h, rows, at] = (value - high.astype(F32)).astype(BF16)

    def widen(h):
        base = jnp.where(core == 0, PLANE, h * 8)

        @pl.loop(0, 8)
        def _(s):
            for axis in range(3):
                value = ag[0, base + s, axis]
                other = turn(value)
                for j, both in enumerate((jnp.where(first, value, other), jnp.where(first, other, value))):
                    high = both.astype(BF16).astype(F32)
                    tile = jnp.where(first, high, both - high).astype(BF16)
                    at = pl.ds(pl.multiple_of(s * 64 + j * 32, 32), 32)
                    wide[h, at, axis * 128:axis * 128 + 128] = tile
                    if axis == 0:
                        wide[h, at, 384:512] = tile

    def arrange(step, h):
        base = jnp.where(core == 0, PLANE, h * 8)

        @pl.loop(0, 8)
        def _(s):
            values = [ag[step, base + s, axis] for axis in range(3)]
            others = [turn(value) for value in values]
            for j in range(2):
                left, right = (values, others) if j == 0 else (others, values)
                lx, ly, lz = (jnp.where(first, v, 0.0).astype(BF16) for v in left)
                ry, rz = (jnp.where(first, 0.0, v).astype(BF16) for v in right[1:])
                yx = jnp.where(first, left[1], right[0]).astype(BF16)
                for k, half, tile in ((0, 0, lx), (1, 0, yx), (2, 0, lz), (2, 1, lx), (3, 0, ry), (4, 0, rz),
                                      (4, 1, ly), (5, 1, lz)):
                    at = pl.ds(pl.multiple_of(k * BLOCK + s * 64 + j * 32, 32), 32)
                    narrow[h, at, half * 128:half * 128 + 128] = tile

    def dot(left, right):
        return jnp.dot(left, right, preferred_element_type=F32)

    def product(t, group):
        h, w, rows = places(t, group)

        def both(k, lo, hi):
            at = slice(k * BLOCK, k * BLOCK + BLOCK)
            return dot(mob_high[h, rows, at], wide[w, :, lo:hi]) + dot(mob_low[h, rows, at], wide[w, :, lo:hi])

        xy, yz, zx = both(1, 0, 256), both(4, 128, 384), both(2, 256, 512)
        return (both(0, 0, 128) + xy[:, 128:] + zx[:, :128],
                both(3, 128, 256) + xy[:, :128] + yz[:, 128:],
                both(5, 256, 384) + zx[:, 128:] + yz[:, :128])

    def halves(i, upper):
        return pl.ds(pl.multiple_of(i * 64 + upper * 32, 32), 32)

    def pack(i):
        chunk = []
        for axis in range(3):
            low, high = acc[axis, halves(i, 0), :], acc[axis, halves(i, 1), :]
            chunk.append(jnp.where(first, low + turn(low), high + turn(high)))
        return chunk

    def pack_wide(i):
        low, high = halves(i, 0), halves(i, 1)
        xy_low, xy_high = acc_wide[low, :128], acc_wide[high, :128]
        z_low, z_high = acc_wide[low, 128:], acc_wide[high, 128:]
        return (jnp.where(first, xy_low, turn(xy_high)), jnp.where(first, turn(xy_low), xy_high),
                jnp.where(first, z_low, turn(z_high)))

    def scatter(step, group, packer):
        slot = jnp.where(core == 0, chip, z)
        near = jnp.where(core == 0, y, lax.rem(z, 4))
        for d in (2, 1, 3, 0):
            j = lax.rem(near + d, 4)
            q = group * 4 + j
            for axis, value in enumerate(packer(j)):
                rs_send[step, q, axis] = value
            device = (jnp.where(core == 0, group * 2, row), jnp.where(core == 0, z * 4 + j, q * 4 + y))

            def send(q=q, device=device):
                remote(rs_send.at[step, q], rs.at[step, slot], rs_sent.at[step], rs_recv.at[step], device).start()

            if d:
                send()
            else:
                pl.when(q != slot)(send)

                @pl.when(q == slot)
                def _(q=q):
                    rs[step, slot] = rs_send[step, q]

    def collect(step):
        @pl.when(core == 0)
        def _():
            wait_recv(rs.at[step, pl.ds(0, PLANE - 1)], rs_recv.at[step])
            for axis in range(3):
                packed[step + 1, axis] = sum((rs[step, s, axis] for s in range(1, PLANE)), rs[step, 0, axis])

        @pl.when(core == 1)
        def _():
            wait_recv(rs.at[step, pl.ds(0, LINE - 1)], rs_recv.at[step])
            for axis in range(3):
                packed[step + 1, axis] = sum((rs[step, s, axis] for s in range(1, LINE)), rs[step, 0, axis])

    def wait_line(step):
        wait_recv(ag.at[step, pl.ds(0, LINE - 1)], ag_recv.at[step, 0])

    def wait_plane(step):
        wait_recv(ag.at[step, pl.ds(0, PLANE - 1)], ag_recv.at[step, 1])

    def wait_vector(step):
        pl.when(core == 0)(lambda: wait_line(step))
        pl.when(core == 1)(lambda: wait_plane(step))

    front = lax.broadcasted_iota(jnp.int32, (1, 128), 1) < HALF

    def fold(value):
        line = jnp.sum(value, axis=0, keepdims=True)
        return line + turn(line)

    def inner(left, right):
        return fold(sum(left[axis] * right[axis] for axis in range(3)))

    def reduce_plane(k, values):
        for n, value in values:
            red_src[2 * k, :, n * 128:n * 128 + 128] = value
        for spot in PLANE_ORDER:
            remote(red_src.at[2 * k], red_one.at[k, chip], red_sem.at[k, 0], red_sem.at[k, 1], plane_at(*spot)).start()
        red_one[k, chip] = red_src[2 * k]

    def reduce_line(k):
        def send(device):
            remote(red_src.at[2 * k + 1], red_two.at[k, core, z], red_sem.at[k, 2], red_sem.at[k, 3], device).start()

        wait_recv(red_one.at[k, pl.ds(0, PLANE - 1)], red_sem.at[k, 1])
        red_src[2 * k + 1] = sum((red_one[k, s] for s in range(1, PLANE)), red_one[k, 0])
        for dz in LINE_ORDER:
            send(line_at(dz))
            if k == 1:
                send(line_mate(dz))
        if k == 1:
            send(sibling)
        red_two[k, core, z] = red_src[2 * k + 1]

    def reduced(k, c):
        return sum((red_two[k, c, s] for s in range(1, LINE)), red_two[k, c, 0])

    @pl.loop(0, 2)
    def _(t):
        build(t)

    wait_vector(0)
    widen(0)

    @pl.when(core == 1)
    def _():
        widen(1)

    @pl.loop(0, 4)
    def _(t):
        group = group_of(t)

        @pl.when(t >= 2)
        def _():
            build(t)

        more = (core == 1) & (lax.rem(t, 2) == 1)
        for axis, value in enumerate(product(t, group)):
            acc[axis] = jnp.where(more, acc[axis], 0.0) + value

        @pl.when((core == 0) | (lax.rem(t, 2) == 1))
        def _():
            scatter(0, group, pack)

    collect(0)
    gather(1)
    reduce_plane(0, ((0, inner(packed.at[0], packed.at[0])), (1, inner(packed.at[0], packed.at[1]))))

    @pl.loop(1, ITERS)
    def _(step):
        wait_vector(step)
        arrange(step, 0)

        @pl.when(core == 1)
        def _():
            arrange(step, 1)

        @pl.loop(0, 4)
        def _(t):
            group = group_of(t)
            h, w, rows = places(t, group)
            more = (core == 1) & (lax.rem(t, 2) == 1) & (step == 1)
            acc_wide[...] = jnp.where(more, acc_wide[...], 0.0) + dot(mob_high[h, rows, :], narrow[w])

            @pl.when((step == 1) & ((core == 0) | (lax.rem(t, 2) == 1)))
            def _():
                scatter(1, group, pack_wide)

            @pl.when(step == 2)
            def _():
                pl.when((t == 0) & (core == 0))(lambda: wait_plane(2))
                pl.when((t == 0) & (core == 1))(lambda: wait_line(2))
                at = jnp.where(core == 0, 0, PLANE) + group * 4
                total = part[...]
                for i in range(4):
                    for axis, value in enumerate(pack_wide(i)):
                        total = total + value * ag[2, at + i, axis]
                part[...] = total

        @pl.when(step == 1)
        def _():
            reduce_line(0)
            collect(1)
            wait_recv(red_two.at[0, 0, pl.ds(0, LINE - 1)], red_sem.at[0, 3])
            total = reduced(0, core)
            moments[0] = jnp.broadcast_to(total[:, 128:256] / total[:, 0:128], (32, 128))
            a1 = moments[0]
            for axis in range(3):
                y1 = packed[1, axis]
                packed[2, axis] = packed[2, axis] - a1 * y1
                first_dir[axis] = y1 - a1 * packed[0, axis]
            gather(2)
            remote(first_dir, mate.at[0], mate_sem.at[2], mate_sem.at[3], sibling).start()
            remote(packed.at[2], mate.at[1], mate_sem.at[2], mate_sem.at[3], sibling).start()

    reduce_plane(1, ((0, red_src[0][:, 0:128]), (1, red_src[0][:, 128:256]),
                     (2, inner(first_dir, first_dir)), (3, inner(first_dir, packed.at[2])),
                     (4, inner(packed.at[2], packed.at[2])), (5, fold(part[...]))))
    reduce_line(1)
    wait_recv(red_one.at[1, pl.ds(0, 2 * LINE - 1)], red_sem.at[1, 3])
    low, high = reduced(1, 0), reduced(1, 1)
    for k in range(6):
        at = slice(k * 128, k * 128 + 128)
        moments[k + 1, 0:8] = jnp.broadcast_to(jnp.where(front, low[:, at], high[:, at]), (8, 128))
    moments[7, 0:8] = jnp.zeros((8, 128), F32)
    moments[8, 0:8] = jnp.ones((8, 128), F32)
    m0, m1, e1, f1, g, third, zero, one = (moments[k, 0:8] for k in range(1, 9))

    a1, a2, bb2 = m1 / m0, f1 / e1, e1 / m0
    e2 = g - a2 * f1 - bb2 * e1
    bb3 = e2 / e1
    a3 = (third - a2 * g - bb2 * (f1 + a1 * e1)) / e2 - a2
    d1, d2, d3 = 1.0 + a1, 1.0 + a2, 1.0 + a3
    scale = (d1 + d2 + d3) / ITERS
    current = (d1 / scale, jnp.sqrt(bb2) / scale, zero, d2 / scale, jnp.sqrt(bb3) / scale, d3 / scale)
    partner = (one, zero, zero, one, zero, one)

    def inverse_three(m):
        c00, c01, c02 = m[3] * m[5] - m[4] * m[4], m[2] * m[4] - m[1] * m[5], m[1] * m[4] - m[2] * m[3]
        c11, c12, c22 = m[0] * m[5] - m[2] * m[2], m[1] * m[2] - m[0] * m[4], m[0] * m[3] - m[1] * m[1]
        over = 1.0 / (m[0] * c00 + m[1] * c01 + m[2] * c02)
        return tuple(c * over for c in (c00, c01, c02, c11, c12, c22))

    def newton(_, state):
        now, other = state
        return (tuple(0.5 * (u + v) for u, v in zip(now, inverse_three(other))),
                tuple(0.5 * (u + v) for u, v in zip(other, inverse_three(now))))

    current, partner = lax.fori_loop(0, 20, newton, (current, partner))
    size = jnp.sqrt(scale)
    beta = jnp.sqrt(m0)
    r1, r2, r3 = (current[k] * size for k in range(3))
    f2, f3 = beta * r2 / jnp.sqrt(e1), beta * r3 / jnp.sqrt(e2)
    wait_recv(mate, mate_sem.at[3])
    c0, c1, c2 = (jnp.concatenate([c, c, c, c], axis=0) for c in (r1 - f3 * bb2, f2 - f3 * a2, f3))
    for axis in range(3):
        out_ref[axis] = (c0 * z_ref[axis] + c1 * jnp.where(keep, first_dir[axis], turn(mate[0, axis]))
                         + c2 * jnp.where(keep, packed[2, axis], turn(mate[1, axis])))

    wait_send(posrow.at[0], pos_sem.at[0])
    wait_send(z_mate, mate_sem.at[0])
    wait_send(mate, mate_sem.at[2])
    wait_send(posbuf.at[pl.ds(0, 22)], pos_sem.at[2])
    wait_send(ag.at[2, pl.ds(0, 22)], ag_send.at[2])
    for k, count in enumerate((LINE - 1, 2 * LINE - 1)):
        wait_send(red_one.at[k, pl.ds(0, PLANE - 1)], red_sem.at[k, 0])
        wait_send(red_one.at[k, pl.ds(0, count)], red_sem.at[k, 2])
    for step in range(2):
        @pl.when(core == 0)
        def _(step=step):
            wait_send(ag.at[step, pl.ds(0, LINE - 1)], ag_send.at[step])
            wait_send(rs_send.at[step, pl.ds(0, PLANE - 1)], rs_sent.at[step])

        @pl.when(core == 1)
        def _(step=step):
            wait_send(ag.at[step, pl.ds(0, PLANE - 1)], ag_send.at[step])
            wait_send(rs_send.at[step, pl.ds(0, LINE - 1)], rs_sent.at[step])


def shards(positions, start_vector):
    chunk = (3, 32, 128)
    return pl.pallas_call(
        kernel,
        out_shape=jax.ShapeDtypeStruct(start_vector.shape, F32),
        in_specs=[pl.BlockSpec(memory_space=pltpu.HBM)] * 2,
        out_specs=pl.BlockSpec(memory_space=pltpu.VMEM),
        scratch_shapes=[
            pltpu.VMEM((2, 1, 128), F32),
            pltpu.VMEM((PLANE + LINE, 1, 256), F32),
            pltpu.VMEM((2, 3, BLOCK, 128), F32),
            pltpu.VMEM((2, 8, BLOCK), F32),
            pltpu.VMEM((2, BLOCK, 6 * BLOCK), BF16),
            pltpu.VMEM((2, BLOCK, 6 * BLOCK), BF16),
            pltpu.VMEM((2, BLOCK, 512), BF16),
            pltpu.VMEM((2, 6 * BLOCK, 256), BF16),
            pltpu.VMEM((3, PLANE + LINE) + chunk, F32),
            pltpu.VMEM((2, PLANE) + chunk, F32),
            pltpu.VMEM((2, PLANE) + chunk, F32),
            pltpu.VMEM((3,) + chunk, F32),
            pltpu.VMEM(chunk, F32),
            pltpu.VMEM((2,) + chunk, F32),
            pltpu.VMEM((3, 256, 128), F32),
            pltpu.VMEM((256, 256), F32),
            pltpu.VMEM((32, 128), F32),
            pltpu.VMEM((4, 1, WIDTH), F32),
            pltpu.VMEM((2, PLANE, 1, WIDTH), F32),
            pltpu.VMEM((2, 2, LINE, 1, WIDTH), F32),
            pltpu.VMEM((9, 32, 128), F32),
            pltpu.VMEM((3, 32), jnp.int32),
            pltpu.VMEM((8, 128), F32),
            pltpu.VMEM(chunk, F32),
            pltpu.VMEM(chunk, F32),
            pltpu.SemaphoreType.DMA((2,)),
            pltpu.SemaphoreType.DMA((4,)),
            pltpu.SemaphoreType.DMA((4,)),
            pltpu.SemaphoreType.DMA((3, 2)),
            pltpu.SemaphoreType.DMA((3,)),
            pltpu.SemaphoreType.DMA((2,)),
            pltpu.SemaphoreType.DMA((2,)),
            pltpu.SemaphoreType.DMA((2, 4)),
        ],
        compiler_params=pltpu.CompilerParams(
            collective_id=0, has_side_effects=True, vmem_limit_bytes=40 * 1024 * 1024),
    )(positions, start_vector)


def solution(mesh):
    in_specs = (P(None, ("row", "col")), P(None, ("row", "col"), None))
    out_specs = P(None, ("row", "col"), None)
    return jax.shard_map(shards, mesh=mesh, in_specs=in_specs, out_specs=out_specs, check_vma=False)
```

```python
import jax
import jax.numpy as jnp
from jax import lax
from jax.experimental import pallas as pl
from jax.experimental.pallas import tpu as pltpu
from jax.sharding import PartitionSpec as P

ITERS = 3
RADIUS = 0.4
MESH = pl.DeviceIdType.MESH
F32 = jnp.float32
BF16 = jnp.bfloat16

PLANE, LINE = 16, 8
LINE_ORDER = (4, 3, 5, 2, 6, 1, 7)
PLANE_ORDER = ((2, 2), (1, 2), (2, 1), (3, 2), (2, 3), (1, 1), (3, 3), (1, 3), (3, 1), (2, 0), (0, 2),
               (1, 0), (0, 1), (3, 0), (0, 3))
LINE_NEAR = (2, 6, 1, 7)
PLANE_NEAR = ((2, 0), (0, 2), (1, 0), (0, 1), (3, 0), (0, 3))
HALF = 64
BLOCK = 512
WIDTH = 768


def kernel(pos_hbm, z_hbm, out_ref, posrow, posbuf, colbc, lanevec, mob_high, mob_low, wide, narrow, ag, rs, rs_send,
           packed, first_dir, mate, acc, acc_wide, part, red_src, red_one, red_two, moments, pos_ref, flatten, z_ref,
           z_mate, load_sem, mate_sem, pos_sem, line_sem, plane_sem, ag_send, rs_recv, rs_sent, red_sem):
    row, col = lax.axis_index("row"), lax.axis_index("col")
    x, core = lax.div(row, 2), lax.rem(row, 2)
    z, y = lax.div(col, 4), lax.rem(col, 4)
    chip = x * 4 + y
    my_line = PLANE + z

    xs = [lax.rem(x + d, 4) for d in range(4)]
    ys = [lax.rem(y + d, 4) for d in range(4)]
    zs = [lax.rem(z + d, 8) for d in range(8)]

    def plane_at(dx, dy):
        return (xs[dx] * 2 + core, z * 4 + ys[dy])

    def line_at(dz):
        return (row, zs[dz] * 4 + y)

    def line_mate(dz):
        return (x * 2 + 1 - core, zs[dz] * 4 + y)

    sibling = (x * 2 + 1 - core, col)

    def remote(src, dst, send, recv, device):
        return pltpu.make_async_remote_copy(
            src_ref=src, dst_ref=dst, send_sem=send, recv_sem=recv, device_id=device, device_id_type=MESH)

    def wait_recv(ref, sem):
        remote(ref, ref, sem, sem, (row, col)).wait_recv()

    def wait_send(ref, sem):
        remote(ref, ref, sem, sem, (row, col)).wait_send()

    first = lax.broadcasted_iota(jnp.int32, (32, 128), 1) < HALF
    keep = first == (core == 0)

    def turn(value):
        return pltpu.roll(value, HALF, 1)

    load_pos = pltpu.make_async_copy(pos_hbm, pos_ref, load_sem.at[0])
    load_pos.start()
    load_z = pltpu.make_async_copy(z_hbm, z_ref, load_sem.at[1])
    load_z.start()
    barrier = pltpu.get_barrier_semaphore()

    def signal(device):
        pl.semaphore_signal(barrier, inc=1, device_id=device, device_id_type=MESH)

    signal(sibling)
    for dx, dy in PLANE_ORDER:
        signal(plane_at(dx, dy))
    for dz in LINE_ORDER:
        signal(line_at(dz))
        signal(line_mate(dz))

    flatten[...] = jnp.zeros_like(flatten)
    acc[...] = jnp.zeros_like(acc)
    acc_wide[...] = jnp.zeros_like(acc_wide)
    part[...] = jnp.zeros_like(part)
    for k in range(2):
        red_src[2 * k] = jnp.zeros((1, WIDTH), F32)
    load_pos.wait()
    flatten[0:3, 0:32] = pos_ref[...].astype(F32)
    rows3 = flatten[...]
    posrow[core] = rows3[0:1] + pltpu.roll(rows3[1:2], 32, 1) + pltpu.roll(rows3[2:3], 64, 1)
    load_z.wait()
    pl.semaphore_wait(barrier, 30)

    remote(posrow.at[core], posrow.at[core], pos_sem.at[0], pos_sem.at[1], sibling).start()
    remote(z_ref, z_mate, mate_sem.at[0], mate_sem.at[1], sibling).start()
    wait_recv(posrow.at[0], pos_sem.at[1])
    both = jnp.concatenate([posrow[0], posrow[1]], axis=1)
    posbuf[chip] = both
    posbuf[my_line] = both
    for n, spot in enumerate(PLANE_ORDER):
        if n < 7:
            remote(posbuf.at[my_line], posbuf.at[my_line], pos_sem.at[2], pos_sem.at[3],
                   line_at(LINE_ORDER[n])).start()
        remote(posbuf.at[chip], posbuf.at[chip], pos_sem.at[2], pos_sem.at[3], plane_at(*spot)).start()
    wait_recv(z_mate, mate_sem.at[1])
    for axis in range(3):
        packed[0, axis] = jnp.where(keep, z_ref[axis], turn(z_mate[axis]))

    lower, upper = pl.ds(0, 16), pl.ds(16, 16)

    def gather(step):
        def to_line():
            for n, dz in enumerate(LINE_NEAR):
                remote(packed.at[step], ag.at[step, my_line], ag_send.at[step], line_sem.at[step, n],
                       line_at(dz)).start()

        def to_plane():
            for n, spot in enumerate(PLANE_NEAR):
                remote(packed.at[step], ag.at[step, chip], ag_send.at[step], plane_sem.at[step, n],
                       plane_at(*spot)).start()

        last = step == 2
        pl.when(core == 0)(to_line)
        pl.when((core == 1) | last)(to_plane)
        pl.when((core == 1) & last)(to_line)
        ag[step, chip] = packed[step]
        ag[step, my_line] = packed[step]

    def forward(step):
        def pass_on(slot, rows, sem, device):
            ref = ag.at[step, slot] if rows is None else ag.at[step, slot, :, rows, :]
            remote(ref, ref, ag_send.at[step], sem.at[step, 6], device).start()

        def on_line():
            for n, dz in ((0, 2), (1, 6)):
                slot = PLANE + zs[8 - dz]
                wait_recv(ag.at[step, slot], line_sem.at[step, n])
                pass_on(slot, (lower, upper)[n], line_sem, line_at(dz))
                pass_on(slot, None, line_sem, line_at(dz // 2 if dz == 2 else 7))

        def on_plane():
            for n, (dx, dy) in enumerate(PLANE_NEAR):
                slot = xs[(4 - dx) % 4] * 4 + ys[(4 - dy) % 4]
                wait_recv(ag.at[step, slot], plane_sem.at[step, n])
                for d in (2, 1, 3):
                    if dx:
                        pass_on(slot, lower, plane_sem, plane_at(0, d))
                    else:
                        pass_on(slot, upper, plane_sem, plane_at(d, 0))

        last = step == 2
        pl.when(core == 0)(on_line)
        pl.when((core == 1) | last)(on_plane)
        pl.when((core == 1) & last)(on_line)

    gather(0)
    narrow[...] = jnp.zeros_like(narrow)
    wait_recv(posbuf.at[pl.ds(0, 22)], pos_sem.at[3])

    lane_of = lax.broadcasted_iota(jnp.int32, (BLOCK, 128), 1)
    bead_of = lax.broadcasted_iota(jnp.int32, (BLOCK, 128), 0) & 31
    entry_of = lax.broadcasted_iota(jnp.int32, (128, BLOCK), 0)
    column_of = lax.broadcasted_iota(jnp.int32, (128, BLOCK), 1) & 31
    owner_of = lax.broadcasted_iota(jnp.int32, (16, BLOCK), 1) >> 5
    source_of = lax.broadcasted_iota(jnp.int32, (16, BLOCK), 0)
    ones = jnp.ones((128, 128), BF16)

    def place(at, d):
        return posbuf[at + d // 2][:, (d % 2) * 128:(d % 2) * 128 + 128]

    @pl.loop(0, 2)
    def _(h):
        rows_at = jnp.where(core == 0, h, 2) * 8
        lanes_at = jnp.where(core == 0, 2, h) * 8
        spread = jnp.concatenate([jnp.broadcast_to(place(rows_at, d), (32, 128)) for d in range(16)], axis=0)
        flat = jnp.concatenate([place(lanes_at, d) for d in range(16)], axis=0).astype(BF16)
        for axis in range(3):
            own = jnp.where(lane_of == axis * 32 + bead_of, spread, 0.0).astype(BF16)
            colbc[h, axis] = jnp.dot(own, ones, preferred_element_type=F32)
            pick = jnp.where(entry_of == axis * 32 + column_of, 1.0, 0.0).astype(BF16)
            moved = jnp.dot(flat, pick, preferred_element_type=F32)
            lanevec[h, axis:axis + 1, :] = jnp.sum(jnp.where(owner_of == source_of, moved, 0.0), axis=0, keepdims=True)

    def group_of(t):
        d = jnp.where(t == 0, 2, jnp.where(t == 1, 1, jnp.where(t == 2, 3, 0)))
        return jnp.where(core == 0, lax.rem(x + d, 4), lax.rem(lax.div(z, 4) + 1 + lax.div(t, 2), 2))

    def places(t, group):
        h = jnp.where(core == 0, lax.div(group, 2), lax.rem(t, 2))
        rt = jnp.where(core == 0, lax.rem(group, 2), group)
        return h, jnp.where(core == 0, 0, h), pl.ds(pl.multiple_of(rt * 256, 256), 256)

    def build(t):
        h, _, span = places(t, group_of(t))

        @pl.loop(0, 16, unroll=2)
        def _(r):
            rows = pl.ds(pl.multiple_of(span.start + r * 16, 16), 16)
            mine = [colbc[h, axis, rows, :] for axis in range(3)]
            for tile in range(4):
                lanes = slice(tile * 128, tile * 128 + 128)
                d = [mine[axis] - lanevec[h, axis:axis + 1, lanes] for axis in range(3)]
                squared = d[0] * d[0] + d[1] * d[1] + d[2] * d[2]
                root = lax.rsqrt(jnp.where(squared > 0.5, squared, 1e30))
                inverse = root * root
                prefactor = (0.75 * RADIUS) * root
                iso = prefactor * (1.0 + (2.0 / 3.0 * RADIUS * RADIUS) * inverse)
                along = (prefactor * inverse) * (1.0 - (2.0 * RADIUS * RADIUS) * inverse)
                s = [along * d[axis] for axis in range(3)]
                parts = (s[0] * d[0] + iso, s[0] * d[1], s[0] * d[2], s[1] * d[1] + iso, s[1] * d[2],
                         s[2] * d[2] + iso)
                for k, value in enumerate(parts):
                    high = value.astype(BF16)
                    at = slice(k * BLOCK + tile * 128, k * BLOCK + tile * 128 + 128)
                    mob_high[h, rows, at] = high
                    mob_low[h, rows, at] = (value - high.astype(F32)).astype(BF16)

    def widen(h):
        base = jnp.where(core == 0, PLANE, h * 8)

        @pl.loop(0, 8)
        def _(s):
            for axis in range(3):
                value = ag[0, base + s, axis]
                other = turn(value)
                for j, both in enumerate((jnp.where(first, value, other), jnp.where(first, other, value))):
                    high = both.astype(BF16).astype(F32)
                    tile = jnp.where(first, high, both - high).astype(BF16)
                    at = pl.ds(pl.multiple_of(s * 64 + j * 32, 32), 32)
                    wide[h, at, axis * 128:axis * 128 + 128] = tile
                    if axis == 0:
                        wide[h, at, 384:512] = tile

    def arrange(step, h):
        base = jnp.where(core == 0, PLANE, h * 8)

        @pl.loop(0, 8)
        def _(s):
            values = [ag[step, base + s, axis] for axis in range(3)]
            others = [turn(value) for value in values]
            for j in range(2):
                left, right = (values, others) if j == 0 else (others, values)
                lx, ly, lz = (jnp.where(first, v, 0.0).astype(BF16) for v in left)
                ry, rz = (jnp.where(first, 0.0, v).astype(BF16) for v in right[1:])
                yx = jnp.where(first, left[1], right[0]).astype(BF16)
                for k, half, tile in ((0, 0, lx), (1, 0, yx), (2, 0, lz), (2, 1, lx), (3, 0, ry), (4, 0, rz),
                                      (4, 1, ly), (5, 1, lz)):
                    at = pl.ds(pl.multiple_of(k * BLOCK + s * 64 + j * 32, 32), 32)
                    narrow[h, at, half * 128:half * 128 + 128] = tile

    def dot(left, right):
        return jnp.dot(left, right, preferred_element_type=F32)

    def product(t, group):
        h, w, rows = places(t, group)

        def both(k, lo, hi):
            at = slice(k * BLOCK, k * BLOCK + BLOCK)
            return dot(mob_high[h, rows, at], wide[w, :, lo:hi]) + dot(mob_low[h, rows, at], wide[w, :, lo:hi])

        xy, yz, zx = both(1, 0, 256), both(4, 128, 384), both(2, 256, 512)
        return (both(0, 0, 128) + xy[:, 128:] + zx[:, :128],
                both(3, 128, 256) + xy[:, :128] + yz[:, 128:],
                both(5, 256, 384) + zx[:, 128:] + yz[:, :128])

    def halves(i, upper):
        return pl.ds(pl.multiple_of(i * 64 + upper * 32, 32), 32)

    def pack(i):
        chunk = []
        for axis in range(3):
            low, high = acc[axis, halves(i, 0), :], acc[axis, halves(i, 1), :]
            chunk.append(jnp.where(first, low + turn(low), high + turn(high)))
        return chunk

    def pack_wide(i):
        low, high = halves(i, 0), halves(i, 1)
        xy_low, xy_high = acc_wide[low, :128], acc_wide[high, :128]
        z_low, z_high = acc_wide[low, 128:], acc_wide[high, 128:]
        return (jnp.where(first, xy_low, turn(xy_high)), jnp.where(first, turn(xy_low), xy_high),
                jnp.where(first, z_low, turn(z_high)))

    def scatter(step, group, packer):
        slot = jnp.where(core == 0, chip, z)
        near = jnp.where(core == 0, y, lax.rem(z, 4))
        for d in (2, 1, 3, 0):
            j = lax.rem(near + d, 4)
            q = group * 4 + j
            for axis, value in enumerate(packer(j)):
                rs_send[step, q, axis] = value
            device = (jnp.where(core == 0, group * 2, row), jnp.where(core == 0, z * 4 + j, q * 4 + y))

            def send(q=q, device=device):
                remote(rs_send.at[step, q], rs.at[step, slot], rs_sent.at[step], rs_recv.at[step], device).start()

            if d:
                send()
            else:
                pl.when(q != slot)(send)

                @pl.when(q == slot)
                def _(q=q):
                    rs[step, slot] = rs_send[step, q]

    def collect(step):
        @pl.when(core == 0)
        def _():
            wait_recv(rs.at[step, pl.ds(0, PLANE - 1)], rs_recv.at[step])
            for axis in range(3):
                packed[step + 1, axis] = sum((rs[step, s, axis] for s in range(1, PLANE)), rs[step, 0, axis])

        @pl.when(core == 1)
        def _():
            wait_recv(rs.at[step, pl.ds(0, LINE - 1)], rs_recv.at[step])
            for axis in range(3):
                packed[step + 1, axis] = sum((rs[step, s, axis] for s in range(1, LINE)), rs[step, 0, axis])

    def wait_line(step):
        for n in (2, 3):
            wait_recv(ag.at[step, 0], line_sem.at[step, n])
        wait_recv(ag.at[step, pl.ds(0, 3)], line_sem.at[step, 6])

    def wait_plane(step):
        wait_recv(ag.at[step, pl.ds(0, 9)], plane_sem.at[step, 6])

    def wait_vector(step):
        pl.when(core == 0)(lambda: wait_line(step))
        pl.when(core == 1)(lambda: wait_plane(step))

    front = lax.broadcasted_iota(jnp.int32, (1, 128), 1) < HALF

    def fold(value):
        line = jnp.sum(value, axis=0, keepdims=True)
        return line + turn(line)

    def inner(left, right):
        return fold(sum(left[axis] * right[axis] for axis in range(3)))

    def reduce_plane(k, values):
        for n, value in values:
            red_src[2 * k, :, n * 128:n * 128 + 128] = value
        for spot in PLANE_ORDER:
            remote(red_src.at[2 * k], red_one.at[k, chip], red_sem.at[k, 0], red_sem.at[k, 1], plane_at(*spot)).start()
        red_one[k, chip] = red_src[2 * k]

    def reduce_line(k):
        def send(device):
            remote(red_src.at[2 * k + 1], red_two.at[k, core, z], red_sem.at[k, 2], red_sem.at[k, 3], device).start()

        wait_recv(red_one.at[k, pl.ds(0, PLANE - 1)], red_sem.at[k, 1])
        red_src[2 * k + 1] = sum((red_one[k, s] for s in range(1, PLANE)), red_one[k, 0])
        for dz in LINE_ORDER:
            send(line_at(dz))
            if k == 1:
                send(line_mate(dz))
        if k == 1:
            send(sibling)
        red_two[k, core, z] = red_src[2 * k + 1]

    def reduced(k, c):
        return sum((red_two[k, c, s] for s in range(1, LINE)), red_two[k, c, 0])

    forward(0)

    @pl.loop(0, 2)
    def _(t):
        build(t)

    wait_vector(0)
    widen(0)

    @pl.when(core == 1)
    def _():
        widen(1)

    @pl.loop(0, 4)
    def _(t):
        group = group_of(t)

        @pl.when(t >= 2)
        def _():
            build(t)

        more = (core == 1) & (lax.rem(t, 2) == 1)
        for axis, value in enumerate(product(t, group)):
            acc[axis] = jnp.where(more, acc[axis], 0.0) + value

        @pl.when((core == 0) | (lax.rem(t, 2) == 1))
        def _():
            scatter(0, group, pack)

    collect(0)
    gather(1)
    reduce_plane(0, ((0, inner(packed.at[0], packed.at[0])), (1, inner(packed.at[0], packed.at[1]))))

    @pl.loop(1, ITERS)
    def _(step):
        forward(step)
        wait_vector(step)
        arrange(step, 0)

        @pl.when(core == 1)
        def _():
            arrange(step, 1)

        @pl.loop(0, 4)
        def _(t):
            group = group_of(t)
            h, w, rows = places(t, group)
            more = (core == 1) & (lax.rem(t, 2) == 1) & (step == 1)
            acc_wide[...] = jnp.where(more, acc_wide[...], 0.0) + dot(mob_high[h, rows, :], narrow[w])

            @pl.when((step == 1) & ((core == 0) | (lax.rem(t, 2) == 1)))
            def _():
                scatter(1, group, pack_wide)

            @pl.when(step == 2)
            def _():
                pl.when((t == 0) & (core == 0))(lambda: wait_plane(2))
                pl.when((t == 0) & (core == 1))(lambda: wait_line(2))
                at = jnp.where(core == 0, 0, PLANE) + group * 4
                total = part[...]
                for i in range(4):
                    for axis, value in enumerate(pack_wide(i)):
                        total = total + value * ag[2, at + i, axis]
                part[...] = total

        @pl.when(step == 1)
        def _():
            reduce_line(0)
            collect(1)
            wait_recv(red_two.at[0, 0, pl.ds(0, LINE - 1)], red_sem.at[0, 3])
            total = reduced(0, core)
            moments[0] = jnp.broadcast_to(total[:, 128:256] / total[:, 0:128], (32, 128))
            a1 = moments[0]
            for axis in range(3):
                y1 = packed[1, axis]
                packed[2, axis] = packed[2, axis] - a1 * y1
                first_dir[axis] = y1 - a1 * packed[0, axis]
            gather(2)
            remote(first_dir, mate.at[0], mate_sem.at[2], mate_sem.at[3], sibling).start()
            remote(packed.at[2], mate.at[1], mate_sem.at[2], mate_sem.at[3], sibling).start()

    reduce_plane(1, ((0, red_src[0][:, 0:128]), (1, red_src[0][:, 128:256]),
                     (2, inner(first_dir, first_dir)), (3, inner(first_dir, packed.at[2])),
                     (4, inner(packed.at[2], packed.at[2])), (5, fold(part[...]))))
    reduce_line(1)
    wait_recv(red_one.at[1, pl.ds(0, 2 * LINE - 1)], red_sem.at[1, 3])
    low, high = reduced(1, 0), reduced(1, 1)
    for k in range(6):
        at = slice(k * 128, k * 128 + 128)
        moments[k + 1, 0:8] = jnp.broadcast_to(jnp.where(front, low[:, at], high[:, at]), (8, 128))
    moments[7, 0:8] = jnp.zeros((8, 128), F32)
    moments[8, 0:8] = jnp.ones((8, 128), F32)
    m0, m1, e1, f1, g, third, zero, one = (moments[k, 0:8] for k in range(1, 9))

    a1, a2, bb2 = m1 / m0, f1 / e1, e1 / m0
    e2 = g - a2 * f1 - bb2 * e1
    bb3 = e2 / e1
    a3 = (third - a2 * g - bb2 * (f1 + a1 * e1)) / e2 - a2
    d1, d2, d3 = 1.0 + a1, 1.0 + a2, 1.0 + a3
    scale = (d1 + d2 + d3) / ITERS
    current = (d1 / scale, jnp.sqrt(bb2) / scale, zero, d2 / scale, jnp.sqrt(bb3) / scale, d3 / scale)
    partner = (one, zero, zero, one, zero, one)

    def inverse_three(m):
        c00, c01, c02 = m[3] * m[5] - m[4] * m[4], m[2] * m[4] - m[1] * m[5], m[1] * m[4] - m[2] * m[3]
        c11, c12, c22 = m[0] * m[5] - m[2] * m[2], m[1] * m[2] - m[0] * m[4], m[0] * m[3] - m[1] * m[1]
        over = 1.0 / (m[0] * c00 + m[1] * c01 + m[2] * c02)
        return tuple(c * over for c in (c00, c01, c02, c11, c12, c22))

    def newton(_, state):
        now, other = state
        return (tuple(0.5 * (u + v) for u, v in zip(now, inverse_three(other))),
                tuple(0.5 * (u + v) for u, v in zip(other, inverse_three(now))))

    current, partner = lax.fori_loop(0, 20, newton, (current, partner))
    size = jnp.sqrt(scale)
    beta = jnp.sqrt(m0)
    r1, r2, r3 = (current[k] * size for k in range(3))
    f2, f3 = beta * r2 / jnp.sqrt(e1), beta * r3 / jnp.sqrt(e2)
    wait_recv(mate, mate_sem.at[3])
    c0, c1, c2 = (jnp.concatenate([c, c, c, c], axis=0) for c in (r1 - f3 * bb2, f2 - f3 * a2, f3))
    for axis in range(3):
        out_ref[axis] = (c0 * z_ref[axis] + c1 * jnp.where(keep, first_dir[axis], turn(mate[0, axis]))
                         + c2 * jnp.where(keep, packed[2, axis], turn(mate[1, axis])))

    wait_send(posrow.at[0], pos_sem.at[0])
    wait_send(z_mate, mate_sem.at[0])
    wait_send(mate, mate_sem.at[2])
    wait_send(posbuf.at[pl.ds(0, 22)], pos_sem.at[2])
    wait_send(ag.at[2, pl.ds(0, 22)], ag_send.at[2])
    for k, count in enumerate((LINE - 1, 2 * LINE - 1)):
        wait_send(red_one.at[k, pl.ds(0, PLANE - 1)], red_sem.at[k, 0])
        wait_send(red_one.at[k, pl.ds(0, count)], red_sem.at[k, 2])
    for step in range(2):
        @pl.when(core == 0)
        def _(step=step):
            wait_send(ag.at[step, pl.ds(0, LINE - 1)], ag_send.at[step])
            wait_send(rs_send.at[step, pl.ds(0, PLANE - 1)], rs_sent.at[step])

        @pl.when(core == 1)
        def _(step=step):
            wait_send(ag.at[step, pl.ds(0, PLANE - 1)], ag_send.at[step])
            wait_send(rs_send.at[step, pl.ds(0, LINE - 1)], rs_sent.at[step])


def shards(positions, start_vector):
    chunk = (3, 32, 128)
    return pl.pallas_call(
        kernel,
        out_shape=jax.ShapeDtypeStruct(start_vector.shape, F32),
        in_specs=[pl.BlockSpec(memory_space=pltpu.HBM)] * 2,
        out_specs=pl.BlockSpec(memory_space=pltpu.VMEM),
        scratch_shapes=[
            pltpu.VMEM((2, 1, 128), F32),
            pltpu.VMEM((PLANE + LINE, 1, 256), F32),
            pltpu.VMEM((2, 3, BLOCK, 128), F32),
            pltpu.VMEM((2, 8, BLOCK), F32),
            pltpu.VMEM((2, BLOCK, 6 * BLOCK), BF16),
            pltpu.VMEM((2, BLOCK, 6 * BLOCK), BF16),
            pltpu.VMEM((2, BLOCK, 512), BF16),
            pltpu.VMEM((2, 6 * BLOCK, 256), BF16),
            pltpu.VMEM((3, PLANE + LINE) + chunk, F32),
            pltpu.VMEM((2, PLANE) + chunk, F32),
            pltpu.VMEM((2, PLANE) + chunk, F32),
            pltpu.VMEM((3,) + chunk, F32),
            pltpu.VMEM(chunk, F32),
            pltpu.VMEM((2,) + chunk, F32),
            pltpu.VMEM((3, 256, 128), F32),
            pltpu.VMEM((256, 256), F32),
            pltpu.VMEM((32, 128), F32),
            pltpu.VMEM((4, 1, WIDTH), F32),
            pltpu.VMEM((2, PLANE, 1, WIDTH), F32),
            pltpu.VMEM((2, 2, LINE, 1, WIDTH), F32),
            pltpu.VMEM((9, 32, 128), F32),
            pltpu.VMEM((3, 32), jnp.int32),
            pltpu.VMEM((8, 128), F32),
            pltpu.VMEM(chunk, F32),
            pltpu.VMEM(chunk, F32),
            pltpu.SemaphoreType.DMA((2,)),
            pltpu.SemaphoreType.DMA((4,)),
            pltpu.SemaphoreType.DMA((4,)),
            pltpu.SemaphoreType.DMA((3, 7)),
            pltpu.SemaphoreType.DMA((3, 7)),
            pltpu.SemaphoreType.DMA((3,)),
            pltpu.SemaphoreType.DMA((2,)),
            pltpu.SemaphoreType.DMA((2,)),
            pltpu.SemaphoreType.DMA((2, 4)),
        ],
        compiler_params=pltpu.CompilerParams(
            collective_id=0, has_side_effects=True, vmem_limit_bytes=40 * 1024 * 1024),
    )(positions, start_vector)


def solution(mesh):
    in_specs = (P(None, ("row", "col")), P(None, ("row", "col"), None))
    out_specs = P(None, ("row", "col"), None)
    return jax.shard_map(shards, mesh=mesh, in_specs=in_specs, out_specs=out_specs, check_vma=False)
```

```python
import functools

import jax
import jax.numpy as jnp
from jax import lax
from jax.experimental import pallas as pl
from jax.experimental.pallas import tpu as pltpu
from jax.sharding import PartitionSpec as P

ITERS = 3
RADIUS = 0.4
MESH = pl.DeviceIdType.MESH
F32 = jnp.float32
BF16 = jnp.bfloat16

PLANE, LINE = 16, 8
PLACES = ((0, 0), (0, 1), (0, 3), (1, 0), (3, 0), (2, 0), (0, 2), (1, 1), (3, 3), (1, 3), (3, 1),
          (1, 2), (2, 1), (3, 2), (2, 3), (2, 2))
STEPS = (0, 1, 7, 2, 6, 3, 5, 4)


def seen_in_plane(dx, dy):
    return PLACES.index((-dx % 4, -dy % 4))


def seen_in_line(dz):
    return PLANE + STEPS.index(-dz % 8)


HALF = 64
BLOCK = 512
WIDTH = 768


def kernel(pos_hbm, z_hbm, out_ref, posrow, posbuf, colbc, lanevec, mob_high, mob_low, wide, narrow, ag, rs, rs_send,
           packed, first_dir, mate, acc, acc_wide, part, red_src, red_one, red_two, moments, pos_ref, flatten, z_ref,
           z_mate, load_sem, mate_sem, pos_sem, line_sem, plane_sem, ag_send, rs_recv, rs_sent, red_sem):
    row, col = lax.axis_index("row"), lax.axis_index("col")
    x, core = lax.div(row, 2), lax.rem(row, 2)
    z, y = lax.div(col, 4), lax.rem(col, 4)

    xs = [lax.rem(x + d, 4) for d in range(4)]
    ys = [lax.rem(y + d, 4) for d in range(4)]
    zs = [lax.rem(z + d, 8) for d in range(8)]

    def plane_at(dx, dy):
        return (xs[dx] * 2 + core, z * 4 + ys[dy])

    far_places, far_steps = PLACES[:0:-1], STEPS[:0:-1]

    def line_at(dz):
        return (row, zs[dz] * 4 + y)

    def line_mate(dz):
        return (x * 2 + 1 - core, zs[dz] * 4 + y)

    sibling = (x * 2 + 1 - core, col)

    def remote(src, dst, send, recv, device):
        return pltpu.make_async_remote_copy(
            src_ref=src, dst_ref=dst, send_sem=send, recv_sem=recv, device_id=device, device_id_type=MESH)

    def wait_recv(ref, sem):
        remote(ref, ref, sem, sem, (row, col)).wait_recv()

    def wait_send(ref, sem):
        remote(ref, ref, sem, sem, (row, col)).wait_send()

    first = lax.broadcasted_iota(jnp.int32, (32, 128), 1) < HALF
    keep = first == (core == 0)

    def turn(value):
        return pltpu.roll(value, HALF, 1)

    load_pos = pltpu.make_async_copy(pos_hbm, pos_ref, load_sem.at[0])
    load_pos.start()
    load_z = pltpu.make_async_copy(z_hbm, z_ref, load_sem.at[1])
    load_z.start()
    barrier = pltpu.get_barrier_semaphore()

    def signal(device):
        pl.semaphore_signal(barrier, inc=1, device_id=device, device_id_type=MESH)

    signal(sibling)
    for dx, dy in far_places:
        signal(plane_at(dx, dy))
    for dz in far_steps:
        signal(line_at(dz))
        signal(line_mate(dz))

    flatten[...] = jnp.zeros_like(flatten)
    acc[...] = jnp.zeros_like(acc)
    acc_wide[...] = jnp.zeros_like(acc_wide)
    part[...] = jnp.zeros_like(part)
    for k in range(2):
        red_src[2 * k] = jnp.zeros((1, WIDTH), F32)
    load_pos.wait()
    flatten[0:3, 0:32] = pos_ref[...].astype(F32)
    rows3 = flatten[...]
    posrow[core] = rows3[0:1] + pltpu.roll(rows3[1:2], 32, 1) + pltpu.roll(rows3[2:3], 64, 1)
    load_z.wait()
    pl.semaphore_wait(barrier, 30)

    remote(posrow.at[core], posrow.at[core], pos_sem.at[0], pos_sem.at[1], sibling).start()
    remote(z_ref, z_mate, mate_sem.at[0], mate_sem.at[1], sibling).start()
    wait_recv(posrow.at[0], pos_sem.at[1])
    both = jnp.concatenate([posrow[0], posrow[1]], axis=1)
    posbuf[0] = both
    posbuf[PLANE] = both
    for n, spot in enumerate(far_places):
        if n < 7:
            remote(posbuf.at[PLANE], posbuf.at[seen_in_line(far_steps[n])], pos_sem.at[2], pos_sem.at[3],
                   line_at(far_steps[n])).start()
        remote(posbuf.at[0], posbuf.at[seen_in_plane(*spot)], pos_sem.at[2], pos_sem.at[3], plane_at(*spot)).start()
    wait_recv(z_mate, mate_sem.at[1])
    for axis in range(3):
        packed[0, axis] = jnp.where(keep, z_ref[axis], turn(z_mate[axis]))

    def gather(step):
        def to_line():
            for dz in STEPS[1:]:
                slot = seen_in_line(dz)
                remote(packed.at[step], ag.at[step, slot], ag_send.at[step], line_sem.at[step, (slot - PLANE) // 4],
                       line_at(dz)).start()

        def to_plane():
            for spot in PLACES[1:]:
                slot = seen_in_plane(*spot)
                remote(packed.at[step], ag.at[step, slot], ag_send.at[step], plane_sem.at[step, slot // 8],
                       plane_at(*spot)).start()

        last = step == 2
        pl.when(core == 0)(to_line)
        pl.when((core == 1) | last)(to_plane)
        pl.when((core == 1) & last)(to_line)
        ag[step, 0] = packed[step]
        ag[step, PLANE] = packed[step]

    def wait_line(step, part_of):
        wait_recv(ag.at[step, pl.ds(0, 4 if part_of else 3)], line_sem.at[step, part_of])

    def wait_plane(step, part_of):
        wait_recv(ag.at[step, pl.ds(0, 8 if part_of else 7)], plane_sem.at[step, part_of])

    gather(0)
    narrow[...] = jnp.zeros_like(narrow)
    wait_recv(posbuf.at[pl.ds(0, 22)], pos_sem.at[3])

    lane_of = lax.broadcasted_iota(jnp.int32, (BLOCK, 128), 1)
    bead_of = lax.broadcasted_iota(jnp.int32, (BLOCK, 128), 0) & 31
    entry_of = lax.broadcasted_iota(jnp.int32, (128, BLOCK), 0)
    column_of = lax.broadcasted_iota(jnp.int32, (128, BLOCK), 1) & 31
    owner_of = lax.broadcasted_iota(jnp.int32, (16, BLOCK), 1) >> 5
    source_of = lax.broadcasted_iota(jnp.int32, (16, BLOCK), 0)
    ones = jnp.ones((128, 128), BF16)

    def place(at, d):
        return posbuf[at + d // 2][:, (d % 2) * 128:(d % 2) * 128 + 128]

    @pl.loop(0, 2)
    def _(h):
        rows_at = jnp.where(core == 0, h, 2) * 8
        lanes_at = jnp.where(core == 0, 2, h) * 8
        spread = jnp.concatenate([jnp.broadcast_to(place(rows_at, d), (32, 128)) for d in range(16)], axis=0)
        flat = jnp.concatenate([place(lanes_at, d) for d in range(16)], axis=0).astype(BF16)
        for axis in range(3):
            own = jnp.where(lane_of == axis * 32 + bead_of, spread, 0.0).astype(BF16)
            colbc[h, axis] = jnp.dot(own, ones, preferred_element_type=F32)
            pick = jnp.where(entry_of == axis * 32 + column_of, 1.0, 0.0).astype(BF16)
            moved = jnp.dot(flat, pick, preferred_element_type=F32)
            lanevec[h, axis:axis + 1, :] = jnp.sum(jnp.where(owner_of == source_of, moved, 0.0), axis=0, keepdims=True)

    def tile_of(t):
        return jnp.where(core == 0, 3 - t, 1 - lax.div(t, 2))

    def places(t):
        tile = tile_of(t)
        h = jnp.where(core == 0, lax.div(tile, 2), lax.rem(t, 2))
        rt = jnp.where(core == 0, lax.rem(tile, 2), tile)
        return h, jnp.where(core == 0, 0, h), pl.ds(pl.multiple_of(rt * 256, 256), 256)

    def build(t):
        h, _, span = places(t)

        @pl.loop(0, 16, unroll=2)
        def _(r):
            rows = pl.ds(pl.multiple_of(span.start + r * 16, 16), 16)
            mine = [colbc[h, axis, rows, :] for axis in range(3)]
            for tile in range(4):
                lanes = slice(tile * 128, tile * 128 + 128)
                d = [mine[axis] - lanevec[h, axis:axis + 1, lanes] for axis in range(3)]
                squared = d[0] * d[0] + d[1] * d[1] + d[2] * d[2]
                root = lax.rsqrt(jnp.where(squared > 0.5, squared, 1e30))
                inverse = root * root
                prefactor = (0.75 * RADIUS) * root
                iso = prefactor * (1.0 + (2.0 / 3.0 * RADIUS * RADIUS) * inverse)
                along = (prefactor * inverse) * (1.0 - (2.0 * RADIUS * RADIUS) * inverse)
                s = [along * d[axis] for axis in range(3)]
                parts = (s[0] * d[0] + iso, s[0] * d[1], s[0] * d[2], s[1] * d[1] + iso, s[1] * d[2],
                         s[2] * d[2] + iso)
                for k, value in enumerate(parts):
                    high = value.astype(BF16)
                    at = (tile // 2) * 1536 + k * 256 + (tile % 2) * 128
                    at = slice(at, at + 128)
                    mob_high[h, rows, at] = high
                    mob_low[h, rows, at] = (value - high.astype(F32)).astype(BF16)

    def widen(h):
        base = jnp.where(core == 0, PLANE, h * 8)

        @pl.loop(0, 8)
        def _(s):
            for axis in range(3):
                value = ag[0, base + s, axis]
                other = turn(value)
                for j, both in enumerate((jnp.where(first, value, other), jnp.where(first, other, value))):
                    high = both.astype(BF16).astype(F32)
                    tile = jnp.where(first, high, both - high).astype(BF16)
                    at = pl.ds(pl.multiple_of(s * 64 + j * 32, 32), 32)
                    wide[h, at, axis * 128:axis * 128 + 128] = tile
                    if axis == 0:
                        wide[h, at, 384:512] = tile

    def arrange(step, base, w, quarter):
        @pl.loop(0, 4)
        def _(s):
            values = [ag[step, base + s, axis] for axis in range(3)]
            others = [turn(value) for value in values]
            for j in range(2):
                left, right = (values, others) if j == 0 else (others, values)
                lx, ly, lz = (jnp.where(first, v, 0.0).astype(BF16) for v in left)
                ry, rz = (jnp.where(first, 0.0, v).astype(BF16) for v in right[1:])
                yx = jnp.where(first, left[1], right[0]).astype(BF16)
                for k, half, tile in ((0, 0, lx), (1, 0, yx), (2, 0, lz), (2, 1, lx), (3, 0, ry), (4, 0, rz),
                                      (4, 1, ly), (5, 1, lz)):
                    at = pl.ds(pl.multiple_of(quarter * 1536 + k * 256 + s * 64 + j * 32, 32), 32)
                    narrow[w, at, half * 128:half * 128 + 128] = tile

    def arrange_half(step, part_of):
        @pl.when(core == 0)
        def _():
            wait_line(step, part_of)
            arrange(step, PLANE + 4 * part_of, 0, part_of)

        @pl.when(core == 1)
        def _():
            wait_plane(step, part_of)

            @pl.loop(0, 2)
            def _(quarter):
                arrange(step, 8 * part_of + 4 * quarter, part_of, quarter)

    def dot(left, right):
        return jnp.dot(left, right, preferred_element_type=F32)

    def product(t):
        h, w, rows = places(t)

        def both(k, lo, hi):
            total = 0.0
            for quarter in range(2):
                at = slice(quarter * 1536 + k * 256, quarter * 1536 + k * 256 + 256)
                right = wide[w, quarter * 256:quarter * 256 + 256, lo:hi]
                total = total + dot(mob_high[h, rows, at], right) + dot(mob_low[h, rows, at], right)
            return total

        xy, yz, zx = both(1, 0, 256), both(4, 128, 384), both(2, 256, 512)
        return (both(0, 0, 128) + xy[:, 128:] + zx[:, :128],
                both(3, 128, 256) + xy[:, :128] + yz[:, 128:],
                both(5, 256, 384) + zx[:, 128:] + yz[:, :128])

    def halves(i, upper):
        return pl.ds(pl.multiple_of(i * 64 + upper * 32, 32), 32)

    def pack(_, i):
        chunk = []
        for axis in range(3):
            low, high = acc[axis, halves(i, 0), :], acc[axis, halves(i, 1), :]
            chunk.append(jnp.where(first, low + turn(low), high + turn(high)))
        return chunk

    def pack_wide(tile, i):
        low, high = halves(i, 0), halves(i, 1)
        xy_low, xy_high = acc_wide[tile, low, :128], acc_wide[tile, high, :128]
        z_low, z_high = acc_wide[tile, low, 128:], acc_wide[tile, high, 128:]
        return (jnp.where(first, xy_low, turn(xy_high)), jnp.where(first, turn(xy_low), xy_high),
                jnp.where(first, z_low, turn(z_high)))

    def scatter(step, t, packer):
        def send_plane(tile):
            for i in (3, 2, 1, 0):
                spot = PLACES[tile * 4 + i]
                for axis, value in enumerate(packer(tile, i)):
                    rs_send[step, tile * 4 + i, axis] = value
                if tile * 4 + i == 0:
                    rs[step, 0] = rs_send[step, 0]
                else:
                    remote(rs_send.at[step, tile * 4 + i], rs.at[step, seen_in_plane(*spot)], rs_sent.at[step],
                           rs_recv.at[step], plane_at(*spot)).start()

        def send_line(tile):
            for i in (3, 2, 1, 0):
                dz = STEPS[tile * 4 + i]
                for axis, value in enumerate(packer(tile, i)):
                    rs_send[step, tile * 4 + i, axis] = value
                if dz == 0:
                    rs[step, 0] = rs_send[step, 0]
                else:
                    remote(rs_send.at[step, tile * 4 + i], rs.at[step, seen_in_line(dz) - PLANE], rs_sent.at[step],
                           rs_recv.at[step], line_at(dz)).start()

        for n in range(4):
            pl.when((core == 0) & (t == n))(functools.partial(send_plane, 3 - n))
        for n in range(2):
            pl.when((core == 1) & (t == 2 * n + 1))(functools.partial(send_line, 1 - n))

    def collect(step):
        @pl.when(core == 0)
        def _():
            wait_recv(rs.at[step, pl.ds(0, PLANE - 1)], rs_recv.at[step])
            for axis in range(3):
                packed[step + 1, axis] = sum((rs[step, s, axis] for s in range(1, PLANE)), rs[step, 0, axis])

        @pl.when(core == 1)
        def _():
            wait_recv(rs.at[step, pl.ds(0, LINE - 1)], rs_recv.at[step])
            for axis in range(3):
                packed[step + 1, axis] = sum((rs[step, s, axis] for s in range(1, LINE)), rs[step, 0, axis])

    front = lax.broadcasted_iota(jnp.int32, (1, 128), 1) < HALF

    def fold(value):
        line = jnp.sum(value, axis=0, keepdims=True)
        return line + turn(line)

    def inner(left, right):
        return fold(sum(left[axis] * right[axis] for axis in range(3)))

    def reduce_plane(k, values):
        for n, value in values:
            red_src[2 * k, :, n * 128:n * 128 + 128] = value
        for spot in far_places:
            remote(red_src.at[2 * k], red_one.at[k, seen_in_plane(*spot)], red_sem.at[k, 0], red_sem.at[k, 1], plane_at(*spot)).start()
        red_one[k, 0] = red_src[2 * k]

    def reduce_line(k):
        def send(dz, device):
            slot = seen_in_line(dz) - PLANE
            remote(red_src.at[2 * k + 1], red_two.at[k, core, slot], red_sem.at[k, 2], red_sem.at[k, 3], device).start()

        wait_recv(red_one.at[k, pl.ds(0, PLANE - 1)], red_sem.at[k, 1])
        red_src[2 * k + 1] = sum((red_one[k, s] for s in range(1, PLANE)), red_one[k, 0])
        for dz in far_steps:
            send(dz, line_at(dz))
            if k == 1:
                send(dz, line_mate(dz))
        if k == 1:
            send(0, sibling)
        red_two[k, core, 0] = red_src[2 * k + 1]

    def reduced(k, c):
        return sum((red_two[k, c, s] for s in range(1, LINE)), red_two[k, c, 0])

    @pl.loop(0, 2)
    def _(t):
        build(t)

    @pl.when(core == 0)
    def _():
        wait_line(0, 0)
        wait_line(0, 1)

    @pl.when(core == 1)
    def _():
        wait_plane(0, 0)
        wait_plane(0, 1)
        widen(1)

    widen(0)

    @pl.loop(0, 4)
    def _(t):
        @pl.when(t >= 2)
        def _():
            build(t)

        more = (core == 1) & (lax.rem(t, 2) == 1)
        for axis, value in enumerate(product(t)):
            acc[axis] = jnp.where(more, acc[axis], 0.0) + value
        scatter(0, t, pack)

    collect(0)
    gather(1)
    reduce_plane(0, ((0, inner(packed.at[0], packed.at[0])), (1, inner(packed.at[0], packed.at[1]))))

    @pl.loop(1, ITERS)
    def _(step):
        def unit(part_of, t):
            tile = tile_of(t)
            quarter = jnp.where(core == 0, part_of, lax.rem(t, 2))
            h = jnp.where(core == 0, lax.div(tile, 2), part_of)
            w = jnp.where(core == 0, 0, part_of)
            rt = jnp.where(core == 0, lax.rem(tile, 2), tile)
            inner_at = pl.ds(pl.multiple_of(quarter * 1536, 1536), 1536)
            rows = pl.ds(pl.multiple_of(rt * 256, 256), 256)
            return tile, dot(mob_high[h, rows, inner_at], narrow[w, inner_at, :])

        arrange_half(step, 0)

        @pl.loop(0, 4)
        def _(t):
            tile, value = unit(0, t)
            more = (core == 1) & (lax.rem(t, 2) == 1)
            acc_wide[tile] = jnp.where(more, acc_wide[tile], 0.0) + value

        arrange_half(step, 1)

        @pl.loop(0, 4)
        def _(t):
            tile, value = unit(1, t)
            acc_wide[tile] += value

            @pl.when(step == 1)
            def _():
                scatter(1, t, pack_wide)

            @pl.when((step == 2) & (t == 0) & (core == 0))
            def _():
                wait_plane(2, 0)
                wait_plane(2, 1)

            @pl.when((step == 2) & (t == 0) & (core == 1))
            def _():
                wait_line(2, 0)
                wait_line(2, 1)

            @pl.when((step == 2) & ((core == 0) | (lax.rem(t, 2) == 1)))
            def _():
                at = jnp.where(core == 0, 0, PLANE) + tile * 4
                total = part[...]
                for i in range(4):
                    for axis, value in enumerate(pack_wide(tile, i)):
                        total = total + value * ag[2, at + i, axis]
                part[...] = total

        @pl.when(step == 1)
        def _():
            reduce_line(0)
            collect(1)
            wait_recv(red_two.at[0, 0, pl.ds(0, LINE - 1)], red_sem.at[0, 3])
            total = reduced(0, core)
            moments[0] = jnp.broadcast_to(total[:, 128:256] / total[:, 0:128], (32, 128))
            a1 = moments[0]
            for axis in range(3):
                y1 = packed[1, axis]
                packed[2, axis] = packed[2, axis] - a1 * y1
                first_dir[axis] = y1 - a1 * packed[0, axis]
            gather(2)
            remote(first_dir, mate.at[0], mate_sem.at[2], mate_sem.at[3], sibling).start()
            remote(packed.at[2], mate.at[1], mate_sem.at[2], mate_sem.at[3], sibling).start()

    reduce_plane(1, ((0, red_src[0][:, 0:128]), (1, red_src[0][:, 128:256]),
                     (2, inner(first_dir, first_dir)), (3, inner(first_dir, packed.at[2])),
                     (4, inner(packed.at[2], packed.at[2])), (5, fold(part[...]))))
    reduce_line(1)
    wait_recv(red_one.at[1, pl.ds(0, 2 * LINE - 1)], red_sem.at[1, 3])
    low, high = reduced(1, 0), reduced(1, 1)
    for k in range(6):
        at = slice(k * 128, k * 128 + 128)
        moments[k + 1, 0:8] = jnp.broadcast_to(jnp.where(front, low[:, at], high[:, at]), (8, 128))
    moments[7, 0:8] = jnp.zeros((8, 128), F32)
    moments[8, 0:8] = jnp.ones((8, 128), F32)
    m0, m1, e1, f1, g, third, zero, one = (moments[k, 0:8] for k in range(1, 9))

    a1, a2, bb2 = m1 / m0, f1 / e1, e1 / m0
    e2 = g - a2 * f1 - bb2 * e1
    bb3 = e2 / e1
    a3 = (third - a2 * g - bb2 * (f1 + a1 * e1)) / e2 - a2
    d1, d2, d3 = 1.0 + a1, 1.0 + a2, 1.0 + a3
    scale = (d1 + d2 + d3) / ITERS
    current = (d1 / scale, jnp.sqrt(bb2) / scale, zero, d2 / scale, jnp.sqrt(bb3) / scale, d3 / scale)
    partner = (one, zero, zero, one, zero, one)

    def inverse_three(m):
        c00, c01, c02 = m[3] * m[5] - m[4] * m[4], m[2] * m[4] - m[1] * m[5], m[1] * m[4] - m[2] * m[3]
        c11, c12, c22 = m[0] * m[5] - m[2] * m[2], m[1] * m[2] - m[0] * m[4], m[0] * m[3] - m[1] * m[1]
        over = 1.0 / (m[0] * c00 + m[1] * c01 + m[2] * c02)
        return tuple(c * over for c in (c00, c01, c02, c11, c12, c22))

    def newton(_, state):
        now, other = state
        return (tuple(0.5 * (u + v) for u, v in zip(now, inverse_three(other))),
                tuple(0.5 * (u + v) for u, v in zip(other, inverse_three(now))))

    current, partner = lax.fori_loop(0, 20, newton, (current, partner))
    size = jnp.sqrt(scale)
    beta = jnp.sqrt(m0)
    r1, r2, r3 = (current[k] * size for k in range(3))
    f2, f3 = beta * r2 / jnp.sqrt(e1), beta * r3 / jnp.sqrt(e2)
    wait_recv(mate, mate_sem.at[3])
    c0, c1, c2 = (jnp.concatenate([c, c, c, c], axis=0) for c in (r1 - f3 * bb2, f2 - f3 * a2, f3))
    for axis in range(3):
        out_ref[axis] = (c0 * z_ref[axis] + c1 * jnp.where(keep, first_dir[axis], turn(mate[0, axis]))
                         + c2 * jnp.where(keep, packed[2, axis], turn(mate[1, axis])))

    wait_send(posrow.at[0], pos_sem.at[0])
    wait_send(z_mate, mate_sem.at[0])
    wait_send(mate, mate_sem.at[2])
    wait_send(posbuf.at[pl.ds(0, 22)], pos_sem.at[2])
    wait_send(ag.at[2, pl.ds(0, 22)], ag_send.at[2])
    for k, count in enumerate((LINE - 1, 2 * LINE - 1)):
        wait_send(red_one.at[k, pl.ds(0, PLANE - 1)], red_sem.at[k, 0])
        wait_send(red_one.at[k, pl.ds(0, count)], red_sem.at[k, 2])
    for step in range(2):
        @pl.when(core == 0)
        def _(step=step):
            wait_send(ag.at[step, pl.ds(0, LINE - 1)], ag_send.at[step])
            wait_send(rs_send.at[step, pl.ds(0, PLANE - 1)], rs_sent.at[step])

        @pl.when(core == 1)
        def _(step=step):
            wait_send(ag.at[step, pl.ds(0, PLANE - 1)], ag_send.at[step])
            wait_send(rs_send.at[step, pl.ds(0, LINE - 1)], rs_sent.at[step])


def shards(positions, start_vector):
    chunk = (3, 32, 128)
    return pl.pallas_call(
        kernel,
        out_shape=jax.ShapeDtypeStruct(start_vector.shape, F32),
        in_specs=[pl.BlockSpec(memory_space=pltpu.HBM)] * 2,
        out_specs=pl.BlockSpec(memory_space=pltpu.VMEM),
        scratch_shapes=[
            pltpu.VMEM((2, 1, 128), F32),
            pltpu.VMEM((PLANE + LINE, 1, 256), F32),
            pltpu.VMEM((2, 3, BLOCK, 128), F32),
            pltpu.VMEM((2, 8, BLOCK), F32),
            pltpu.VMEM((2, BLOCK, 6 * BLOCK), BF16),
            pltpu.VMEM((2, BLOCK, 6 * BLOCK), BF16),
            pltpu.VMEM((2, BLOCK, 512), BF16),
            pltpu.VMEM((2, 6 * BLOCK, 256), BF16),
            pltpu.VMEM((3, PLANE + LINE) + chunk, F32),
            pltpu.VMEM((2, PLANE) + chunk, F32),
            pltpu.VMEM((2, PLANE) + chunk, F32),
            pltpu.VMEM((3,) + chunk, F32),
            pltpu.VMEM(chunk, F32),
            pltpu.VMEM((2,) + chunk, F32),
            pltpu.VMEM((3, 256, 128), F32),
            pltpu.VMEM((4, 256, 256), F32),
            pltpu.VMEM((32, 128), F32),
            pltpu.VMEM((4, 1, WIDTH), F32),
            pltpu.VMEM((2, PLANE, 1, WIDTH), F32),
            pltpu.VMEM((2, 2, LINE, 1, WIDTH), F32),
            pltpu.VMEM((9, 32, 128), F32),
            pltpu.VMEM((3, 32), jnp.int32),
            pltpu.VMEM((8, 128), F32),
            pltpu.VMEM(chunk, F32),
            pltpu.VMEM(chunk, F32),
            pltpu.SemaphoreType.DMA((2,)),
            pltpu.SemaphoreType.DMA((4,)),
            pltpu.SemaphoreType.DMA((4,)),
            pltpu.SemaphoreType.DMA((3, 2)),
            pltpu.SemaphoreType.DMA((3, 2)),
            pltpu.SemaphoreType.DMA((3,)),
            pltpu.SemaphoreType.DMA((2,)),
            pltpu.SemaphoreType.DMA((2,)),
            pltpu.SemaphoreType.DMA((2, 4)),
        ],
        compiler_params=pltpu.CompilerParams(
            collective_id=0, has_side_effects=True, vmem_limit_bytes=40 * 1024 * 1024),
    )(positions, start_vector)


def solution(mesh):
    in_specs = (P(None, ("row", "col")), P(None, ("row", "col"), None))
    out_specs = P(None, ("row", "col"), None)
    return jax.shard_map(shards, mesh=mesh, in_specs=in_specs, out_specs=out_specs, check_vma=False)
```

```python
import functools

import jax
import jax.numpy as jnp
from jax import lax
from jax.experimental import pallas as pl
from jax.experimental.pallas import tpu as pltpu
from jax.sharding import PartitionSpec as P

ITERS = 3
RADIUS = 0.4
MESH = pl.DeviceIdType.MESH
F32 = jnp.float32
BF16 = jnp.bfloat16

PLANE, LINE = 16, 8
PLACES = ((0, 0), (0, 1), (0, 3), (1, 0), (3, 0), (2, 0), (0, 2), (1, 1), (3, 3), (1, 3), (3, 1),
          (1, 2), (2, 1), (3, 2), (2, 3), (2, 2))
STEPS = (0, 1, 7, 2, 6, 3, 5, 4)


def seen_in_plane(dx, dy):
    return PLACES.index((-dx % 4, -dy % 4))


def seen_in_line(dz):
    return PLANE + STEPS.index(-dz % 8)


HALF = 64
BLOCK = 512
WIDTH = 768


def kernel(pos_hbm, z_hbm, w_ref, u_ref, sum_ref, posrow, posbuf, colbc, lanevec, mob_high, mob_low, wide, narrow, ag, rs, rs_send,
           packed, first_dir, mate, acc, acc_wide, part, red_src, red_one, red_two, moments, pos_ref, flatten, z_ref,
           z_mate, load_sem, mate_sem, pos_sem, line_sem, plane_sem, ag_send, rs_recv, rs_sent, red_sem):
    row, col = lax.axis_index("row"), lax.axis_index("col")
    x, core = lax.div(row, 2), lax.rem(row, 2)
    z, y = lax.div(col, 4), lax.rem(col, 4)

    xs = [lax.rem(x + d, 4) for d in range(4)]
    ys = [lax.rem(y + d, 4) for d in range(4)]
    zs = [lax.rem(z + d, 8) for d in range(8)]

    def plane_at(dx, dy):
        return (xs[dx] * 2 + core, z * 4 + ys[dy])

    far_places, far_steps = PLACES[:0:-1], STEPS[:0:-1]

    def line_at(dz):
        return (row, zs[dz] * 4 + y)

    def line_mate(dz):
        return (x * 2 + 1 - core, zs[dz] * 4 + y)

    sibling = (x * 2 + 1 - core, col)

    def remote(src, dst, send, recv, device):
        return pltpu.make_async_remote_copy(
            src_ref=src, dst_ref=dst, send_sem=send, recv_sem=recv, device_id=device, device_id_type=MESH)

    def wait_recv(ref, sem):
        remote(ref, ref, sem, sem, (row, col)).wait_recv()

    def wait_send(ref, sem):
        remote(ref, ref, sem, sem, (row, col)).wait_send()

    first = lax.broadcasted_iota(jnp.int32, (32, 128), 1) < HALF
    keep = first == (core == 0)

    def turn(value):
        return pltpu.roll(value, HALF, 1)

    load_pos = pltpu.make_async_copy(pos_hbm, pos_ref, load_sem.at[0])
    load_pos.start()
    load_z = pltpu.make_async_copy(z_hbm, z_ref, load_sem.at[1])
    load_z.start()
    barrier = pltpu.get_barrier_semaphore()

    def signal(device):
        pl.semaphore_signal(barrier, inc=1, device_id=device, device_id_type=MESH)

    signal(sibling)
    for dx, dy in far_places:
        signal(plane_at(dx, dy))
    for dz in far_steps:
        signal(line_at(dz))
        signal(line_mate(dz))

    flatten[...] = jnp.zeros_like(flatten)
    acc[...] = jnp.zeros_like(acc)
    acc_wide[...] = jnp.zeros_like(acc_wide)
    part[...] = jnp.zeros_like(part)
    for k in range(2):
        red_src[2 * k] = jnp.zeros((1, WIDTH), F32)
    load_pos.wait()
    flatten[0:3, 0:32] = pos_ref[...].astype(F32)
    rows3 = flatten[...]
    posrow[core] = rows3[0:1] + pltpu.roll(rows3[1:2], 32, 1) + pltpu.roll(rows3[2:3], 64, 1)
    load_z.wait()
    pl.semaphore_wait(barrier, 30)

    remote(posrow.at[core], posrow.at[core], pos_sem.at[0], pos_sem.at[1], sibling).start()
    remote(z_ref, z_mate, mate_sem.at[0], mate_sem.at[1], sibling).start()
    wait_recv(posrow.at[0], pos_sem.at[1])
    both = jnp.concatenate([posrow[0], posrow[1]], axis=1)
    posbuf[0] = both
    posbuf[PLANE] = both
    for n, spot in enumerate(far_places):
        if n < 7:
            remote(posbuf.at[PLANE], posbuf.at[seen_in_line(far_steps[n])], pos_sem.at[2], pos_sem.at[3],
                   line_at(far_steps[n])).start()
        remote(posbuf.at[0], posbuf.at[seen_in_plane(*spot)], pos_sem.at[2], pos_sem.at[3], plane_at(*spot)).start()
    wait_recv(z_mate, mate_sem.at[1])
    for axis in range(3):
        packed[0, axis] = jnp.where(keep, z_ref[axis], turn(z_mate[axis]))

    def gather(step):
        def to_line():
            for dz in STEPS[1:]:
                slot = seen_in_line(dz)
                remote(packed.at[step], ag.at[step, slot], ag_send.at[step], line_sem.at[step, (slot - PLANE) // 4],
                       line_at(dz)).start()

        def to_plane():
            for spot in PLACES[1:]:
                slot = seen_in_plane(*spot)
                remote(packed.at[step], ag.at[step, slot], ag_send.at[step], plane_sem.at[step, slot // 8],
                       plane_at(*spot)).start()

        last = step == 2
        pl.when(core == 0)(to_line)
        pl.when((core == 1) | last)(to_plane)
        pl.when((core == 1) & last)(to_line)
        ag[step, 0] = packed[step]
        ag[step, PLANE] = packed[step]

    def wait_line(step, part_of):
        wait_recv(ag.at[step, pl.ds(0, 4 if part_of else 3)], line_sem.at[step, part_of])

    def wait_plane(step, part_of):
        wait_recv(ag.at[step, pl.ds(0, 8 if part_of else 7)], plane_sem.at[step, part_of])

    gather(0)
    narrow[...] = jnp.zeros_like(narrow)
    wait_recv(posbuf.at[pl.ds(0, 22)], pos_sem.at[3])

    lane_of = lax.broadcasted_iota(jnp.int32, (BLOCK, 128), 1)
    bead_of = lax.broadcasted_iota(jnp.int32, (BLOCK, 128), 0) & 31
    entry_of = lax.broadcasted_iota(jnp.int32, (128, BLOCK), 0)
    column_of = lax.broadcasted_iota(jnp.int32, (128, BLOCK), 1) & 31
    owner_of = lax.broadcasted_iota(jnp.int32, (16, BLOCK), 1) >> 5
    source_of = lax.broadcasted_iota(jnp.int32, (16, BLOCK), 0)
    ones = jnp.ones((128, 128), BF16)

    def place(at, d):
        return posbuf[at + d // 2][:, (d % 2) * 128:(d % 2) * 128 + 128]

    @pl.loop(0, 2)
    def _(h):
        rows_at = jnp.where(core == 0, h, 2) * 8
        lanes_at = jnp.where(core == 0, 2, h) * 8
        spread = jnp.concatenate([jnp.broadcast_to(place(rows_at, d), (32, 128)) for d in range(16)], axis=0)
        flat = jnp.concatenate([place(lanes_at, d) for d in range(16)], axis=0).astype(BF16)
        for axis in range(3):
            own = jnp.where(lane_of == axis * 32 + bead_of, spread, 0.0).astype(BF16)
            colbc[h, axis] = jnp.dot(own, ones, preferred_element_type=F32)
            pick = jnp.where(entry_of == axis * 32 + column_of, 1.0, 0.0).astype(BF16)
            moved = jnp.dot(flat, pick, preferred_element_type=F32)
            lanevec[h, axis:axis + 1, :] = jnp.sum(jnp.where(owner_of == source_of, moved, 0.0), axis=0, keepdims=True)

    def tile_of(t):
        return jnp.where(core == 0, 3 - t, 1 - lax.div(t, 2))

    def places(t):
        tile = tile_of(t)
        h = jnp.where(core == 0, lax.div(tile, 2), lax.rem(t, 2))
        rt = jnp.where(core == 0, lax.rem(tile, 2), tile)
        return h, jnp.where(core == 0, 0, h), pl.ds(pl.multiple_of(rt * 256, 256), 256)

    def build(t):
        h, _, span = places(t)

        @pl.loop(0, 16, unroll=2)
        def _(r):
            rows = pl.ds(pl.multiple_of(span.start + r * 16, 16), 16)
            mine = [colbc[h, axis, rows, :] for axis in range(3)]
            for tile in range(4):
                lanes = slice(tile * 128, tile * 128 + 128)
                d = [mine[axis] - lanevec[h, axis:axis + 1, lanes] for axis in range(3)]
                squared = d[0] * d[0] + d[1] * d[1] + d[2] * d[2]
                root = lax.rsqrt(jnp.where(squared > 0.5, squared, 1e30))
                inverse = root * root
                prefactor = (0.75 * RADIUS) * root
                iso = prefactor * (1.0 + (2.0 / 3.0 * RADIUS * RADIUS) * inverse)
                along = (prefactor * inverse) * (1.0 - (2.0 * RADIUS * RADIUS) * inverse)
                s = [along * d[axis] for axis in range(3)]
                parts = (s[0] * d[0] + iso, s[0] * d[1], s[0] * d[2], s[1] * d[1] + iso, s[1] * d[2],
                         s[2] * d[2] + iso)
                for k, value in enumerate(parts):
                    high = value.astype(BF16)
                    at = (tile // 2) * 1536 + k * 256 + (tile % 2) * 128
                    at = slice(at, at + 128)
                    mob_high[h, rows, at] = high
                    mob_low[h, rows, at] = (value - high.astype(F32)).astype(BF16)

    def widen(h):
        base = jnp.where(core == 0, PLANE, h * 8)

        @pl.loop(0, 8)
        def _(s):
            for axis in range(3):
                value = ag[0, base + s, axis]
                other = turn(value)
                for j, both in enumerate((jnp.where(first, value, other), jnp.where(first, other, value))):
                    high = both.astype(BF16).astype(F32)
                    tile = jnp.where(first, high, both - high).astype(BF16)
                    at = pl.ds(pl.multiple_of(s * 64 + j * 32, 32), 32)
                    wide[h, at, axis * 128:axis * 128 + 128] = tile
                    if axis == 0:
                        wide[h, at, 384:512] = tile

    def arrange(step, base, w, quarter):
        @pl.loop(0, 4)
        def _(s):
            values = [ag[step, base + s, axis] for axis in range(3)]
            others = [turn(value) for value in values]
            for j in range(2):
                left, right = (values, others) if j == 0 else (others, values)
                lx, ly, lz = (jnp.where(first, v, 0.0).astype(BF16) for v in left)
                ry, rz = (jnp.where(first, 0.0, v).astype(BF16) for v in right[1:])
                yx = jnp.where(first, left[1], right[0]).astype(BF16)
                for k, half, tile in ((0, 0, lx), (1, 0, yx), (2, 0, lz), (2, 1, lx), (3, 0, ry), (4, 0, rz),
                                      (4, 1, ly), (5, 1, lz)):
                    at = pl.ds(pl.multiple_of(quarter * 1536 + k * 256 + s * 64 + j * 32, 32), 32)
                    narrow[w, at, half * 128:half * 128 + 128] = tile

    def arrange_half(step, part_of):
        @pl.when(core == 0)
        def _():
            wait_line(step, part_of)
            arrange(step, PLANE + 4 * part_of, 0, part_of)

        @pl.when(core == 1)
        def _():
            wait_plane(step, part_of)

            @pl.loop(0, 2)
            def _(quarter):
                arrange(step, 8 * part_of + 4 * quarter, part_of, quarter)

    def dot(left, right):
        return jnp.dot(left, right, preferred_element_type=F32)

    def product(t):
        h, w, rows = places(t)

        def both(k, lo, hi):
            total = 0.0
            for quarter in range(2):
                at = slice(quarter * 1536 + k * 256, quarter * 1536 + k * 256 + 256)
                right = wide[w, quarter * 256:quarter * 256 + 256, lo:hi]
                total = total + dot(mob_high[h, rows, at], right) + dot(mob_low[h, rows, at], right)
            return total

        xy, yz, zx = both(1, 0, 256), both(4, 128, 384), both(2, 256, 512)
        return (both(0, 0, 128) + xy[:, 128:] + zx[:, :128],
                both(3, 128, 256) + xy[:, :128] + yz[:, 128:],
                both(5, 256, 384) + zx[:, 128:] + yz[:, :128])

    def halves(i, upper):
        return pl.ds(pl.multiple_of(i * 64 + upper * 32, 32), 32)

    def pack(_, i):
        chunk = []
        for axis in range(3):
            low, high = acc[axis, halves(i, 0), :], acc[axis, halves(i, 1), :]
            chunk.append(jnp.where(first, low + turn(low), high + turn(high)))
        return chunk

    def pack_wide(tile, i):
        low, high = halves(i, 0), halves(i, 1)
        xy_low, xy_high = acc_wide[tile, low, :128], acc_wide[tile, high, :128]
        z_low, z_high = acc_wide[tile, low, 128:], acc_wide[tile, high, 128:]
        return (jnp.where(first, xy_low, turn(xy_high)), jnp.where(first, turn(xy_low), xy_high),
                jnp.where(first, z_low, turn(z_high)))

    def scatter(step, t, packer):
        def send_plane(tile):
            for i in (3, 2, 1, 0):
                spot = PLACES[tile * 4 + i]
                for axis, value in enumerate(packer(tile, i)):
                    rs_send[step, tile * 4 + i, axis] = value
                if tile * 4 + i == 0:
                    rs[step, 0] = rs_send[step, 0]
                else:
                    remote(rs_send.at[step, tile * 4 + i], rs.at[step, seen_in_plane(*spot)], rs_sent.at[step],
                           rs_recv.at[step], plane_at(*spot)).start()

        def send_line(tile):
            for i in (3, 2, 1, 0):
                dz = STEPS[tile * 4 + i]
                for axis, value in enumerate(packer(tile, i)):
                    rs_send[step, tile * 4 + i, axis] = value
                if dz == 0:
                    rs[step, 0] = rs_send[step, 0]
                else:
                    remote(rs_send.at[step, tile * 4 + i], rs.at[step, seen_in_line(dz) - PLANE], rs_sent.at[step],
                           rs_recv.at[step], line_at(dz)).start()

        for n in range(4):
            pl.when((core == 0) & (t == n))(functools.partial(send_plane, 3 - n))
        for n in range(2):
            pl.when((core == 1) & (t == 2 * n + 1))(functools.partial(send_line, 1 - n))

    def collect(step):
        @pl.when(core == 0)
        def _():
            wait_recv(rs.at[step, pl.ds(0, PLANE - 1)], rs_recv.at[step])
            for axis in range(3):
                packed[step + 1, axis] = sum((rs[step, s, axis] for s in range(1, PLANE)), rs[step, 0, axis])

        @pl.when(core == 1)
        def _():
            wait_recv(rs.at[step, pl.ds(0, LINE - 1)], rs_recv.at[step])
            for axis in range(3):
                packed[step + 1, axis] = sum((rs[step, s, axis] for s in range(1, LINE)), rs[step, 0, axis])

    front = lax.broadcasted_iota(jnp.int32, (1, 128), 1) < HALF

    def fold(value):
        line = jnp.sum(value, axis=0, keepdims=True)
        return line + turn(line)

    def inner(left, right):
        return fold(sum(left[axis] * right[axis] for axis in range(3)))

    def reduce_plane(k, values):
        for n, value in values:
            red_src[2 * k, :, n * 128:n * 128 + 128] = value
        for spot in far_places:
            remote(red_src.at[2 * k], red_one.at[k, seen_in_plane(*spot)], red_sem.at[k, 0], red_sem.at[k, 1], plane_at(*spot)).start()
        red_one[k, 0] = red_src[2 * k]

    def reduce_line(k):
        def send(dz, device):
            slot = seen_in_line(dz) - PLANE
            remote(red_src.at[2 * k + 1], red_two.at[k, core, slot], red_sem.at[k, 2], red_sem.at[k, 3], device).start()

        wait_recv(red_one.at[k, pl.ds(0, PLANE - 1)], red_sem.at[k, 1])
        red_src[2 * k + 1] = sum((red_one[k, s] for s in range(1, PLANE)), red_one[k, 0])
        for dz in far_steps:
            send(dz, line_at(dz))
            if k == 1:
                send(dz, line_mate(dz))
        if k == 1:
            send(0, sibling)
        red_two[k, core, 0] = red_src[2 * k + 1]

    def reduced(k, c):
        return sum((red_two[k, c, s] for s in range(1, LINE)), red_two[k, c, 0])

    @pl.loop(0, 2)
    def _(t):
        build(t)

    @pl.when(core == 0)
    def _():
        wait_line(0, 0)
        wait_line(0, 1)

    @pl.when(core == 1)
    def _():
        wait_plane(0, 0)
        wait_plane(0, 1)
        widen(1)

    widen(0)

    @pl.loop(0, 4)
    def _(t):
        @pl.when(t >= 2)
        def _():
            build(t)

        more = (core == 1) & (lax.rem(t, 2) == 1)
        for axis, value in enumerate(product(t)):
            acc[axis] = jnp.where(more, acc[axis], 0.0) + value
        scatter(0, t, pack)

    collect(0)
    gather(1)
    reduce_plane(0, ((0, inner(packed.at[0], packed.at[0])), (1, inner(packed.at[0], packed.at[1]))))

    @pl.loop(1, ITERS)
    def _(step):
        def unit(part_of, t):
            tile = tile_of(t)
            quarter = jnp.where(core == 0, part_of, lax.rem(t, 2))
            h = jnp.where(core == 0, lax.div(tile, 2), part_of)
            w = jnp.where(core == 0, 0, part_of)
            rt = jnp.where(core == 0, lax.rem(tile, 2), tile)
            inner_at = pl.ds(pl.multiple_of(quarter * 1536, 1536), 1536)
            rows = pl.ds(pl.multiple_of(rt * 256, 256), 256)
            return tile, dot(mob_high[h, rows, inner_at], narrow[w, inner_at, :])

        arrange_half(step, 0)

        @pl.loop(0, 4)
        def _(t):
            tile, value = unit(0, t)
            more = (core == 1) & (lax.rem(t, 2) == 1)
            acc_wide[tile] = jnp.where(more, acc_wide[tile], 0.0) + value

        arrange_half(step, 1)

        @pl.loop(0, 4)
        def _(t):
            tile, value = unit(1, t)
            acc_wide[tile] += value

            @pl.when(step == 1)
            def _():
                scatter(1, t, pack_wide)

            @pl.when((step == 2) & (t == 0) & (core == 0))
            def _():
                wait_plane(2, 0)
                wait_plane(2, 1)

            @pl.when((step == 2) & (t == 0) & (core == 1))
            def _():
                wait_line(2, 0)
                wait_line(2, 1)

            @pl.when((step == 2) & ((core == 0) | (lax.rem(t, 2) == 1)))
            def _():
                at = jnp.where(core == 0, 0, PLANE) + tile * 4
                total = part[...]
                for i in range(4):
                    for axis, value in enumerate(pack_wide(tile, i)):
                        total = total + value * ag[2, at + i, axis]
                part[...] = total

        @pl.when(step == 1)
        def _():
            reduce_line(0)
            collect(1)
            wait_recv(red_two.at[0, 0, pl.ds(0, LINE - 1)], red_sem.at[0, 3])
            total = reduced(0, core)
            moments[...] = jnp.broadcast_to(total[:, 128:256] / total[:, 0:128], (32, 128))
            a1 = moments[...]
            for axis in range(3):
                y1 = packed[1, axis]
                packed[2, axis] = packed[2, axis] - a1 * y1
                first_dir[axis] = y1 - a1 * packed[0, axis]
            gather(2)
            remote(first_dir, mate.at[0], mate_sem.at[2], mate_sem.at[3], sibling).start()
            remote(packed.at[2], mate.at[1], mate_sem.at[2], mate_sem.at[3], sibling).start()

    reduce_plane(1, ((0, red_src[0][:, 0:128]), (1, red_src[0][:, 128:256]),
                     (2, inner(first_dir, first_dir)), (3, inner(first_dir, packed.at[2])),
                     (4, inner(packed.at[2], packed.at[2])), (5, fold(part[...]))))
    reduce_line(1)
    wait_recv(mate, mate_sem.at[3])
    for axis in range(3):
        w_ref[axis] = jnp.where(keep, first_dir[axis], turn(mate[0, axis]))
        u_ref[axis] = jnp.where(keep, packed[2, axis], turn(mate[1, axis]))
    wait_recv(red_one.at[1, pl.ds(0, 2 * LINE - 1)], red_sem.at[1, 3])
    low, high = reduced(1, 0), reduced(1, 1)
    for k in range(6):
        at = slice(k * 128, k * 128 + 128)
        sum_ref[k] = jnp.broadcast_to(jnp.where(front, low[:, at], high[:, at]), (8, 128))
    sum_ref[6] = jnp.zeros((8, 128), F32)
    sum_ref[7] = jnp.ones((8, 128), F32)

    wait_send(posrow.at[0], pos_sem.at[0])
    wait_send(z_mate, mate_sem.at[0])
    wait_send(mate, mate_sem.at[2])
    wait_send(posbuf.at[pl.ds(0, 22)], pos_sem.at[2])
    wait_send(ag.at[2, pl.ds(0, 22)], ag_send.at[2])
    for k, count in enumerate((LINE - 1, 2 * LINE - 1)):
        wait_send(red_one.at[k, pl.ds(0, PLANE - 1)], red_sem.at[k, 0])
        wait_send(red_one.at[k, pl.ds(0, count)], red_sem.at[k, 2])
    for step in range(2):
        @pl.when(core == 0)
        def _(step=step):
            wait_send(ag.at[step, pl.ds(0, LINE - 1)], ag_send.at[step])
            wait_send(rs_send.at[step, pl.ds(0, PLANE - 1)], rs_sent.at[step])

        @pl.when(core == 1)
        def _(step=step):
            wait_send(ag.at[step, pl.ds(0, PLANE - 1)], ag_send.at[step])
            wait_send(rs_send.at[step, pl.ds(0, LINE - 1)], rs_sent.at[step])


def finish(z_ref, w_ref, u_ref, sum_ref, out_ref):
    m0, m1, e1, f1, g, third, zero, one = (sum_ref[k] for k in range(8))

    a1, a2, bb2 = m1 / m0, f1 / e1, e1 / m0
    e2 = g - a2 * f1 - bb2 * e1
    bb3 = e2 / e1
    a3 = (third - a2 * g - bb2 * (f1 + a1 * e1)) / e2 - a2
    d1, d2, d3 = 1.0 + a1, 1.0 + a2, 1.0 + a3
    scale = (d1 + d2 + d3) / ITERS
    current = (d1 / scale, jnp.sqrt(bb2) / scale, zero, d2 / scale, jnp.sqrt(bb3) / scale, d3 / scale)
    partner = (one, zero, zero, one, zero, one)

    def inverse_three(m):
        c00, c01, c02 = m[3] * m[5] - m[4] * m[4], m[2] * m[4] - m[1] * m[5], m[1] * m[4] - m[2] * m[3]
        c11, c12, c22 = m[0] * m[5] - m[2] * m[2], m[1] * m[2] - m[0] * m[4], m[0] * m[3] - m[1] * m[1]
        over = 1.0 / (m[0] * c00 + m[1] * c01 + m[2] * c02)
        return tuple(c * over for c in (c00, c01, c02, c11, c12, c22))

    def newton(_, state):
        now, other = state
        return (tuple(0.5 * (u + v) for u, v in zip(now, inverse_three(other))),
                tuple(0.5 * (u + v) for u, v in zip(other, inverse_three(now))))

    current, partner = lax.fori_loop(0, 20, newton, (current, partner))
    size = jnp.sqrt(scale)
    beta = jnp.sqrt(m0)
    r1, r2, r3 = (current[k] * size for k in range(3))
    f2, f3 = beta * r2 / jnp.sqrt(e1), beta * r3 / jnp.sqrt(e2)
    c0, c1, c2 = (jnp.concatenate([c, c, c, c], axis=0) for c in (r1 - f3 * bb2, f2 - f3 * a2, f3))
    for axis in range(3):
        out_ref[axis] = c0 * z_ref[axis] + c1 * w_ref[axis] + c2 * u_ref[axis]


def shards(positions, start_vector):
    chunk = (3, 32, 128)
    vmem = pl.BlockSpec(memory_space=pltpu.VMEM)
    whole = jax.ShapeDtypeStruct(chunk, F32)
    w, u, sums = pl.pallas_call(
        kernel,
        out_shape=(whole, whole, jax.ShapeDtypeStruct((8, 8, 128), F32)),
        in_specs=[pl.BlockSpec(memory_space=pltpu.HBM)] * 2,
        out_specs=(vmem, vmem, vmem),
        scratch_shapes=[
            pltpu.VMEM((2, 1, 128), F32),
            pltpu.VMEM((PLANE + LINE, 1, 256), F32),
            pltpu.VMEM((2, 3, BLOCK, 128), F32),
            pltpu.VMEM((2, 8, BLOCK), F32),
            pltpu.VMEM((2, BLOCK, 6 * BLOCK), BF16),
            pltpu.VMEM((2, BLOCK, 6 * BLOCK), BF16),
            pltpu.VMEM((2, BLOCK, 512), BF16),
            pltpu.VMEM((2, 6 * BLOCK, 256), BF16),
            pltpu.VMEM((3, PLANE + LINE) + chunk, F32),
            pltpu.VMEM((2, PLANE) + chunk, F32),
            pltpu.VMEM((2, PLANE) + chunk, F32),
            pltpu.VMEM((3,) + chunk, F32),
            pltpu.VMEM(chunk, F32),
            pltpu.VMEM((2,) + chunk, F32),
            pltpu.VMEM((3, 256, 128), F32),
            pltpu.VMEM((4, 256, 256), F32),
            pltpu.VMEM((32, 128), F32),
            pltpu.VMEM((4, 1, WIDTH), F32),
            pltpu.VMEM((2, PLANE, 1, WIDTH), F32),
            pltpu.VMEM((2, 2, LINE, 1, WIDTH), F32),
            pltpu.VMEM((32, 128), F32),
            pltpu.VMEM((3, 32), jnp.int32),
            pltpu.VMEM((8, 128), F32),
            pltpu.VMEM(chunk, F32),
            pltpu.VMEM(chunk, F32),
            pltpu.SemaphoreType.DMA((2,)),
            pltpu.SemaphoreType.DMA((4,)),
            pltpu.SemaphoreType.DMA((4,)),
            pltpu.SemaphoreType.DMA((3, 2)),
            pltpu.SemaphoreType.DMA((3, 2)),
            pltpu.SemaphoreType.DMA((3,)),
            pltpu.SemaphoreType.DMA((2,)),
            pltpu.SemaphoreType.DMA((2,)),
            pltpu.SemaphoreType.DMA((2, 4)),
        ],
        compiler_params=pltpu.CompilerParams(
            collective_id=0, has_side_effects=True, vmem_limit_bytes=40 * 1024 * 1024),
    )(positions, start_vector)
    return pl.pallas_call(
        finish, out_shape=whole, in_specs=[vmem] * 4, out_specs=vmem,
    )(start_vector, w, u, sums)


def solution(mesh):
    in_specs = (P(None, ("row", "col")), P(None, ("row", "col"), None))
    out_specs = P(None, ("row", "col"), None)
    return jax.shard_map(shards, mesh=mesh, in_specs=in_specs, out_specs=out_specs, check_vma=False)
```

```python
import functools

import jax
import jax.numpy as jnp
from jax import lax
from jax.experimental import pallas as pl
from jax.experimental.pallas import tpu as pltpu
from jax.sharding import PartitionSpec as P

ITERS = 3
RADIUS = 0.4
MESH = pl.DeviceIdType.MESH
F32 = jnp.float32
BF16 = jnp.bfloat16

PLANE, LINE = 16, 8
PLACES = ((0, 0), (2, 0), (0, 2), (2, 2), (0, 1), (3, 0), (1, 1), (1, 3), (3, 2), (2, 1),
          (0, 3), (1, 0), (3, 3), (3, 1), (1, 2), (2, 3))
NEEDED = 10
STEPS = (0, 1, 7, 2, 6, 3, 5, 4)


def seen_in_plane(dx, dy):
    return PLACES.index((-dx % 4, -dy % 4))


def seen_in_line(dz):
    return PLANE + STEPS.index(-dz % 8)


HALF = 64
BLOCK = 512
WIDTH = 768


def kernel(pos_hbm, z_hbm, out_ref, posrow, posbuf, colbc, lanevec, mob_high, mob_low, wide, narrow, ag, rs, rs_send,
           packed, first_dir, mate, acc, acc_wide, part, red_src, red_one, red_two, moments, pos_ref, flatten, z_ref,
           z_mate, load_sem, mate_sem, pos_sem, line_sem, plane_sem, ag_send, rs_recv, rs_sent, red_sem):
    row, col = lax.axis_index("row"), lax.axis_index("col")
    x, core = lax.div(row, 2), lax.rem(row, 2)
    z, y = lax.div(col, 4), lax.rem(col, 4)

    xs = [lax.rem(x + d, 4) for d in range(4)]
    ys = [lax.rem(y + d, 4) for d in range(4)]
    zs = [lax.rem(z + d, 8) for d in range(8)]

    def plane_at(dx, dy):
        return (xs[dx] * 2 + core, z * 4 + ys[dy])

    far_places, far_steps = PLACES[:0:-1], STEPS[:0:-1]

    def line_at(dz):
        return (row, zs[dz] * 4 + y)

    def line_mate(dz):
        return (x * 2 + 1 - core, zs[dz] * 4 + y)

    sibling = (x * 2 + 1 - core, col)

    def remote(src, dst, send, recv, device):
        return pltpu.make_async_remote_copy(
            src_ref=src, dst_ref=dst, send_sem=send, recv_sem=recv, device_id=device, device_id_type=MESH)

    def wait_recv(ref, sem):
        remote(ref, ref, sem, sem, (row, col)).wait_recv()

    def wait_send(ref, sem):
        remote(ref, ref, sem, sem, (row, col)).wait_send()

    first = lax.broadcasted_iota(jnp.int32, (32, 128), 1) < HALF
    keep = first == (core == 0)

    def turn(value):
        return pltpu.roll(value, HALF, 1)

    load_pos = pltpu.make_async_copy(pos_hbm, pos_ref, load_sem.at[0])
    load_pos.start()
    load_z = pltpu.make_async_copy(z_hbm, z_ref, load_sem.at[1])
    load_z.start()
    barrier = pltpu.get_barrier_semaphore()

    def signal(device):
        pl.semaphore_signal(barrier, inc=1, device_id=device, device_id_type=MESH)

    signal(sibling)
    for dx, dy in far_places:
        signal(plane_at(dx, dy))
    for dz in far_steps:
        signal(line_at(dz))
        signal(line_mate(dz))

    flatten[...] = jnp.zeros_like(flatten)
    acc[...] = jnp.zeros_like(acc)
    acc_wide[...] = jnp.zeros_like(acc_wide)
    part[...] = jnp.zeros_like(part)
    ag[2, NEEDED:PLANE] = jnp.zeros((PLANE - NEEDED, 3, 32, 128), F32)
    for k in range(2):
        red_src[2 * k] = jnp.zeros((1, WIDTH), F32)
    load_pos.wait()
    flatten[0:3, 0:32] = pos_ref[...].astype(F32)
    rows3 = flatten[...]
    posrow[core] = rows3[0:1] + pltpu.roll(rows3[1:2], 32, 1) + pltpu.roll(rows3[2:3], 64, 1)
    load_z.wait()
    pl.semaphore_wait(barrier, 30)

    remote(posrow.at[core], posrow.at[core], pos_sem.at[0], pos_sem.at[1], sibling).start()
    remote(z_ref, z_mate, mate_sem.at[0], mate_sem.at[1], sibling).start()
    wait_recv(posrow.at[0], pos_sem.at[1])
    both = jnp.concatenate([posrow[0], posrow[1]], axis=1)
    posbuf[0] = both
    posbuf[PLANE] = both
    for n, spot in enumerate(far_places):
        if n < 7:
            remote(posbuf.at[PLANE], posbuf.at[seen_in_line(far_steps[n])], pos_sem.at[2], pos_sem.at[3],
                   line_at(far_steps[n])).start()
        remote(posbuf.at[0], posbuf.at[seen_in_plane(*spot)], pos_sem.at[2], pos_sem.at[3], plane_at(*spot)).start()
    wait_recv(z_mate, mate_sem.at[1])
    for axis in range(3):
        packed[0, axis] = jnp.where(keep, z_ref[axis], turn(z_mate[axis]))

    def gather(step):
        def to_line():
            for dz in STEPS[1:]:
                slot = seen_in_line(dz)
                remote(packed.at[step], ag.at[step, slot], ag_send.at[step], line_sem.at[step, (slot - PLANE) // 4],
                       line_at(dz)).start()

        def to_plane(needed):
            for spot in PLACES[1:]:
                slot = seen_in_plane(*spot)
                if (slot < NEEDED) == needed:
                    remote(packed.at[step], ag.at[step, slot], ag_send.at[step], plane_sem.at[step, slot // 8],
                           plane_at(*spot)).start()

        last = step == 2
        pl.when(core == 0)(to_line)
        pl.when((core == 1) | last)(lambda: to_plane(True))
        pl.when((core == 1) & jnp.logical_not(last))(lambda: to_plane(False))
        pl.when((core == 1) & last)(to_line)
        ag[step, 0] = packed[step]
        ag[step, PLANE] = packed[step]

    def wait_line(step, part_of):
        wait_recv(ag.at[step, pl.ds(0, 4 if part_of else 3)], line_sem.at[step, part_of])

    def wait_plane(step, part_of, last=False):
        if part_of == 0:
            wait_recv(ag.at[step, pl.ds(0, 7)], plane_sem.at[step, 0])
        else:
            wait_recv(ag.at[step, pl.ds(0, NEEDED - 8 if last else 8)], plane_sem.at[step, 1])

    gather(0)
    narrow[...] = jnp.zeros_like(narrow)
    wait_recv(posbuf.at[pl.ds(0, 22)], pos_sem.at[3])

    lane_of = lax.broadcasted_iota(jnp.int32, (BLOCK, 128), 1)
    bead_of = lax.broadcasted_iota(jnp.int32, (BLOCK, 128), 0) & 31
    entry_of = lax.broadcasted_iota(jnp.int32, (128, BLOCK), 0)
    column_of = lax.broadcasted_iota(jnp.int32, (128, BLOCK), 1) & 31
    owner_of = lax.broadcasted_iota(jnp.int32, (16, BLOCK), 1) >> 5
    source_of = lax.broadcasted_iota(jnp.int32, (16, BLOCK), 0)
    ones = jnp.ones((128, 128), BF16)

    def place(at, d):
        return posbuf[at + d // 2][:, (d % 2) * 128:(d % 2) * 128 + 128]

    @pl.loop(0, 2)
    def _(h):
        rows_at = jnp.where(core == 0, h, 2) * 8
        lanes_at = jnp.where(core == 0, 2, h) * 8
        spread = jnp.concatenate([jnp.broadcast_to(place(rows_at, d), (32, 128)) for d in range(16)], axis=0)
        flat = jnp.concatenate([place(lanes_at, d) for d in range(16)], axis=0).astype(BF16)
        for axis in range(3):
            own = jnp.where(lane_of == axis * 32 + bead_of, spread, 0.0).astype(BF16)
            colbc[h, axis] = jnp.dot(own, ones, preferred_element_type=F32)
            pick = jnp.where(entry_of == axis * 32 + column_of, 1.0, 0.0).astype(BF16)
            moved = jnp.dot(flat, pick, preferred_element_type=F32)
            lanevec[h, axis:axis + 1, :] = jnp.sum(jnp.where(owner_of == source_of, moved, 0.0), axis=0, keepdims=True)

    def tile_of(t):
        return jnp.where(core == 0, 3 - t, 1 - lax.div(t, 2))

    def places(t):
        tile = tile_of(t)
        h = jnp.where(core == 0, lax.div(tile, 2), lax.rem(t, 2))
        rt = jnp.where(core == 0, lax.rem(tile, 2), tile)
        return h, jnp.where(core == 0, 0, h), pl.ds(pl.multiple_of(rt * 256, 256), 256)

    def build(t):
        h, _, span = places(t)

        @pl.loop(0, 16, unroll=2)
        def _(r):
            rows = pl.ds(pl.multiple_of(span.start + r * 16, 16), 16)
            mine = [colbc[h, axis, rows, :] for axis in range(3)]
            for tile in range(4):
                lanes = slice(tile * 128, tile * 128 + 128)
                d = [mine[axis] - lanevec[h, axis:axis + 1, lanes] for axis in range(3)]
                squared = d[0] * d[0] + d[1] * d[1] + d[2] * d[2]
                root = lax.rsqrt(jnp.where(squared > 0.5, squared, 1e30))
                inverse = root * root
                prefactor = (0.75 * RADIUS) * root
                iso = prefactor * (1.0 + (2.0 / 3.0 * RADIUS * RADIUS) * inverse)
                along = (prefactor * inverse) * (1.0 - (2.0 * RADIUS * RADIUS) * inverse)
                s = [along * d[axis] for axis in range(3)]
                parts = (s[0] * d[0] + iso, s[0] * d[1], s[0] * d[2], s[1] * d[1] + iso, s[1] * d[2],
                         s[2] * d[2] + iso)
                for k, value in enumerate(parts):
                    high = value.astype(BF16)
                    at = (tile // 2) * 1536 + k * 256 + (tile % 2) * 128
                    at = slice(at, at + 128)
                    mob_high[h, rows, at] = high
                    mob_low[h, rows, at] = (value - high.astype(F32)).astype(BF16)

    def widen(h):
        base = jnp.where(core == 0, PLANE, h * 8)

        @pl.loop(0, 8)
        def _(s):
            for axis in range(3):
                value = ag[0, base + s, axis]
                other = turn(value)
                for j, both in enumerate((jnp.where(first, value, other), jnp.where(first, other, value))):
                    high = both.astype(BF16).astype(F32)
                    tile = jnp.where(first, high, both - high).astype(BF16)
                    at = pl.ds(pl.multiple_of(s * 64 + j * 32, 32), 32)
                    wide[h, at, axis * 128:axis * 128 + 128] = tile
                    if axis == 0:
                        wide[h, at, 384:512] = tile

    def arrange(step, base, w, quarter, weight):
        @pl.loop(0, 4)
        def _(s):
            values = [ag[step, base + s, axis] * weight for axis in range(3)]
            others = [turn(value) for value in values]
            for j in range(2):
                left, right = (values, others) if j == 0 else (others, values)
                lx, ly, lz = (jnp.where(first, v, 0.0).astype(BF16) for v in left)
                ry, rz = (jnp.where(first, 0.0, v).astype(BF16) for v in right[1:])
                yx = jnp.where(first, left[1], right[0]).astype(BF16)
                for k, half, tile in ((0, 0, lx), (1, 0, yx), (2, 0, lz), (2, 1, lx), (3, 0, ry), (4, 0, rz),
                                      (4, 1, ly), (5, 1, lz)):
                    at = pl.ds(pl.multiple_of(quarter * 1536 + k * 256 + s * 64 + j * 32, 32), 32)
                    narrow[w, at, half * 128:half * 128 + 128] = tile

    def arrange_half(step, part_of):
        @pl.when(core == 0)
        def _():
            wait_line(step, part_of)
            arrange(step, PLANE + 4 * part_of, 0, part_of, 1.0)

        @pl.when(core == 1)
        def _():
            if part_of == 0:
                wait_plane(step, 0)
            else:
                pl.when(step == 1)(lambda: wait_plane(step, 1))
                pl.when(step == 2)(lambda: wait_plane(step, 1, True))

            @pl.loop(0, 2)
            def _(quarter):
                slot = 8 * part_of + 4 * quarter

                @pl.when((step == 1) | (slot < NEEDED))
                def _():
                    arrange(step, slot, part_of, quarter, jnp.where((step == 2) & (slot >= 4), 2.0, 1.0))

    def dot(left, right):
        return jnp.dot(left, right, preferred_element_type=F32)

    def product(t):
        h, w, rows = places(t)

        def both(k, lo, hi):
            total = 0.0
            for quarter in range(2):
                at = slice(quarter * 1536 + k * 256, quarter * 1536 + k * 256 + 256)
                right = wide[w, quarter * 256:quarter * 256 + 256, lo:hi]
                total = total + dot(mob_high[h, rows, at], right) + dot(mob_low[h, rows, at], right)
            return total

        xy, yz, zx = both(1, 0, 256), both(4, 128, 384), both(2, 256, 512)
        return (both(0, 0, 128) + xy[:, 128:] + zx[:, :128],
                both(3, 128, 256) + xy[:, :128] + yz[:, 128:],
                both(5, 256, 384) + zx[:, 128:] + yz[:, :128])

    def halves(i, upper):
        return pl.ds(pl.multiple_of(i * 64 + upper * 32, 32), 32)

    def pack(_, i):
        chunk = []
        for axis in range(3):
            low, high = acc[axis, halves(i, 0), :], acc[axis, halves(i, 1), :]
            chunk.append(jnp.where(first, low + turn(low), high + turn(high)))
        return chunk

    def pack_wide(tile, i):
        low, high = halves(i, 0), halves(i, 1)
        xy_low, xy_high = acc_wide[tile, low, :128], acc_wide[tile, high, :128]
        z_low, z_high = acc_wide[tile, low, 128:], acc_wide[tile, high, 128:]
        return (jnp.where(first, xy_low, turn(xy_high)), jnp.where(first, turn(xy_low), xy_high),
                jnp.where(first, z_low, turn(z_high)))

    def scatter(step, t, packer):
        def send_plane(tile):
            for i in (3, 2, 1, 0):
                spot = PLACES[tile * 4 + i]
                for axis, value in enumerate(packer(tile, i)):
                    rs_send[step, tile * 4 + i, axis] = value
                if tile * 4 + i == 0:
                    rs[step, 0] = rs_send[step, 0]
                else:
                    remote(rs_send.at[step, tile * 4 + i], rs.at[step, seen_in_plane(*spot)], rs_sent.at[step],
                           rs_recv.at[step], plane_at(*spot)).start()

        def send_line(tile):
            for i in (3, 2, 1, 0):
                dz = STEPS[tile * 4 + i]
                for axis, value in enumerate(packer(tile, i)):
                    rs_send[step, tile * 4 + i, axis] = value
                if dz == 0:
                    rs[step, 0] = rs_send[step, 0]
                else:
                    remote(rs_send.at[step, tile * 4 + i], rs.at[step, seen_in_line(dz) - PLANE], rs_sent.at[step],
                           rs_recv.at[step], line_at(dz)).start()

        for n in range(4):
            pl.when((core == 0) & (t == n))(functools.partial(send_plane, 3 - n))
        for n in range(2):
            pl.when((core == 1) & (t == 2 * n + 1))(functools.partial(send_line, 1 - n))

    def collect(step):
        @pl.when(core == 0)
        def _():
            wait_recv(rs.at[step, pl.ds(0, PLANE - 1)], rs_recv.at[step])
            for axis in range(3):
                packed[step + 1, axis] = sum((rs[step, s, axis] for s in range(1, PLANE)), rs[step, 0, axis])

        @pl.when(core == 1)
        def _():
            wait_recv(rs.at[step, pl.ds(0, LINE - 1)], rs_recv.at[step])
            for axis in range(3):
                packed[step + 1, axis] = sum((rs[step, s, axis] for s in range(1, LINE)), rs[step, 0, axis])

    front = lax.broadcasted_iota(jnp.int32, (1, 128), 1) < HALF

    def fold(value):
        line = jnp.sum(value, axis=0, keepdims=True)
        return line + turn(line)

    def inner(left, right):
        return fold(sum(left[axis] * right[axis] for axis in range(3)))

    def reduce_plane(k, values):
        for n, value in values:
            red_src[2 * k, :, n * 128:n * 128 + 128] = value
        for spot in far_places:
            remote(red_src.at[2 * k], red_one.at[k, seen_in_plane(*spot)], red_sem.at[k, 0], red_sem.at[k, 1], plane_at(*spot)).start()
        red_one[k, 0] = red_src[2 * k]

    def reduce_line(k):
        def send(dz, device):
            slot = seen_in_line(dz) - PLANE
            remote(red_src.at[2 * k + 1], red_two.at[k, core, slot], red_sem.at[k, 2], red_sem.at[k, 3], device).start()

        wait_recv(red_one.at[k, pl.ds(0, PLANE - 1)], red_sem.at[k, 1])
        red_src[2 * k + 1] = sum((red_one[k, s] for s in range(1, PLANE)), red_one[k, 0])
        for dz in far_steps:
            send(dz, line_at(dz))
            if k == 1:
                send(dz, line_mate(dz))
        if k == 1:
            send(0, sibling)
        red_two[k, core, 0] = red_src[2 * k + 1]

    def reduced(k, c):
        return sum((red_two[k, c, s] for s in range(1, LINE)), red_two[k, c, 0])

    @pl.loop(0, 2)
    def _(t):
        build(t)

    @pl.when(core == 0)
    def _():
        wait_line(0, 0)
        wait_line(0, 1)

    @pl.when(core == 1)
    def _():
        wait_plane(0, 0)
        wait_plane(0, 1)
        widen(1)

    widen(0)

    @pl.loop(0, 4)
    def _(t):
        @pl.when(t >= 2)
        def _():
            build(t)

        more = (core == 1) & (lax.rem(t, 2) == 1)
        for axis, value in enumerate(product(t)):
            acc[axis] = jnp.where(more, acc[axis], 0.0) + value
        scatter(0, t, pack)

    collect(0)
    gather(1)
    reduce_plane(0, ((0, inner(packed.at[0], packed.at[0])), (1, inner(packed.at[0], packed.at[1]))))

    @pl.loop(1, ITERS)
    def _(step):
        def unit(part_of, t):
            tile = tile_of(t)
            quarter = jnp.where(core == 0, part_of, lax.rem(t, 2))
            h = jnp.where(core == 0, lax.div(tile, 2), part_of)
            w = jnp.where(core == 0, 0, part_of)
            rt = jnp.where(core == 0, lax.rem(tile, 2), tile)
            inner_at = pl.ds(pl.multiple_of(quarter * 1536, 1536), 1536)
            rows = pl.ds(pl.multiple_of(rt * 256, 256), 256)
            return tile, dot(mob_high[h, rows, inner_at], narrow[w, inner_at, :])

        arrange_half(step, 0)

        @pl.loop(0, 4)
        def _(t):
            @pl.when((step == 1) | (core == 1) | (t > 0))
            def _():
                tile, value = unit(0, t)
                more = (core == 1) & (lax.rem(t, 2) == 1)
                acc_wide[tile] = jnp.where(more, acc_wide[tile], 0.0) + value

        arrange_half(step, 1)

        @pl.loop(0, 4)
        def _(t):
            @pl.when((step == 1) | jnp.where(core == 1, lax.rem(t, 2) == 0, t > 0))
            def _():
                tile, value = unit(1, t)
                acc_wide[tile] += value

            @pl.when(step == 1)
            def _():
                scatter(1, t, pack_wide)

            @pl.when((step == 2) & (t == 0) & (core == 0))
            def _():
                wait_plane(2, 0)
                wait_plane(2, 1, True)

            @pl.when((step == 2) & (t == 0) & (core == 1))
            def _():
                wait_line(2, 0)
                wait_line(2, 1)

            @pl.when((step == 2) & jnp.where(core == 1, lax.rem(t, 2) == 1, t > 0))
            def _():
                tile = tile_of(t)
                at = jnp.where(core == 0, 0, PLANE) + tile * 4
                total = jnp.zeros((32, 128), F32)
                for i in range(4):
                    for axis, value in enumerate(pack_wide(tile, i)):
                        total = total + value * ag[2, at + i, axis]
                part[...] += total * jnp.where((core == 0) & (tile > 0), 2.0, 1.0)

        @pl.when(step == 1)
        def _():
            reduce_line(0)
            collect(1)
            wait_recv(red_two.at[0, 0, pl.ds(0, LINE - 1)], red_sem.at[0, 3])
            total = reduced(0, core)
            moments[0] = jnp.broadcast_to(total[:, 128:256] / total[:, 0:128], (32, 128))
            a1 = moments[0]
            for axis in range(3):
                y1 = packed[1, axis]
                packed[2, axis] = packed[2, axis] - a1 * y1
                first_dir[axis] = y1 - a1 * packed[0, axis]
            gather(2)
            remote(first_dir, mate.at[0], mate_sem.at[2], mate_sem.at[3], sibling).start()
            remote(packed.at[2], mate.at[1], mate_sem.at[2], mate_sem.at[3], sibling).start()

    reduce_plane(1, ((0, red_src[0][:, 0:128]), (1, red_src[0][:, 128:256]),
                     (2, inner(first_dir, first_dir)), (3, inner(first_dir, packed.at[2])),
                     (4, inner(packed.at[2], packed.at[2])), (5, fold(part[...]))))
    reduce_line(1)
    wait_recv(red_one.at[1, pl.ds(0, 2 * LINE - 1)], red_sem.at[1, 3])
    low, high = reduced(1, 0), reduced(1, 1)
    for k in range(6):
        at = slice(k * 128, k * 128 + 128)
        moments[k + 1, 0:8] = jnp.broadcast_to(jnp.where(front, low[:, at], high[:, at]), (8, 128))
    moments[7, 0:8] = jnp.zeros((8, 128), F32)
    moments[8, 0:8] = jnp.ones((8, 128), F32)
    m0, m1, e1, f1, g, third, zero, one = (moments[k, 0:8] for k in range(1, 9))

    a1, a2, bb2 = m1 / m0, f1 / e1, e1 / m0
    e2 = g - a2 * f1 - bb2 * e1
    bb3 = e2 / e1
    a3 = (third - a2 * g - bb2 * (f1 + a1 * e1)) / e2 - a2
    d1, d2, d3 = 1.0 + a1, 1.0 + a2, 1.0 + a3
    scale = (d1 + d2 + d3) / ITERS
    current = (d1 / scale, jnp.sqrt(bb2) / scale, zero, d2 / scale, jnp.sqrt(bb3) / scale, d3 / scale)
    partner = (one, zero, zero, one, zero, one)

    def inverse_three(m):
        c00, c01, c02 = m[3] * m[5] - m[4] * m[4], m[2] * m[4] - m[1] * m[5], m[1] * m[4] - m[2] * m[3]
        c11, c12, c22 = m[0] * m[5] - m[2] * m[2], m[1] * m[2] - m[0] * m[4], m[0] * m[3] - m[1] * m[1]
        over = 1.0 / (m[0] * c00 + m[1] * c01 + m[2] * c02)
        return tuple(c * over for c in (c00, c01, c02, c11, c12, c22))

    def newton(_, state):
        now, other = state
        return (tuple(0.5 * (u + v) for u, v in zip(now, inverse_three(other))),
                tuple(0.5 * (u + v) for u, v in zip(other, inverse_three(now))))

    current, partner = lax.fori_loop(0, 20, newton, (current, partner))
    size = jnp.sqrt(scale)
    beta = jnp.sqrt(m0)
    r1, r2, r3 = (current[k] * size for k in range(3))
    f2, f3 = beta * r2 / jnp.sqrt(e1), beta * r3 / jnp.sqrt(e2)
    wait_recv(mate, mate_sem.at[3])
    c0, c1, c2 = (jnp.concatenate([c, c, c, c], axis=0) for c in (r1 - f3 * bb2, f2 - f3 * a2, f3))
    for axis in range(3):
        out_ref[axis] = (c0 * z_ref[axis] + c1 * jnp.where(keep, first_dir[axis], turn(mate[0, axis]))
                         + c2 * jnp.where(keep, packed[2, axis], turn(mate[1, axis])))

    wait_send(posrow.at[0], pos_sem.at[0])
    wait_send(z_mate, mate_sem.at[0])
    wait_send(mate, mate_sem.at[2])
    wait_send(posbuf.at[pl.ds(0, 22)], pos_sem.at[2])
    wait_send(ag.at[2, pl.ds(0, NEEDED - 1 + LINE - 1)], ag_send.at[2])
    for k, count in enumerate((LINE - 1, 2 * LINE - 1)):
        wait_send(red_one.at[k, pl.ds(0, PLANE - 1)], red_sem.at[k, 0])
        wait_send(red_one.at[k, pl.ds(0, count)], red_sem.at[k, 2])
    for step in range(2):
        @pl.when(core == 0)
        def _(step=step):
            wait_send(ag.at[step, pl.ds(0, LINE - 1)], ag_send.at[step])
            wait_send(rs_send.at[step, pl.ds(0, PLANE - 1)], rs_sent.at[step])

        @pl.when(core == 1)
        def _(step=step):
            wait_send(ag.at[step, pl.ds(0, PLANE - 1)], ag_send.at[step])
            wait_send(rs_send.at[step, pl.ds(0, LINE - 1)], rs_sent.at[step])


def shards(positions, start_vector):
    chunk = (3, 32, 128)
    return pl.pallas_call(
        kernel,
        out_shape=jax.ShapeDtypeStruct(start_vector.shape, F32),
        in_specs=[pl.BlockSpec(memory_space=pltpu.HBM)] * 2,
        out_specs=pl.BlockSpec(memory_space=pltpu.VMEM),
        scratch_shapes=[
            pltpu.VMEM((2, 1, 128), F32),
            pltpu.VMEM((PLANE + LINE, 1, 256), F32),
            pltpu.VMEM((2, 3, BLOCK, 128), F32),
            pltpu.VMEM((2, 8, BLOCK), F32),
            pltpu.VMEM((2, BLOCK, 6 * BLOCK), BF16),
            pltpu.VMEM((2, BLOCK, 6 * BLOCK), BF16),
            pltpu.VMEM((2, BLOCK, 512), BF16),
            pltpu.VMEM((2, 6 * BLOCK, 256), BF16),
            pltpu.VMEM((3, PLANE + LINE) + chunk, F32),
            pltpu.VMEM((2, PLANE) + chunk, F32),
            pltpu.VMEM((2, PLANE) + chunk, F32),
            pltpu.VMEM((3,) + chunk, F32),
            pltpu.VMEM(chunk, F32),
            pltpu.VMEM((2,) + chunk, F32),
            pltpu.VMEM((3, 256, 128), F32),
            pltpu.VMEM((4, 256, 256), F32),
            pltpu.VMEM((32, 128), F32),
            pltpu.VMEM((4, 1, WIDTH), F32),
            pltpu.VMEM((2, PLANE, 1, WIDTH), F32),
            pltpu.VMEM((2, 2, LINE, 1, WIDTH), F32),
            pltpu.VMEM((9, 32, 128), F32),
            pltpu.VMEM((3, 32), jnp.int32),
            pltpu.VMEM((8, 128), F32),
            pltpu.VMEM(chunk, F32),
            pltpu.VMEM(chunk, F32),
            pltpu.SemaphoreType.DMA((2,)),
            pltpu.SemaphoreType.DMA((4,)),
            pltpu.SemaphoreType.DMA((4,)),
            pltpu.SemaphoreType.DMA((3, 2)),
            pltpu.SemaphoreType.DMA((3, 2)),
            pltpu.SemaphoreType.DMA((3,)),
            pltpu.SemaphoreType.DMA((2,)),
            pltpu.SemaphoreType.DMA((2,)),
            pltpu.SemaphoreType.DMA((2, 4)),
        ],
        compiler_params=pltpu.CompilerParams(
            collective_id=0, has_side_effects=True, vmem_limit_bytes=40 * 1024 * 1024),
    )(positions, start_vector)


def solution(mesh):
    in_specs = (P(None, ("row", "col")), P(None, ("row", "col"), None))
    out_specs = P(None, ("row", "col"), None)
    return jax.shard_map(shards, mesh=mesh, in_specs=in_specs, out_specs=out_specs, check_vma=False)
```

```python
import functools

import jax
import jax.numpy as jnp
from jax import lax
from jax.experimental import pallas as pl
from jax.experimental.pallas import tpu as pltpu
from jax.sharding import PartitionSpec as P

ITERS = 3
RADIUS = 0.4
MESH = pl.DeviceIdType.MESH
F32 = jnp.float32
BF16 = jnp.bfloat16

PLANE, LINE = 16, 8
PLACES = ((0, 0), (2, 0), (0, 2), (2, 2), (0, 1), (3, 0), (1, 1), (1, 3), (3, 2), (2, 1),
          (0, 3), (1, 0), (3, 3), (3, 1), (1, 2), (2, 3))
NEEDED = 10
STEPS = (0, 1, 7, 2, 6, 3, 5, 4)


def seen_in_plane(dx, dy):
    return PLACES.index((-dx % 4, -dy % 4))


def seen_in_line(dz):
    return PLANE + STEPS.index(-dz % 8)


HALF = 64
BLOCK = 512
WIDTH = 768


def kernel(pos_hbm, z_hbm, out_ref, posbuf, colbc, lanevec, mob_high, mob_low, wide, narrow, ag, rs, rs_send,
           packed, first_dir, mate, acc, acc_wide, part, red_src, red_one, red_two, moments, pos_ref, flatten, z_ref,
           z_mate, load_sem, mate_sem, pos_sem, line_sem, plane_sem, ag_send, rs_recv, rs_sent, red_sem):
    row, col = lax.axis_index("row"), lax.axis_index("col")
    x, core = lax.div(row, 2), lax.rem(row, 2)
    z, y = lax.div(col, 4), lax.rem(col, 4)

    xs = [lax.rem(x + d, 4) for d in range(4)]
    ys = [lax.rem(y + d, 4) for d in range(4)]
    zs = [lax.rem(z + d, 8) for d in range(8)]

    def plane_at(dx, dy):
        return (xs[dx] * 2 + core, z * 4 + ys[dy])

    far_places = sorted(PLACES[1:], key=lambda spot: -min(spot[0], 4 - spot[0]) - min(spot[1], 4 - spot[1]))
    far_steps = STEPS[:0:-1]

    def line_at(dz):
        return (row, zs[dz] * 4 + y)

    def line_mate(dz):
        return (x * 2 + 1 - core, zs[dz] * 4 + y)

    def plane_mate(dx, dy):
        return (xs[dx] * 2 + 1 - core, z * 4 + ys[dy])

    sibling = (x * 2 + 1 - core, col)

    def remote(src, dst, send, recv, device):
        return pltpu.make_async_remote_copy(
            src_ref=src, dst_ref=dst, send_sem=send, recv_sem=recv, device_id=device, device_id_type=MESH)

    def wait_recv(ref, sem):
        remote(ref, ref, sem, sem, (row, col)).wait_recv()

    def wait_send(ref, sem):
        remote(ref, ref, sem, sem, (row, col)).wait_send()

    first = lax.broadcasted_iota(jnp.int32, (32, 128), 1) < HALF
    keep = first == (core == 0)

    def turn(value):
        return pltpu.roll(value, HALF, 1)

    load_pos = pltpu.make_async_copy(pos_hbm, pos_ref, load_sem.at[0])
    load_pos.start()
    load_z = pltpu.make_async_copy(z_hbm, z_ref, load_sem.at[1])
    load_z.start()
    barrier = pltpu.get_barrier_semaphore()

    def signal(device):
        pl.semaphore_signal(barrier, inc=1, device_id=device, device_id_type=MESH)

    signal(sibling)
    for spot in far_places:
        signal(plane_at(*spot))
        signal(plane_mate(*spot))
    for dz in far_steps:
        signal(line_at(dz))
        signal(line_mate(dz))

    flatten[...] = jnp.zeros_like(flatten)
    acc[...] = jnp.zeros_like(acc)
    acc_wide[...] = jnp.zeros_like(acc_wide)
    part[...] = jnp.zeros_like(part)
    ag[2, NEEDED:PLANE] = jnp.zeros((PLANE - NEEDED, 3, 32, 128), F32)
    for k in range(2):
        red_src[2 * k] = jnp.zeros((1, WIDTH), F32)
    load_pos.wait()
    flatten[0:3, 0:32] = pos_ref[...].astype(F32)
    rows3 = flatten[...]
    own_place = core
    posbuf[own_place] = rows3[0:1] + pltpu.roll(rows3[1:2], 32, 1) + pltpu.roll(rows3[2:3], 64, 1)
    load_z.wait()
    pl.semaphore_wait(barrier, 45)

    def send_place(slot, device):
        at = slot * 2 + core
        remote(posbuf.at[own_place], posbuf.at[at], pos_sem.at[0], pos_sem.at[1], device).start()

    for n, spot in enumerate(far_places):
        if n < 7:
            send_place(seen_in_line(far_steps[n]), line_at(far_steps[n]))
            send_place(seen_in_line(far_steps[n]), line_mate(far_steps[n]))
        send_place(seen_in_plane(*spot), plane_at(*spot))
        send_place(seen_in_plane(*spot), plane_mate(*spot))
    send_place(0, sibling)
    send_place(PLANE, sibling)
    remote(z_ref, z_mate, mate_sem.at[0], mate_sem.at[1], sibling).start()
    posbuf[2 * PLANE + core] = posbuf[own_place]
    wait_recv(z_mate, mate_sem.at[1])
    for axis in range(3):
        packed[0, axis] = jnp.where(keep, z_ref[axis], turn(z_mate[axis]))

    def gather(step):
        def to_line():
            for dz in far_steps:
                slot = seen_in_line(dz)
                remote(packed.at[step], ag.at[step, slot], ag_send.at[step], line_sem.at[step, (slot - PLANE) // 4],
                       line_at(dz)).start()

        def to_plane(needed):
            for spot in far_places:
                slot = seen_in_plane(*spot)
                if (slot < NEEDED) == needed:
                    remote(packed.at[step], ag.at[step, slot], ag_send.at[step], plane_sem.at[step, slot // 8],
                           plane_at(*spot)).start()

        last = step == 2
        pl.when(core == 0)(to_line)
        pl.when((core == 1) | last)(lambda: to_plane(True))
        pl.when((core == 1) & jnp.logical_not(last))(lambda: to_plane(False))
        pl.when((core == 1) & last)(to_line)
        ag[step, 0] = packed[step]
        ag[step, PLANE] = packed[step]

    def wait_line(step, part_of):
        wait_recv(ag.at[step, pl.ds(0, 4 if part_of else 3)], line_sem.at[step, part_of])

    def wait_plane(step, part_of, last=False):
        if part_of == 0:
            wait_recv(ag.at[step, pl.ds(0, 7)], plane_sem.at[step, 0])
        else:
            wait_recv(ag.at[step, pl.ds(0, NEEDED - 8 if last else 8)], plane_sem.at[step, 1])

    gather(0)
    narrow[...] = jnp.zeros_like(narrow)
    wait_recv(posbuf.at[pl.ds(0, 46)], pos_sem.at[1])

    lane_of = lax.broadcasted_iota(jnp.int32, (BLOCK, 128), 1)
    bead_of = lax.broadcasted_iota(jnp.int32, (BLOCK, 128), 0) & 31
    entry_of = lax.broadcasted_iota(jnp.int32, (128, BLOCK), 0)
    column_of = lax.broadcasted_iota(jnp.int32, (128, BLOCK), 1) & 31
    owner_of = lax.broadcasted_iota(jnp.int32, (16, BLOCK), 1) >> 5
    source_of = lax.broadcasted_iota(jnp.int32, (16, BLOCK), 0)
    ones = jnp.ones((128, 128), BF16)

    def place(at, d):
        return posbuf[at + d]

    @pl.loop(0, 2)
    def _(h):
        rows_at = jnp.where(core == 0, h, 2) * 16
        lanes_at = jnp.where(core == 0, 2, h) * 16
        spread = jnp.concatenate([jnp.broadcast_to(place(rows_at, d), (32, 128)) for d in range(16)], axis=0)
        flat = jnp.concatenate([place(lanes_at, d) for d in range(16)], axis=0).astype(BF16)
        for axis in range(3):
            own = jnp.where(lane_of == axis * 32 + bead_of, spread, 0.0).astype(BF16)
            colbc[h, axis] = jnp.dot(own, ones, preferred_element_type=F32)
            pick = jnp.where(entry_of == axis * 32 + column_of, 1.0, 0.0).astype(BF16)
            moved = jnp.dot(flat, pick, preferred_element_type=F32)
            lanevec[h, axis:axis + 1, :] = jnp.sum(jnp.where(owner_of == source_of, moved, 0.0), axis=0, keepdims=True)

    def tile_of(t):
        return jnp.where(core == 0, 3 - t, 1 - lax.div(t, 2))

    def places(t):
        tile = tile_of(t)
        h = jnp.where(core == 0, lax.div(tile, 2), lax.rem(t, 2))
        rt = jnp.where(core == 0, lax.rem(tile, 2), tile)
        return h, jnp.where(core == 0, 0, h), pl.ds(pl.multiple_of(rt * 256, 256), 256)

    def build(t):
        h, _, span = places(t)

        @pl.loop(0, 16, unroll=2)
        def _(r):
            rows = pl.ds(pl.multiple_of(span.start + r * 16, 16), 16)
            mine = [colbc[h, axis, rows, :] for axis in range(3)]
            for tile in range(4):
                lanes = slice(tile * 128, tile * 128 + 128)
                d = [mine[axis] - lanevec[h, axis:axis + 1, lanes] for axis in range(3)]
                squared = d[0] * d[0] + d[1] * d[1] + d[2] * d[2]
                root = lax.rsqrt(jnp.where(squared > 0.5, squared, 1e30))
                inverse = root * root
                prefactor = (0.75 * RADIUS) * root
                iso = prefactor * (1.0 + (2.0 / 3.0 * RADIUS * RADIUS) * inverse)
                along = (prefactor * inverse) * (1.0 - (2.0 * RADIUS * RADIUS) * inverse)
                s = [along * d[axis] for axis in range(3)]
                parts = (s[0] * d[0] + iso, s[0] * d[1], s[0] * d[2], s[1] * d[1] + iso, s[1] * d[2],
                         s[2] * d[2] + iso)
                for k, value in enumerate(parts):
                    high = value.astype(BF16)
                    at = (tile // 2) * 1536 + k * 256 + (tile % 2) * 128
                    at = slice(at, at + 128)
                    mob_high[h, rows, at] = high
                    mob_low[h, rows, at] = (value - high.astype(F32)).astype(BF16)

    def widen(h):
        base = jnp.where(core == 0, PLANE, h * 8)

        @pl.loop(0, 8)
        def _(s):
            for axis in range(3):
                value = ag[0, base + s, axis]
                other = turn(value)
                for j, both in enumerate((jnp.where(first, value, other), jnp.where(first, other, value))):
                    high = both.astype(BF16).astype(F32)
                    tile = jnp.where(first, high, both - high).astype(BF16)
                    at = pl.ds(pl.multiple_of(s * 64 + j * 32, 32), 32)
                    wide[h, at, axis * 128:axis * 128 + 128] = tile
                    if axis == 0:
                        wide[h, at, 384:512] = tile

    def arrange(step, base, w, quarter, weight):
        @pl.loop(0, 4)
        def _(s):
            values = [ag[step, base + s, axis] * weight for axis in range(3)]
            others = [turn(value) for value in values]
            for j in range(2):
                left, right = (values, others) if j == 0 else (others, values)
                lx, ly, lz = (jnp.where(first, v, 0.0).astype(BF16) for v in left)
                ry, rz = (jnp.where(first, 0.0, v).astype(BF16) for v in right[1:])
                yx = jnp.where(first, left[1], right[0]).astype(BF16)
                for k, half, tile in ((0, 0, lx), (1, 0, yx), (2, 0, lz), (2, 1, lx), (3, 0, ry), (4, 0, rz),
                                      (4, 1, ly), (5, 1, lz)):
                    at = pl.ds(pl.multiple_of(quarter * 1536 + k * 256 + s * 64 + j * 32, 32), 32)
                    narrow[w, at, half * 128:half * 128 + 128] = tile

    def arrange_half(step, part_of):
        @pl.when(core == 0)
        def _():
            wait_line(step, part_of)
            arrange(step, PLANE + 4 * part_of, 0, part_of, 1.0)

        @pl.when(core == 1)
        def _():
            if part_of == 0:
                wait_plane(step, 0)
            else:
                pl.when(step == 1)(lambda: wait_plane(step, 1))
                pl.when(step == 2)(lambda: wait_plane(step, 1, True))

            @pl.loop(0, 2)
            def _(quarter):
                slot = 8 * part_of + 4 * quarter

                @pl.when((step == 1) | (slot < NEEDED))
                def _():
                    arrange(step, slot, part_of, quarter, jnp.where((step == 2) & (slot >= 4), 2.0, 1.0))

    def dot(left, right):
        return jnp.dot(left, right, preferred_element_type=F32)

    def product(t):
        h, w, rows = places(t)

        def both(k, lo, hi):
            total = 0.0
            for quarter in range(2):
                at = slice(quarter * 1536 + k * 256, quarter * 1536 + k * 256 + 256)
                right = wide[w, quarter * 256:quarter * 256 + 256, lo:hi]
                total = total + dot(mob_high[h, rows, at], right) + dot(mob_low[h, rows, at], right)
            return total

        xy, yz, zx = both(1, 0, 256), both(4, 128, 384), both(2, 256, 512)
        return (both(0, 0, 128) + xy[:, 128:] + zx[:, :128],
                both(3, 128, 256) + xy[:, :128] + yz[:, 128:],
                both(5, 256, 384) + zx[:, 128:] + yz[:, :128])

    def halves(i, upper):
        return pl.ds(pl.multiple_of(i * 64 + upper * 32, 32), 32)

    def pack(_, i):
        chunk = []
        for axis in range(3):
            low, high = acc[axis, halves(i, 0), :], acc[axis, halves(i, 1), :]
            chunk.append(jnp.where(first, low + turn(low), high + turn(high)))
        return chunk

    def pack_wide(tile, i):
        low, high = halves(i, 0), halves(i, 1)
        xy_low, xy_high = acc_wide[tile, low, :128], acc_wide[tile, high, :128]
        z_low, z_high = acc_wide[tile, low, 128:], acc_wide[tile, high, 128:]
        return (jnp.where(first, xy_low, turn(xy_high)), jnp.where(first, turn(xy_low), xy_high),
                jnp.where(first, z_low, turn(z_high)))

    def scatter(step, t, packer):
        def send_plane(tile):
            for i in (3, 2, 1, 0):
                spot = PLACES[tile * 4 + i]
                for axis, value in enumerate(packer(tile, i)):
                    rs_send[step, tile * 4 + i, axis] = value
                if tile * 4 + i == 0:
                    rs[step, 0] = rs_send[step, 0]
                else:
                    remote(rs_send.at[step, tile * 4 + i], rs.at[step, seen_in_plane(*spot)], rs_sent.at[step],
                           rs_recv.at[step], plane_at(*spot)).start()

        def send_line(tile):
            for i in (3, 2, 1, 0):
                dz = STEPS[tile * 4 + i]
                for axis, value in enumerate(packer(tile, i)):
                    rs_send[step, tile * 4 + i, axis] = value
                if dz == 0:
                    rs[step, 0] = rs_send[step, 0]
                else:
                    remote(rs_send.at[step, tile * 4 + i], rs.at[step, seen_in_line(dz) - PLANE], rs_sent.at[step],
                           rs_recv.at[step], line_at(dz)).start()

        for n in range(4):
            pl.when((core == 0) & (t == n))(functools.partial(send_plane, 3 - n))
        for n in range(2):
            pl.when((core == 1) & (t == 2 * n + 1))(functools.partial(send_line, 1 - n))

    def collect(step):
        @pl.when(core == 0)
        def _():
            wait_recv(rs.at[step, pl.ds(0, PLANE - 1)], rs_recv.at[step])
            for axis in range(3):
                packed[step + 1, axis] = sum((rs[step, s, axis] for s in range(1, PLANE)), rs[step, 0, axis])

        @pl.when(core == 1)
        def _():
            wait_recv(rs.at[step, pl.ds(0, LINE - 1)], rs_recv.at[step])
            for axis in range(3):
                packed[step + 1, axis] = sum((rs[step, s, axis] for s in range(1, LINE)), rs[step, 0, axis])

    front = lax.broadcasted_iota(jnp.int32, (1, 128), 1) < HALF

    def fold(value):
        line = jnp.sum(value, axis=0, keepdims=True)
        return line + turn(line)

    def inner(left, right):
        return fold(sum(left[axis] * right[axis] for axis in range(3)))

    def reduce_plane(k, values):
        for n, value in values:
            red_src[2 * k, :, n * 128:n * 128 + 128] = value
        for spot in far_places:
            remote(red_src.at[2 * k], red_one.at[k, seen_in_plane(*spot)], red_sem.at[k, 0], red_sem.at[k, 1], plane_at(*spot)).start()
        red_one[k, 0] = red_src[2 * k]

    def reduce_line(k):
        def send(dz, device):
            slot = seen_in_line(dz) - PLANE
            remote(red_src.at[2 * k + 1], red_two.at[k, core, slot], red_sem.at[k, 2], red_sem.at[k, 3], device).start()

        wait_recv(red_one.at[k, pl.ds(0, PLANE - 1)], red_sem.at[k, 1])
        red_src[2 * k + 1] = sum((red_one[k, s] for s in range(1, PLANE)), red_one[k, 0])
        for dz in far_steps:
            send(dz, line_at(dz))
            if k == 1:
                send(dz, line_mate(dz))
        if k == 1:
            send(0, sibling)
        red_two[k, core, 0] = red_src[2 * k + 1]

    def reduced(k, c):
        return sum((red_two[k, c, s] for s in range(1, LINE)), red_two[k, c, 0])

    @pl.loop(0, 2)
    def _(t):
        build(t)

    @pl.when(core == 0)
    def _():
        wait_line(0, 0)
        wait_line(0, 1)

    @pl.when(core == 1)
    def _():
        wait_plane(0, 0)
        wait_plane(0, 1)
        widen(1)

    widen(0)

    @pl.loop(0, 4)
    def _(t):
        @pl.when(t >= 2)
        def _():
            build(t)

        more = (core == 1) & (lax.rem(t, 2) == 1)
        for axis, value in enumerate(product(t)):
            acc[axis] = jnp.where(more, acc[axis], 0.0) + value
        scatter(0, t, pack)

    collect(0)
    gather(1)
    reduce_plane(0, ((0, inner(packed.at[0], packed.at[0])), (1, inner(packed.at[0], packed.at[1]))))

    @pl.loop(1, ITERS)
    def _(step):
        def unit(part_of, t):
            tile = tile_of(t)
            quarter = jnp.where(core == 0, part_of, lax.rem(t, 2))
            h = jnp.where(core == 0, lax.div(tile, 2), part_of)
            w = jnp.where(core == 0, 0, part_of)
            rt = jnp.where(core == 0, lax.rem(tile, 2), tile)
            inner_at = pl.ds(pl.multiple_of(quarter * 1536, 1536), 1536)
            rows = pl.ds(pl.multiple_of(rt * 256, 256), 256)
            return tile, dot(mob_high[h, rows, inner_at], narrow[w, inner_at, :])

        arrange_half(step, 0)

        @pl.loop(0, 4)
        def _(t):
            @pl.when((step == 1) | (core == 1) | (t > 0))
            def _():
                tile, value = unit(0, t)
                more = (core == 1) & (lax.rem(t, 2) == 1)
                acc_wide[tile] = jnp.where(more, acc_wide[tile], 0.0) + value

        arrange_half(step, 1)

        @pl.loop(0, 4)
        def _(t):
            @pl.when((step == 1) | jnp.where(core == 1, lax.rem(t, 2) == 0, t > 0))
            def _():
                tile, value = unit(1, t)
                acc_wide[tile] += value

            @pl.when(step == 1)
            def _():
                scatter(1, t, pack_wide)

            @pl.when((step == 2) & (t == 0) & (core == 0))
            def _():
                wait_plane(2, 0)
                wait_plane(2, 1, True)

            @pl.when((step == 2) & (t == 0) & (core == 1))
            def _():
                wait_line(2, 0)
                wait_line(2, 1)

            @pl.when((step == 2) & jnp.where(core == 1, lax.rem(t, 2) == 1, t > 0))
            def _():
                tile = tile_of(t)
                at = jnp.where(core == 0, 0, PLANE) + tile * 4
                total = jnp.zeros((32, 128), F32)
                for i in range(4):
                    for axis, value in enumerate(pack_wide(tile, i)):
                        total = total + value * ag[2, at + i, axis]
                part[...] += total * jnp.where((core == 0) & (tile > 0), 2.0, 1.0)

        @pl.when(step == 1)
        def _():
            reduce_line(0)
            collect(1)
            wait_recv(red_two.at[0, 0, pl.ds(0, LINE - 1)], red_sem.at[0, 3])
            total = reduced(0, core)
            moments[0] = jnp.broadcast_to(total[:, 128:256] / total[:, 0:128], (32, 128))
            a1 = moments[0]
            for axis in range(3):
                y1 = packed[1, axis]
                packed[2, axis] = packed[2, axis] - a1 * y1
                first_dir[axis] = y1 - a1 * packed[0, axis]
            gather(2)
            remote(first_dir, mate.at[0], mate_sem.at[2], mate_sem.at[3], sibling).start()
            remote(packed.at[2], mate.at[1], mate_sem.at[2], mate_sem.at[3], sibling).start()

    reduce_plane(1, ((0, red_src[0][:, 0:128]), (1, red_src[0][:, 128:256]),
                     (2, inner(first_dir, first_dir)), (3, inner(first_dir, packed.at[2])),
                     (4, inner(packed.at[2], packed.at[2])), (5, fold(part[...]))))
    reduce_line(1)
    wait_recv(red_one.at[1, pl.ds(0, 2 * LINE - 1)], red_sem.at[1, 3])
    low, high = reduced(1, 0), reduced(1, 1)
    for k in range(6):
        at = slice(k * 128, k * 128 + 128)
        moments[k + 1, 0:8] = jnp.broadcast_to(jnp.where(front, low[:, at], high[:, at]), (8, 128))
    moments[7, 0:8] = jnp.zeros((8, 128), F32)
    moments[8, 0:8] = jnp.ones((8, 128), F32)
    m0, m1, e1, f1, g, third, zero, one = (moments[k, 0:8] for k in range(1, 9))

    a1, a2, bb2 = m1 / m0, f1 / e1, e1 / m0
    e2 = g - a2 * f1 - bb2 * e1
    bb3 = e2 / e1
    a3 = (third - a2 * g - bb2 * (f1 + a1 * e1)) / e2 - a2
    d1, d2, d3 = 1.0 + a1, 1.0 + a2, 1.0 + a3
    scale = (d1 + d2 + d3) / ITERS
    current = (d1 / scale, jnp.sqrt(bb2) / scale, zero, d2 / scale, jnp.sqrt(bb3) / scale, d3 / scale)
    partner = (one, zero, zero, one, zero, one)

    def inverse_three(m):
        c00, c01, c02 = m[3] * m[5] - m[4] * m[4], m[2] * m[4] - m[1] * m[5], m[1] * m[4] - m[2] * m[3]
        c11, c12, c22 = m[0] * m[5] - m[2] * m[2], m[1] * m[2] - m[0] * m[4], m[0] * m[3] - m[1] * m[1]
        over = 1.0 / (m[0] * c00 + m[1] * c01 + m[2] * c02)
        return tuple(c * over for c in (c00, c01, c02, c11, c12, c22))

    def newton(_, state):
        now, other = state
        return (tuple(0.5 * (u + v) for u, v in zip(now, inverse_three(other))),
                tuple(0.5 * (u + v) for u, v in zip(other, inverse_three(now))))

    current, partner = lax.fori_loop(0, 20, newton, (current, partner))
    size = jnp.sqrt(scale)
    beta = jnp.sqrt(m0)
    r1, r2, r3 = (current[k] * size for k in range(3))
    f2, f3 = beta * r2 / jnp.sqrt(e1), beta * r3 / jnp.sqrt(e2)
    wait_recv(mate, mate_sem.at[3])
    c0, c1, c2 = (jnp.concatenate([c, c, c, c], axis=0) for c in (r1 - f3 * bb2, f2 - f3 * a2, f3))
    for axis in range(3):
        out_ref[axis] = (c0 * z_ref[axis] + c1 * jnp.where(keep, first_dir[axis], turn(mate[0, axis]))
                         + c2 * jnp.where(keep, packed[2, axis], turn(mate[1, axis])))

    wait_send(z_mate, mate_sem.at[0])
    wait_send(mate, mate_sem.at[2])
    wait_send(posbuf.at[pl.ds(0, 46)], pos_sem.at[0])
    wait_send(ag.at[2, pl.ds(0, NEEDED - 1 + LINE - 1)], ag_send.at[2])
    for k, count in enumerate((LINE - 1, 2 * LINE - 1)):
        wait_send(red_one.at[k, pl.ds(0, PLANE - 1)], red_sem.at[k, 0])
        wait_send(red_one.at[k, pl.ds(0, count)], red_sem.at[k, 2])
    for step in range(2):
        @pl.when(core == 0)
        def _(step=step):
            wait_send(ag.at[step, pl.ds(0, LINE - 1)], ag_send.at[step])
            wait_send(rs_send.at[step, pl.ds(0, PLANE - 1)], rs_sent.at[step])

        @pl.when(core == 1)
        def _(step=step):
            wait_send(ag.at[step, pl.ds(0, PLANE - 1)], ag_send.at[step])
            wait_send(rs_send.at[step, pl.ds(0, LINE - 1)], rs_sent.at[step])


def shards(positions, start_vector):
    chunk = (3, 32, 128)
    return pl.pallas_call(
        kernel,
        out_shape=jax.ShapeDtypeStruct(start_vector.shape, F32),
        in_specs=[pl.BlockSpec(memory_space=pltpu.HBM)] * 2,
        out_specs=pl.BlockSpec(memory_space=pltpu.VMEM),
        scratch_shapes=[
            pltpu.VMEM((2 * (PLANE + LINE), 1, 128), F32),
            pltpu.VMEM((2, 3, BLOCK, 128), F32),
            pltpu.VMEM((2, 8, BLOCK), F32),
            pltpu.VMEM((2, BLOCK, 6 * BLOCK), BF16),
            pltpu.VMEM((2, BLOCK, 6 * BLOCK), BF16),
            pltpu.VMEM((2, BLOCK, 512), BF16),
            pltpu.VMEM((2, 6 * BLOCK, 256), BF16),
            pltpu.VMEM((3, PLANE + LINE) + chunk, F32),
            pltpu.VMEM((2, PLANE) + chunk, F32),
            pltpu.VMEM((2, PLANE) + chunk, F32),
            pltpu.VMEM((3,) + chunk, F32),
            pltpu.VMEM(chunk, F32),
            pltpu.VMEM((2,) + chunk, F32),
            pltpu.VMEM((3, 256, 128), F32),
            pltpu.VMEM((4, 256, 256), F32),
            pltpu.VMEM((32, 128), F32),
            pltpu.VMEM((4, 1, WIDTH), F32),
            pltpu.VMEM((2, PLANE, 1, WIDTH), F32),
            pltpu.VMEM((2, 2, LINE, 1, WIDTH), F32),
            pltpu.VMEM((9, 32, 128), F32),
            pltpu.VMEM((3, 32), jnp.int32),
            pltpu.VMEM((8, 128), F32),
            pltpu.VMEM(chunk, F32),
            pltpu.VMEM(chunk, F32),
            pltpu.SemaphoreType.DMA((2,)),
            pltpu.SemaphoreType.DMA((4,)),
            pltpu.SemaphoreType.DMA((2,)),
            pltpu.SemaphoreType.DMA((3, 2)),
            pltpu.SemaphoreType.DMA((3, 2)),
            pltpu.SemaphoreType.DMA((3,)),
            pltpu.SemaphoreType.DMA((2,)),
            pltpu.SemaphoreType.DMA((2,)),
            pltpu.SemaphoreType.DMA((2, 4)),
        ],
        compiler_params=pltpu.CompilerParams(
            collective_id=0, has_side_effects=True, vmem_limit_bytes=40 * 1024 * 1024),
    )(positions, start_vector)


def solution(mesh):
    in_specs = (P(None, ("row", "col")), P(None, ("row", "col"), None))
    out_specs = P(None, ("row", "col"), None)
    return jax.shard_map(shards, mesh=mesh, in_specs=in_specs, out_specs=out_specs, check_vma=False)
```

```python
import functools

import jax
import jax.numpy as jnp
from jax import lax
from jax.experimental import pallas as pl
from jax.experimental.pallas import tpu as pltpu
from jax.sharding import PartitionSpec as P

ITERS = 3
RADIUS = 0.4
MESH = pl.DeviceIdType.MESH
F32 = jnp.float32
BF16 = jnp.bfloat16

PLANE, LINE = 16, 8
PLACES = ((0, 0), (2, 0), (0, 2), (2, 2), (0, 1), (3, 0), (1, 1), (1, 3), (3, 2), (2, 1),
          (0, 3), (1, 0), (3, 3), (3, 1), (1, 2), (2, 3))
NEEDED = 10
STEPS = (0, 1, 7, 2, 6, 3, 5, 4)


def seen_in_plane(dx, dy):
    return PLACES.index((-dx % 4, -dy % 4))


def seen_in_line(dz):
    return PLANE + STEPS.index(-dz % 8)


HALF = 64
BLOCK = 512
WIDTH = 768


def kernel(pos_hbm, z_hbm, out_ref, posrow, posbuf, colbc, lanevec, mob_high, mob_low, wide, narrow, ag, rs, rs_send,
           packed, first_dir, mate, acc, acc_wide, part, red_src, red_one, red_two, moments, pos_ref, flatten, z_ref,
           z_mate, load_sem, mate_sem, pos_sem, line_sem, plane_sem, ag_send, rs_recv, rs_sent, red_sem):
    row, col = lax.axis_index("row"), lax.axis_index("col")
    x, core = lax.div(row, 2), lax.rem(row, 2)
    z, y = lax.div(col, 4), lax.rem(col, 4)

    xs = [lax.rem(x + d, 4) for d in range(4)]
    ys = [lax.rem(y + d, 4) for d in range(4)]
    zs = [lax.rem(z + d, 8) for d in range(8)]

    def plane_at(dx, dy):
        return (xs[dx] * 2 + core, z * 4 + ys[dy])

    far_places, far_steps = PLACES[:0:-1], STEPS[:0:-1]

    def line_at(dz):
        return (row, zs[dz] * 4 + y)

    def line_mate(dz):
        return (x * 2 + 1 - core, zs[dz] * 4 + y)

    sibling = (x * 2 + 1 - core, col)

    def remote(src, dst, send, recv, device):
        return pltpu.make_async_remote_copy(
            src_ref=src, dst_ref=dst, send_sem=send, recv_sem=recv, device_id=device, device_id_type=MESH)

    def wait_recv(ref, sem):
        remote(ref, ref, sem, sem, (row, col)).wait_recv()

    def wait_send(ref, sem):
        remote(ref, ref, sem, sem, (row, col)).wait_send()

    first = lax.broadcasted_iota(jnp.int32, (32, 128), 1) < HALF
    keep = first == (core == 0)

    def turn(value):
        return pltpu.roll(value, HALF, 1)

    load_pos = pltpu.make_async_copy(pos_hbm, pos_ref, load_sem.at[0])
    load_pos.start()
    load_z = pltpu.make_async_copy(z_hbm, z_ref, load_sem.at[1])
    load_z.start()
    barrier = pltpu.get_barrier_semaphore()

    def signal(device):
        pl.semaphore_signal(barrier, inc=1, device_id=device, device_id_type=MESH)

    signal(sibling)
    for dx, dy in far_places:
        signal(plane_at(dx, dy))
    for dz in far_steps:
        signal(line_at(dz))
        signal(line_mate(dz))

    flatten[...] = jnp.zeros_like(flatten)
    acc[...] = jnp.zeros_like(acc)
    acc_wide[...] = jnp.zeros_like(acc_wide)
    part[...] = jnp.zeros_like(part)
    ag[2, NEEDED:PLANE] = jnp.zeros((PLANE - NEEDED, 3, 32, 128), F32)
    for k in range(2):
        red_src[2 * k] = jnp.zeros((1, WIDTH), F32)
    load_pos.wait()
    flatten[0:3, 0:32] = pos_ref[...].astype(F32)
    rows3 = flatten[...]
    posrow[core] = rows3[0:1] + pltpu.roll(rows3[1:2], 32, 1) + pltpu.roll(rows3[2:3], 64, 1)
    load_z.wait()
    pl.semaphore_wait(barrier, 30)

    remote(posrow.at[core], posrow.at[core], pos_sem.at[0], pos_sem.at[1], sibling).start()
    remote(z_ref, z_mate, mate_sem.at[0], mate_sem.at[1], sibling).start()
    wait_recv(posrow.at[0], pos_sem.at[1])
    both = jnp.concatenate([posrow[0], posrow[1]], axis=1)
    posbuf[0] = both
    posbuf[PLANE] = both
    for n, spot in enumerate(far_places):
        if n < 7:
            remote(posbuf.at[PLANE], posbuf.at[seen_in_line(far_steps[n])], pos_sem.at[2], pos_sem.at[3],
                   line_at(far_steps[n])).start()
        remote(posbuf.at[0], posbuf.at[seen_in_plane(*spot)], pos_sem.at[2], pos_sem.at[3], plane_at(*spot)).start()
    wait_recv(z_mate, mate_sem.at[1])
    for axis in range(3):
        packed[0, axis] = jnp.where(keep, z_ref[axis], turn(z_mate[axis]))

    def gather(step):
        def to_line():
            for dz in STEPS[1:]:
                slot = seen_in_line(dz)
                remote(packed.at[step], ag.at[step, slot], ag_send.at[step], line_sem.at[step, (slot - PLANE) // 4],
                       line_at(dz)).start()

        def to_plane(needed):
            for spot in PLACES[1:]:
                slot = seen_in_plane(*spot)
                if (slot < NEEDED) == needed:
                    remote(packed.at[step], ag.at[step, slot], ag_send.at[step], plane_sem.at[step, slot // 8],
                           plane_at(*spot)).start()

        last = step == 2
        pl.when(core == 0)(to_line)
        pl.when((core == 1) | last)(lambda: to_plane(True))
        pl.when((core == 1) & jnp.logical_not(last))(lambda: to_plane(False))
        pl.when((core == 1) & last)(to_line)
        ag[step, 0] = packed[step]
        ag[step, PLANE] = packed[step]

    def wait_line(step, part_of):
        wait_recv(ag.at[step, pl.ds(0, 4 if part_of else 3)], line_sem.at[step, part_of])

    def wait_plane(step, part_of, last=False):
        if part_of == 0:
            wait_recv(ag.at[step, pl.ds(0, 7)], plane_sem.at[step, 0])
        else:
            wait_recv(ag.at[step, pl.ds(0, NEEDED - 8 if last else 8)], plane_sem.at[step, 1])

    gather(0)
    narrow[...] = jnp.zeros_like(narrow)
    wait_recv(posbuf.at[pl.ds(0, 22)], pos_sem.at[3])

    lane_of = lax.broadcasted_iota(jnp.int32, (BLOCK, 128), 1)
    bead_of = lax.broadcasted_iota(jnp.int32, (BLOCK, 128), 0) & 31
    entry_of = lax.broadcasted_iota(jnp.int32, (128, BLOCK), 0)
    column_of = lax.broadcasted_iota(jnp.int32, (128, BLOCK), 1) & 31
    owner_of = lax.broadcasted_iota(jnp.int32, (16, BLOCK), 1) >> 5
    source_of = lax.broadcasted_iota(jnp.int32, (16, BLOCK), 0)
    ones = jnp.ones((128, 128), BF16)

    def place(at, d):
        return posbuf[at + d // 2][:, (d % 2) * 128:(d % 2) * 128 + 128]

    @pl.loop(0, 2)
    def _(h):
        rows_at = jnp.where(core == 0, h, 2) * 8
        lanes_at = jnp.where(core == 0, 2, h) * 8
        spread = jnp.concatenate([jnp.broadcast_to(place(rows_at, d), (32, 128)) for d in range(16)], axis=0)
        flat = jnp.concatenate([place(lanes_at, d) for d in range(16)], axis=0).astype(BF16)
        for axis in range(3):
            own = jnp.where(lane_of == axis * 32 + bead_of, spread, 0.0).astype(BF16)
            colbc[h, axis] = jnp.dot(own, ones, preferred_element_type=F32)
            pick = jnp.where(entry_of == axis * 32 + column_of, 1.0, 0.0).astype(BF16)
            moved = jnp.dot(flat, pick, preferred_element_type=F32)
            lanevec[h, axis:axis + 1, :] = jnp.sum(jnp.where(owner_of == source_of, moved, 0.0), axis=0, keepdims=True)

    def tile_of(t):
        return jnp.where(core == 0, lax.rem(4 - t, 4), 1 - lax.div(t, 2))

    def places(t):
        tile = tile_of(t)
        h = jnp.where(core == 0, lax.div(tile, 2), lax.rem(t, 2))
        rt = jnp.where(core == 0, lax.rem(tile, 2), tile)
        return h, jnp.where(core == 0, 0, h), pl.ds(pl.multiple_of(rt * 256, 256), 256)

    def build(t):
        h, _, span = places(t)

        @pl.loop(0, 16, unroll=2)
        def _(r):
            rows = pl.ds(pl.multiple_of(span.start + r * 16, 16), 16)
            mine = [colbc[h, axis, rows, :] for axis in range(3)]
            for tile in range(4):
                lanes = slice(tile * 128, tile * 128 + 128)
                d = [mine[axis] - lanevec[h, axis:axis + 1, lanes] for axis in range(3)]
                squared = d[0] * d[0] + d[1] * d[1] + d[2] * d[2]
                root = lax.rsqrt(jnp.where(squared > 0.5, squared, 1e30))
                inverse = root * root
                prefactor = (0.75 * RADIUS) * root
                iso = prefactor * (1.0 + (2.0 / 3.0 * RADIUS * RADIUS) * inverse)
                along = (prefactor * inverse) * (1.0 - (2.0 * RADIUS * RADIUS) * inverse)
                s = [along * d[axis] for axis in range(3)]
                parts = (s[0] * d[0] + iso, s[0] * d[1], s[0] * d[2], s[1] * d[1] + iso, s[1] * d[2],
                         s[2] * d[2] + iso)
                for k, value in enumerate(parts):
                    high = value.astype(BF16)
                    at = (tile // 2) * 1536 + k * 256 + (tile % 2) * 128
                    at = slice(at, at + 128)
                    mob_high[h, rows, at] = high
                    mob_low[h, rows, at] = (value - high.astype(F32)).astype(BF16)

    def widen(h):
        base = jnp.where(core == 0, PLANE, h * 8)

        @pl.loop(0, 8)
        def _(s):
            for axis in range(3):
                value = ag[0, base + s, axis]
                other = turn(value)
                for j, both in enumerate((jnp.where(first, value, other), jnp.where(first, other, value))):
                    high = both.astype(BF16).astype(F32)
                    tile = jnp.where(first, high, both - high).astype(BF16)
                    at = pl.ds(pl.multiple_of(s * 64 + j * 32, 32), 32)
                    wide[h, at, axis * 128:axis * 128 + 128] = tile
                    if axis == 0:
                        wide[h, at, 384:512] = tile

    def arrange(step, base, w, quarter, weight):
        @pl.loop(0, 4)
        def _(s):
            values = [ag[step, base + s, axis] * weight for axis in range(3)]
            others = [turn(value) for value in values]
            for j in range(2):
                left, right = (values, others) if j == 0 else (others, values)
                lx, ly, lz = (jnp.where(first, v, 0.0).astype(BF16) for v in left)
                ry, rz = (jnp.where(first, 0.0, v).astype(BF16) for v in right[1:])
                yx = jnp.where(first, left[1], right[0]).astype(BF16)
                for k, half, tile in ((0, 0, lx), (1, 0, yx), (2, 0, lz), (2, 1, lx), (3, 0, ry), (4, 0, rz),
                                      (4, 1, ly), (5, 1, lz)):
                    at = pl.ds(pl.multiple_of(quarter * 1536 + k * 256 + s * 64 + j * 32, 32), 32)
                    narrow[w, at, half * 128:half * 128 + 128] = tile

    def arrange_half(step, part_of):
        @pl.when(core == 0)
        def _():
            wait_line(step, part_of)
            arrange(step, PLANE + 4 * part_of, 0, part_of, 1.0)

        @pl.when(core == 1)
        def _():
            if part_of == 0:
                wait_plane(step, 0)
            else:
                pl.when(step == 1)(lambda: wait_plane(step, 1))
                pl.when(step == 2)(lambda: wait_plane(step, 1, True))

            @pl.loop(0, 2)
            def _(quarter):
                slot = 8 * part_of + 4 * quarter

                @pl.when((step == 1) | (slot < NEEDED))
                def _():
                    arrange(step, slot, part_of, quarter, jnp.where((step == 2) & (slot >= 4), 2.0, 1.0))

    def dot(left, right):
        return jnp.dot(left, right, preferred_element_type=F32)

    def product(t):
        h, w, rows = places(t)

        def both(k, lo, hi):
            total = 0.0
            for quarter in range(2):
                at = slice(quarter * 1536 + k * 256, quarter * 1536 + k * 256 + 256)
                right = wide[w, quarter * 256:quarter * 256 + 256, lo:hi]
                total = total + dot(mob_high[h, rows, at], right) + dot(mob_low[h, rows, at], right)
            return total

        xy, yz, zx = both(1, 0, 256), both(4, 128, 384), both(2, 256, 512)
        return (both(0, 0, 128) + xy[:, 128:] + zx[:, :128],
                both(3, 128, 256) + xy[:, :128] + yz[:, 128:],
                both(5, 256, 384) + zx[:, 128:] + yz[:, :128])

    def halves(i, upper):
        return pl.ds(pl.multiple_of(i * 64 + upper * 32, 32), 32)

    def pack(_, i):
        chunk = []
        for axis in range(3):
            low, high = acc[axis, halves(i, 0), :], acc[axis, halves(i, 1), :]
            chunk.append(jnp.where(first, low + turn(low), high + turn(high)))
        return chunk

    def pack_wide(tile, i):
        low, high = halves(i, 0), halves(i, 1)
        xy_low, xy_high = acc_wide[tile, low, :128], acc_wide[tile, high, :128]
        z_low, z_high = acc_wide[tile, low, 128:], acc_wide[tile, high, 128:]
        return (jnp.where(first, xy_low, turn(xy_high)), jnp.where(first, turn(xy_low), xy_high),
                jnp.where(first, z_low, turn(z_high)))

    def scatter(step, t, packer):
        def send_plane(tile):
            for i in (3, 2, 1, 0):
                spot = PLACES[tile * 4 + i]
                for axis, value in enumerate(packer(tile, i)):
                    rs_send[step, tile * 4 + i, axis] = value
                if tile * 4 + i == 0:
                    rs[step, 0] = rs_send[step, 0]
                else:
                    remote(rs_send.at[step, tile * 4 + i], rs.at[step, seen_in_plane(*spot)], rs_sent.at[step],
                           rs_recv.at[step], plane_at(*spot)).start()

        def send_line(tile):
            for i in (3, 2, 1, 0):
                dz = STEPS[tile * 4 + i]
                for axis, value in enumerate(packer(tile, i)):
                    rs_send[step, tile * 4 + i, axis] = value
                if dz == 0:
                    rs[step, 0] = rs_send[step, 0]
                else:
                    remote(rs_send.at[step, tile * 4 + i], rs.at[step, seen_in_line(dz) - PLANE], rs_sent.at[step],
                           rs_recv.at[step], line_at(dz)).start()

        for n in range(4):
            pl.when((core == 0) & (t == n))(functools.partial(send_plane, (4 - n) % 4))
        for n in range(2):
            pl.when((core == 1) & (t == 2 * n + 1))(functools.partial(send_line, 1 - n))

    def collect(step):
        @pl.when(core == 0)
        def _():
            wait_recv(rs.at[step, pl.ds(0, PLANE - 1)], rs_recv.at[step])
            for axis in range(3):
                packed[step + 1, axis] = sum((rs[step, s, axis] for s in range(1, PLANE)), rs[step, 0, axis])

        @pl.when(core == 1)
        def _():
            wait_recv(rs.at[step, pl.ds(0, LINE - 1)], rs_recv.at[step])
            for axis in range(3):
                packed[step + 1, axis] = sum((rs[step, s, axis] for s in range(1, LINE)), rs[step, 0, axis])

    front = lax.broadcasted_iota(jnp.int32, (1, 128), 1) < HALF

    def fold(value):
        line = jnp.sum(value, axis=0, keepdims=True)
        return line + turn(line)

    def inner(left, right):
        return fold(sum(left[axis] * right[axis] for axis in range(3)))

    def reduce_plane(k, values):
        for n, value in values:
            red_src[2 * k, :, n * 128:n * 128 + 128] = value
        for spot in far_places:
            remote(red_src.at[2 * k], red_one.at[k, seen_in_plane(*spot)], red_sem.at[k, 0], red_sem.at[k, 1], plane_at(*spot)).start()
        red_one[k, 0] = red_src[2 * k]

    def reduce_line(k):
        def send(dz, device):
            slot = seen_in_line(dz) - PLANE
            remote(red_src.at[2 * k + 1], red_two.at[k, core, slot], red_sem.at[k, 2], red_sem.at[k, 3], device).start()

        wait_recv(red_one.at[k, pl.ds(0, PLANE - 1)], red_sem.at[k, 1])
        red_src[2 * k + 1] = sum((red_one[k, s] for s in range(1, PLANE)), red_one[k, 0])
        for dz in far_steps:
            send(dz, line_at(dz))
            if k == 1:
                send(dz, line_mate(dz))
        if k == 1:
            send(0, sibling)
        red_two[k, core, 0] = red_src[2 * k + 1]

    def reduced(k, c):
        return sum((red_two[k, c, s] for s in range(1, LINE)), red_two[k, c, 0])

    @pl.loop(0, 2)
    def _(t):
        build(t)

    @pl.when(core == 0)
    def _():
        wait_line(0, 0)
        wait_line(0, 1)

    @pl.when(core == 1)
    def _():
        wait_plane(0, 0)
        wait_plane(0, 1)
        widen(1)

    widen(0)

    @pl.loop(0, 4)
    def _(t):
        @pl.when(t >= 2)
        def _():
            build(t)

        more = (core == 1) & (lax.rem(t, 2) == 1)
        for axis, value in enumerate(product(t)):
            acc[axis] = jnp.where(more, acc[axis], 0.0) + value
        scatter(0, t, pack)

    collect(0)
    gather(1)
    reduce_plane(0, ((0, inner(packed.at[0], packed.at[0])), (1, inner(packed.at[0], packed.at[1]))))

    @pl.loop(1, ITERS)
    def _(step):
        def unit(part_of, t):
            tile = tile_of(t)
            quarter = jnp.where(core == 0, part_of, lax.rem(t, 2))
            h = jnp.where(core == 0, lax.div(tile, 2), part_of)
            w = jnp.where(core == 0, 0, part_of)
            rt = jnp.where(core == 0, lax.rem(tile, 2), tile)
            inner_at = pl.ds(pl.multiple_of(quarter * 1536, 1536), 1536)
            rows = pl.ds(pl.multiple_of(rt * 256, 256), 256)
            return tile, dot(mob_high[h, rows, inner_at], narrow[w, inner_at, :])

        arrange_half(step, 0)

        @pl.loop(0, 4)
        def _(t):
            @pl.when((step == 1) | (core == 1) | (t != 1))
            def _():
                tile, value = unit(0, t)
                more = (core == 1) & (lax.rem(t, 2) == 1)
                acc_wide[tile] = jnp.where(more, acc_wide[tile], 0.0) + value

        arrange_half(step, 1)

        @pl.loop(0, 4)
        def _(t):
            @pl.when((step == 1) | jnp.where(core == 1, lax.rem(t, 2) == 0, t != 1))
            def _():
                tile, value = unit(1, t)
                acc_wide[tile] += value

            @pl.when(step == 1)
            def _():
                scatter(1, t, pack_wide)

            @pl.when((step == 2) & (t == 0) & (core == 0))
            def _():
                wait_plane(2, 0)
                wait_plane(2, 1, True)

            @pl.when((step == 2) & (t == 0) & (core == 1))
            def _():
                wait_line(2, 0)
                wait_line(2, 1)

            @pl.when((step == 2) & jnp.where(core == 1, lax.rem(t, 2) == 1, t != 1))
            def _():
                tile = tile_of(t)
                at = jnp.where(core == 0, 0, PLANE) + tile * 4
                total = jnp.zeros((32, 128), F32)
                for i in range(4):
                    for axis, value in enumerate(pack_wide(tile, i)):
                        total = total + value * ag[2, at + i, axis]
                part[...] += total * jnp.where((core == 0) & (tile > 0), 2.0, 1.0)

        @pl.when(step == 1)
        def _():
            reduce_line(0)
            collect(1)
            wait_recv(red_two.at[0, 0, pl.ds(0, LINE - 1)], red_sem.at[0, 3])
            total = reduced(0, core)
            moments[0] = jnp.broadcast_to(total[:, 128:256] / total[:, 0:128], (32, 128))
            a1 = moments[0]
            for axis in range(3):
                y1 = packed[1, axis]
                packed[2, axis] = packed[2, axis] - a1 * y1
                first_dir[axis] = y1 - a1 * packed[0, axis]
            gather(2)
            remote(first_dir, mate.at[0], mate_sem.at[2], mate_sem.at[3], sibling).start()
            remote(packed.at[2], mate.at[1], mate_sem.at[2], mate_sem.at[3], sibling).start()

    reduce_plane(1, ((0, red_src[0][:, 0:128]), (1, red_src[0][:, 128:256]),
                     (2, inner(first_dir, first_dir)), (3, inner(first_dir, packed.at[2])),
                     (4, inner(packed.at[2], packed.at[2])), (5, fold(part[...]))))
    reduce_line(1)
    wait_recv(red_one.at[1, pl.ds(0, 2 * LINE - 1)], red_sem.at[1, 3])
    low, high = reduced(1, 0), reduced(1, 1)
    for k in range(6):
        at = slice(k * 128, k * 128 + 128)
        moments[k + 1, 0:8] = jnp.broadcast_to(jnp.where(front, low[:, at], high[:, at]), (8, 128))
    moments[7, 0:8] = jnp.zeros((8, 128), F32)
    moments[8, 0:8] = jnp.ones((8, 128), F32)
    m0, m1, e1, f1, g, third, zero, one = (moments[k, 0:8] for k in range(1, 9))

    a1, a2, bb2 = m1 / m0, f1 / e1, e1 / m0
    e2 = g - a2 * f1 - bb2 * e1
    bb3 = e2 / e1
    a3 = (third - a2 * g - bb2 * (f1 + a1 * e1)) / e2 - a2
    d1, d2, d3 = 1.0 + a1, 1.0 + a2, 1.0 + a3
    scale = (d1 + d2 + d3) / ITERS
    current = (d1 / scale, jnp.sqrt(bb2) / scale, zero, d2 / scale, jnp.sqrt(bb3) / scale, d3 / scale)
    partner = (one, zero, zero, one, zero, one)

    def inverse_three(m):
        c00, c01, c02 = m[3] * m[5] - m[4] * m[4], m[2] * m[4] - m[1] * m[5], m[1] * m[4] - m[2] * m[3]
        c11, c12, c22 = m[0] * m[5] - m[2] * m[2], m[1] * m[2] - m[0] * m[4], m[0] * m[3] - m[1] * m[1]
        over = 1.0 / (m[0] * c00 + m[1] * c01 + m[2] * c02)
        return tuple(c * over for c in (c00, c01, c02, c11, c12, c22))

    def newton(_, state):
        now, other = state
        return (tuple(0.5 * (u + v) for u, v in zip(now, inverse_three(other))),
                tuple(0.5 * (u + v) for u, v in zip(other, inverse_three(now))))

    current, partner = lax.fori_loop(0, 20, newton, (current, partner))
    size = jnp.sqrt(scale)
    beta = jnp.sqrt(m0)
    r1, r2, r3 = (current[k] * size for k in range(3))
    f2, f3 = beta * r2 / jnp.sqrt(e1), beta * r3 / jnp.sqrt(e2)
    wait_recv(mate, mate_sem.at[3])
    c0, c1, c2 = (jnp.concatenate([c, c, c, c], axis=0) for c in (r1 - f3 * bb2, f2 - f3 * a2, f3))
    for axis in range(3):
        out_ref[axis] = (c0 * z_ref[axis] + c1 * jnp.where(keep, first_dir[axis], turn(mate[0, axis]))
                         + c2 * jnp.where(keep, packed[2, axis], turn(mate[1, axis])))

    wait_send(posrow.at[0], pos_sem.at[0])
    wait_send(z_mate, mate_sem.at[0])
    wait_send(mate, mate_sem.at[2])
    wait_send(posbuf.at[pl.ds(0, 22)], pos_sem.at[2])
    wait_send(ag.at[2, pl.ds(0, NEEDED - 1 + LINE - 1)], ag_send.at[2])
    for k, count in enumerate((LINE - 1, 2 * LINE - 1)):
        wait_send(red_one.at[k, pl.ds(0, PLANE - 1)], red_sem.at[k, 0])
        wait_send(red_one.at[k, pl.ds(0, count)], red_sem.at[k, 2])
    for step in range(2):
        @pl.when(core == 0)
        def _(step=step):
            wait_send(ag.at[step, pl.ds(0, LINE - 1)], ag_send.at[step])
            wait_send(rs_send.at[step, pl.ds(0, PLANE - 1)], rs_sent.at[step])

        @pl.when(core == 1)
        def _(step=step):
            wait_send(ag.at[step, pl.ds(0, PLANE - 1)], ag_send.at[step])
            wait_send(rs_send.at[step, pl.ds(0, LINE - 1)], rs_sent.at[step])


def shards(positions, start_vector):
    chunk = (3, 32, 128)
    return pl.pallas_call(
        kernel,
        out_shape=jax.ShapeDtypeStruct(start_vector.shape, F32),
        in_specs=[pl.BlockSpec(memory_space=pltpu.HBM)] * 2,
        out_specs=pl.BlockSpec(memory_space=pltpu.VMEM),
        scratch_shapes=[
            pltpu.VMEM((2, 1, 128), F32),
            pltpu.VMEM((PLANE + LINE, 1, 256), F32),
            pltpu.VMEM((2, 3, BLOCK, 128), F32),
            pltpu.VMEM((2, 8, BLOCK), F32),
            pltpu.VMEM((2, BLOCK, 6 * BLOCK), BF16),
            pltpu.VMEM((2, BLOCK, 6 * BLOCK), BF16),
            pltpu.VMEM((2, BLOCK, 512), BF16),
            pltpu.VMEM((2, 6 * BLOCK, 256), BF16),
            pltpu.VMEM((3, PLANE + LINE) + chunk, F32),
            pltpu.VMEM((2, PLANE) + chunk, F32),
            pltpu.VMEM((2, PLANE) + chunk, F32),
            pltpu.VMEM((3,) + chunk, F32),
            pltpu.VMEM(chunk, F32),
            pltpu.VMEM((2,) + chunk, F32),
            pltpu.VMEM((3, 256, 128), F32),
            pltpu.VMEM((4, 256, 256), F32),
            pltpu.VMEM((32, 128), F32),
            pltpu.VMEM((4, 1, WIDTH), F32),
            pltpu.VMEM((2, PLANE, 1, WIDTH), F32),
            pltpu.VMEM((2, 2, LINE, 1, WIDTH), F32),
            pltpu.VMEM((9, 32, 128), F32),
            pltpu.VMEM((3, 32), jnp.int32),
            pltpu.VMEM((8, 128), F32),
            pltpu.VMEM(chunk, F32),
            pltpu.VMEM(chunk, F32),
            pltpu.SemaphoreType.DMA((2,)),
            pltpu.SemaphoreType.DMA((4,)),
            pltpu.SemaphoreType.DMA((4,)),
            pltpu.SemaphoreType.DMA((3, 2)),
            pltpu.SemaphoreType.DMA((3, 2)),
            pltpu.SemaphoreType.DMA((3,)),
            pltpu.SemaphoreType.DMA((2,)),
            pltpu.SemaphoreType.DMA((2,)),
            pltpu.SemaphoreType.DMA((2, 4)),
        ],
        compiler_params=pltpu.CompilerParams(
            collective_id=0, has_side_effects=True, vmem_limit_bytes=40 * 1024 * 1024),
    )(positions, start_vector)


def solution(mesh):
    in_specs = (P(None, ("row", "col")), P(None, ("row", "col"), None))
    out_specs = P(None, ("row", "col"), None)
    return jax.shard_map(shards, mesh=mesh, in_specs=in_specs, out_specs=out_specs, check_vma=False)
```

```python
import functools

import jax
import jax.numpy as jnp
from jax import lax
from jax.experimental import pallas as pl
from jax.experimental.pallas import tpu as pltpu
from jax.sharding import PartitionSpec as P

ITERS = 3
RADIUS = 0.4
MESH = pl.DeviceIdType.MESH
F32 = jnp.float32
BF16 = jnp.bfloat16

PLANE, LINE = 16, 8
PLACES = ((0, 0), (2, 0), (0, 2), (2, 2), (0, 1), (3, 0), (1, 1), (1, 3), (3, 2), (2, 1),
          (0, 3), (1, 0), (3, 3), (3, 1), (1, 2), (2, 3))
NEEDED = 10
STEPS = (0, 1, 7, 2, 6, 3, 5, 4)


def seen_in_plane(dx, dy):
    return PLACES.index((-dx % 4, -dy % 4))


def seen_in_line(dz):
    return PLANE + STEPS.index(-dz % 8)


HALF = 64
BLOCK = 512
WIDTH = 768


def kernel(pos_ref, z_ref, out_ref, posrow, posbuf, colbc, lanevec, mob_high, mob_low, wide, narrow, ag, rs, rs_send,
           packed, first_dir, mate, acc, acc_wide, part, red_src, red_one, red_two, moments, flatten,
           z_mate, mate_sem, pos_sem, line_sem, plane_sem, ag_send, rs_recv, rs_sent, red_sem):
    row, col = lax.axis_index("row"), lax.axis_index("col")
    x, core = lax.div(row, 2), lax.rem(row, 2)
    z, y = lax.div(col, 4), lax.rem(col, 4)

    xs = [lax.rem(x + d, 4) for d in range(4)]
    ys = [lax.rem(y + d, 4) for d in range(4)]
    zs = [lax.rem(z + d, 8) for d in range(8)]

    def plane_at(dx, dy):
        return (xs[dx] * 2 + core, z * 4 + ys[dy])

    far_places, far_steps = PLACES[:0:-1], STEPS[:0:-1]

    def line_at(dz):
        return (row, zs[dz] * 4 + y)

    def line_mate(dz):
        return (x * 2 + 1 - core, zs[dz] * 4 + y)

    sibling = (x * 2 + 1 - core, col)

    def remote(src, dst, send, recv, device):
        return pltpu.make_async_remote_copy(
            src_ref=src, dst_ref=dst, send_sem=send, recv_sem=recv, device_id=device, device_id_type=MESH)

    def wait_recv(ref, sem):
        remote(ref, ref, sem, sem, (row, col)).wait_recv()

    def wait_send(ref, sem):
        remote(ref, ref, sem, sem, (row, col)).wait_send()

    first = lax.broadcasted_iota(jnp.int32, (32, 128), 1) < HALF
    keep = first == (core == 0)

    def turn(value):
        return pltpu.roll(value, HALF, 1)

    barrier = pltpu.get_barrier_semaphore()

    def signal(device):
        pl.semaphore_signal(barrier, inc=1, device_id=device, device_id_type=MESH)

    signal(sibling)
    for dx, dy in far_places:
        signal(plane_at(dx, dy))
    for dz in far_steps:
        signal(line_at(dz))
        signal(line_mate(dz))

    flatten[...] = jnp.zeros_like(flatten)
    flatten[0:3, 0:32] = pos_ref[...].astype(F32)
    rows3 = flatten[...]
    posrow[core] = rows3[0:1] + pltpu.roll(rows3[1:2], 32, 1) + pltpu.roll(rows3[2:3], 64, 1)
    pl.semaphore_wait(barrier, 30)

    remote(posrow.at[core], posrow.at[core], pos_sem.at[0], pos_sem.at[1], sibling).start()
    remote(z_ref, z_mate, mate_sem.at[0], mate_sem.at[1], sibling).start()
    wait_recv(posrow.at[0], pos_sem.at[1])
    both = jnp.concatenate([posrow[0], posrow[1]], axis=1)
    posbuf[0] = both
    posbuf[PLANE] = both
    for n, spot in enumerate(far_places):
        if n < 7:
            remote(posbuf.at[PLANE], posbuf.at[seen_in_line(far_steps[n])], pos_sem.at[2], pos_sem.at[3],
                   line_at(far_steps[n])).start()
        remote(posbuf.at[0], posbuf.at[seen_in_plane(*spot)], pos_sem.at[2], pos_sem.at[3], plane_at(*spot)).start()
    wait_recv(z_mate, mate_sem.at[1])
    for axis in range(3):
        packed[0, axis] = jnp.where(keep, z_ref[axis], turn(z_mate[axis]))

    def gather(step):
        def to_line():
            for dz in STEPS[1:]:
                slot = seen_in_line(dz)
                remote(packed.at[step], ag.at[step, slot], ag_send.at[step], line_sem.at[step, (slot - PLANE) // 4],
                       line_at(dz)).start()

        def to_plane(needed):
            for spot in PLACES[1:]:
                slot = seen_in_plane(*spot)
                if (slot < NEEDED) == needed:
                    remote(packed.at[step], ag.at[step, slot], ag_send.at[step], plane_sem.at[step, slot // 8],
                           plane_at(*spot)).start()

        last = step == 2
        pl.when(core == 0)(to_line)
        pl.when((core == 1) | last)(lambda: to_plane(True))
        pl.when((core == 1) & jnp.logical_not(last))(lambda: to_plane(False))
        pl.when((core == 1) & last)(to_line)
        ag[step, 0] = packed[step]
        ag[step, PLANE] = packed[step]

    def wait_line(step, part_of):
        wait_recv(ag.at[step, pl.ds(0, 4 if part_of else 3)], line_sem.at[step, part_of])

    def wait_plane(step, part_of, last=False):
        if part_of == 0:
            wait_recv(ag.at[step, pl.ds(0, 7)], plane_sem.at[step, 0])
        else:
            wait_recv(ag.at[step, pl.ds(0, NEEDED - 8 if last else 8)], plane_sem.at[step, 1])

    gather(0)
    acc[...] = jnp.zeros_like(acc)
    acc_wide[...] = jnp.zeros_like(acc_wide)
    part[...] = jnp.zeros_like(part)
    ag[2, NEEDED:PLANE] = jnp.zeros((PLANE - NEEDED, 3, 32, 128), F32)
    for k in range(2):
        red_src[2 * k] = jnp.zeros((1, WIDTH), F32)
    narrow[...] = jnp.zeros_like(narrow)
    wait_recv(posbuf.at[pl.ds(0, 22)], pos_sem.at[3])

    lane_of = lax.broadcasted_iota(jnp.int32, (BLOCK, 128), 1)
    bead_of = lax.broadcasted_iota(jnp.int32, (BLOCK, 128), 0) & 31
    entry_of = lax.broadcasted_iota(jnp.int32, (128, BLOCK), 0)
    column_of = lax.broadcasted_iota(jnp.int32, (128, BLOCK), 1) & 31
    owner_of = lax.broadcasted_iota(jnp.int32, (16, BLOCK), 1) >> 5
    source_of = lax.broadcasted_iota(jnp.int32, (16, BLOCK), 0)
    ones = jnp.ones((128, 128), BF16)

    def place(at, d):
        return posbuf[at + d // 2][:, (d % 2) * 128:(d % 2) * 128 + 128]

    @pl.loop(0, 2)
    def _(h):
        rows_at = jnp.where(core == 0, h, 2) * 8
        lanes_at = jnp.where(core == 0, 2, h) * 8
        spread = jnp.concatenate([jnp.broadcast_to(place(rows_at, d), (32, 128)) for d in range(16)], axis=0)
        flat = jnp.concatenate([place(lanes_at, d) for d in range(16)], axis=0).astype(BF16)
        for axis in range(3):
            own = jnp.where(lane_of == axis * 32 + bead_of, spread, 0.0).astype(BF16)
            colbc[h, axis] = jnp.dot(own, ones, preferred_element_type=F32)
            pick = jnp.where(entry_of == axis * 32 + column_of, 1.0, 0.0).astype(BF16)
            moved = jnp.dot(flat, pick, preferred_element_type=F32)
            lanevec[h, axis:axis + 1, :] = jnp.sum(jnp.where(owner_of == source_of, moved, 0.0), axis=0, keepdims=True)

    def tile_of(t):
        return jnp.where(core == 0, lax.rem(4 - t, 4), 1 - lax.div(t, 2))

    def places(t):
        tile = tile_of(t)
        h = jnp.where(core == 0, lax.div(tile, 2), lax.rem(t, 2))
        rt = jnp.where(core == 0, lax.rem(tile, 2), tile)
        return h, jnp.where(core == 0, 0, h), pl.ds(pl.multiple_of(rt * 256, 256), 256)

    def build(t):
        h, _, span = places(t)

        @pl.loop(0, 16, unroll=2)
        def _(r):
            rows = pl.ds(pl.multiple_of(span.start + r * 16, 16), 16)
            mine = [colbc[h, axis, rows, :] for axis in range(3)]
            for tile in range(4):
                lanes = slice(tile * 128, tile * 128 + 128)
                d = [mine[axis] - lanevec[h, axis:axis + 1, lanes] for axis in range(3)]
                squared = d[0] * d[0] + d[1] * d[1] + d[2] * d[2]
                root = lax.rsqrt(jnp.where(squared > 0.5, squared, 1e30))
                inverse = root * root
                prefactor = (0.75 * RADIUS) * root
                iso = prefactor * (1.0 + (2.0 / 3.0 * RADIUS * RADIUS) * inverse)
                along = (prefactor * inverse) * (1.0 - (2.0 * RADIUS * RADIUS) * inverse)
                s = [along * d[axis] for axis in range(3)]
                parts = (s[0] * d[0] + iso, s[0] * d[1], s[0] * d[2], s[1] * d[1] + iso, s[1] * d[2],
                         s[2] * d[2] + iso)
                for k, value in enumerate(parts):
                    high = value.astype(BF16)
                    at = (tile // 2) * 1536 + k * 256 + (tile % 2) * 128
                    at = slice(at, at + 128)
                    mob_high[h, rows, at] = high
                    mob_low[h, rows, at] = (value - high.astype(F32)).astype(BF16)

    def widen(h):
        base = jnp.where(core == 0, PLANE, h * 8)

        @pl.loop(0, 8)
        def _(s):
            for axis in range(3):
                value = ag[0, base + s, axis]
                other = turn(value)
                for j, both in enumerate((jnp.where(first, value, other), jnp.where(first, other, value))):
                    high = both.astype(BF16).astype(F32)
                    tile = jnp.where(first, high, both - high).astype(BF16)
                    at = pl.ds(pl.multiple_of(s * 64 + j * 32, 32), 32)
                    wide[h, at, axis * 128:axis * 128 + 128] = tile
                    if axis == 0:
                        wide[h, at, 384:512] = tile

    def arrange(step, base, w, quarter, weight):
        @pl.loop(0, 4)
        def _(s):
            values = [ag[step, base + s, axis] * weight for axis in range(3)]
            others = [turn(value) for value in values]
            for j in range(2):
                left, right = (values, others) if j == 0 else (others, values)
                lx, ly, lz = (jnp.where(first, v, 0.0).astype(BF16) for v in left)
                ry, rz = (jnp.where(first, 0.0, v).astype(BF16) for v in right[1:])
                yx = jnp.where(first, left[1], right[0]).astype(BF16)
                for k, half, tile in ((0, 0, lx), (1, 0, yx), (2, 0, lz), (2, 1, lx), (3, 0, ry), (4, 0, rz),
                                      (4, 1, ly), (5, 1, lz)):
                    at = pl.ds(pl.multiple_of(quarter * 1536 + k * 256 + s * 64 + j * 32, 32), 32)
                    narrow[w, at, half * 128:half * 128 + 128] = tile

    def arrange_half(step, part_of):
        @pl.when(core == 0)
        def _():
            wait_line(step, part_of)
            arrange(step, PLANE + 4 * part_of, 0, part_of, 1.0)

        @pl.when(core == 1)
        def _():
            if part_of == 0:
                wait_plane(step, 0)
            else:
                pl.when(step == 1)(lambda: wait_plane(step, 1))
                pl.when(step == 2)(lambda: wait_plane(step, 1, True))

            @pl.loop(0, 2)
            def _(quarter):
                slot = 8 * part_of + 4 * quarter

                @pl.when((step == 1) | (slot < NEEDED))
                def _():
                    arrange(step, slot, part_of, quarter, jnp.where((step == 2) & (slot >= 4), 2.0, 1.0))

    def dot(left, right):
        return jnp.dot(left, right, preferred_element_type=F32)

    def product(t):
        h, w, rows = places(t)

        def both(k, lo, hi):
            total = 0.0
            for quarter in range(2):
                at = slice(quarter * 1536 + k * 256, quarter * 1536 + k * 256 + 256)
                right = wide[w, quarter * 256:quarter * 256 + 256, lo:hi]
                total = total + dot(mob_high[h, rows, at], right) + dot(mob_low[h, rows, at], right)
            return total

        xy, yz, zx = both(1, 0, 256), both(4, 128, 384), both(2, 256, 512)
        return (both(0, 0, 128) + xy[:, 128:] + zx[:, :128],
                both(3, 128, 256) + xy[:, :128] + yz[:, 128:],
                both(5, 256, 384) + zx[:, 128:] + yz[:, :128])

    def halves(i, upper):
        return pl.ds(pl.multiple_of(i * 64 + upper * 32, 32), 32)

    def pack(_, i):
        chunk = []
        for axis in range(3):
            low, high = acc[axis, halves(i, 0), :], acc[axis, halves(i, 1), :]
            chunk.append(jnp.where(first, low + turn(low), high + turn(high)))
        return chunk

    def pack_wide(tile, i):
        low, high = halves(i, 0), halves(i, 1)
        xy_low, xy_high = acc_wide[tile, low, :128], acc_wide[tile, high, :128]
        z_low, z_high = acc_wide[tile, low, 128:], acc_wide[tile, high, 128:]
        return (jnp.where(first, xy_low, turn(xy_high)), jnp.where(first, turn(xy_low), xy_high),
                jnp.where(first, z_low, turn(z_high)))

    def scatter(step, t, packer):
        def send_plane(tile):
            for i in (3, 2, 1, 0):
                spot = PLACES[tile * 4 + i]
                for axis, value in enumerate(packer(tile, i)):
                    rs_send[step, tile * 4 + i, axis] = value
                if tile * 4 + i == 0:
                    rs[step, 0] = rs_send[step, 0]
                else:
                    remote(rs_send.at[step, tile * 4 + i], rs.at[step, seen_in_plane(*spot)], rs_sent.at[step],
                           rs_recv.at[step], plane_at(*spot)).start()

        def send_line(tile):
            for i in (3, 2, 1, 0):
                dz = STEPS[tile * 4 + i]
                for axis, value in enumerate(packer(tile, i)):
                    rs_send[step, tile * 4 + i, axis] = value
                if dz == 0:
                    rs[step, 0] = rs_send[step, 0]
                else:
                    remote(rs_send.at[step, tile * 4 + i], rs.at[step, seen_in_line(dz) - PLANE], rs_sent.at[step],
                           rs_recv.at[step], line_at(dz)).start()

        for n in range(4):
            pl.when((core == 0) & (t == n))(functools.partial(send_plane, (4 - n) % 4))
        for n in range(2):
            pl.when((core == 1) & (t == 2 * n + 1))(functools.partial(send_line, 1 - n))

    def collect(step):
        @pl.when(core == 0)
        def _():
            wait_recv(rs.at[step, pl.ds(0, PLANE - 1)], rs_recv.at[step])
            for axis in range(3):
                packed[step + 1, axis] = sum((rs[step, s, axis] for s in range(1, PLANE)), rs[step, 0, axis])

        @pl.when(core == 1)
        def _():
            wait_recv(rs.at[step, pl.ds(0, LINE - 1)], rs_recv.at[step])
            for axis in range(3):
                packed[step + 1, axis] = sum((rs[step, s, axis] for s in range(1, LINE)), rs[step, 0, axis])

    front = lax.broadcasted_iota(jnp.int32, (1, 128), 1) < HALF

    def fold(value):
        line = jnp.sum(value, axis=0, keepdims=True)
        return line + turn(line)

    def inner(left, right):
        return fold(sum(left[axis] * right[axis] for axis in range(3)))

    def reduce_plane(k, values):
        for n, value in values:
            red_src[2 * k, :, n * 128:n * 128 + 128] = value
        for spot in far_places:
            remote(red_src.at[2 * k], red_one.at[k, seen_in_plane(*spot)], red_sem.at[k, 0], red_sem.at[k, 1], plane_at(*spot)).start()
        red_one[k, 0] = red_src[2 * k]

    def reduce_line(k):
        def send(dz, device):
            slot = seen_in_line(dz) - PLANE
            remote(red_src.at[2 * k + 1], red_two.at[k, core, slot], red_sem.at[k, 2], red_sem.at[k, 3], device).start()

        wait_recv(red_one.at[k, pl.ds(0, PLANE - 1)], red_sem.at[k, 1])
        red_src[2 * k + 1] = sum((red_one[k, s] for s in range(1, PLANE)), red_one[k, 0])
        for dz in far_steps:
            send(dz, line_at(dz))
            if k == 1:
                send(dz, line_mate(dz))
        if k == 1:
            send(0, sibling)
        red_two[k, core, 0] = red_src[2 * k + 1]

    def reduced(k, c):
        return sum((red_two[k, c, s] for s in range(1, LINE)), red_two[k, c, 0])

    @pl.loop(0, 2)
    def _(t):
        build(t)

    @pl.when(core == 0)
    def _():
        wait_line(0, 0)
        wait_line(0, 1)

    @pl.when(core == 1)
    def _():
        wait_plane(0, 0)
        wait_plane(0, 1)
        widen(1)

    widen(0)

    @pl.loop(0, 4)
    def _(t):
        @pl.when(t >= 2)
        def _():
            build(t)

        more = (core == 1) & (lax.rem(t, 2) == 1)
        for axis, value in enumerate(product(t)):
            acc[axis] = jnp.where(more, acc[axis], 0.0) + value
        scatter(0, t, pack)

    collect(0)
    gather(1)
    reduce_plane(0, ((0, inner(packed.at[0], packed.at[0])), (1, inner(packed.at[0], packed.at[1]))))

    @pl.loop(1, ITERS)
    def _(step):
        def unit(part_of, t):
            tile = tile_of(t)
            quarter = jnp.where(core == 0, part_of, lax.rem(t, 2))
            h = jnp.where(core == 0, lax.div(tile, 2), part_of)
            w = jnp.where(core == 0, 0, part_of)
            rt = jnp.where(core == 0, lax.rem(tile, 2), tile)
            inner_at = pl.ds(pl.multiple_of(quarter * 1536, 1536), 1536)
            rows = pl.ds(pl.multiple_of(rt * 256, 256), 256)
            return tile, dot(mob_high[h, rows, inner_at], narrow[w, inner_at, :])

        arrange_half(step, 0)

        @pl.loop(0, 4)
        def _(t):
            @pl.when((step == 1) | (core == 1) | (t != 1))
            def _():
                tile, value = unit(0, t)
                more = (core == 1) & (lax.rem(t, 2) == 1)
                acc_wide[tile] = jnp.where(more, acc_wide[tile], 0.0) + value

        arrange_half(step, 1)

        @pl.loop(0, 4)
        def _(t):
            @pl.when((step == 1) | jnp.where(core == 1, lax.rem(t, 2) == 0, t != 1))
            def _():
                tile, value = unit(1, t)
                acc_wide[tile] += value

            @pl.when(step == 1)
            def _():
                scatter(1, t, pack_wide)

            @pl.when((step == 2) & (t == 0) & (core == 0))
            def _():
                wait_plane(2, 0)
                wait_plane(2, 1, True)

            @pl.when((step == 2) & (t == 0) & (core == 1))
            def _():
                wait_line(2, 0)
                wait_line(2, 1)

            @pl.when((step == 2) & jnp.where(core == 1, lax.rem(t, 2) == 1, t != 1))
            def _():
                tile = tile_of(t)
                at = jnp.where(core == 0, 0, PLANE) + tile * 4
                total = jnp.zeros((32, 128), F32)
                for i in range(4):
                    for axis, value in enumerate(pack_wide(tile, i)):
                        total = total + value * ag[2, at + i, axis]
                part[...] += total * jnp.where((core == 0) & (tile > 0), 2.0, 1.0)

        @pl.when(step == 1)
        def _():
            reduce_line(0)
            collect(1)
            wait_recv(red_two.at[0, 0, pl.ds(0, LINE - 1)], red_sem.at[0, 3])
            total = reduced(0, core)
            moments[0] = jnp.broadcast_to(total[:, 128:256] / total[:, 0:128], (32, 128))
            a1 = moments[0]
            for axis in range(3):
                y1 = packed[1, axis]
                packed[2, axis] = packed[2, axis] - a1 * y1
                first_dir[axis] = y1 - a1 * packed[0, axis]
            gather(2)
            remote(first_dir, mate.at[0], mate_sem.at[2], mate_sem.at[3], sibling).start()
            remote(packed.at[2], mate.at[1], mate_sem.at[2], mate_sem.at[3], sibling).start()

    reduce_plane(1, ((0, red_src[0][:, 0:128]), (1, red_src[0][:, 128:256]),
                     (2, inner(first_dir, first_dir)), (3, inner(first_dir, packed.at[2])),
                     (4, inner(packed.at[2], packed.at[2])), (5, fold(part[...]))))
    reduce_line(1)
    wait_recv(red_one.at[1, pl.ds(0, 2 * LINE - 1)], red_sem.at[1, 3])
    low, high = reduced(1, 0), reduced(1, 1)
    for k in range(6):
        at = slice(k * 128, k * 128 + 128)
        moments[k + 1, 0:8] = jnp.broadcast_to(jnp.where(front, low[:, at], high[:, at]), (8, 128))
    moments[7, 0:8] = jnp.zeros((8, 128), F32)
    moments[8, 0:8] = jnp.ones((8, 128), F32)
    m0, m1, e1, f1, g, third, zero, one = (moments[k, 0:8] for k in range(1, 9))

    a1, a2, bb2 = m1 / m0, f1 / e1, e1 / m0
    e2 = g - a2 * f1 - bb2 * e1
    bb3 = e2 / e1
    a3 = (third - a2 * g - bb2 * (f1 + a1 * e1)) / e2 - a2
    d1, d2, d3 = 1.0 + a1, 1.0 + a2, 1.0 + a3
    scale = (d1 + d2 + d3) / ITERS
    current = (d1 / scale, jnp.sqrt(bb2) / scale, zero, d2 / scale, jnp.sqrt(bb3) / scale, d3 / scale)
    partner = (one, zero, zero, one, zero, one)

    def inverse_three(m):
        c00, c01, c02 = m[3] * m[5] - m[4] * m[4], m[2] * m[4] - m[1] * m[5], m[1] * m[4] - m[2] * m[3]
        c11, c12, c22 = m[0] * m[5] - m[2] * m[2], m[1] * m[2] - m[0] * m[4], m[0] * m[3] - m[1] * m[1]
        over = 1.0 / (m[0] * c00 + m[1] * c01 + m[2] * c02)
        return tuple(c * over for c in (c00, c01, c02, c11, c12, c22))

    def newton(_, state):
        now, other = state
        return (tuple(0.5 * (u + v) for u, v in zip(now, inverse_three(other))),
                tuple(0.5 * (u + v) for u, v in zip(other, inverse_three(now))))

    current, partner = lax.fori_loop(0, 20, newton, (current, partner))
    size = jnp.sqrt(scale)
    beta = jnp.sqrt(m0)
    r1, r2, r3 = (current[k] * size for k in range(3))
    f2, f3 = beta * r2 / jnp.sqrt(e1), beta * r3 / jnp.sqrt(e2)
    wait_recv(mate, mate_sem.at[3])
    c0, c1, c2 = (jnp.concatenate([c, c, c, c], axis=0) for c in (r1 - f3 * bb2, f2 - f3 * a2, f3))
    for axis in range(3):
        out_ref[axis] = (c0 * z_ref[axis] + c1 * jnp.where(keep, first_dir[axis], turn(mate[0, axis]))
                         + c2 * jnp.where(keep, packed[2, axis], turn(mate[1, axis])))

    wait_send(posrow.at[0], pos_sem.at[0])
    wait_send(z_mate, mate_sem.at[0])
    wait_send(mate, mate_sem.at[2])
    wait_send(posbuf.at[pl.ds(0, 22)], pos_sem.at[2])
    wait_send(ag.at[2, pl.ds(0, NEEDED - 1 + LINE - 1)], ag_send.at[2])
    for k, count in enumerate((LINE - 1, 2 * LINE - 1)):
        wait_send(red_one.at[k, pl.ds(0, PLANE - 1)], red_sem.at[k, 0])
        wait_send(red_one.at[k, pl.ds(0, count)], red_sem.at[k, 2])
    for step in range(2):
        @pl.when(core == 0)
        def _(step=step):
            wait_send(ag.at[step, pl.ds(0, LINE - 1)], ag_send.at[step])
            wait_send(rs_send.at[step, pl.ds(0, PLANE - 1)], rs_sent.at[step])

        @pl.when(core == 1)
        def _(step=step):
            wait_send(ag.at[step, pl.ds(0, PLANE - 1)], ag_send.at[step])
            wait_send(rs_send.at[step, pl.ds(0, LINE - 1)], rs_sent.at[step])


def shards(positions, start_vector):
    chunk = (3, 32, 128)
    return pl.pallas_call(
        kernel,
        out_shape=jax.ShapeDtypeStruct(start_vector.shape, F32),
        in_specs=[pl.BlockSpec(memory_space=pltpu.VMEM)] * 2,
        out_specs=pl.BlockSpec(memory_space=pltpu.VMEM),
        scratch_shapes=[
            pltpu.VMEM((2, 1, 128), F32),
            pltpu.VMEM((PLANE + LINE, 1, 256), F32),
            pltpu.VMEM((2, 3, BLOCK, 128), F32),
            pltpu.VMEM((2, 8, BLOCK), F32),
            pltpu.VMEM((2, BLOCK, 6 * BLOCK), BF16),
            pltpu.VMEM((2, BLOCK, 6 * BLOCK), BF16),
            pltpu.VMEM((2, BLOCK, 512), BF16),
            pltpu.VMEM((2, 6 * BLOCK, 256), BF16),
            pltpu.VMEM((3, PLANE + LINE) + chunk, F32),
            pltpu.VMEM((2, PLANE) + chunk, F32),
            pltpu.VMEM((2, PLANE) + chunk, F32),
            pltpu.VMEM((3,) + chunk, F32),
            pltpu.VMEM(chunk, F32),
            pltpu.VMEM((2,) + chunk, F32),
            pltpu.VMEM((3, 256, 128), F32),
            pltpu.VMEM((4, 256, 256), F32),
            pltpu.VMEM((32, 128), F32),
            pltpu.VMEM((4, 1, WIDTH), F32),
            pltpu.VMEM((2, PLANE, 1, WIDTH), F32),
            pltpu.VMEM((2, 2, LINE, 1, WIDTH), F32),
            pltpu.VMEM((9, 32, 128), F32),
            pltpu.VMEM((8, 128), F32),
            pltpu.VMEM(chunk, F32),
            pltpu.SemaphoreType.DMA((4,)),
            pltpu.SemaphoreType.DMA((4,)),
            pltpu.SemaphoreType.DMA((3, 2)),
            pltpu.SemaphoreType.DMA((3, 2)),
            pltpu.SemaphoreType.DMA((3,)),
            pltpu.SemaphoreType.DMA((2,)),
            pltpu.SemaphoreType.DMA((2,)),
            pltpu.SemaphoreType.DMA((2, 4)),
        ],
        compiler_params=pltpu.CompilerParams(
            collective_id=0, has_side_effects=True, vmem_limit_bytes=40 * 1024 * 1024),
    )(positions, start_vector)


def solution(mesh):
    in_specs = (P(None, ("row", "col")), P(None, ("row", "col"), None))
    out_specs = P(None, ("row", "col"), None)
    return jax.shard_map(shards, mesh=mesh, in_specs=in_specs, out_specs=out_specs, check_vma=False)
```

```python
import functools

import jax
import jax.numpy as jnp
from jax import lax
from jax.experimental import pallas as pl
from jax.experimental.pallas import tpu as pltpu
from jax.sharding import PartitionSpec as P

ITERS = 3
RADIUS = 0.4
MESH = pl.DeviceIdType.MESH
F32 = jnp.float32
BF16 = jnp.bfloat16

PLANE, LINE = 16, 8
PLACES = ((0, 0), (2, 0), (0, 2), (2, 2), (0, 1), (3, 0), (1, 1), (1, 3), (3, 2), (2, 1),
          (0, 3), (1, 0), (3, 3), (3, 1), (1, 2), (2, 3))
NEEDED = 10
STEPS = (0, 4, 1, 2, 3, 5, 6, 7)
NEEDED_LINE = 5


def seen_in_plane(dx, dy):
    return PLACES.index((-dx % 4, -dy % 4))


def seen_in_line(dz):
    return PLANE + STEPS.index(-dz % 8)


HALF = 64
BLOCK = 512
WIDTH = 768


def kernel(pos_ref, z_ref, out_ref, posrow, posbuf, colbc, lanevec, mob_high, mob_low, wide, narrow, ag, rs, rs_send,
           packed, first_dir, mate, acc, acc_wide, part, red_src, red_one, red_two, moments, flatten,
           z_mate, mate_sem, pos_sem, line_sem, plane_sem, ag_send, rs_recv, rs_sent, red_sem):
    row, col = lax.axis_index("row"), lax.axis_index("col")
    x, core = lax.div(row, 2), lax.rem(row, 2)
    z, y = lax.div(col, 4), lax.rem(col, 4)

    xs = [lax.rem(x + d, 4) for d in range(4)]
    ys = [lax.rem(y + d, 4) for d in range(4)]
    zs = [lax.rem(z + d, 8) for d in range(8)]

    def plane_at(dx, dy):
        return (xs[dx] * 2 + core, z * 4 + ys[dy])

    far_places, far_steps = PLACES[:0:-1], STEPS[:0:-1]

    def line_at(dz):
        return (row, zs[dz] * 4 + y)

    def line_mate(dz):
        return (x * 2 + 1 - core, zs[dz] * 4 + y)

    sibling = (x * 2 + 1 - core, col)

    def remote(src, dst, send, recv, device):
        return pltpu.make_async_remote_copy(
            src_ref=src, dst_ref=dst, send_sem=send, recv_sem=recv, device_id=device, device_id_type=MESH)

    def wait_recv(ref, sem):
        remote(ref, ref, sem, sem, (row, col)).wait_recv()

    def wait_send(ref, sem):
        remote(ref, ref, sem, sem, (row, col)).wait_send()

    first = lax.broadcasted_iota(jnp.int32, (32, 128), 1) < HALF
    keep = first == (core == 0)

    def turn(value):
        return pltpu.roll(value, HALF, 1)

    barrier = pltpu.get_barrier_semaphore()

    def signal(device):
        pl.semaphore_signal(barrier, inc=1, device_id=device, device_id_type=MESH)

    signal(sibling)
    for dx, dy in far_places:
        signal(plane_at(dx, dy))
    for dz in far_steps:
        signal(line_at(dz))
        signal(line_mate(dz))

    flatten[...] = jnp.zeros_like(flatten)
    flatten[0:3, 0:32] = pos_ref[...].astype(F32)
    rows3 = flatten[...]
    posrow[core] = rows3[0:1] + pltpu.roll(rows3[1:2], 32, 1) + pltpu.roll(rows3[2:3], 64, 1)
    pl.semaphore_wait(barrier, 30)

    remote(posrow.at[core], posrow.at[core], pos_sem.at[0], pos_sem.at[1], sibling).start()
    remote(z_ref, z_mate, mate_sem.at[0], mate_sem.at[1], sibling).start()
    wait_recv(posrow.at[0], pos_sem.at[1])
    both = jnp.concatenate([posrow[0], posrow[1]], axis=1)
    posbuf[0] = both
    posbuf[PLANE] = both
    for n, spot in enumerate(far_places):
        if n < 7:
            remote(posbuf.at[PLANE], posbuf.at[seen_in_line(far_steps[n])], pos_sem.at[2], pos_sem.at[3],
                   line_at(far_steps[n])).start()
        remote(posbuf.at[0], posbuf.at[seen_in_plane(*spot)], pos_sem.at[2], pos_sem.at[3], plane_at(*spot)).start()
    wait_recv(z_mate, mate_sem.at[1])
    for axis in range(3):
        packed[0, axis] = jnp.where(keep, z_ref[axis], turn(z_mate[axis]))

    def gather(step):
        def to_line(needed):
            for dz in far_steps:
                slot = seen_in_line(dz)
                if (slot - PLANE < NEEDED_LINE) == needed:
                    remote(packed.at[step], ag.at[step, slot], ag_send.at[step],
                           line_sem.at[step, (slot - PLANE) // 4], line_at(dz)).start()

        def to_plane(needed):
            for spot in far_places:
                slot = seen_in_plane(*spot)
                if (slot < NEEDED) == needed:
                    remote(packed.at[step], ag.at[step, slot], ag_send.at[step], plane_sem.at[step, slot // 8],
                           plane_at(*spot)).start()

        last = step == 2
        pl.when(core == 0)(lambda: to_line(True))
        pl.when((core == 0) & jnp.logical_not(last))(lambda: to_line(False))
        pl.when((core == 1) | last)(lambda: to_plane(True))
        pl.when((core == 0) == last)(lambda: to_plane(False))
        pl.when((core == 1) & last)(lambda: to_line(True))
        pl.when((core == 1) & last)(lambda: to_line(False))
        ag[step, 0] = packed[step]
        ag[step, PLANE] = packed[step]

    def wait_line(step, part_of, last=False):
        if part_of == 0:
            wait_recv(ag.at[step, pl.ds(0, 3)], line_sem.at[step, 0])
        else:
            wait_recv(ag.at[step, pl.ds(0, NEEDED_LINE - 4 if last else 4)], line_sem.at[step, 1])

    def wait_plane(step, part_of, last=False):
        if part_of == 0:
            wait_recv(ag.at[step, pl.ds(0, 7)], plane_sem.at[step, 0])
        else:
            wait_recv(ag.at[step, pl.ds(0, NEEDED - 8 if last else 8)], plane_sem.at[step, 1])

    gather(0)
    acc[...] = jnp.zeros_like(acc)
    acc_wide[...] = jnp.zeros_like(acc_wide)
    part[...] = jnp.zeros_like(part)

    @pl.when(core == 0)
    def _():
        ag[2, PLANE + NEEDED_LINE:] = jnp.zeros((LINE - NEEDED_LINE, 3, 32, 128), F32)

    @pl.when(core == 1)
    def _():
        ag[2, NEEDED:PLANE] = jnp.zeros((PLANE - NEEDED, 3, 32, 128), F32)

    for k in range(2):
        red_src[2 * k] = jnp.zeros((1, WIDTH), F32)
    narrow[...] = jnp.zeros_like(narrow)
    wait_recv(posbuf.at[pl.ds(0, 22)], pos_sem.at[3])

    lane_of = lax.broadcasted_iota(jnp.int32, (BLOCK, 128), 1)
    bead_of = lax.broadcasted_iota(jnp.int32, (BLOCK, 128), 0) & 31
    entry_of = lax.broadcasted_iota(jnp.int32, (128, BLOCK), 0)
    column_of = lax.broadcasted_iota(jnp.int32, (128, BLOCK), 1) & 31
    owner_of = lax.broadcasted_iota(jnp.int32, (16, BLOCK), 1) >> 5
    source_of = lax.broadcasted_iota(jnp.int32, (16, BLOCK), 0)
    ones = jnp.ones((128, 128), BF16)

    def place(at, d):
        return posbuf[at + d // 2][:, (d % 2) * 128:(d % 2) * 128 + 128]

    @pl.loop(0, 2)
    def _(h):
        rows_at = jnp.where(core == 0, h, 2) * 8
        lanes_at = jnp.where(core == 0, 2, h) * 8
        spread = jnp.concatenate([jnp.broadcast_to(place(rows_at, d), (32, 128)) for d in range(16)], axis=0)
        flat = jnp.concatenate([place(lanes_at, d) for d in range(16)], axis=0).astype(BF16)
        for axis in range(3):
            own = jnp.where(lane_of == axis * 32 + bead_of, spread, 0.0).astype(BF16)
            colbc[h, axis] = jnp.dot(own, ones, preferred_element_type=F32)
            pick = jnp.where(entry_of == axis * 32 + column_of, 1.0, 0.0).astype(BF16)
            moved = jnp.dot(flat, pick, preferred_element_type=F32)
            lanevec[h, axis:axis + 1, :] = jnp.sum(jnp.where(owner_of == source_of, moved, 0.0), axis=0, keepdims=True)

    def tile_of(t):
        return jnp.where(core == 0, lax.rem(4 - t, 4), 1 - lax.div(t, 2))

    def places(t):
        tile = tile_of(t)
        h = jnp.where(core == 0, lax.div(tile, 2), lax.rem(t, 2))
        rt = jnp.where(core == 0, lax.rem(tile, 2), tile)
        return h, jnp.where(core == 0, 0, h), pl.ds(pl.multiple_of(rt * 256, 256), 256)

    def build(t):
        h, _, span = places(t)

        @pl.loop(0, 16, unroll=2)
        def _(r):
            rows = pl.ds(pl.multiple_of(span.start + r * 16, 16), 16)
            mine = [colbc[h, axis, rows, :] for axis in range(3)]
            for tile in range(4):
                lanes = slice(tile * 128, tile * 128 + 128)
                d = [mine[axis] - lanevec[h, axis:axis + 1, lanes] for axis in range(3)]
                squared = d[0] * d[0] + d[1] * d[1] + d[2] * d[2]
                root = lax.rsqrt(jnp.where(squared > 0.5, squared, 1e30))
                inverse = root * root
                prefactor = (0.75 * RADIUS) * root
                iso = prefactor * (1.0 + (2.0 / 3.0 * RADIUS * RADIUS) * inverse)
                along = (prefactor * inverse) * (1.0 - (2.0 * RADIUS * RADIUS) * inverse)
                s = [along * d[axis] for axis in range(3)]
                parts = (s[0] * d[0] + iso, s[0] * d[1], s[0] * d[2], s[1] * d[1] + iso, s[1] * d[2],
                         s[2] * d[2] + iso)
                for k, value in enumerate(parts):
                    high = value.astype(BF16)
                    at = (tile // 2) * 1536 + k * 256 + (tile % 2) * 128
                    at = slice(at, at + 128)
                    mob_high[h, rows, at] = high
                    mob_low[h, rows, at] = (value - high.astype(F32)).astype(BF16)

    def widen(h):
        base = jnp.where(core == 0, PLANE, h * 8)

        @pl.loop(0, 8)
        def _(s):
            for axis in range(3):
                value = ag[0, base + s, axis]
                other = turn(value)
                for j, both in enumerate((jnp.where(first, value, other), jnp.where(first, other, value))):
                    high = both.astype(BF16).astype(F32)
                    tile = jnp.where(first, high, both - high).astype(BF16)
                    at = pl.ds(pl.multiple_of(s * 64 + j * 32, 32), 32)
                    wide[h, at, axis * 128:axis * 128 + 128] = tile
                    if axis == 0:
                        wide[h, at, 384:512] = tile

    def arrange(step, base, w, quarter, weight):
        @pl.loop(0, 4)
        def _(s):
            values = [ag[step, base + s, axis] * weight(s) for axis in range(3)]
            others = [turn(value) for value in values]
            for j in range(2):
                left, right = (values, others) if j == 0 else (others, values)
                lx, ly, lz = (jnp.where(first, v, 0.0).astype(BF16) for v in left)
                ry, rz = (jnp.where(first, 0.0, v).astype(BF16) for v in right[1:])
                yx = jnp.where(first, left[1], right[0]).astype(BF16)
                for k, half, tile in ((0, 0, lx), (1, 0, yx), (2, 0, lz), (2, 1, lx), (3, 0, ry), (4, 0, rz),
                                      (4, 1, ly), (5, 1, lz)):
                    at = pl.ds(pl.multiple_of(quarter * 1536 + k * 256 + s * 64 + j * 32, 32), 32)
                    narrow[w, at, half * 128:half * 128 + 128] = tile

    def arrange_half(step, part_of):
        @pl.when(core == 0)
        def _():
            if part_of == 0:
                wait_line(step, 0)
            else:
                pl.when(step == 1)(lambda: wait_line(step, 1))
                pl.when(step == 2)(lambda: wait_line(step, 1, True))
            arrange(step, PLANE + 4 * part_of, 0, part_of,
                    lambda s: jnp.where((step == 2) & (4 * part_of + s >= 2), 2.0, 1.0))

        @pl.when(core == 1)
        def _():
            if part_of == 0:
                wait_plane(step, 0)
            else:
                pl.when(step == 1)(lambda: wait_plane(step, 1))
                pl.when(step == 2)(lambda: wait_plane(step, 1, True))

            @pl.loop(0, 2)
            def _(quarter):
                slot = 8 * part_of + 4 * quarter

                @pl.when((step == 1) | (slot < NEEDED))
                def _():
                    arrange(step, slot, part_of, quarter, lambda s: jnp.where((step == 2) & (slot >= 4), 2.0, 1.0))

    def dot(left, right):
        return jnp.dot(left, right, preferred_element_type=F32)

    def product(t):
        h, w, rows = places(t)

        def both(k, lo, hi):
            total = 0.0
            for quarter in range(2):
                at = slice(quarter * 1536 + k * 256, quarter * 1536 + k * 256 + 256)
                right = wide[w, quarter * 256:quarter * 256 + 256, lo:hi]
                total = total + dot(mob_high[h, rows, at], right) + dot(mob_low[h, rows, at], right)
            return total

        xy, yz, zx = both(1, 0, 256), both(4, 128, 384), both(2, 256, 512)
        return (both(0, 0, 128) + xy[:, 128:] + zx[:, :128],
                both(3, 128, 256) + xy[:, :128] + yz[:, 128:],
                both(5, 256, 384) + zx[:, 128:] + yz[:, :128])

    def halves(i, upper):
        return pl.ds(pl.multiple_of(i * 64 + upper * 32, 32), 32)

    def pack(_, i):
        chunk = []
        for axis in range(3):
            low, high = acc[axis, halves(i, 0), :], acc[axis, halves(i, 1), :]
            chunk.append(jnp.where(first, low + turn(low), high + turn(high)))
        return chunk

    def pack_wide(tile, i):
        low, high = halves(i, 0), halves(i, 1)
        xy_low, xy_high = acc_wide[tile, low, :128], acc_wide[tile, high, :128]
        z_low, z_high = acc_wide[tile, low, 128:], acc_wide[tile, high, 128:]
        return (jnp.where(first, xy_low, turn(xy_high)), jnp.where(first, turn(xy_low), xy_high),
                jnp.where(first, z_low, turn(z_high)))

    def scatter(step, t, packer):
        def send_plane(tile):
            for i in (3, 2, 1, 0):
                spot = PLACES[tile * 4 + i]
                for axis, value in enumerate(packer(tile, i)):
                    rs_send[step, tile * 4 + i, axis] = value
                if tile * 4 + i == 0:
                    rs[step, 0] = rs_send[step, 0]
                else:
                    remote(rs_send.at[step, tile * 4 + i], rs.at[step, seen_in_plane(*spot)], rs_sent.at[step],
                           rs_recv.at[step], plane_at(*spot)).start()

        def send_line(tile):
            for i in (3, 2, 1, 0):
                dz = STEPS[tile * 4 + i]
                for axis, value in enumerate(packer(tile, i)):
                    rs_send[step, tile * 4 + i, axis] = value
                if dz == 0:
                    rs[step, 0] = rs_send[step, 0]
                else:
                    remote(rs_send.at[step, tile * 4 + i], rs.at[step, seen_in_line(dz) - PLANE], rs_sent.at[step],
                           rs_recv.at[step], line_at(dz)).start()

        for n in range(4):
            pl.when((core == 0) & (t == n))(functools.partial(send_plane, (4 - n) % 4))
        for n in range(2):
            pl.when((core == 1) & (t == 2 * n + 1))(functools.partial(send_line, 1 - n))

    def collect(step):
        @pl.when(core == 0)
        def _():
            wait_recv(rs.at[step, pl.ds(0, PLANE - 1)], rs_recv.at[step])
            for axis in range(3):
                packed[step + 1, axis] = sum((rs[step, s, axis] for s in range(1, PLANE)), rs[step, 0, axis])

        @pl.when(core == 1)
        def _():
            wait_recv(rs.at[step, pl.ds(0, LINE - 1)], rs_recv.at[step])
            for axis in range(3):
                packed[step + 1, axis] = sum((rs[step, s, axis] for s in range(1, LINE)), rs[step, 0, axis])

    front = lax.broadcasted_iota(jnp.int32, (1, 128), 1) < HALF

    def fold(value):
        line = jnp.sum(value, axis=0, keepdims=True)
        return line + turn(line)

    def inner(left, right):
        return fold(sum(left[axis] * right[axis] for axis in range(3)))

    def reduce_plane(k, values):
        for n, value in values:
            red_src[2 * k, :, n * 128:n * 128 + 128] = value
        for spot in far_places:
            remote(red_src.at[2 * k], red_one.at[k, seen_in_plane(*spot)], red_sem.at[k, 0], red_sem.at[k, 1], plane_at(*spot)).start()
        red_one[k, 0] = red_src[2 * k]

    def reduce_line(k):
        def send(dz, device):
            slot = seen_in_line(dz) - PLANE
            remote(red_src.at[2 * k + 1], red_two.at[k, core, slot], red_sem.at[k, 2], red_sem.at[k, 3], device).start()

        wait_recv(red_one.at[k, pl.ds(0, PLANE - 1)], red_sem.at[k, 1])
        red_src[2 * k + 1] = sum((red_one[k, s] for s in range(1, PLANE)), red_one[k, 0])
        for dz in far_steps:
            send(dz, line_at(dz))
            if k == 1:
                send(dz, line_mate(dz))
        if k == 1:
            send(0, sibling)
        red_two[k, core, 0] = red_src[2 * k + 1]

    def reduced(k, c):
        return sum((red_two[k, c, s] for s in range(1, LINE)), red_two[k, c, 0])

    @pl.loop(0, 2)
    def _(t):
        build(t)

    @pl.when(core == 0)
    def _():
        wait_line(0, 0)
        wait_line(0, 1)

    @pl.when(core == 1)
    def _():
        wait_plane(0, 0)
        wait_plane(0, 1)
        widen(1)

    widen(0)

    @pl.loop(0, 4)
    def _(t):
        @pl.when(t >= 2)
        def _():
            build(t)

        more = (core == 1) & (lax.rem(t, 2) == 1)
        for axis, value in enumerate(product(t)):
            acc[axis] = jnp.where(more, acc[axis], 0.0) + value
        scatter(0, t, pack)

    collect(0)
    gather(1)
    reduce_plane(0, ((0, inner(packed.at[0], packed.at[0])), (1, inner(packed.at[0], packed.at[1]))))

    @pl.loop(1, ITERS)
    def _(step):
        def unit(part_of, t):
            tile = tile_of(t)
            quarter = jnp.where(core == 0, part_of, lax.rem(t, 2))
            h = jnp.where(core == 0, lax.div(tile, 2), part_of)
            w = jnp.where(core == 0, 0, part_of)
            rt = jnp.where(core == 0, lax.rem(tile, 2), tile)
            inner_at = pl.ds(pl.multiple_of(quarter * 1536, 1536), 1536)
            rows = pl.ds(pl.multiple_of(rt * 256, 256), 256)
            return tile, dot(mob_high[h, rows, inner_at], narrow[w, inner_at, :])

        arrange_half(step, 0)

        @pl.loop(0, 4)
        def _(t):
            tile, value = unit(0, t)
            more = (core == 1) & (lax.rem(t, 2) == 1)
            acc_wide[tile] = jnp.where(more, acc_wide[tile], 0.0) + value

        arrange_half(step, 1)

        @pl.loop(0, 4)
        def _(t):
            @pl.when((step == 1) | (core == 0) | (lax.rem(t, 2) == 0))
            def _():
                tile, value = unit(1, t)
                acc_wide[tile] += value

            @pl.when(step == 1)
            def _():
                scatter(1, t, pack_wide)

            @pl.when((step == 2) & (t == 0) & (core == 0))
            def _():
                wait_plane(2, 0)
                wait_plane(2, 1)

            @pl.when((step == 2) & (t == 0) & (core == 1))
            def _():
                wait_line(2, 0)
                wait_line(2, 1)

            @pl.when((step == 2) & ((core == 0) | (lax.rem(t, 2) == 1)))
            def _():
                tile = tile_of(t)
                at = jnp.where(core == 0, 0, PLANE) + tile * 4
                total = jnp.zeros((32, 128), F32)
                for i in range(4):
                    for axis, value in enumerate(pack_wide(tile, i)):
                        total = total + value * ag[2, at + i, axis]
                part[...] += total

        @pl.when(step == 1)
        def _():
            reduce_line(0)
            collect(1)
            wait_recv(red_two.at[0, 0, pl.ds(0, LINE - 1)], red_sem.at[0, 3])
            total = reduced(0, core)
            moments[0] = jnp.broadcast_to(total[:, 128:256] / total[:, 0:128], (32, 128))
            a1 = moments[0]
            for axis in range(3):
                y1 = packed[1, axis]
                packed[2, axis] = packed[2, axis] - a1 * y1
                first_dir[axis] = y1 - a1 * packed[0, axis]
            gather(2)
            remote(first_dir, mate.at[0], mate_sem.at[2], mate_sem.at[3], sibling).start()
            remote(packed.at[2], mate.at[1], mate_sem.at[2], mate_sem.at[3], sibling).start()

    reduce_plane(1, ((0, red_src[0][:, 0:128]), (1, red_src[0][:, 128:256]),
                     (2, inner(first_dir, first_dir)), (3, inner(first_dir, packed.at[2])),
                     (4, inner(packed.at[2], packed.at[2])), (5, fold(part[...]))))
    reduce_line(1)
    wait_recv(red_one.at[1, pl.ds(0, 2 * LINE - 1)], red_sem.at[1, 3])
    low, high = reduced(1, 0), reduced(1, 1)
    for k in range(6):
        at = slice(k * 128, k * 128 + 128)
        moments[k + 1, 0:8] = jnp.broadcast_to(jnp.where(front, low[:, at], high[:, at]), (8, 128))
    moments[7, 0:8] = jnp.zeros((8, 128), F32)
    moments[8, 0:8] = jnp.ones((8, 128), F32)
    m0, m1, e1, f1, g, third, zero, one = (moments[k, 0:8] for k in range(1, 9))

    a1, a2, bb2 = m1 / m0, f1 / e1, e1 / m0
    e2 = g - a2 * f1 - bb2 * e1
    bb3 = e2 / e1
    a3 = (third - a2 * g - bb2 * (f1 + a1 * e1)) / e2 - a2
    d1, d2, d3 = 1.0 + a1, 1.0 + a2, 1.0 + a3
    scale = (d1 + d2 + d3) / ITERS
    current = (d1 / scale, jnp.sqrt(bb2) / scale, zero, d2 / scale, jnp.sqrt(bb3) / scale, d3 / scale)
    partner = (one, zero, zero, one, zero, one)

    def inverse_three(m):
        c00, c01, c02 = m[3] * m[5] - m[4] * m[4], m[2] * m[4] - m[1] * m[5], m[1] * m[4] - m[2] * m[3]
        c11, c12, c22 = m[0] * m[5] - m[2] * m[2], m[1] * m[2] - m[0] * m[4], m[0] * m[3] - m[1] * m[1]
        over = 1.0 / (m[0] * c00 + m[1] * c01 + m[2] * c02)
        return tuple(c * over for c in (c00, c01, c02, c11, c12, c22))

    def newton(_, state):
        now, other = state
        return (tuple(0.5 * (u + v) for u, v in zip(now, inverse_three(other))),
                tuple(0.5 * (u + v) for u, v in zip(other, inverse_three(now))))

    current, partner = lax.fori_loop(0, 20, newton, (current, partner))
    size = jnp.sqrt(scale)
    beta = jnp.sqrt(m0)
    r1, r2, r3 = (current[k] * size for k in range(3))
    f2, f3 = beta * r2 / jnp.sqrt(e1), beta * r3 / jnp.sqrt(e2)
    wait_recv(mate, mate_sem.at[3])
    c0, c1, c2 = (jnp.concatenate([c, c, c, c], axis=0) for c in (r1 - f3 * bb2, f2 - f3 * a2, f3))
    for axis in range(3):
        out_ref[axis] = (c0 * z_ref[axis] + c1 * jnp.where(keep, first_dir[axis], turn(mate[0, axis]))
                         + c2 * jnp.where(keep, packed[2, axis], turn(mate[1, axis])))

    wait_send(posrow.at[0], pos_sem.at[0])
    wait_send(z_mate, mate_sem.at[0])
    wait_send(mate, mate_sem.at[2])
    wait_send(posbuf.at[pl.ds(0, 22)], pos_sem.at[2])
    pl.when(core == 0)(lambda: wait_send(ag.at[2, pl.ds(0, NEEDED_LINE - 1 + PLANE - 1)], ag_send.at[2]))
    pl.when(core == 1)(lambda: wait_send(ag.at[2, pl.ds(0, NEEDED - 1 + LINE - 1)], ag_send.at[2]))
    for k, count in enumerate((LINE - 1, 2 * LINE - 1)):
        wait_send(red_one.at[k, pl.ds(0, PLANE - 1)], red_sem.at[k, 0])
        wait_send(red_one.at[k, pl.ds(0, count)], red_sem.at[k, 2])
    for step in range(2):
        @pl.when(core == 0)
        def _(step=step):
            wait_send(ag.at[step, pl.ds(0, LINE - 1)], ag_send.at[step])
            wait_send(rs_send.at[step, pl.ds(0, PLANE - 1)], rs_sent.at[step])

        @pl.when(core == 1)
        def _(step=step):
            wait_send(ag.at[step, pl.ds(0, PLANE - 1)], ag_send.at[step])
            wait_send(rs_send.at[step, pl.ds(0, LINE - 1)], rs_sent.at[step])


def shards(positions, start_vector):
    chunk = (3, 32, 128)
    return pl.pallas_call(
        kernel,
        out_shape=jax.ShapeDtypeStruct(start_vector.shape, F32),
        in_specs=[pl.BlockSpec(memory_space=pltpu.VMEM)] * 2,
        out_specs=pl.BlockSpec(memory_space=pltpu.VMEM),
        scratch_shapes=[
            pltpu.VMEM((2, 1, 128), F32),
            pltpu.VMEM((PLANE + LINE, 1, 256), F32),
            pltpu.VMEM((2, 3, BLOCK, 128), F32),
            pltpu.VMEM((2, 8, BLOCK), F32),
            pltpu.VMEM((2, BLOCK, 6 * BLOCK), BF16),
            pltpu.VMEM((2, BLOCK, 6 * BLOCK), BF16),
            pltpu.VMEM((2, BLOCK, 512), BF16),
            pltpu.VMEM((2, 6 * BLOCK, 256), BF16),
            pltpu.VMEM((3, PLANE + LINE) + chunk, F32),
            pltpu.VMEM((2, PLANE) + chunk, F32),
            pltpu.VMEM((2, PLANE) + chunk, F32),
            pltpu.VMEM((3,) + chunk, F32),
            pltpu.VMEM(chunk, F32),
            pltpu.VMEM((2,) + chunk, F32),
            pltpu.VMEM((3, 256, 128), F32),
            pltpu.VMEM((4, 256, 256), F32),
            pltpu.VMEM((32, 128), F32),
            pltpu.VMEM((4, 1, WIDTH), F32),
            pltpu.VMEM((2, PLANE, 1, WIDTH), F32),
            pltpu.VMEM((2, 2, LINE, 1, WIDTH), F32),
            pltpu.VMEM((9, 32, 128), F32),
            pltpu.VMEM((8, 128), F32),
            pltpu.VMEM(chunk, F32),
            pltpu.SemaphoreType.DMA((4,)),
            pltpu.SemaphoreType.DMA((4,)),
            pltpu.SemaphoreType.DMA((3, 2)),
            pltpu.SemaphoreType.DMA((3, 2)),
            pltpu.SemaphoreType.DMA((3,)),
            pltpu.SemaphoreType.DMA((2,)),
            pltpu.SemaphoreType.DMA((2,)),
            pltpu.SemaphoreType.DMA((2, 4)),
        ],
        compiler_params=pltpu.CompilerParams(
            collective_id=0, has_side_effects=True, vmem_limit_bytes=40 * 1024 * 1024),
    )(positions, start_vector)


def solution(mesh):
    in_specs = (P(None, ("row", "col")), P(None, ("row", "col"), None))
    out_specs = P(None, ("row", "col"), None)
    return jax.shard_map(shards, mesh=mesh, in_specs=in_specs, out_specs=out_specs, check_vma=False)
```

```python
import functools

import jax
import jax.numpy as jnp
from jax import lax
from jax.experimental import pallas as pl
from jax.experimental.pallas import tpu as pltpu
from jax.sharding import PartitionSpec as P

ITERS = 3
RADIUS = 0.4
MESH = pl.DeviceIdType.MESH
F32 = jnp.float32
BF16 = jnp.bfloat16

PLANE, LINE = 16, 8
PLACES = ((0, 0), (2, 0), (0, 2), (2, 2), (0, 1), (3, 0), (1, 1), (1, 3), (3, 2), (2, 1),
          (0, 3), (1, 0), (3, 3), (3, 1), (1, 2), (2, 3))
NEEDED = 10
ORDER = ((0, 1), (0, 3), (1, 0), (3, 0), (2, 0), (0, 2), (1, 1), (3, 3), (1, 3), (3, 1),
         (1, 2), (2, 1), (3, 2), (2, 3), (2, 2))
STEPS = (0, 1, 7, 2, 6, 3, 5, 4)


def seen_in_plane(dx, dy):
    return PLACES.index((-dx % 4, -dy % 4))


def seen_in_line(dz):
    return PLANE + STEPS.index(-dz % 8)


HALF = 64
BLOCK = 512
WIDTH = 768


def kernel(pos_ref, z_ref, out_ref, posrow, posbuf, colbc, lanevec, mob_high, mob_low, wide, narrow, ag, rs, rs_send,
           packed, first_dir, mate, acc, acc_wide, part, red_src, red_one, red_two, moments, flatten,
           z_mate, mate_sem, pos_sem, line_sem, plane_sem, ag_send, rs_recv, rs_sent, red_sem):
    row, col = lax.axis_index("row"), lax.axis_index("col")
    x, core = lax.div(row, 2), lax.rem(row, 2)
    z, y = lax.div(col, 4), lax.rem(col, 4)

    xs = [lax.rem(x + d, 4) for d in range(4)]
    ys = [lax.rem(y + d, 4) for d in range(4)]
    zs = [lax.rem(z + d, 8) for d in range(8)]

    def plane_at(dx, dy):
        return (xs[dx] * 2 + core, z * 4 + ys[dy])

    far_places, far_steps = PLACES[:0:-1], STEPS[:0:-1]

    def line_at(dz):
        return (row, zs[dz] * 4 + y)

    def line_mate(dz):
        return (x * 2 + 1 - core, zs[dz] * 4 + y)

    sibling = (x * 2 + 1 - core, col)

    def remote(src, dst, send, recv, device):
        return pltpu.make_async_remote_copy(
            src_ref=src, dst_ref=dst, send_sem=send, recv_sem=recv, device_id=device, device_id_type=MESH)

    def wait_recv(ref, sem):
        remote(ref, ref, sem, sem, (row, col)).wait_recv()

    def wait_send(ref, sem):
        remote(ref, ref, sem, sem, (row, col)).wait_send()

    first = lax.broadcasted_iota(jnp.int32, (32, 128), 1) < HALF
    keep = first == (core == 0)

    def turn(value):
        return pltpu.roll(value, HALF, 1)

    barrier = pltpu.get_barrier_semaphore()

    def signal(device):
        pl.semaphore_signal(barrier, inc=1, device_id=device, device_id_type=MESH)

    signal(sibling)
    for dx, dy in far_places:
        signal(plane_at(dx, dy))
    for dz in far_steps:
        signal(line_at(dz))
        signal(line_mate(dz))

    flatten[...] = jnp.zeros_like(flatten)
    flatten[0:3, 0:32] = pos_ref[...].astype(F32)
    rows3 = flatten[...]
    posrow[core] = rows3[0:1] + pltpu.roll(rows3[1:2], 32, 1) + pltpu.roll(rows3[2:3], 64, 1)
    pl.semaphore_wait(barrier, 30)

    remote(posrow.at[core], posrow.at[core], pos_sem.at[0], pos_sem.at[1], sibling).start()
    remote(z_ref, z_mate, mate_sem.at[0], mate_sem.at[1], sibling).start()
    wait_recv(posrow.at[0], pos_sem.at[1])
    both = jnp.concatenate([posrow[0], posrow[1]], axis=1)
    posbuf[0] = both
    posbuf[PLANE] = both
    for n, spot in enumerate(far_places):
        if n < 7:
            remote(posbuf.at[PLANE], posbuf.at[seen_in_line(far_steps[n])], pos_sem.at[2], pos_sem.at[3],
                   line_at(far_steps[n])).start()
        remote(posbuf.at[0], posbuf.at[seen_in_plane(*spot)], pos_sem.at[2], pos_sem.at[3], plane_at(*spot)).start()
    wait_recv(z_mate, mate_sem.at[1])
    for axis in range(3):
        packed[0, axis] = jnp.where(keep, z_ref[axis], turn(z_mate[axis]))

    def gather(step):
        def to_line():
            for dz in STEPS[1:]:
                slot = seen_in_line(dz)
                remote(packed.at[step], ag.at[step, slot], ag_send.at[step], line_sem.at[step, (slot - PLANE) // 4],
                       line_at(dz)).start()

        def to_plane(some):
            for spot in ORDER:
                slot = seen_in_plane(*spot)
                if slot < NEEDED or not some:
                    remote(packed.at[step], ag.at[step, slot], ag_send.at[step], plane_sem.at[step, slot // 8],
                           plane_at(*spot)).start()

        last = step == 2
        pl.when(core == 0)(to_line)
        pl.when(last)(lambda: to_plane(True))
        pl.when((core == 1) & jnp.logical_not(last))(lambda: to_plane(False))
        pl.when((core == 1) & last)(to_line)
        ag[step, 0] = packed[step]
        ag[step, PLANE] = packed[step]

    def wait_line(step, part_of):
        wait_recv(ag.at[step, pl.ds(0, 4 if part_of else 3)], line_sem.at[step, part_of])

    def wait_plane(step, part_of, last=False):
        if part_of == 0:
            wait_recv(ag.at[step, pl.ds(0, 7)], plane_sem.at[step, 0])
        else:
            wait_recv(ag.at[step, pl.ds(0, NEEDED - 8 if last else 8)], plane_sem.at[step, 1])

    gather(0)
    acc[...] = jnp.zeros_like(acc)
    acc_wide[...] = jnp.zeros_like(acc_wide)
    part[...] = jnp.zeros_like(part)
    ag[2, NEEDED:PLANE] = jnp.zeros((PLANE - NEEDED, 3, 32, 128), F32)
    for k in range(2):
        red_src[2 * k] = jnp.zeros((1, WIDTH), F32)
    narrow[...] = jnp.zeros_like(narrow)
    wait_recv(posbuf.at[pl.ds(0, 22)], pos_sem.at[3])

    lane_of = lax.broadcasted_iota(jnp.int32, (BLOCK, 128), 1)
    bead_of = lax.broadcasted_iota(jnp.int32, (BLOCK, 128), 0) & 31
    entry_of = lax.broadcasted_iota(jnp.int32, (128, BLOCK), 0)
    column_of = lax.broadcasted_iota(jnp.int32, (128, BLOCK), 1) & 31
    owner_of = lax.broadcasted_iota(jnp.int32, (16, BLOCK), 1) >> 5
    source_of = lax.broadcasted_iota(jnp.int32, (16, BLOCK), 0)
    ones = jnp.ones((128, 128), BF16)

    def place(at, d):
        return posbuf[at + d // 2][:, (d % 2) * 128:(d % 2) * 128 + 128]

    @pl.loop(0, 2)
    def _(h):
        rows_at = jnp.where(core == 0, h, 2) * 8
        lanes_at = jnp.where(core == 0, 2, h) * 8
        spread = jnp.concatenate([jnp.broadcast_to(place(rows_at, d), (32, 128)) for d in range(16)], axis=0)
        flat = jnp.concatenate([place(lanes_at, d) for d in range(16)], axis=0).astype(BF16)
        for axis in range(3):
            own = jnp.where(lane_of == axis * 32 + bead_of, spread, 0.0).astype(BF16)
            colbc[h, axis] = jnp.dot(own, ones, preferred_element_type=F32)
            pick = jnp.where(entry_of == axis * 32 + column_of, 1.0, 0.0).astype(BF16)
            moved = jnp.dot(flat, pick, preferred_element_type=F32)
            lanevec[h, axis:axis + 1, :] = jnp.sum(jnp.where(owner_of == source_of, moved, 0.0), axis=0, keepdims=True)

    def tile_of(t):
        return jnp.where(core == 0, lax.rem(4 - t, 4), 1 - lax.div(t, 2))

    def places(t):
        tile = tile_of(t)
        h = jnp.where(core == 0, lax.div(tile, 2), lax.rem(t, 2))
        rt = jnp.where(core == 0, lax.rem(tile, 2), tile)
        return h, jnp.where(core == 0, 0, h), pl.ds(pl.multiple_of(rt * 256, 256), 256)

    def build(t):
        h, _, span = places(t)

        @pl.loop(0, 16, unroll=2)
        def _(r):
            rows = pl.ds(pl.multiple_of(span.start + r * 16, 16), 16)
            mine = [colbc[h, axis, rows, :] for axis in range(3)]
            for tile in range(4):
                lanes = slice(tile * 128, tile * 128 + 128)
                d = [mine[axis] - lanevec[h, axis:axis + 1, lanes] for axis in range(3)]
                squared = d[0] * d[0] + d[1] * d[1] + d[2] * d[2]
                root = lax.rsqrt(jnp.where(squared > 0.5, squared, 1e30))
                inverse = root * root
                prefactor = (0.75 * RADIUS) * root
                iso = prefactor * (1.0 + (2.0 / 3.0 * RADIUS * RADIUS) * inverse)
                along = (prefactor * inverse) * (1.0 - (2.0 * RADIUS * RADIUS) * inverse)
                s = [along * d[axis] for axis in range(3)]
                parts = (s[0] * d[0] + iso, s[0] * d[1], s[0] * d[2], s[1] * d[1] + iso, s[1] * d[2],
                         s[2] * d[2] + iso)
                for k, value in enumerate(parts):
                    high = value.astype(BF16)
                    at = (tile // 2) * 1536 + k * 256 + (tile % 2) * 128
                    at = slice(at, at + 128)
                    mob_high[h, rows, at] = high
                    mob_low[h, rows, at] = (value - high.astype(F32)).astype(BF16)

    def widen(h):
        base = jnp.where(core == 0, PLANE, h * 8)

        @pl.loop(0, 8)
        def _(s):
            for axis in range(3):
                value = ag[0, base + s, axis]
                other = turn(value)
                for j, both in enumerate((jnp.where(first, value, other), jnp.where(first, other, value))):
                    high = both.astype(BF16).astype(F32)
                    tile = jnp.where(first, high, both - high).astype(BF16)
                    at = pl.ds(pl.multiple_of(s * 64 + j * 32, 32), 32)
                    wide[h, at, axis * 128:axis * 128 + 128] = tile
                    if axis == 0:
                        wide[h, at, 384:512] = tile

    def arrange(step, base, w, quarter, weight):
        @pl.loop(0, 4)
        def _(s):
            values = [ag[step, base + s, axis] * weight for axis in range(3)]
            others = [turn(value) for value in values]
            for j in range(2):
                left, right = (values, others) if j == 0 else (others, values)
                lx, ly, lz = (jnp.where(first, v, 0.0).astype(BF16) for v in left)
                ry, rz = (jnp.where(first, 0.0, v).astype(BF16) for v in right[1:])
                yx = jnp.where(first, left[1], right[0]).astype(BF16)
                for k, half, tile in ((0, 0, lx), (1, 0, yx), (2, 0, lz), (2, 1, lx), (3, 0, ry), (4, 0, rz),
                                      (4, 1, ly), (5, 1, lz)):
                    at = pl.ds(pl.multiple_of(quarter * 1536 + k * 256 + s * 64 + j * 32, 32), 32)
                    narrow[w, at, half * 128:half * 128 + 128] = tile

    def arrange_half(step, part_of):
        @pl.when(core == 0)
        def _():
            wait_line(step, part_of)
            arrange(step, PLANE + 4 * part_of, 0, part_of, 1.0)

        @pl.when(core == 1)
        def _():
            if part_of == 0:
                wait_plane(step, 0)
            else:
                pl.when(step == 1)(lambda: wait_plane(step, 1))
                pl.when(step == 2)(lambda: wait_plane(step, 1, True))

            @pl.loop(0, 2)
            def _(quarter):
                slot = 8 * part_of + 4 * quarter

                @pl.when((step == 1) | (slot < NEEDED))
                def _():
                    arrange(step, slot, part_of, quarter, jnp.where((step == 2) & (slot >= 4), 2.0, 1.0))

    def dot(left, right):
        return jnp.dot(left, right, preferred_element_type=F32)

    def product(t):
        h, w, rows = places(t)

        def both(k, lo, hi):
            total = 0.0
            for quarter in range(2):
                at = slice(quarter * 1536 + k * 256, quarter * 1536 + k * 256 + 256)
                right = wide[w, quarter * 256:quarter * 256 + 256, lo:hi]
                total = total + dot(mob_high[h, rows, at], right) + dot(mob_low[h, rows, at], right)
            return total

        xy, yz, zx = both(1, 0, 256), both(4, 128, 384), both(2, 256, 512)
        return (both(0, 0, 128) + xy[:, 128:] + zx[:, :128],
                both(3, 128, 256) + xy[:, :128] + yz[:, 128:],
                both(5, 256, 384) + zx[:, 128:] + yz[:, :128])

    def halves(i, upper):
        return pl.ds(pl.multiple_of(i * 64 + upper * 32, 32), 32)

    def pack(_, i):
        chunk = []
        for axis in range(3):
            low, high = acc[axis, halves(i, 0), :], acc[axis, halves(i, 1), :]
            chunk.append(jnp.where(first, low + turn(low), high + turn(high)))
        return chunk

    def pack_wide(tile, i):
        low, high = halves(i, 0), halves(i, 1)
        xy_low, xy_high = acc_wide[tile, low, :128], acc_wide[tile, high, :128]
        z_low, z_high = acc_wide[tile, low, 128:], acc_wide[tile, high, 128:]
        return (jnp.where(first, xy_low, turn(xy_high)), jnp.where(first, turn(xy_low), xy_high),
                jnp.where(first, z_low, turn(z_high)))

    def scatter(step, t, packer):
        def send_plane(tile):
            for i in (3, 2, 1, 0):
                spot = PLACES[tile * 4 + i]
                for axis, value in enumerate(packer(tile, i)):
                    rs_send[step, tile * 4 + i, axis] = value
                if tile * 4 + i == 0:
                    rs[step, 0] = rs_send[step, 0]
                else:
                    remote(rs_send.at[step, tile * 4 + i], rs.at[step, seen_in_plane(*spot)], rs_sent.at[step],
                           rs_recv.at[step], plane_at(*spot)).start()

        def send_line(tile):
            for i in (3, 2, 1, 0):
                dz = STEPS[tile * 4 + i]
                for axis, value in enumerate(packer(tile, i)):
                    rs_send[step, tile * 4 + i, axis] = value
                if dz == 0:
                    rs[step, 0] = rs_send[step, 0]
                else:
                    remote(rs_send.at[step, tile * 4 + i], rs.at[step, seen_in_line(dz) - PLANE], rs_sent.at[step],
                           rs_recv.at[step], line_at(dz)).start()

        for n in range(4):
            pl.when((core == 0) & (t == n))(functools.partial(send_plane, (4 - n) % 4))
        for n in range(2):
            pl.when((core == 1) & (t == 2 * n + 1))(functools.partial(send_line, 1 - n))

    def collect(step):
        @pl.when(core == 0)
        def _():
            wait_recv(rs.at[step, pl.ds(0, PLANE - 1)], rs_recv.at[step])
            for axis in range(3):
                packed[step + 1, axis] = sum((rs[step, s, axis] for s in range(1, PLANE)), rs[step, 0, axis])

        @pl.when(core == 1)
        def _():
            wait_recv(rs.at[step, pl.ds(0, LINE - 1)], rs_recv.at[step])
            for axis in range(3):
                packed[step + 1, axis] = sum((rs[step, s, axis] for s in range(1, LINE)), rs[step, 0, axis])

    front = lax.broadcasted_iota(jnp.int32, (1, 128), 1) < HALF

    def fold(value):
        line = jnp.sum(value, axis=0, keepdims=True)
        return line + turn(line)

    def inner(left, right):
        return fold(sum(left[axis] * right[axis] for axis in range(3)))

    def reduce_plane(k, values):
        for n, value in values:
            red_src[2 * k, :, n * 128:n * 128 + 128] = value
        for spot in far_places:
            remote(red_src.at[2 * k], red_one.at[k, seen_in_plane(*spot)], red_sem.at[k, 0], red_sem.at[k, 1], plane_at(*spot)).start()
        red_one[k, 0] = red_src[2 * k]

    def reduce_line(k):
        def send(dz, device):
            slot = seen_in_line(dz) - PLANE
            remote(red_src.at[2 * k + 1], red_two.at[k, core, slot], red_sem.at[k, 2], red_sem.at[k, 3], device).start()

        wait_recv(red_one.at[k, pl.ds(0, PLANE - 1)], red_sem.at[k, 1])
        red_src[2 * k + 1] = sum((red_one[k, s] for s in range(1, PLANE)), red_one[k, 0])
        for dz in far_steps:
            send(dz, line_at(dz))
            if k == 1:
                send(dz, line_mate(dz))
        if k == 1:
            send(0, sibling)
        red_two[k, core, 0] = red_src[2 * k + 1]

    def reduced(k, c):
        return sum((red_two[k, c, s] for s in range(1, LINE)), red_two[k, c, 0])

    @pl.loop(0, 2)
    def _(t):
        build(t)

    @pl.when(core == 0)
    def _():
        wait_line(0, 0)
        wait_line(0, 1)

    @pl.when(core == 1)
    def _():
        wait_plane(0, 0)
        wait_plane(0, 1)
        widen(1)

    widen(0)

    @pl.loop(0, 4)
    def _(t):
        @pl.when(t >= 2)
        def _():
            build(t)

        more = (core == 1) & (lax.rem(t, 2) == 1)
        for axis, value in enumerate(product(t)):
            acc[axis] = jnp.where(more, acc[axis], 0.0) + value
        scatter(0, t, pack)

    collect(0)
    gather(1)
    reduce_plane(0, ((0, inner(packed.at[0], packed.at[0])), (1, inner(packed.at[0], packed.at[1]))))

    @pl.loop(1, ITERS)
    def _(step):
        def unit(part_of, t):
            tile = tile_of(t)
            quarter = jnp.where(core == 0, part_of, lax.rem(t, 2))
            h = jnp.where(core == 0, lax.div(tile, 2), part_of)
            w = jnp.where(core == 0, 0, part_of)
            rt = jnp.where(core == 0, lax.rem(tile, 2), tile)
            inner_at = pl.ds(pl.multiple_of(quarter * 1536, 1536), 1536)
            rows = pl.ds(pl.multiple_of(rt * 256, 256), 256)
            return tile, dot(mob_high[h, rows, inner_at], narrow[w, inner_at, :])

        arrange_half(step, 0)

        @pl.loop(0, 4)
        def _(t):
            @pl.when((step == 1) | (core == 1) | (t != 1))
            def _():
                tile, value = unit(0, t)
                more = (core == 1) & (lax.rem(t, 2) == 1)
                acc_wide[tile] = jnp.where(more, acc_wide[tile], 0.0) + value

        arrange_half(step, 1)

        @pl.loop(0, 4)
        def _(t):
            @pl.when((step == 1) | jnp.where(core == 1, lax.rem(t, 2) == 0, t != 1))
            def _():
                tile, value = unit(1, t)
                acc_wide[tile] += value

            @pl.when(step == 1)
            def _():
                scatter(1, t, pack_wide)

            @pl.when((step == 2) & (t == 0) & (core == 0))
            def _():
                wait_plane(2, 0)
                wait_plane(2, 1, True)

            @pl.when((step == 2) & (t == 0) & (core == 1))
            def _():
                wait_line(2, 0)
                wait_line(2, 1)

            @pl.when((step == 2) & jnp.where(core == 1, lax.rem(t, 2) == 1, t != 1))
            def _():
                tile = tile_of(t)
                at = jnp.where(core == 0, 0, PLANE) + tile * 4
                total = jnp.zeros((32, 128), F32)
                for i in range(4):
                    for axis, value in enumerate(pack_wide(tile, i)):
                        total = total + value * ag[2, at + i, axis]
                part[...] += total * jnp.where((core == 0) & (tile > 0), 2.0, 1.0)

        @pl.when(step == 1)
        def _():
            reduce_line(0)
            collect(1)
            wait_recv(red_two.at[0, 0, pl.ds(0, LINE - 1)], red_sem.at[0, 3])
            total = reduced(0, core)
            moments[0] = jnp.broadcast_to(total[:, 128:256] / total[:, 0:128], (32, 128))
            a1 = moments[0]
            for axis in range(3):
                y1 = packed[1, axis]
                packed[2, axis] = packed[2, axis] - a1 * y1
                first_dir[axis] = y1 - a1 * packed[0, axis]
            gather(2)
            remote(first_dir, mate.at[0], mate_sem.at[2], mate_sem.at[3], sibling).start()
            remote(packed.at[2], mate.at[1], mate_sem.at[2], mate_sem.at[3], sibling).start()

    reduce_plane(1, ((0, red_src[0][:, 0:128]), (1, red_src[0][:, 128:256]),
                     (2, inner(first_dir, first_dir)), (3, inner(first_dir, packed.at[2])),
                     (4, inner(packed.at[2], packed.at[2])), (5, fold(part[...]))))
    reduce_line(1)
    wait_recv(red_one.at[1, pl.ds(0, 2 * LINE - 1)], red_sem.at[1, 3])
    low, high = reduced(1, 0), reduced(1, 1)
    for k in range(6):
        at = slice(k * 128, k * 128 + 128)
        moments[k + 1, 0:8] = jnp.broadcast_to(jnp.where(front, low[:, at], high[:, at]), (8, 128))
    moments[7, 0:8] = jnp.zeros((8, 128), F32)
    moments[8, 0:8] = jnp.ones((8, 128), F32)
    m0, m1, e1, f1, g, third, zero, one = (moments[k, 0:8] for k in range(1, 9))

    a1, a2, bb2 = m1 / m0, f1 / e1, e1 / m0
    e2 = g - a2 * f1 - bb2 * e1
    bb3 = e2 / e1
    a3 = (third - a2 * g - bb2 * (f1 + a1 * e1)) / e2 - a2
    d1, d2, d3 = 1.0 + a1, 1.0 + a2, 1.0 + a3
    scale = (d1 + d2 + d3) / ITERS
    current = (d1 / scale, jnp.sqrt(bb2) / scale, zero, d2 / scale, jnp.sqrt(bb3) / scale, d3 / scale)
    partner = (one, zero, zero, one, zero, one)

    def inverse_three(m):
        c00, c01, c02 = m[3] * m[5] - m[4] * m[4], m[2] * m[4] - m[1] * m[5], m[1] * m[4] - m[2] * m[3]
        c11, c12, c22 = m[0] * m[5] - m[2] * m[2], m[1] * m[2] - m[0] * m[4], m[0] * m[3] - m[1] * m[1]
        over = 1.0 / (m[0] * c00 + m[1] * c01 + m[2] * c02)
        return tuple(c * over for c in (c00, c01, c02, c11, c12, c22))

    def newton(_, state):
        now, other = state
        return (tuple(0.5 * (u + v) for u, v in zip(now, inverse_three(other))),
                tuple(0.5 * (u + v) for u, v in zip(other, inverse_three(now))))

    current, partner = lax.fori_loop(0, 20, newton, (current, partner))
    size = jnp.sqrt(scale)
    beta = jnp.sqrt(m0)
    r1, r2, r3 = (current[k] * size for k in range(3))
    f2, f3 = beta * r2 / jnp.sqrt(e1), beta * r3 / jnp.sqrt(e2)
    wait_recv(mate, mate_sem.at[3])
    c0, c1, c2 = (jnp.concatenate([c, c, c, c], axis=0) for c in (r1 - f3 * bb2, f2 - f3 * a2, f3))
    for axis in range(3):
        out_ref[axis] = (c0 * z_ref[axis] + c1 * jnp.where(keep, first_dir[axis], turn(mate[0, axis]))
                         + c2 * jnp.where(keep, packed[2, axis], turn(mate[1, axis])))

    wait_send(posrow.at[0], pos_sem.at[0])
    wait_send(z_mate, mate_sem.at[0])
    wait_send(mate, mate_sem.at[2])
    wait_send(posbuf.at[pl.ds(0, 22)], pos_sem.at[2])
    wait_send(ag.at[2, pl.ds(0, NEEDED - 1 + LINE - 1)], ag_send.at[2])
    for k, count in enumerate((LINE - 1, 2 * LINE - 1)):
        wait_send(red_one.at[k, pl.ds(0, PLANE - 1)], red_sem.at[k, 0])
        wait_send(red_one.at[k, pl.ds(0, count)], red_sem.at[k, 2])
    for step in range(2):
        @pl.when(core == 0)
        def _(step=step):
            wait_send(ag.at[step, pl.ds(0, LINE - 1)], ag_send.at[step])
            wait_send(rs_send.at[step, pl.ds(0, PLANE - 1)], rs_sent.at[step])

        @pl.when(core == 1)
        def _(step=step):
            wait_send(ag.at[step, pl.ds(0, PLANE - 1)], ag_send.at[step])
            wait_send(rs_send.at[step, pl.ds(0, LINE - 1)], rs_sent.at[step])


def shards(positions, start_vector):
    chunk = (3, 32, 128)
    return pl.pallas_call(
        kernel,
        out_shape=jax.ShapeDtypeStruct(start_vector.shape, F32),
        in_specs=[pl.BlockSpec(memory_space=pltpu.VMEM)] * 2,
        out_specs=pl.BlockSpec(memory_space=pltpu.VMEM),
        scratch_shapes=[
            pltpu.VMEM((2, 1, 128), F32),
            pltpu.VMEM((PLANE + LINE, 1, 256), F32),
            pltpu.VMEM((2, 3, BLOCK, 128), F32),
            pltpu.VMEM((2, 8, BLOCK), F32),
            pltpu.VMEM((2, BLOCK, 6 * BLOCK), BF16),
            pltpu.VMEM((2, BLOCK, 6 * BLOCK), BF16),
            pltpu.VMEM((2, BLOCK, 512), BF16),
            pltpu.VMEM((2, 6 * BLOCK, 256), BF16),
            pltpu.VMEM((3, PLANE + LINE) + chunk, F32),
            pltpu.VMEM((2, PLANE) + chunk, F32),
            pltpu.VMEM((2, PLANE) + chunk, F32),
            pltpu.VMEM((3,) + chunk, F32),
            pltpu.VMEM(chunk, F32),
            pltpu.VMEM((2,) + chunk, F32),
            pltpu.VMEM((3, 256, 128), F32),
            pltpu.VMEM((4, 256, 256), F32),
            pltpu.VMEM((32, 128), F32),
            pltpu.VMEM((4, 1, WIDTH), F32),
            pltpu.VMEM((2, PLANE, 1, WIDTH), F32),
            pltpu.VMEM((2, 2, LINE, 1, WIDTH), F32),
            pltpu.VMEM((9, 32, 128), F32),
            pltpu.VMEM((8, 128), F32),
            pltpu.VMEM(chunk, F32),
            pltpu.SemaphoreType.DMA((4,)),
            pltpu.SemaphoreType.DMA((4,)),
            pltpu.SemaphoreType.DMA((3, 2)),
            pltpu.SemaphoreType.DMA((3, 2)),
            pltpu.SemaphoreType.DMA((3,)),
            pltpu.SemaphoreType.DMA((2,)),
            pltpu.SemaphoreType.DMA((2,)),
            pltpu.SemaphoreType.DMA((2, 4)),
        ],
        compiler_params=pltpu.CompilerParams(
            collective_id=0, has_side_effects=True, vmem_limit_bytes=40 * 1024 * 1024),
    )(positions, start_vector)


def solution(mesh):
    in_specs = (P(None, ("row", "col")), P(None, ("row", "col"), None))
    out_specs = P(None, ("row", "col"), None)
    return jax.shard_map(shards, mesh=mesh, in_specs=in_specs, out_specs=out_specs, check_vma=False)
```

```python
import functools

import jax
import jax.numpy as jnp
from jax import lax
from jax.experimental import pallas as pl
from jax.experimental.pallas import tpu as pltpu
from jax.sharding import PartitionSpec as P

ITERS = 3
RADIUS = 0.4
MESH = pl.DeviceIdType.MESH
F32 = jnp.float32
BF16 = jnp.bfloat16

PLANE, LINE = 16, 8
PLACES = ((0, 0), (2, 0), (0, 2), (2, 2), (0, 1), (3, 0), (1, 1), (1, 3), (3, 2), (2, 1),
          (0, 3), (1, 0), (3, 3), (3, 1), (1, 2), (2, 3))
NEEDED = 10
ORDER = ((0, 1), (0, 3), (1, 0), (3, 0), (2, 0), (0, 2), (1, 1), (3, 3), (1, 3), (3, 1),
         (1, 2), (2, 1), (3, 2), (2, 3), (2, 2))
STEPS = (0, 4, 3, 6, 1, 5, 2, 7)
NEEDED_LINE = 5
ORDER_LINE = (1, 7, 2, 6, 3, 5, 4)


def seen_in_plane(dx, dy):
    return PLACES.index((-dx % 4, -dy % 4))


def seen_in_line(dz):
    return PLANE + STEPS.index(-dz % 8)


HALF = 64
BLOCK = 512
WIDTH = 768


def kernel(pos_ref, z_ref, out_ref, posrow, posbuf, colbc, lanevec, mob_high, mob_low, wide, narrow, ag, rs, rs_send,
           packed, first_dir, mate, acc, acc_wide, part, red_src, red_one, red_two, moments, flatten,
           z_mate, mate_sem, pos_sem, line_sem, plane_sem, ag_send, rs_recv, rs_sent, red_sem):
    row, col = lax.axis_index("row"), lax.axis_index("col")
    x, core = lax.div(row, 2), lax.rem(row, 2)
    z, y = lax.div(col, 4), lax.rem(col, 4)

    xs = [lax.rem(x + d, 4) for d in range(4)]
    ys = [lax.rem(y + d, 4) for d in range(4)]
    zs = [lax.rem(z + d, 8) for d in range(8)]

    def plane_at(dx, dy):
        return (xs[dx] * 2 + core, z * 4 + ys[dy])

    far_places, far_steps = PLACES[:0:-1], (4, 3, 5, 2, 6, 1, 7)

    def line_at(dz):
        return (row, zs[dz] * 4 + y)

    def line_mate(dz):
        return (x * 2 + 1 - core, zs[dz] * 4 + y)

    sibling = (x * 2 + 1 - core, col)

    def remote(src, dst, send, recv, device):
        return pltpu.make_async_remote_copy(
            src_ref=src, dst_ref=dst, send_sem=send, recv_sem=recv, device_id=device, device_id_type=MESH)

    def wait_recv(ref, sem):
        remote(ref, ref, sem, sem, (row, col)).wait_recv()

    def wait_send(ref, sem):
        remote(ref, ref, sem, sem, (row, col)).wait_send()

    first = lax.broadcasted_iota(jnp.int32, (32, 128), 1) < HALF
    keep = first == (core == 0)

    def turn(value):
        return pltpu.roll(value, HALF, 1)

    barrier = pltpu.get_barrier_semaphore()

    def signal(device):
        pl.semaphore_signal(barrier, inc=1, device_id=device, device_id_type=MESH)

    signal(sibling)
    for dx, dy in far_places:
        signal(plane_at(dx, dy))
    for dz in far_steps:
        signal(line_at(dz))
        signal(line_mate(dz))

    flatten[...] = jnp.zeros_like(flatten)
    flatten[0:3, 0:32] = pos_ref[...].astype(F32)
    rows3 = flatten[...]
    posrow[core] = rows3[0:1] + pltpu.roll(rows3[1:2], 32, 1) + pltpu.roll(rows3[2:3], 64, 1)
    pl.semaphore_wait(barrier, 30)

    remote(posrow.at[core], posrow.at[core], pos_sem.at[0], pos_sem.at[1], sibling).start()
    remote(z_ref, z_mate, mate_sem.at[0], mate_sem.at[1], sibling).start()
    wait_recv(posrow.at[0], pos_sem.at[1])
    both = jnp.concatenate([posrow[0], posrow[1]], axis=1)
    posbuf[0] = both
    posbuf[PLANE] = both
    for n, spot in enumerate(far_places):
        if n < 7:
            remote(posbuf.at[PLANE], posbuf.at[seen_in_line(far_steps[n])], pos_sem.at[2], pos_sem.at[3],
                   line_at(far_steps[n])).start()
        remote(posbuf.at[0], posbuf.at[seen_in_plane(*spot)], pos_sem.at[2], pos_sem.at[3], plane_at(*spot)).start()
    wait_recv(z_mate, mate_sem.at[1])
    for axis in range(3):
        packed[0, axis] = jnp.where(keep, z_ref[axis], turn(z_mate[axis]))

    def gather(step):
        def to_line(needed):
            for dz in ORDER_LINE:
                slot = seen_in_line(dz)
                if slot - PLANE < NEEDED_LINE or not needed:
                    remote(packed.at[step], ag.at[step, slot], ag_send.at[step],
                           line_sem.at[step, (slot - PLANE) // 4], line_at(dz)).start()

        def to_plane(some):
            for spot in ORDER:
                slot = seen_in_plane(*spot)
                if slot < NEEDED or not some:
                    remote(packed.at[step], ag.at[step, slot], ag_send.at[step], plane_sem.at[step, slot // 8],
                           plane_at(*spot)).start()

        last = step == 2
        pl.when((core == 0) & last)(lambda: to_line(True))
        pl.when((core == 0) & jnp.logical_not(last))(lambda: to_line(False))
        pl.when((core == 1) & last)(lambda: to_plane(True))
        pl.when((core == 0) == last)(lambda: to_plane(False))
        pl.when((core == 1) & last)(lambda: to_line(False))
        ag[step, 0] = packed[step]
        ag[step, PLANE] = packed[step]

    def wait_line(step, part_of, last=False):
        if part_of == 0:
            wait_recv(ag.at[step, pl.ds(0, 3)], line_sem.at[step, 0])
        else:
            wait_recv(ag.at[step, pl.ds(0, NEEDED_LINE - 4 if last else 4)], line_sem.at[step, 1])

    def wait_plane(step, part_of, last=False):
        if part_of == 0:
            wait_recv(ag.at[step, pl.ds(0, 7)], plane_sem.at[step, 0])
        else:
            wait_recv(ag.at[step, pl.ds(0, NEEDED - 8 if last else 8)], plane_sem.at[step, 1])

    gather(0)
    acc[...] = jnp.zeros_like(acc)
    acc_wide[...] = jnp.zeros_like(acc_wide)
    part[...] = jnp.zeros_like(part)

    @pl.when(core == 0)
    def _():
        ag[2, PLANE + NEEDED_LINE:] = jnp.zeros((LINE - NEEDED_LINE, 3, 32, 128), F32)

    @pl.when(core == 1)
    def _():
        ag[2, NEEDED:PLANE] = jnp.zeros((PLANE - NEEDED, 3, 32, 128), F32)

    for k in range(2):
        red_src[2 * k] = jnp.zeros((1, WIDTH), F32)
    narrow[...] = jnp.zeros_like(narrow)
    wait_recv(posbuf.at[pl.ds(0, 22)], pos_sem.at[3])

    lane_of = lax.broadcasted_iota(jnp.int32, (BLOCK, 128), 1)
    bead_of = lax.broadcasted_iota(jnp.int32, (BLOCK, 128), 0) & 31
    entry_of = lax.broadcasted_iota(jnp.int32, (128, BLOCK), 0)
    column_of = lax.broadcasted_iota(jnp.int32, (128, BLOCK), 1) & 31
    owner_of = lax.broadcasted_iota(jnp.int32, (16, BLOCK), 1) >> 5
    source_of = lax.broadcasted_iota(jnp.int32, (16, BLOCK), 0)
    ones = jnp.ones((128, 128), BF16)

    def place(at, d):
        return posbuf[at + d // 2][:, (d % 2) * 128:(d % 2) * 128 + 128]

    @pl.loop(0, 2)
    def _(h):
        rows_at = jnp.where(core == 0, h, 2) * 8
        lanes_at = jnp.where(core == 0, 2, h) * 8
        spread = jnp.concatenate([jnp.broadcast_to(place(rows_at, d), (32, 128)) for d in range(16)], axis=0)
        flat = jnp.concatenate([place(lanes_at, d) for d in range(16)], axis=0).astype(BF16)
        for axis in range(3):
            own = jnp.where(lane_of == axis * 32 + bead_of, spread, 0.0).astype(BF16)
            colbc[h, axis] = jnp.dot(own, ones, preferred_element_type=F32)
            pick = jnp.where(entry_of == axis * 32 + column_of, 1.0, 0.0).astype(BF16)
            moved = jnp.dot(flat, pick, preferred_element_type=F32)
            lanevec[h, axis:axis + 1, :] = jnp.sum(jnp.where(owner_of == source_of, moved, 0.0), axis=0, keepdims=True)

    def tile_of(t):
        return jnp.where(core == 0, lax.rem(4 - t, 4), lax.div(t, 2))

    def places(t):
        tile = tile_of(t)
        h = jnp.where(core == 0, lax.div(tile, 2), lax.rem(t, 2))
        rt = jnp.where(core == 0, lax.rem(tile, 2), tile)
        return h, jnp.where(core == 0, 0, h), pl.ds(pl.multiple_of(rt * 256, 256), 256)

    def build(t):
        h, _, span = places(t)

        @pl.loop(0, 16, unroll=2)
        def _(r):
            rows = pl.ds(pl.multiple_of(span.start + r * 16, 16), 16)
            mine = [colbc[h, axis, rows, :] for axis in range(3)]
            for tile in range(4):
                lanes = slice(tile * 128, tile * 128 + 128)
                d = [mine[axis] - lanevec[h, axis:axis + 1, lanes] for axis in range(3)]
                squared = d[0] * d[0] + d[1] * d[1] + d[2] * d[2]
                root = lax.rsqrt(jnp.where(squared > 0.5, squared, 1e30))
                inverse = root * root
                prefactor = (0.75 * RADIUS) * root
                iso = prefactor * (1.0 + (2.0 / 3.0 * RADIUS * RADIUS) * inverse)
                along = (prefactor * inverse) * (1.0 - (2.0 * RADIUS * RADIUS) * inverse)
                s = [along * d[axis] for axis in range(3)]
                parts = (s[0] * d[0] + iso, s[0] * d[1], s[0] * d[2], s[1] * d[1] + iso, s[1] * d[2],
                         s[2] * d[2] + iso)
                for k, value in enumerate(parts):
                    high = value.astype(BF16)
                    at = (tile // 2) * 1536 + k * 256 + (tile % 2) * 128
                    at = slice(at, at + 128)
                    mob_high[h, rows, at] = high
                    mob_low[h, rows, at] = (value - high.astype(F32)).astype(BF16)

    def widen(h):
        base = jnp.where(core == 0, PLANE, h * 8)

        @pl.loop(0, 8)
        def _(s):
            for axis in range(3):
                value = ag[0, base + s, axis]
                other = turn(value)
                for j, both in enumerate((jnp.where(first, value, other), jnp.where(first, other, value))):
                    high = both.astype(BF16).astype(F32)
                    tile = jnp.where(first, high, both - high).astype(BF16)
                    at = pl.ds(pl.multiple_of(s * 64 + j * 32, 32), 32)
                    wide[h, at, axis * 128:axis * 128 + 128] = tile
                    if axis == 0:
                        wide[h, at, 384:512] = tile

    def arrange(step, base, w, quarter, weight):
        @pl.loop(0, 4)
        def _(s):
            values = [ag[step, base + s, axis] * weight(s) for axis in range(3)]
            others = [turn(value) for value in values]
            for j in range(2):
                left, right = (values, others) if j == 0 else (others, values)
                lx, ly, lz = (jnp.where(first, v, 0.0).astype(BF16) for v in left)
                ry, rz = (jnp.where(first, 0.0, v).astype(BF16) for v in right[1:])
                yx = jnp.where(first, left[1], right[0]).astype(BF16)
                for k, half, tile in ((0, 0, lx), (1, 0, yx), (2, 0, lz), (2, 1, lx), (3, 0, ry), (4, 0, rz),
                                      (4, 1, ly), (5, 1, lz)):
                    at = pl.ds(pl.multiple_of(quarter * 1536 + k * 256 + s * 64 + j * 32, 32), 32)
                    narrow[w, at, half * 128:half * 128 + 128] = tile

    def arrange_half(step, part_of):
        @pl.when(core == 0)
        def _():
            if part_of == 0:
                wait_line(step, 0)
            else:
                pl.when(step == 1)(lambda: wait_line(step, 1))
                pl.when(step == 2)(lambda: wait_line(step, 1, True))
            arrange(step, PLANE + 4 * part_of, 0, part_of,
                    lambda s: jnp.where((step == 2) & (4 * part_of + s >= 2), 2.0, 1.0))

        @pl.when(core == 1)
        def _():
            if part_of == 0:
                wait_plane(step, 0)
            else:
                pl.when(step == 1)(lambda: wait_plane(step, 1))
                pl.when(step == 2)(lambda: wait_plane(step, 1, True))

            @pl.loop(0, 2)
            def _(quarter):
                slot = 8 * part_of + 4 * quarter

                @pl.when((step == 1) | (slot < NEEDED))
                def _():
                    arrange(step, slot, part_of, quarter, lambda s: jnp.where((step == 2) & (slot >= 4), 2.0, 1.0))

    def dot(left, right):
        return jnp.dot(left, right, preferred_element_type=F32)

    def product(t):
        h, w, rows = places(t)

        def both(k, lo, hi):
            total = 0.0
            for quarter in range(2):
                at = slice(quarter * 1536 + k * 256, quarter * 1536 + k * 256 + 256)
                right = wide[w, quarter * 256:quarter * 256 + 256, lo:hi]
                total = total + dot(mob_high[h, rows, at], right) + dot(mob_low[h, rows, at], right)
            return total

        xy, yz, zx = both(1, 0, 256), both(4, 128, 384), both(2, 256, 512)
        return (both(0, 0, 128) + xy[:, 128:] + zx[:, :128],
                both(3, 128, 256) + xy[:, :128] + yz[:, 128:],
                both(5, 256, 384) + zx[:, 128:] + yz[:, :128])

    def halves(i, upper):
        return pl.ds(pl.multiple_of(i * 64 + upper * 32, 32), 32)

    def pack(_, i):
        chunk = []
        for axis in range(3):
            low, high = acc[axis, halves(i, 0), :], acc[axis, halves(i, 1), :]
            chunk.append(jnp.where(first, low + turn(low), high + turn(high)))
        return chunk

    def pack_wide(tile, i):
        low, high = halves(i, 0), halves(i, 1)
        xy_low, xy_high = acc_wide[tile, low, :128], acc_wide[tile, high, :128]
        z_low, z_high = acc_wide[tile, low, 128:], acc_wide[tile, high, 128:]
        return (jnp.where(first, xy_low, turn(xy_high)), jnp.where(first, turn(xy_low), xy_high),
                jnp.where(first, z_low, turn(z_high)))

    def scatter(step, t, packer):
        def send_plane(tile):
            for i in (3, 2, 1, 0):
                spot = PLACES[tile * 4 + i]
                for axis, value in enumerate(packer(tile, i)):
                    rs_send[step, tile * 4 + i, axis] = value
                if tile * 4 + i == 0:
                    rs[step, 0] = rs_send[step, 0]
                else:
                    remote(rs_send.at[step, tile * 4 + i], rs.at[step, seen_in_plane(*spot)], rs_sent.at[step],
                           rs_recv.at[step], plane_at(*spot)).start()

        def send_line(tile):
            for i in (1, 2, 3, 0):
                dz = STEPS[tile * 4 + i]
                for axis, value in enumerate(packer(tile, i)):
                    rs_send[step, tile * 4 + i, axis] = value
                if dz == 0:
                    rs[step, 0] = rs_send[step, 0]
                else:
                    remote(rs_send.at[step, tile * 4 + i], rs.at[step, seen_in_line(dz) - PLANE], rs_sent.at[step],
                           rs_recv.at[step], line_at(dz)).start()

        for n in range(4):
            pl.when((core == 0) & (t == n))(functools.partial(send_plane, (4 - n) % 4))
        for n in range(2):
            pl.when((core == 1) & (t == 2 * n + 1))(functools.partial(send_line, n))

    def collect(step):
        @pl.when(core == 0)
        def _():
            wait_recv(rs.at[step, pl.ds(0, PLANE - 1)], rs_recv.at[step])
            for axis in range(3):
                packed[step + 1, axis] = sum((rs[step, s, axis] for s in range(1, PLANE)), rs[step, 0, axis])

        @pl.when(core == 1)
        def _():
            wait_recv(rs.at[step, pl.ds(0, LINE - 1)], rs_recv.at[step])
            for axis in range(3):
                packed[step + 1, axis] = sum((rs[step, s, axis] for s in range(1, LINE)), rs[step, 0, axis])

    front = lax.broadcasted_iota(jnp.int32, (1, 128), 1) < HALF

    def fold(value):
        line = jnp.sum(value, axis=0, keepdims=True)
        return line + turn(line)

    def inner(left, right):
        return fold(sum(left[axis] * right[axis] for axis in range(3)))

    def reduce_plane(k, values):
        for n, value in values:
            red_src[2 * k, :, n * 128:n * 128 + 128] = value
        for spot in far_places:
            remote(red_src.at[2 * k], red_one.at[k, seen_in_plane(*spot)], red_sem.at[k, 0], red_sem.at[k, 1], plane_at(*spot)).start()
        red_one[k, 0] = red_src[2 * k]

    def reduce_line(k):
        def send(dz, device):
            slot = seen_in_line(dz) - PLANE
            remote(red_src.at[2 * k + 1], red_two.at[k, core, slot], red_sem.at[k, 2], red_sem.at[k, 3], device).start()

        wait_recv(red_one.at[k, pl.ds(0, PLANE - 1)], red_sem.at[k, 1])
        red_src[2 * k + 1] = sum((red_one[k, s] for s in range(1, PLANE)), red_one[k, 0])
        for dz in far_steps:
            send(dz, line_at(dz))
            if k == 1:
                send(dz, line_mate(dz))
        if k == 1:
            send(0, sibling)
        red_two[k, core, 0] = red_src[2 * k + 1]

    def reduced(k, c):
        return sum((red_two[k, c, s] for s in range(1, LINE)), red_two[k, c, 0])

    @pl.loop(0, 2)
    def _(t):
        build(t)

    @pl.when(core == 0)
    def _():
        wait_line(0, 0)
        wait_line(0, 1)

    @pl.when(core == 1)
    def _():
        wait_plane(0, 0)
        wait_plane(0, 1)
        widen(1)

    widen(0)

    @pl.loop(0, 4)
    def _(t):
        @pl.when(t >= 2)
        def _():
            build(t)

        more = (core == 1) & (lax.rem(t, 2) == 1)
        for axis, value in enumerate(product(t)):
            acc[axis] = jnp.where(more, acc[axis], 0.0) + value
        scatter(0, t, pack)

    collect(0)
    gather(1)
    reduce_plane(0, ((0, inner(packed.at[0], packed.at[0])), (1, inner(packed.at[0], packed.at[1]))))

    @pl.loop(1, ITERS)
    def _(step):
        def unit(part_of, t):
            tile = tile_of(t)
            quarter = jnp.where(core == 0, part_of, lax.rem(t, 2))
            h = jnp.where(core == 0, lax.div(tile, 2), part_of)
            w = jnp.where(core == 0, 0, part_of)
            rt = jnp.where(core == 0, lax.rem(tile, 2), tile)
            inner_at = pl.ds(pl.multiple_of(quarter * 1536, 1536), 1536)
            rows = pl.ds(pl.multiple_of(rt * 256, 256), 256)
            return tile, dot(mob_high[h, rows, inner_at], narrow[w, inner_at, :])

        arrange_half(step, 0)

        @pl.loop(0, 4)
        def _(t):
            tile, value = unit(0, t)
            more = (core == 1) & (lax.rem(t, 2) == 1)
            acc_wide[tile] = jnp.where(more, acc_wide[tile], 0.0) + value

        arrange_half(step, 1)

        @pl.loop(0, 4)
        def _(t):
            @pl.when((step == 1) | (core == 0) | (lax.rem(t, 2) == 0))
            def _():
                tile, value = unit(1, t)
                acc_wide[tile] += value

            @pl.when(step == 1)
            def _():
                scatter(1, t, pack_wide)

            @pl.when((step == 2) & (t == 0) & (core == 0))
            def _():
                wait_plane(2, 0)
                wait_plane(2, 1)

            @pl.when((step == 2) & (t == 0) & (core == 1))
            def _():
                wait_line(2, 0)
                wait_line(2, 1)

            @pl.when((step == 2) & ((core == 0) | (lax.rem(t, 2) == 1)))
            def _():
                tile = tile_of(t)
                at = jnp.where(core == 0, 0, PLANE) + tile * 4
                total = jnp.zeros((32, 128), F32)
                for i in range(4):
                    for axis, value in enumerate(pack_wide(tile, i)):
                        total = total + value * ag[2, at + i, axis]
                part[...] += total

        @pl.when(step == 1)
        def _():
            reduce_line(0)
            collect(1)
            wait_recv(red_two.at[0, 0, pl.ds(0, LINE - 1)], red_sem.at[0, 3])
            total = reduced(0, core)
            moments[0] = jnp.broadcast_to(total[:, 128:256] / total[:, 0:128], (32, 128))
            a1 = moments[0]
            for axis in range(3):
                y1 = packed[1, axis]
                packed[2, axis] = packed[2, axis] - a1 * y1
                first_dir[axis] = y1 - a1 * packed[0, axis]
            gather(2)
            remote(first_dir, mate.at[0], mate_sem.at[2], mate_sem.at[3], sibling).start()
            remote(packed.at[2], mate.at[1], mate_sem.at[2], mate_sem.at[3], sibling).start()

    reduce_plane(1, ((0, red_src[0][:, 0:128]), (1, red_src[0][:, 128:256]),
                     (2, inner(first_dir, first_dir)), (3, inner(first_dir, packed.at[2])),
                     (4, inner(packed.at[2], packed.at[2])), (5, fold(part[...]))))
    reduce_line(1)
    wait_recv(red_one.at[1, pl.ds(0, 2 * LINE - 1)], red_sem.at[1, 3])
    low, high = reduced(1, 0), reduced(1, 1)
    for k in range(6):
        at = slice(k * 128, k * 128 + 128)
        moments[k + 1, 0:8] = jnp.broadcast_to(jnp.where(front, low[:, at], high[:, at]), (8, 128))
    moments[7, 0:8] = jnp.zeros((8, 128), F32)
    moments[8, 0:8] = jnp.ones((8, 128), F32)
    m0, m1, e1, f1, g, third, zero, one = (moments[k, 0:8] for k in range(1, 9))

    a1, a2, bb2 = m1 / m0, f1 / e1, e1 / m0
    e2 = g - a2 * f1 - bb2 * e1
    bb3 = e2 / e1
    a3 = (third - a2 * g - bb2 * (f1 + a1 * e1)) / e2 - a2
    d1, d2, d3 = 1.0 + a1, 1.0 + a2, 1.0 + a3
    scale = (d1 + d2 + d3) / ITERS
    current = (d1 / scale, jnp.sqrt(bb2) / scale, zero, d2 / scale, jnp.sqrt(bb3) / scale, d3 / scale)
    partner = (one, zero, zero, one, zero, one)

    def inverse_three(m):
        c00, c01, c02 = m[3] * m[5] - m[4] * m[4], m[2] * m[4] - m[1] * m[5], m[1] * m[4] - m[2] * m[3]
        c11, c12, c22 = m[0] * m[5] - m[2] * m[2], m[1] * m[2] - m[0] * m[4], m[0] * m[3] - m[1] * m[1]
        over = 1.0 / (m[0] * c00 + m[1] * c01 + m[2] * c02)
        return tuple(c * over for c in (c00, c01, c02, c11, c12, c22))

    def newton(_, state):
        now, other = state
        return (tuple(0.5 * (u + v) for u, v in zip(now, inverse_three(other))),
                tuple(0.5 * (u + v) for u, v in zip(other, inverse_three(now))))

    current, partner = lax.fori_loop(0, 20, newton, (current, partner))
    size = jnp.sqrt(scale)
    beta = jnp.sqrt(m0)
    r1, r2, r3 = (current[k] * size for k in range(3))
    f2, f3 = beta * r2 / jnp.sqrt(e1), beta * r3 / jnp.sqrt(e2)
    wait_recv(mate, mate_sem.at[3])
    c0, c1, c2 = (jnp.concatenate([c, c, c, c], axis=0) for c in (r1 - f3 * bb2, f2 - f3 * a2, f3))
    for axis in range(3):
        out_ref[axis] = (c0 * z_ref[axis] + c1 * jnp.where(keep, first_dir[axis], turn(mate[0, axis]))
                         + c2 * jnp.where(keep, packed[2, axis], turn(mate[1, axis])))

    wait_send(posrow.at[0], pos_sem.at[0])
    wait_send(z_mate, mate_sem.at[0])
    wait_send(mate, mate_sem.at[2])
    wait_send(posbuf.at[pl.ds(0, 22)], pos_sem.at[2])
    pl.when(core == 0)(lambda: wait_send(ag.at[2, pl.ds(0, NEEDED_LINE - 1 + PLANE - 1)], ag_send.at[2]))
    pl.when(core == 1)(lambda: wait_send(ag.at[2, pl.ds(0, NEEDED - 1 + LINE - 1)], ag_send.at[2]))
    for k, count in enumerate((LINE - 1, 2 * LINE - 1)):
        wait_send(red_one.at[k, pl.ds(0, PLANE - 1)], red_sem.at[k, 0])
        wait_send(red_one.at[k, pl.ds(0, count)], red_sem.at[k, 2])
    for step in range(2):
        @pl.when(core == 0)
        def _(step=step):
            wait_send(ag.at[step, pl.ds(0, LINE - 1)], ag_send.at[step])
            wait_send(rs_send.at[step, pl.ds(0, PLANE - 1)], rs_sent.at[step])

        @pl.when(core == 1)
        def _(step=step):
            wait_send(ag.at[step, pl.ds(0, PLANE - 1)], ag_send.at[step])
            wait_send(rs_send.at[step, pl.ds(0, LINE - 1)], rs_sent.at[step])


def shards(positions, start_vector):
    chunk = (3, 32, 128)
    return pl.pallas_call(
        kernel,
        out_shape=jax.ShapeDtypeStruct(start_vector.shape, F32),
        in_specs=[pl.BlockSpec(memory_space=pltpu.VMEM)] * 2,
        out_specs=pl.BlockSpec(memory_space=pltpu.VMEM),
        scratch_shapes=[
            pltpu.VMEM((2, 1, 128), F32),
            pltpu.VMEM((PLANE + LINE, 1, 256), F32),
            pltpu.VMEM((2, 3, BLOCK, 128), F32),
            pltpu.VMEM((2, 8, BLOCK), F32),
            pltpu.VMEM((2, BLOCK, 6 * BLOCK), BF16),
            pltpu.VMEM((2, BLOCK, 6 * BLOCK), BF16),
            pltpu.VMEM((2, BLOCK, 512), BF16),
            pltpu.VMEM((2, 6 * BLOCK, 256), BF16),
            pltpu.VMEM((3, PLANE + LINE) + chunk, F32),
            pltpu.VMEM((2, PLANE) + chunk, F32),
            pltpu.VMEM((2, PLANE) + chunk, F32),
            pltpu.VMEM((3,) + chunk, F32),
            pltpu.VMEM(chunk, F32),
            pltpu.VMEM((2,) + chunk, F32),
            pltpu.VMEM((3, 256, 128), F32),
            pltpu.VMEM((4, 256, 256), F32),
            pltpu.VMEM((32, 128), F32),
            pltpu.VMEM((4, 1, WIDTH), F32),
            pltpu.VMEM((2, PLANE, 1, WIDTH), F32),
            pltpu.VMEM((2, 2, LINE, 1, WIDTH), F32),
            pltpu.VMEM((9, 32, 128), F32),
            pltpu.VMEM((8, 128), F32),
            pltpu.VMEM(chunk, F32),
            pltpu.SemaphoreType.DMA((4,)),
            pltpu.SemaphoreType.DMA((4,)),
            pltpu.SemaphoreType.DMA((3, 2)),
            pltpu.SemaphoreType.DMA((3, 2)),
            pltpu.SemaphoreType.DMA((3,)),
            pltpu.SemaphoreType.DMA((2,)),
            pltpu.SemaphoreType.DMA((2,)),
            pltpu.SemaphoreType.DMA((2, 4)),
        ],
        compiler_params=pltpu.CompilerParams(
            collective_id=0, has_side_effects=True, vmem_limit_bytes=40 * 1024 * 1024),
    )(positions, start_vector)


def solution(mesh):
    in_specs = (P(None, ("row", "col")), P(None, ("row", "col"), None))
    out_specs = P(None, ("row", "col"), None)
    return jax.shard_map(shards, mesh=mesh, in_specs=in_specs, out_specs=out_specs, check_vma=False)
```

```python
import functools

import jax
import jax.numpy as jnp
from jax import lax
from jax.experimental import pallas as pl
from jax.experimental.pallas import tpu as pltpu
from jax.sharding import PartitionSpec as P

ITERS = 3
RADIUS = 0.4
MESH = pl.DeviceIdType.MESH
F32 = jnp.float32
BF16 = jnp.bfloat16

PLANE, LINE = 16, 8
PLACES = ((0, 0), (0, 1), (3, 0), (1, 1), (2, 0), (0, 2), (3, 1), (2, 1), (3, 2), (2, 2),
          (1, 0), (0, 3), (3, 3), (1, 3), (1, 2), (2, 3))
NEEDED = 10
ORDER = ((0, 1), (0, 3), (1, 0), (3, 0), (2, 0), (0, 2), (1, 1), (3, 3), (1, 3), (3, 1),
         (1, 2), (2, 1), (3, 2), (2, 3), (2, 2))
STEPS = (0, 1, 7, 2, 6, 3, 5, 4)


def weight_of(slot):
    return jnp.where((slot == 0) | (slot == 4) | (slot == 5) | (slot == 9), 1.0, 2.0)


def seen_in_plane(dx, dy):
    return PLACES.index((-dx % 4, -dy % 4))


def seen_in_line(dz):
    return PLANE + STEPS.index(-dz % 8)


HALF = 64
BLOCK = 512
WIDTH = 768


def kernel(pos_ref, z_ref, out_ref, posrow, posbuf, colbc, lanevec, mob_high, mob_low, wide, narrow, ag, rs, rs_send,
           packed, first_dir, mate, acc, acc_wide, part, red_src, red_one, red_two, moments, flatten,
           z_mate, mate_sem, pos_sem, line_sem, plane_sem, ag_send, rs_recv, rs_sent, red_sem):
    row, col = lax.axis_index("row"), lax.axis_index("col")
    x, core = lax.div(row, 2), lax.rem(row, 2)
    z, y = lax.div(col, 4), lax.rem(col, 4)

    xs = [lax.rem(x + d, 4) for d in range(4)]
    ys = [lax.rem(y + d, 4) for d in range(4)]
    zs = [lax.rem(z + d, 8) for d in range(8)]

    def plane_at(dx, dy):
        return (xs[dx] * 2 + core, z * 4 + ys[dy])

    far_places, far_steps = PLACES[:0:-1], STEPS[:0:-1]

    def line_at(dz):
        return (row, zs[dz] * 4 + y)

    def line_mate(dz):
        return (x * 2 + 1 - core, zs[dz] * 4 + y)

    sibling = (x * 2 + 1 - core, col)

    def remote(src, dst, send, recv, device):
        return pltpu.make_async_remote_copy(
            src_ref=src, dst_ref=dst, send_sem=send, recv_sem=recv, device_id=device, device_id_type=MESH)

    def wait_recv(ref, sem):
        remote(ref, ref, sem, sem, (row, col)).wait_recv()

    def wait_send(ref, sem):
        remote(ref, ref, sem, sem, (row, col)).wait_send()

    first = lax.broadcasted_iota(jnp.int32, (32, 128), 1) < HALF
    keep = first == (core == 0)

    def turn(value):
        return pltpu.roll(value, HALF, 1)

    barrier = pltpu.get_barrier_semaphore()

    def signal(device):
        pl.semaphore_signal(barrier, inc=1, device_id=device, device_id_type=MESH)

    signal(sibling)
    for dx, dy in far_places:
        signal(plane_at(dx, dy))
    for dz in far_steps:
        signal(line_at(dz))
        signal(line_mate(dz))

    flatten[...] = jnp.zeros_like(flatten)
    flatten[0:3, 0:32] = pos_ref[...].astype(F32)
    rows3 = flatten[...]
    posrow[core] = rows3[0:1] + pltpu.roll(rows3[1:2], 32, 1) + pltpu.roll(rows3[2:3], 64, 1)
    pl.semaphore_wait(barrier, 30)

    remote(posrow.at[core], posrow.at[core], pos_sem.at[0], pos_sem.at[1], sibling).start()
    remote(z_ref, z_mate, mate_sem.at[0], mate_sem.at[1], sibling).start()
    wait_recv(posrow.at[0], pos_sem.at[1])
    both = jnp.concatenate([posrow[0], posrow[1]], axis=1)
    posbuf[0] = both
    posbuf[PLANE] = both
    for n, spot in enumerate(far_places):
        if n < 7:
            remote(posbuf.at[PLANE], posbuf.at[seen_in_line(far_steps[n])], pos_sem.at[2], pos_sem.at[3],
                   line_at(far_steps[n])).start()
        remote(posbuf.at[0], posbuf.at[seen_in_plane(*spot)], pos_sem.at[2], pos_sem.at[3], plane_at(*spot)).start()
    wait_recv(z_mate, mate_sem.at[1])
    for axis in range(3):
        packed[0, axis] = jnp.where(keep, z_ref[axis], turn(z_mate[axis]))

    def gather(step):
        def to_line():
            for dz in STEPS[1:]:
                slot = seen_in_line(dz)
                remote(packed.at[step], ag.at[step, slot], ag_send.at[step], line_sem.at[step, (slot - PLANE) // 4],
                       line_at(dz)).start()

        def to_plane(some):
            for spot in ORDER:
                slot = seen_in_plane(*spot)
                if slot < NEEDED or not some:
                    remote(packed.at[step], ag.at[step, slot], ag_send.at[step], plane_sem.at[step, slot // 8],
                           plane_at(*spot)).start()

        last = step == 2
        pl.when(core == 0)(to_line)
        pl.when(last)(lambda: to_plane(True))
        pl.when((core == 1) & jnp.logical_not(last))(lambda: to_plane(False))
        pl.when((core == 1) & last)(to_line)
        ag[step, 0] = packed[step]
        ag[step, PLANE] = packed[step]

    def wait_line(step, part_of):
        wait_recv(ag.at[step, pl.ds(0, 4 if part_of else 3)], line_sem.at[step, part_of])

    def wait_plane(step, part_of, last=False):
        if part_of == 0:
            wait_recv(ag.at[step, pl.ds(0, 7)], plane_sem.at[step, 0])
        else:
            wait_recv(ag.at[step, pl.ds(0, NEEDED - 8 if last else 8)], plane_sem.at[step, 1])

    gather(0)
    acc[...] = jnp.zeros_like(acc)
    acc_wide[...] = jnp.zeros_like(acc_wide)
    part[...] = jnp.zeros_like(part)
    ag[2, NEEDED:PLANE] = jnp.zeros((PLANE - NEEDED, 3, 32, 128), F32)
    for k in range(2):
        red_src[2 * k] = jnp.zeros((1, WIDTH), F32)
    narrow[...] = jnp.zeros_like(narrow)
    wait_recv(posbuf.at[pl.ds(0, 22)], pos_sem.at[3])

    lane_of = lax.broadcasted_iota(jnp.int32, (BLOCK, 128), 1)
    bead_of = lax.broadcasted_iota(jnp.int32, (BLOCK, 128), 0) & 31
    entry_of = lax.broadcasted_iota(jnp.int32, (128, BLOCK), 0)
    column_of = lax.broadcasted_iota(jnp.int32, (128, BLOCK), 1) & 31
    owner_of = lax.broadcasted_iota(jnp.int32, (16, BLOCK), 1) >> 5
    source_of = lax.broadcasted_iota(jnp.int32, (16, BLOCK), 0)
    ones = jnp.ones((128, 128), BF16)

    def place(at, d):
        return posbuf[at + d // 2][:, (d % 2) * 128:(d % 2) * 128 + 128]

    @pl.loop(0, 2)
    def _(h):
        rows_at = jnp.where(core == 0, h, 2) * 8
        lanes_at = jnp.where(core == 0, 2, h) * 8
        spread = jnp.concatenate([jnp.broadcast_to(place(rows_at, d), (32, 128)) for d in range(16)], axis=0)
        flat = jnp.concatenate([place(lanes_at, d) for d in range(16)], axis=0).astype(BF16)
        for axis in range(3):
            own = jnp.where(lane_of == axis * 32 + bead_of, spread, 0.0).astype(BF16)
            colbc[h, axis] = jnp.dot(own, ones, preferred_element_type=F32)
            pick = jnp.where(entry_of == axis * 32 + column_of, 1.0, 0.0).astype(BF16)
            moved = jnp.dot(flat, pick, preferred_element_type=F32)
            lanevec[h, axis:axis + 1, :] = jnp.sum(jnp.where(owner_of == source_of, moved, 0.0), axis=0, keepdims=True)

    def tile_of(t):
        return jnp.where(core == 0, jnp.where(t < 2, t + 2, 3 - t), 1 - lax.div(t, 2))

    def places(t):
        tile = tile_of(t)
        h = jnp.where(core == 0, lax.div(tile, 2), lax.rem(t, 2))
        rt = jnp.where(core == 0, lax.rem(tile, 2), tile)
        return h, jnp.where(core == 0, 0, h), pl.ds(pl.multiple_of(rt * 256, 256), 256)

    def build(t):
        h, _, span = places(t)

        @pl.loop(0, 16, unroll=2)
        def _(r):
            rows = pl.ds(pl.multiple_of(span.start + r * 16, 16), 16)
            mine = [colbc[h, axis, rows, :] for axis in range(3)]
            for tile in range(4):
                lanes = slice(tile * 128, tile * 128 + 128)
                d = [mine[axis] - lanevec[h, axis:axis + 1, lanes] for axis in range(3)]
                squared = d[0] * d[0] + d[1] * d[1] + d[2] * d[2]
                root = lax.rsqrt(jnp.where(squared > 0.5, squared, 1e30))
                inverse = root * root
                prefactor = (0.75 * RADIUS) * root
                iso = prefactor * (1.0 + (2.0 / 3.0 * RADIUS * RADIUS) * inverse)
                along = (prefactor * inverse) * (1.0 - (2.0 * RADIUS * RADIUS) * inverse)
                s = [along * d[axis] for axis in range(3)]
                parts = (s[0] * d[0] + iso, s[0] * d[1], s[0] * d[2], s[1] * d[1] + iso, s[1] * d[2],
                         s[2] * d[2] + iso)
                for k, value in enumerate(parts):
                    high = value.astype(BF16)
                    at = (tile // 2) * 1536 + k * 256 + (tile % 2) * 128
                    at = slice(at, at + 128)
                    mob_high[h, rows, at] = high
                    mob_low[h, rows, at] = (value - high.astype(F32)).astype(BF16)

    def widen(h):
        base = jnp.where(core == 0, PLANE, h * 8)

        @pl.loop(0, 8)
        def _(s):
            for axis in range(3):
                value = ag[0, base + s, axis]
                other = turn(value)
                for j, both in enumerate((jnp.where(first, value, other), jnp.where(first, other, value))):
                    high = both.astype(BF16).astype(F32)
                    tile = jnp.where(first, high, both - high).astype(BF16)
                    at = pl.ds(pl.multiple_of(s * 64 + j * 32, 32), 32)
                    wide[h, at, axis * 128:axis * 128 + 128] = tile
                    if axis == 0:
                        wide[h, at, 384:512] = tile

    def arrange(step, base, w, quarter, weight):
        @pl.loop(0, 4)
        def _(s):
            values = [ag[step, base + s, axis] * weight(base + s) for axis in range(3)]
            others = [turn(value) for value in values]
            for j in range(2):
                left, right = (values, others) if j == 0 else (others, values)
                lx, ly, lz = (jnp.where(first, v, 0.0).astype(BF16) for v in left)
                ry, rz = (jnp.where(first, 0.0, v).astype(BF16) for v in right[1:])
                yx = jnp.where(first, left[1], right[0]).astype(BF16)
                for k, half, tile in ((0, 0, lx), (1, 0, yx), (2, 0, lz), (2, 1, lx), (3, 0, ry), (4, 0, rz),
                                      (4, 1, ly), (5, 1, lz)):
                    at = pl.ds(pl.multiple_of(quarter * 1536 + k * 256 + s * 64 + j * 32, 32), 32)
                    narrow[w, at, half * 128:half * 128 + 128] = tile

    def arrange_half(step, part_of):
        @pl.when(core == 0)
        def _():
            wait_line(step, part_of)
            arrange(step, PLANE + 4 * part_of, 0, part_of, lambda slot: 1.0)

        @pl.when(core == 1)
        def _():
            if part_of == 0:
                wait_plane(step, 0)
            else:
                pl.when(step == 1)(lambda: wait_plane(step, 1))
                pl.when(step == 2)(lambda: wait_plane(step, 1, True))

            @pl.loop(0, 2)
            def _(quarter):
                slot = 8 * part_of + 4 * quarter

                @pl.when((step == 1) | (slot < NEEDED))
                def _():
                    arrange(step, slot, part_of, quarter,
                            lambda slot: jnp.where(step == 2, weight_of(slot), 1.0))

    def dot(left, right):
        return jnp.dot(left, right, preferred_element_type=F32)

    def product(t):
        h, w, rows = places(t)

        def both(k, lo, hi):
            total = 0.0
            for quarter in range(2):
                at = slice(quarter * 1536 + k * 256, quarter * 1536 + k * 256 + 256)
                right = wide[w, quarter * 256:quarter * 256 + 256, lo:hi]
                total = total + dot(mob_high[h, rows, at], right) + dot(mob_low[h, rows, at], right)
            return total

        xy, yz, zx = both(1, 0, 256), both(4, 128, 384), both(2, 256, 512)
        return (both(0, 0, 128) + xy[:, 128:] + zx[:, :128],
                both(3, 128, 256) + xy[:, :128] + yz[:, 128:],
                both(5, 256, 384) + zx[:, 128:] + yz[:, :128])

    def halves(i, upper):
        return pl.ds(pl.multiple_of(i * 64 + upper * 32, 32), 32)

    def pack(_, i):
        chunk = []
        for axis in range(3):
            low, high = acc[axis, halves(i, 0), :], acc[axis, halves(i, 1), :]
            chunk.append(jnp.where(first, low + turn(low), high + turn(high)))
        return chunk

    def pack_wide(tile, i):
        low, high = halves(i, 0), halves(i, 1)
        xy_low, xy_high = acc_wide[tile, low, :128], acc_wide[tile, high, :128]
        z_low, z_high = acc_wide[tile, low, 128:], acc_wide[tile, high, 128:]
        return (jnp.where(first, xy_low, turn(xy_high)), jnp.where(first, turn(xy_low), xy_high),
                jnp.where(first, z_low, turn(z_high)))

    def scatter(step, t, packer):
        def send_plane(tile):
            for i in (3, 2, 1, 0):
                spot = PLACES[tile * 4 + i]
                for axis, value in enumerate(packer(tile, i)):
                    rs_send[step, tile * 4 + i, axis] = value
                if tile * 4 + i == 0:
                    rs[step, 0] = rs_send[step, 0]
                else:
                    remote(rs_send.at[step, tile * 4 + i], rs.at[step, seen_in_plane(*spot)], rs_sent.at[step],
                           rs_recv.at[step], plane_at(*spot)).start()

        def send_line(tile):
            for i in (3, 2, 1, 0):
                dz = STEPS[tile * 4 + i]
                for axis, value in enumerate(packer(tile, i)):
                    rs_send[step, tile * 4 + i, axis] = value
                if dz == 0:
                    rs[step, 0] = rs_send[step, 0]
                else:
                    remote(rs_send.at[step, tile * 4 + i], rs.at[step, seen_in_line(dz) - PLANE], rs_sent.at[step],
                           rs_recv.at[step], line_at(dz)).start()

        for n in range(4):
            pl.when((core == 0) & (t == n))(functools.partial(send_plane, (2, 3, 1, 0)[n]))
        for n in range(2):
            pl.when((core == 1) & (t == 2 * n + 1))(functools.partial(send_line, 1 - n))

    def collect(step):
        @pl.when(core == 0)
        def _():
            wait_recv(rs.at[step, pl.ds(0, PLANE - 1)], rs_recv.at[step])
            for axis in range(3):
                packed[step + 1, axis] = sum((rs[step, s, axis] for s in range(1, PLANE)), rs[step, 0, axis])

        @pl.when(core == 1)
        def _():
            wait_recv(rs.at[step, pl.ds(0, LINE - 1)], rs_recv.at[step])
            for axis in range(3):
                packed[step + 1, axis] = sum((rs[step, s, axis] for s in range(1, LINE)), rs[step, 0, axis])

    front = lax.broadcasted_iota(jnp.int32, (1, 128), 1) < HALF

    def fold(value):
        line = jnp.sum(value, axis=0, keepdims=True)
        return line + turn(line)

    def inner(left, right):
        return fold(sum(left[axis] * right[axis] for axis in range(3)))

    def reduce_plane(k, values):
        for n, value in values:
            red_src[2 * k, :, n * 128:n * 128 + 128] = value
        for spot in far_places:
            remote(red_src.at[2 * k], red_one.at[k, seen_in_plane(*spot)], red_sem.at[k, 0], red_sem.at[k, 1], plane_at(*spot)).start()
        red_one[k, 0] = red_src[2 * k]

    def reduce_line(k):
        def send(dz, device):
            slot = seen_in_line(dz) - PLANE
            remote(red_src.at[2 * k + 1], red_two.at[k, core, slot], red_sem.at[k, 2], red_sem.at[k, 3], device).start()

        wait_recv(red_one.at[k, pl.ds(0, PLANE - 1)], red_sem.at[k, 1])
        red_src[2 * k + 1] = sum((red_one[k, s] for s in range(1, PLANE)), red_one[k, 0])
        for dz in far_steps:
            send(dz, line_at(dz))
            if k == 1:
                send(dz, line_mate(dz))
        if k == 1:
            send(0, sibling)
        red_two[k, core, 0] = red_src[2 * k + 1]

    def reduced(k, c):
        return sum((red_two[k, c, s] for s in range(1, LINE)), red_two[k, c, 0])

    @pl.loop(0, 2)
    def _(t):
        build(t)

    @pl.when(core == 0)
    def _():
        wait_line(0, 0)
        wait_line(0, 1)

    @pl.when(core == 1)
    def _():
        wait_plane(0, 0)
        wait_plane(0, 1)
        widen(1)

    widen(0)

    @pl.loop(0, 4)
    def _(t):
        @pl.when(t >= 2)
        def _():
            build(t)

        more = (core == 1) & (lax.rem(t, 2) == 1)
        for axis, value in enumerate(product(t)):
            acc[axis] = jnp.where(more, acc[axis], 0.0) + value
        scatter(0, t, pack)

    collect(0)
    gather(1)
    reduce_plane(0, ((0, inner(packed.at[0], packed.at[0])), (1, inner(packed.at[0], packed.at[1]))))

    @pl.loop(1, ITERS)
    def _(step):
        def unit(part_of, t):
            tile = tile_of(t)
            quarter = jnp.where(core == 0, part_of, lax.rem(t, 2))
            h = jnp.where(core == 0, lax.div(tile, 2), part_of)
            w = jnp.where(core == 0, 0, part_of)
            rt = jnp.where(core == 0, lax.rem(tile, 2), tile)
            inner_at = pl.ds(pl.multiple_of(quarter * 1536, 1536), 1536)
            rows = pl.ds(pl.multiple_of(rt * 256, 256), 256)
            return tile, dot(mob_high[h, rows, inner_at], narrow[w, inner_at, :])

        arrange_half(step, 0)

        @pl.loop(0, 4)
        def _(t):
            @pl.when((step == 1) | (core == 1) | (t != 1))
            def _():
                tile, value = unit(0, t)
                more = (core == 1) & (lax.rem(t, 2) == 1)
                acc_wide[tile] = jnp.where(more, acc_wide[tile], 0.0) + value

        arrange_half(step, 1)

        @pl.loop(0, 4)
        def _(t):
            @pl.when((step == 1) | jnp.where(core == 1, lax.rem(t, 2) == 0, t != 1))
            def _():
                tile, value = unit(1, t)
                acc_wide[tile] += value

            @pl.when(step == 1)
            def _():
                scatter(1, t, pack_wide)

            @pl.when((step == 2) & (t == 0) & (core == 0))
            def _():
                wait_plane(2, 0)
                wait_plane(2, 1, True)

            @pl.when((step == 2) & (t == 0) & (core == 1))
            def _():
                wait_line(2, 0)
                wait_line(2, 1)

            @pl.when((step == 2) & jnp.where(core == 1, lax.rem(t, 2) == 1, t != 1))
            def _():
                tile = tile_of(t)
                at = jnp.where(core == 0, 0, PLANE) + tile * 4
                for i in range(4):
                    total = sum(value * ag[2, at + i, axis] for axis, value in enumerate(pack_wide(tile, i)))
                    part[...] += total * jnp.where(core == 0, weight_of(at + i), 1.0)

        @pl.when(step == 1)
        def _():
            reduce_line(0)
            collect(1)
            wait_recv(red_two.at[0, 0, pl.ds(0, LINE - 1)], red_sem.at[0, 3])
            total = reduced(0, core)
            moments[0] = jnp.broadcast_to(total[:, 128:256] / total[:, 0:128], (32, 128))
            a1 = moments[0]
            for axis in range(3):
                y1 = packed[1, axis]
                packed[2, axis] = packed[2, axis] - a1 * y1
                first_dir[axis] = y1 - a1 * packed[0, axis]
            gather(2)
            remote(first_dir, mate.at[0], mate_sem.at[2], mate_sem.at[3], sibling).start()
            remote(packed.at[2], mate.at[1], mate_sem.at[2], mate_sem.at[3], sibling).start()

    reduce_plane(1, ((0, red_src[0][:, 0:128]), (1, red_src[0][:, 128:256]),
                     (2, inner(first_dir, first_dir)), (3, inner(first_dir, packed.at[2])),
                     (4, inner(packed.at[2], packed.at[2])), (5, fold(part[...]))))
    reduce_line(1)
    wait_recv(red_one.at[1, pl.ds(0, 2 * LINE - 1)], red_sem.at[1, 3])
    low, high = reduced(1, 0), reduced(1, 1)
    for k in range(6):
        at = slice(k * 128, k * 128 + 128)
        moments[k + 1, 0:8] = jnp.broadcast_to(jnp.where(front, low[:, at], high[:, at]), (8, 128))
    moments[7, 0:8] = jnp.zeros((8, 128), F32)
    moments[8, 0:8] = jnp.ones((8, 128), F32)
    m0, m1, e1, f1, g, third, zero, one = (moments[k, 0:8] for k in range(1, 9))

    a1, a2, bb2 = m1 / m0, f1 / e1, e1 / m0
    e2 = g - a2 * f1 - bb2 * e1
    bb3 = e2 / e1
    a3 = (third - a2 * g - bb2 * (f1 + a1 * e1)) / e2 - a2
    d1, d2, d3 = 1.0 + a1, 1.0 + a2, 1.0 + a3
    scale = (d1 + d2 + d3) / ITERS
    current = (d1 / scale, jnp.sqrt(bb2) / scale, zero, d2 / scale, jnp.sqrt(bb3) / scale, d3 / scale)
    partner = (one, zero, zero, one, zero, one)

    def inverse_three(m):
        c00, c01, c02 = m[3] * m[5] - m[4] * m[4], m[2] * m[4] - m[1] * m[5], m[1] * m[4] - m[2] * m[3]
        c11, c12, c22 = m[0] * m[5] - m[2] * m[2], m[1] * m[2] - m[0] * m[4], m[0] * m[3] - m[1] * m[1]
        over = 1.0 / (m[0] * c00 + m[1] * c01 + m[2] * c02)
        return tuple(c * over for c in (c00, c01, c02, c11, c12, c22))

    def newton(_, state):
        now, other = state
        return (tuple(0.5 * (u + v) for u, v in zip(now, inverse_three(other))),
                tuple(0.5 * (u + v) for u, v in zip(other, inverse_three(now))))

    current, partner = lax.fori_loop(0, 20, newton, (current, partner))
    size = jnp.sqrt(scale)
    beta = jnp.sqrt(m0)
    r1, r2, r3 = (current[k] * size for k in range(3))
    f2, f3 = beta * r2 / jnp.sqrt(e1), beta * r3 / jnp.sqrt(e2)
    wait_recv(mate, mate_sem.at[3])
    c0, c1, c2 = (jnp.concatenate([c, c, c, c], axis=0) for c in (r1 - f3 * bb2, f2 - f3 * a2, f3))
    for axis in range(3):
        out_ref[axis] = (c0 * z_ref[axis] + c1 * jnp.where(keep, first_dir[axis], turn(mate[0, axis]))
                         + c2 * jnp.where(keep, packed[2, axis], turn(mate[1, axis])))

    wait_send(posrow.at[0], pos_sem.at[0])
    wait_send(z_mate, mate_sem.at[0])
    wait_send(mate, mate_sem.at[2])
    wait_send(posbuf.at[pl.ds(0, 22)], pos_sem.at[2])
    wait_send(ag.at[2, pl.ds(0, NEEDED - 1 + LINE - 1)], ag_send.at[2])
    for k, count in enumerate((LINE - 1, 2 * LINE - 1)):
        wait_send(red_one.at[k, pl.ds(0, PLANE - 1)], red_sem.at[k, 0])
        wait_send(red_one.at[k, pl.ds(0, count)], red_sem.at[k, 2])
    for step in range(2):
        @pl.when(core == 0)
        def _(step=step):
            wait_send(ag.at[step, pl.ds(0, LINE - 1)], ag_send.at[step])
            wait_send(rs_send.at[step, pl.ds(0, PLANE - 1)], rs_sent.at[step])

        @pl.when(core == 1)
        def _(step=step):
            wait_send(ag.at[step, pl.ds(0, PLANE - 1)], ag_send.at[step])
            wait_send(rs_send.at[step, pl.ds(0, LINE - 1)], rs_sent.at[step])


def shards(positions, start_vector):
    chunk = (3, 32, 128)
    return pl.pallas_call(
        kernel,
        out_shape=jax.ShapeDtypeStruct(start_vector.shape, F32),
        in_specs=[pl.BlockSpec(memory_space=pltpu.VMEM)] * 2,
        out_specs=pl.BlockSpec(memory_space=pltpu.VMEM),
        scratch_shapes=[
            pltpu.VMEM((2, 1, 128), F32),
            pltpu.VMEM((PLANE + LINE, 1, 256), F32),
            pltpu.VMEM((2, 3, BLOCK, 128), F32),
            pltpu.VMEM((2, 8, BLOCK), F32),
            pltpu.VMEM((2, BLOCK, 6 * BLOCK), BF16),
            pltpu.VMEM((2, BLOCK, 6 * BLOCK), BF16),
            pltpu.VMEM((2, BLOCK, 512), BF16),
            pltpu.VMEM((2, 6 * BLOCK, 256), BF16),
            pltpu.VMEM((3, PLANE + LINE) + chunk, F32),
            pltpu.VMEM((2, PLANE) + chunk, F32),
            pltpu.VMEM((2, PLANE) + chunk, F32),
            pltpu.VMEM((3,) + chunk, F32),
            pltpu.VMEM(chunk, F32),
            pltpu.VMEM((2,) + chunk, F32),
            pltpu.VMEM((3, 256, 128), F32),
            pltpu.VMEM((4, 256, 256), F32),
            pltpu.VMEM((32, 128), F32),
            pltpu.VMEM((4, 1, WIDTH), F32),
            pltpu.VMEM((2, PLANE, 1, WIDTH), F32),
            pltpu.VMEM((2, 2, LINE, 1, WIDTH), F32),
            pltpu.VMEM((9, 32, 128), F32),
            pltpu.VMEM((8, 128), F32),
            pltpu.VMEM(chunk, F32),
            pltpu.SemaphoreType.DMA((4,)),
            pltpu.SemaphoreType.DMA((4,)),
            pltpu.SemaphoreType.DMA((3, 2)),
            pltpu.SemaphoreType.DMA((3, 2)),
            pltpu.SemaphoreType.DMA((3,)),
            pltpu.SemaphoreType.DMA((2,)),
            pltpu.SemaphoreType.DMA((2,)),
            pltpu.SemaphoreType.DMA((2, 4)),
        ],
        compiler_params=pltpu.CompilerParams(
            collective_id=0, has_side_effects=True, vmem_limit_bytes=40 * 1024 * 1024),
    )(positions, start_vector)


def solution(mesh):
    in_specs = (P(None, ("row", "col")), P(None, ("row", "col"), None))
    out_specs = P(None, ("row", "col"), None)
    return jax.shard_map(shards, mesh=mesh, in_specs=in_specs, out_specs=out_specs, check_vma=False)
```

```python
import functools

import jax
import jax.numpy as jnp
from jax import lax
from jax.experimental import pallas as pl
from jax.experimental.pallas import tpu as pltpu
from jax.sharding import PartitionSpec as P

ITERS = 3
RADIUS = 0.4
MESH = pl.DeviceIdType.MESH
F32 = jnp.float32
BF16 = jnp.bfloat16

PLANE, LINE = 16, 8
PLACES = ((0, 0), (2, 0), (0, 2), (2, 2), (0, 1), (3, 0), (1, 1), (1, 3), (3, 2), (2, 1),
          (0, 3), (1, 0), (3, 3), (3, 1), (1, 2), (2, 3))
NEEDED = 10
ORDER = ((0, 1), (0, 3), (1, 0), (3, 0), (2, 0), (0, 2), (1, 1), (3, 3), (1, 3), (3, 1),
         (1, 2), (2, 1), (3, 2), (2, 3), (2, 2))
STEPS = (0, 1, 7, 2, 6, 3, 5, 4)


def seen_in_plane(dx, dy):
    return PLACES.index((-dx % 4, -dy % 4))


def seen_in_line(dz):
    return PLANE + STEPS.index(-dz % 8)


HALF = 64
BLOCK = 512
WIDTH = 768


def kernel(pos_ref, z_ref, out_ref, posrow, posbuf, colbc, lanevec, mob_high, mob_low, wide, narrow, ag, rs, rs_send,
           packed, first_dir, mate, acc, acc_wide, part, red_src, red_one, red_two, moments, flatten,
           z_mate, mate_sem, pos_sem, line_sem, plane_sem, ag_send, rs_recv, rs_sent, red_sem):
    row, col = lax.axis_index("row"), lax.axis_index("col")
    x, core = lax.div(row, 2), lax.rem(row, 2)
    z, y = lax.div(col, 4), lax.rem(col, 4)

    xs = [lax.rem(x + d, 4) for d in range(4)]
    ys = [lax.rem(y + d, 4) for d in range(4)]
    zs = [lax.rem(z + d, 8) for d in range(8)]

    def plane_at(dx, dy):
        return (xs[dx] * 2 + core, z * 4 + ys[dy])

    far_places, far_steps = PLACES[:0:-1], STEPS[:0:-1]

    def line_at(dz):
        return (row, zs[dz] * 4 + y)

    def line_mate(dz):
        return (x * 2 + 1 - core, zs[dz] * 4 + y)

    sibling = (x * 2 + 1 - core, col)

    def remote(src, dst, send, recv, device):
        return pltpu.make_async_remote_copy(
            src_ref=src, dst_ref=dst, send_sem=send, recv_sem=recv, device_id=device, device_id_type=MESH)

    def wait_recv(ref, sem):
        remote(ref, ref, sem, sem, (row, col)).wait_recv()

    def wait_send(ref, sem):
        remote(ref, ref, sem, sem, (row, col)).wait_send()

    first = lax.broadcasted_iota(jnp.int32, (32, 128), 1) < HALF
    keep = first == (core == 0)

    def turn(value):
        return pltpu.roll(value, HALF, 1)

    barrier = pltpu.get_barrier_semaphore()

    def signal(device):
        pl.semaphore_signal(barrier, inc=1, device_id=device, device_id_type=MESH)

    signal(sibling)
    for dx, dy in far_places:
        signal(plane_at(dx, dy))
    for dz in far_steps:
        signal(line_at(dz))
        signal(line_mate(dz))

    flatten[...] = jnp.zeros_like(flatten)
    flatten[0:3, 0:32] = pos_ref[...].astype(F32)
    rows3 = flatten[...]
    posrow[core] = rows3[0:1] + pltpu.roll(rows3[1:2], 32, 1) + pltpu.roll(rows3[2:3], 64, 1)
    pl.semaphore_wait(barrier, 30)

    remote(posrow.at[core], posrow.at[core], pos_sem.at[0], pos_sem.at[1], sibling).start()
    remote(z_ref, z_mate, mate_sem.at[0], mate_sem.at[1], sibling).start()
    wait_recv(posrow.at[0], pos_sem.at[1])
    both = jnp.concatenate([posrow[0], posrow[1]], axis=1)
    posbuf[0] = both
    posbuf[PLANE] = both
    for n, spot in enumerate(far_places):
        if n < 7:
            remote(posbuf.at[PLANE], posbuf.at[seen_in_line(far_steps[n])], pos_sem.at[2], pos_sem.at[3],
                   line_at(far_steps[n])).start()
        remote(posbuf.at[0], posbuf.at[seen_in_plane(*spot)], pos_sem.at[2], pos_sem.at[3], plane_at(*spot)).start()
    wait_recv(z_mate, mate_sem.at[1])
    for axis in range(3):
        packed[0, axis] = jnp.where(keep, z_ref[axis], turn(z_mate[axis]))

    def gather(step):
        def to_line():
            for dz in STEPS[1:]:
                slot = seen_in_line(dz)
                remote(packed.at[step], ag.at[step, slot], ag_send.at[step], line_sem.at[step, (slot - PLANE) // 4],
                       line_at(dz)).start()

        def to_plane(some):
            for spot in ORDER:
                slot = seen_in_plane(*spot)
                if slot < NEEDED or not some:
                    remote(packed.at[step], ag.at[step, slot], ag_send.at[step], plane_sem.at[step, slot // 8],
                           plane_at(*spot)).start()

        last = step == 2
        pl.when(core == 0)(to_line)
        pl.when(last)(lambda: to_plane(True))
        pl.when((core == 1) & jnp.logical_not(last))(lambda: to_plane(False))
        pl.when((core == 1) & last)(to_line)
        ag[step, 0] = packed[step]
        ag[step, PLANE] = packed[step]

    def wait_line(step, part_of):
        wait_recv(ag.at[step, pl.ds(0, 4 if part_of else 3)], line_sem.at[step, part_of])

    def wait_plane(step, part_of, last=False):
        if part_of == 0:
            wait_recv(ag.at[step, pl.ds(0, 7)], plane_sem.at[step, 0])
        else:
            wait_recv(ag.at[step, pl.ds(0, NEEDED - 8 if last else 8)], plane_sem.at[step, 1])

    gather(0)
    acc[...] = jnp.zeros_like(acc)
    acc_wide[...] = jnp.zeros_like(acc_wide)
    part[...] = jnp.zeros_like(part)
    ag[2, NEEDED:PLANE] = jnp.zeros((PLANE - NEEDED, 3, 32, 128), F32)
    for k in range(2):
        red_src[2 * k] = jnp.zeros((1, WIDTH), F32)
    narrow[...] = jnp.zeros_like(narrow)
    wait_recv(posbuf.at[pl.ds(0, 22)], pos_sem.at[3])

    lane_of = lax.broadcasted_iota(jnp.int32, (BLOCK, 128), 1)
    bead_of = lax.broadcasted_iota(jnp.int32, (BLOCK, 128), 0) & 31
    entry_of = lax.broadcasted_iota(jnp.int32, (128, BLOCK), 0)
    column_of = lax.broadcasted_iota(jnp.int32, (128, BLOCK), 1) & 31
    owner_of = lax.broadcasted_iota(jnp.int32, (16, BLOCK), 1) >> 5
    source_of = lax.broadcasted_iota(jnp.int32, (16, BLOCK), 0)
    ones = jnp.ones((128, 128), BF16)

    def place(at, d):
        return posbuf[at + d // 2][:, (d % 2) * 128:(d % 2) * 128 + 128]

    @pl.loop(0, 2)
    def _(h):
        rows_at = jnp.where(core == 0, h, 2) * 8
        lanes_at = jnp.where(core == 0, 2, h) * 8
        spread = jnp.concatenate([jnp.broadcast_to(place(rows_at, d), (32, 128)) for d in range(16)], axis=0)
        flat = jnp.concatenate([place(lanes_at, d) for d in range(16)], axis=0).astype(BF16)
        for axis in range(3):
            own = jnp.where(lane_of == axis * 32 + bead_of, spread, 0.0).astype(BF16)
            colbc[h, axis] = jnp.dot(own, ones, preferred_element_type=F32)
            pick = jnp.where(entry_of == axis * 32 + column_of, 1.0, 0.0).astype(BF16)
            moved = jnp.dot(flat, pick, preferred_element_type=F32)
            lanevec[h, axis:axis + 1, :] = jnp.sum(jnp.where(owner_of == source_of, moved, 0.0), axis=0, keepdims=True)

    def tile_of(t):
        return jnp.where(core == 0, lax.rem(4 - t, 4), 1 - lax.div(t, 2))

    def places(t):
        tile = tile_of(t)
        h = jnp.where(core == 0, lax.div(tile, 2), lax.rem(t, 2))
        rt = jnp.where(core == 0, lax.rem(tile, 2), tile)
        return h, jnp.where(core == 0, 0, h), pl.ds(pl.multiple_of(rt * 256, 256), 256)

    def build(t):
        h, _, span = places(t)

        @pl.loop(0, 16, unroll=2)
        def _(r):
            rows = pl.ds(pl.multiple_of(span.start + r * 16, 16), 16)
            mine = [colbc[h, axis, rows, :] for axis in range(3)]
            for tile in range(4):
                lanes = slice(tile * 128, tile * 128 + 128)
                d = [mine[axis] - lanevec[h, axis:axis + 1, lanes] for axis in range(3)]
                squared = d[0] * d[0] + d[1] * d[1] + d[2] * d[2]
                root = lax.rsqrt(jnp.where(squared > 0.5, squared, 1e30))
                inverse = root * root
                prefactor = (0.75 * RADIUS) * root
                iso = prefactor * (1.0 + (2.0 / 3.0 * RADIUS * RADIUS) * inverse)
                along = (prefactor * inverse) * (1.0 - (2.0 * RADIUS * RADIUS) * inverse)
                s = [along * d[axis] for axis in range(3)]
                parts = (s[0] * d[0] + iso, s[0] * d[1], s[0] * d[2], s[1] * d[1] + iso, s[1] * d[2],
                         s[2] * d[2] + iso)
                for k, value in enumerate(parts):
                    high = value.astype(BF16)
                    at = (tile // 2) * 1536 + k * 256 + (tile % 2) * 128
                    at = slice(at, at + 128)
                    mob_high[h, rows, at] = high
                    mob_low[h, rows, at] = (value - high.astype(F32)).astype(BF16)

    def widen(h):
        base = jnp.where(core == 0, PLANE, h * 8)

        @pl.loop(0, 8, unroll=4)
        def _(s):
            for axis in range(3):
                value = ag[0, base + s, axis]
                other = turn(value)
                for j, both in enumerate((jnp.where(first, value, other), jnp.where(first, other, value))):
                    high = both.astype(BF16).astype(F32)
                    tile = jnp.where(first, high, both - high).astype(BF16)
                    at = pl.ds(pl.multiple_of(s * 64 + j * 32, 32), 32)
                    wide[h, at, axis * 128:axis * 128 + 128] = tile
                    if axis == 0:
                        wide[h, at, 384:512] = tile

    def arrange(step, base, w, quarter, weight):
        @pl.loop(0, 4, unroll=4)
        def _(s):
            values = [ag[step, base + s, axis] * weight for axis in range(3)]
            others = [turn(value) for value in values]
            for j in range(2):
                left, right = (values, others) if j == 0 else (others, values)
                lx, ly, lz = (jnp.where(first, v, 0.0).astype(BF16) for v in left)
                ry, rz = (jnp.where(first, 0.0, v).astype(BF16) for v in right[1:])
                yx = jnp.where(first, left[1], right[0]).astype(BF16)
                for k, half, tile in ((0, 0, lx), (1, 0, yx), (2, 0, lz), (2, 1, lx), (3, 0, ry), (4, 0, rz),
                                      (4, 1, ly), (5, 1, lz)):
                    at = pl.ds(pl.multiple_of(quarter * 1536 + k * 256 + s * 64 + j * 32, 32), 32)
                    narrow[w, at, half * 128:half * 128 + 128] = tile

    def arrange_half(step, part_of):
        @pl.when(core == 0)
        def _():
            wait_line(step, part_of)
            arrange(step, PLANE + 4 * part_of, 0, part_of, 1.0)

        @pl.when(core == 1)
        def _():
            if part_of == 0:
                wait_plane(step, 0)
            else:
                pl.when(step == 1)(lambda: wait_plane(step, 1))
                pl.when(step == 2)(lambda: wait_plane(step, 1, True))

            @pl.loop(0, 2)
            def _(quarter):
                slot = 8 * part_of + 4 * quarter

                @pl.when((step == 1) | (slot < NEEDED))
                def _():
                    arrange(step, slot, part_of, quarter, jnp.where((step == 2) & (slot >= 4), 2.0, 1.0))

    def dot(left, right):
        return jnp.dot(left, right, preferred_element_type=F32)

    def product(t):
        h, w, rows = places(t)

        def both(k, lo, hi):
            total = 0.0
            for quarter in range(2):
                at = slice(quarter * 1536 + k * 256, quarter * 1536 + k * 256 + 256)
                right = wide[w, quarter * 256:quarter * 256 + 256, lo:hi]
                total = total + dot(mob_high[h, rows, at], right) + dot(mob_low[h, rows, at], right)
            return total

        xy, yz, zx = both(1, 0, 256), both(4, 128, 384), both(2, 256, 512)
        return (both(0, 0, 128) + xy[:, 128:] + zx[:, :128],
                both(3, 128, 256) + xy[:, :128] + yz[:, 128:],
                both(5, 256, 384) + zx[:, 128:] + yz[:, :128])

    def halves(i, upper):
        return pl.ds(pl.multiple_of(i * 64 + upper * 32, 32), 32)

    def pack(_, i):
        chunk = []
        for axis in range(3):
            low, high = acc[axis, halves(i, 0), :], acc[axis, halves(i, 1), :]
            chunk.append(jnp.where(first, low + turn(low), high + turn(high)))
        return chunk

    def pack_wide(tile, i):
        low, high = halves(i, 0), halves(i, 1)
        xy_low, xy_high = acc_wide[tile, low, :128], acc_wide[tile, high, :128]
        z_low, z_high = acc_wide[tile, low, 128:], acc_wide[tile, high, 128:]
        return (jnp.where(first, xy_low, turn(xy_high)), jnp.where(first, turn(xy_low), xy_high),
                jnp.where(first, z_low, turn(z_high)))

    def scatter(step, t, packer):
        def fill(tile):
            chunks = [packer(tile, i) for i in range(4)]
            for i, chunk in enumerate(chunks):
                for axis, value in enumerate(chunk):
                    rs_send[step, tile * 4 + i, axis] = value

        def send_plane(tile):
            fill(tile)
            for i in (3, 2, 1, 0):
                spot = PLACES[tile * 4 + i]
                if tile * 4 + i:
                    remote(rs_send.at[step, tile * 4 + i], rs.at[step, seen_in_plane(*spot)], rs_sent.at[step],
                           rs_recv.at[step], plane_at(*spot)).start()
                else:
                    rs[step, 0] = rs_send[step, 0]

        def send_line(tile):
            fill(tile)
            for i in (3, 2, 1, 0):
                dz = STEPS[tile * 4 + i]
                if dz:
                    remote(rs_send.at[step, tile * 4 + i], rs.at[step, seen_in_line(dz) - PLANE], rs_sent.at[step],
                           rs_recv.at[step], line_at(dz)).start()
                else:
                    rs[step, 0] = rs_send[step, 0]

        for n in range(4):
            pl.when((core == 0) & (t == n))(functools.partial(send_plane, (4 - n) % 4))
        for n in range(2):
            pl.when((core == 1) & (t == 2 * n + 1))(functools.partial(send_line, 1 - n))

    def collect(step):
        @pl.when(core == 0)
        def _():
            wait_recv(rs.at[step, pl.ds(0, PLANE - 1)], rs_recv.at[step])
            for axis in range(3):
                packed[step + 1, axis] = sum((rs[step, s, axis] for s in range(1, PLANE)), rs[step, 0, axis])

        @pl.when(core == 1)
        def _():
            wait_recv(rs.at[step, pl.ds(0, LINE - 1)], rs_recv.at[step])
            for axis in range(3):
                packed[step + 1, axis] = sum((rs[step, s, axis] for s in range(1, LINE)), rs[step, 0, axis])

    front = lax.broadcasted_iota(jnp.int32, (1, 128), 1) < HALF

    def fold(value):
        line = jnp.sum(value, axis=0, keepdims=True)
        return line + turn(line)

    def inner(left, right):
        return fold(sum(left[axis] * right[axis] for axis in range(3)))

    def reduce_plane(k, values):
        for n, value in values:
            red_src[2 * k, :, n * 128:n * 128 + 128] = value
        for spot in far_places:
            remote(red_src.at[2 * k], red_one.at[k, seen_in_plane(*spot)], red_sem.at[k, 0], red_sem.at[k, 1], plane_at(*spot)).start()
        red_one[k, 0] = red_src[2 * k]

    def reduce_line(k):
        def send(dz, device):
            slot = seen_in_line(dz) - PLANE
            remote(red_src.at[2 * k + 1], red_two.at[k, core, slot], red_sem.at[k, 2], red_sem.at[k, 3], device).start()

        wait_recv(red_one.at[k, pl.ds(0, PLANE - 1)], red_sem.at[k, 1])
        red_src[2 * k + 1] = sum((red_one[k, s] for s in range(1, PLANE)), red_one[k, 0])
        for dz in far_steps:
            send(dz, line_at(dz))
            if k == 1:
                send(dz, line_mate(dz))
        if k == 1:
            send(0, sibling)
        red_two[k, core, 0] = red_src[2 * k + 1]

    def reduced(k, c):
        return sum((red_two[k, c, s] for s in range(1, LINE)), red_two[k, c, 0])

    @pl.loop(0, 2)
    def _(t):
        build(t)

    @pl.when(core == 0)
    def _():
        wait_line(0, 0)
        wait_line(0, 1)

    @pl.when(core == 1)
    def _():
        wait_plane(0, 0)
        wait_plane(0, 1)
        widen(1)

    widen(0)

    @pl.loop(0, 4)
    def _(t):
        @pl.when(t >= 2)
        def _():
            build(t)

        more = (core == 1) & (lax.rem(t, 2) == 1)
        for axis, value in enumerate(product(t)):
            acc[axis] = jnp.where(more, acc[axis], 0.0) + value
        scatter(0, t, pack)

    collect(0)
    gather(1)
    reduce_plane(0, ((0, inner(packed.at[0], packed.at[0])), (1, inner(packed.at[0], packed.at[1]))))

    @pl.loop(1, ITERS)
    def _(step):
        def unit(part_of, t):
            tile = tile_of(t)
            quarter = jnp.where(core == 0, part_of, lax.rem(t, 2))
            h = jnp.where(core == 0, lax.div(tile, 2), part_of)
            w = jnp.where(core == 0, 0, part_of)
            rt = jnp.where(core == 0, lax.rem(tile, 2), tile)
            inner_at = pl.ds(pl.multiple_of(quarter * 1536, 1536), 1536)
            rows = pl.ds(pl.multiple_of(rt * 256, 256), 256)
            return tile, dot(mob_high[h, rows, inner_at], narrow[w, inner_at, :])

        arrange_half(step, 0)

        @pl.loop(0, 4)
        def _(t):
            @pl.when((step == 1) | (core == 1) | (t != 1))
            def _():
                tile, value = unit(0, t)
                more = (core == 1) & (lax.rem(t, 2) == 1)
                acc_wide[tile] = jnp.where(more, acc_wide[tile], 0.0) + value

        arrange_half(step, 1)

        @pl.loop(0, 4)
        def _(t):
            @pl.when((step == 1) | jnp.where(core == 1, lax.rem(t, 2) == 0, t != 1))
            def _():
                tile, value = unit(1, t)
                acc_wide[tile] += value

            @pl.when(step == 1)
            def _():
                scatter(1, t, pack_wide)

            @pl.when((step == 2) & (t == 0) & (core == 0))
            def _():
                wait_plane(2, 0)
                wait_plane(2, 1, True)

            @pl.when((step == 2) & (t == 0) & (core == 1))
            def _():
                wait_line(2, 0)
                wait_line(2, 1)

            @pl.when((step == 2) & jnp.where(core == 1, lax.rem(t, 2) == 1, t != 1))
            def _():
                tile = tile_of(t)
                at = jnp.where(core == 0, 0, PLANE) + tile * 4
                total = jnp.zeros((32, 128), F32)
                for i in range(4):
                    for axis, value in enumerate(pack_wide(tile, i)):
                        total = total + value * ag[2, at + i, axis]
                part[...] += total * jnp.where((core == 0) & (tile > 0), 2.0, 1.0)

        @pl.when(step == 1)
        def _():
            reduce_line(0)
            collect(1)
            wait_recv(red_two.at[0, 0, pl.ds(0, LINE - 1)], red_sem.at[0, 3])
            total = reduced(0, core)
            moments[0] = jnp.broadcast_to(total[:, 128:256] / total[:, 0:128], (32, 128))
            a1 = moments[0]
            for axis in range(3):
                y1 = packed[1, axis]
                packed[2, axis] = packed[2, axis] - a1 * y1
                first_dir[axis] = y1 - a1 * packed[0, axis]
            gather(2)
            remote(first_dir, mate.at[0], mate_sem.at[2], mate_sem.at[3], sibling).start()
            remote(packed.at[2], mate.at[1], mate_sem.at[2], mate_sem.at[3], sibling).start()
            early = (red_src[0][:, 0:128], red_src[0][:, 128:256], inner(first_dir, first_dir),
                     inner(first_dir, packed.at[2]), inner(packed.at[2], packed.at[2]))
            for n, value in enumerate(early):
                red_src[2, :, n * 128:n * 128 + 128] = value

    reduce_plane(1, ((5, fold(part[...])),))
    reduce_line(1)
    wait_recv(red_one.at[1, pl.ds(0, 2 * LINE - 1)], red_sem.at[1, 3])
    low, high = reduced(1, 0), reduced(1, 1)
    for k in range(6):
        at = slice(k * 128, k * 128 + 128)
        moments[k + 1, 0:8] = jnp.broadcast_to(jnp.where(front, low[:, at], high[:, at]), (8, 128))
    moments[7, 0:8] = jnp.zeros((8, 128), F32)
    moments[8, 0:8] = jnp.ones((8, 128), F32)
    m0, m1, e1, f1, g, third, zero, one = (moments[k, 0:8] for k in range(1, 9))

    a1, a2, bb2 = m1 / m0, f1 / e1, e1 / m0
    e2 = g - a2 * f1 - bb2 * e1
    bb3 = e2 / e1
    a3 = (third - a2 * g - bb2 * (f1 + a1 * e1)) / e2 - a2
    d1, d2, d3 = 1.0 + a1, 1.0 + a2, 1.0 + a3
    scale = (d1 + d2 + d3) / ITERS
    current = (d1 / scale, jnp.sqrt(bb2) / scale, zero, d2 / scale, jnp.sqrt(bb3) / scale, d3 / scale)
    partner = (one, zero, zero, one, zero, one)

    def inverse_three(m):
        c00, c01, c02 = m[3] * m[5] - m[4] * m[4], m[2] * m[4] - m[1] * m[5], m[1] * m[4] - m[2] * m[3]
        c11, c12, c22 = m[0] * m[5] - m[2] * m[2], m[1] * m[2] - m[0] * m[4], m[0] * m[3] - m[1] * m[1]
        over = 1.0 / (m[0] * c00 + m[1] * c01 + m[2] * c02)
        return tuple(c * over for c in (c00, c01, c02, c11, c12, c22))

    def newton(_, state):
        now, other = state
        return (tuple(0.5 * (u + v) for u, v in zip(now, inverse_three(other))),
                tuple(0.5 * (u + v) for u, v in zip(other, inverse_three(now))))

    current, partner = lax.fori_loop(0, 20, newton, (current, partner))
    size = jnp.sqrt(scale)
    beta = jnp.sqrt(m0)
    r1, r2, r3 = (current[k] * size for k in range(3))
    f2, f3 = beta * r2 / jnp.sqrt(e1), beta * r3 / jnp.sqrt(e2)
    wait_recv(mate, mate_sem.at[3])
    c0, c1, c2 = (jnp.concatenate([c, c, c, c], axis=0) for c in (r1 - f3 * bb2, f2 - f3 * a2, f3))
    for axis in range(3):
        out_ref[axis] = (c0 * z_ref[axis] + c1 * jnp.where(keep, first_dir[axis], turn(mate[0, axis]))
                         + c2 * jnp.where(keep, packed[2, axis], turn(mate[1, axis])))

    wait_send(posrow.at[0], pos_sem.at[0])
    wait_send(z_mate, mate_sem.at[0])
    wait_send(mate, mate_sem.at[2])
    wait_send(posbuf.at[pl.ds(0, 22)], pos_sem.at[2])
    wait_send(ag.at[2, pl.ds(0, NEEDED - 1 + LINE - 1)], ag_send.at[2])
    for k, count in enumerate((LINE - 1, 2 * LINE - 1)):
        wait_send(red_one.at[k, pl.ds(0, PLANE - 1)], red_sem.at[k, 0])
        wait_send(red_one.at[k, pl.ds(0, count)], red_sem.at[k, 2])
    for step in range(2):
        @pl.when(core == 0)
        def _(step=step):
            wait_send(ag.at[step, pl.ds(0, LINE - 1)], ag_send.at[step])
            wait_send(rs_send.at[step, pl.ds(0, PLANE - 1)], rs_sent.at[step])

        @pl.when(core == 1)
        def _(step=step):
            wait_send(ag.at[step, pl.ds(0, PLANE - 1)], ag_send.at[step])
            wait_send(rs_send.at[step, pl.ds(0, LINE - 1)], rs_sent.at[step])


def shards(positions, start_vector):
    chunk = (3, 32, 128)
    return pl.pallas_call(
        kernel,
        out_shape=jax.ShapeDtypeStruct(start_vector.shape, F32),
        in_specs=[pl.BlockSpec(memory_space=pltpu.VMEM)] * 2,
        out_specs=pl.BlockSpec(memory_space=pltpu.VMEM),
        scratch_shapes=[
            pltpu.VMEM((2, 1, 128), F32),
            pltpu.VMEM((PLANE + LINE, 1, 256), F32),
            pltpu.VMEM((2, 3, BLOCK, 128), F32),
            pltpu.VMEM((2, 8, BLOCK), F32),
            pltpu.VMEM((2, BLOCK, 6 * BLOCK), BF16),
            pltpu.VMEM((2, BLOCK, 6 * BLOCK), BF16),
            pltpu.VMEM((2, BLOCK, 512), BF16),
            pltpu.VMEM((2, 6 * BLOCK, 256), BF16),
            pltpu.VMEM((3, PLANE + LINE) + chunk, F32),
            pltpu.VMEM((2, PLANE) + chunk, F32),
            pltpu.VMEM((2, PLANE) + chunk, F32),
            pltpu.VMEM((3,) + chunk, F32),
            pltpu.VMEM(chunk, F32),
            pltpu.VMEM((2,) + chunk, F32),
            pltpu.VMEM((3, 256, 128), F32),
            pltpu.VMEM((4, 256, 256), F32),
            pltpu.VMEM((32, 128), F32),
            pltpu.VMEM((4, 1, WIDTH), F32),
            pltpu.VMEM((2, PLANE, 1, WIDTH), F32),
            pltpu.VMEM((2, 2, LINE, 1, WIDTH), F32),
            pltpu.VMEM((9, 32, 128), F32),
            pltpu.VMEM((8, 128), F32),
            pltpu.VMEM(chunk, F32),
            pltpu.SemaphoreType.DMA((4,)),
            pltpu.SemaphoreType.DMA((4,)),
            pltpu.SemaphoreType.DMA((3, 2)),
            pltpu.SemaphoreType.DMA((3, 2)),
            pltpu.SemaphoreType.DMA((3,)),
            pltpu.SemaphoreType.DMA((2,)),
            pltpu.SemaphoreType.DMA((2,)),
            pltpu.SemaphoreType.DMA((2, 4)),
        ],
        compiler_params=pltpu.CompilerParams(
            collective_id=0, has_side_effects=True, vmem_limit_bytes=40 * 1024 * 1024),
    )(positions, start_vector)


def solution(mesh):
    in_specs = (P(None, ("row", "col")), P(None, ("row", "col"), None))
    out_specs = P(None, ("row", "col"), None)
    return jax.shard_map(shards, mesh=mesh, in_specs=in_specs, out_specs=out_specs, check_vma=False)
```

```python
import jax
import jax.numpy as jnp
from jax import lax
from jax.experimental import pallas as pl
from jax.experimental.pallas import tpu as pltpu
from jax.sharding import PartitionSpec as P

ITERS = 3
RADIUS = 0.4
MESH = pl.DeviceIdType.MESH
F32 = jnp.float32
BF16 = jnp.bfloat16

PLANE, LINE = 16, 8
HALF = 64
BLOCK = 512
WIDTH = 768


def kernel(pos_ref, z_ref, out_ref, posrow, posbuf, colbc, lanevec, mob, narrow, ag, rs, rs_send,
           packed, first_dir, mate, acc_wide, part, red_src, red_one, red_two, moments, flatten,
           z_mate, mate_sem, pos_sem, ag_recv, ag_send, rs_recv, rs_sent, red_sem):
    row, col = lax.axis_index("row"), lax.axis_index("col")
    x, core = lax.div(row, 2), lax.rem(row, 2)
    z, y = lax.div(col, 4), lax.rem(col, 4)

    def in_plane(n, c):
        dx, dy = lax.div(n, 4), lax.rem(n, 4)
        return (lax.rem(x + dx, 4) * 2 + c, z * 4 + lax.rem(y + dy, 4)), lax.rem(4 - dx, 4) * 4 + lax.rem(4 - dy, 4)

    def in_line(n, c):
        return (x * 2 + c, lax.rem(z + n, 8) * 4 + y), lax.rem(8 - n, 8)

    sibling = (x * 2 + 1 - core, col)

    def remote(src, dst, send, recv, device):
        return pltpu.make_async_remote_copy(
            src_ref=src, dst_ref=dst, send_sem=send, recv_sem=recv, device_id=device, device_id_type=MESH)

    def wait_recv(ref, sem):
        remote(ref, ref, sem, sem, (row, col)).wait_recv()

    def wait_send(ref, sem):
        remote(ref, ref, sem, sem, (row, col)).wait_send()

    first = lax.broadcasted_iota(jnp.int32, (32, 128), 1) < HALF
    keep = first == (core == 0)

    def turn(value):
        return pltpu.roll(value, HALF, 1)

    barrier = pltpu.get_barrier_semaphore()

    def signal(device):
        pl.semaphore_signal(barrier, inc=1, device_id=device, device_id_type=MESH)

    signal(sibling)

    @pl.loop(1, PLANE)
    def _(n):
        signal(in_plane(n, core)[0])

    @pl.loop(1, LINE)
    def _(n):
        signal(in_line(n, 0)[0])
        signal(in_line(n, 1)[0])

    flatten[...] = jnp.zeros_like(flatten)
    flatten[0:3, 0:32] = pos_ref[...].astype(F32)
    rows3 = flatten[...]
    posrow[core] = rows3[0:1] + pltpu.roll(rows3[1:2], 32, 1) + pltpu.roll(rows3[2:3], 64, 1)
    pl.semaphore_wait(barrier, 30)

    remote(posrow.at[core], posrow.at[core], pos_sem.at[0], pos_sem.at[1], sibling).start()
    remote(z_ref, z_mate, mate_sem.at[0], mate_sem.at[1], sibling).start()
    wait_recv(posrow.at[0], pos_sem.at[1])
    both = jnp.concatenate([posrow[0], posrow[1]], axis=1)
    posbuf[0] = both
    posbuf[PLANE] = both

    @pl.loop(1, PLANE)
    def _(n):
        device, slot = in_plane(n, core)
        remote(posbuf.at[0], posbuf.at[slot], pos_sem.at[2], pos_sem.at[3], device).start()

    @pl.loop(1, LINE)
    def _(n):
        device, slot = in_line(n, core)
        remote(posbuf.at[PLANE], posbuf.at[PLANE + slot], pos_sem.at[2], pos_sem.at[3], device).start()

    wait_recv(z_mate, mate_sem.at[1])
    for axis in range(3):
        packed[0, axis] = jnp.where(keep, z_ref[axis], turn(z_mate[axis]))

    def gather(step):
        def to_line():
            @pl.loop(1, LINE)
            def _(n):
                device, slot = in_line(n, core)
                remote(packed.at[step], ag.at[step, PLANE + slot], ag_send.at[step], ag_recv.at[step, 0], device).start()

        def to_plane():
            @pl.loop(1, PLANE)
            def _(n):
                device, slot = in_plane(n, core)
                remote(packed.at[step], ag.at[step, slot], ag_send.at[step], ag_recv.at[step, 1], device).start()

        last = step == 2
        pl.when(core == 0)(to_line)
        pl.when((core == 1) | last)(to_plane)
        pl.when((core == 1) & last)(to_line)
        ag[step, 0] = packed[step]
        ag[step, PLANE] = packed[step]

    def wait_line(step):
        wait_recv(ag.at[step, pl.ds(0, LINE - 1)], ag_recv.at[step, 0])

    def wait_plane(step):
        wait_recv(ag.at[step, pl.ds(0, PLANE - 1)], ag_recv.at[step, 1])

    gather(0)
    acc_wide[...] = jnp.zeros_like(acc_wide)
    part[...] = jnp.zeros_like(part)
    for k in range(2):
        red_src[2 * k] = jnp.zeros((1, WIDTH), F32)
    narrow[...] = jnp.zeros_like(narrow)
    wait_recv(posbuf.at[pl.ds(0, 22)], pos_sem.at[3])

    lane_of = lax.broadcasted_iota(jnp.int32, (BLOCK, 128), 1)
    bead_of = lax.broadcasted_iota(jnp.int32, (BLOCK, 128), 0) & 31
    entry_of = lax.broadcasted_iota(jnp.int32, (128, BLOCK), 0)
    column_of = lax.broadcasted_iota(jnp.int32, (128, BLOCK), 1) & 31
    owner_of = lax.broadcasted_iota(jnp.int32, (16, BLOCK), 1) >> 5
    source_of = lax.broadcasted_iota(jnp.int32, (16, BLOCK), 0)
    ones = jnp.ones((128, 128), BF16)

    def place(at, d):
        return posbuf[at + d // 2][:, (d % 2) * 128:(d % 2) * 128 + 128]

    @pl.loop(0, 2)
    def _(h):
        rows_at = jnp.where(core == 0, h, 2) * 8
        lanes_at = jnp.where(core == 0, 2, h) * 8
        spread = jnp.concatenate([jnp.broadcast_to(place(rows_at, d), (32, 128)) for d in range(16)], axis=0)
        flat = jnp.concatenate([place(lanes_at, d) for d in range(16)], axis=0).astype(BF16)
        for axis in range(3):
            own = jnp.where(lane_of == axis * 32 + bead_of, spread, 0.0).astype(BF16)
            colbc[h, axis] = jnp.dot(own, ones, preferred_element_type=F32)
            pick = jnp.where(entry_of == axis * 32 + column_of, 1.0, 0.0).astype(BF16)
            moved = jnp.dot(flat, pick, preferred_element_type=F32)
            lanevec[h, axis:axis + 1, :] = jnp.sum(jnp.where(owner_of == source_of, moved, 0.0), axis=0, keepdims=True)

    def places(t):
        tile = jnp.where(core == 0, jnp.where(t == 0, 2, jnp.where(t == 1, 1, jnp.where(t == 2, 3, 0))),
                         1 - lax.div(t, 2))
        h = jnp.where(core == 0, lax.div(tile, 2), lax.rem(t, 2))
        rt = jnp.where(core == 0, lax.rem(tile, 2), tile)
        return tile, h, jnp.where(core == 0, 0, h), pl.ds(pl.multiple_of(rt * 256, 256), 256)

    def build(t):
        _, h, _, span = places(t)

        @pl.loop(0, 16, unroll=2)
        def _(r):
            rows = pl.ds(pl.multiple_of(span.start + r * 16, 16), 16)
            mine = [colbc[h, axis, rows, :] for axis in range(3)]
            for tile in range(4):
                lanes = slice(tile * 128, tile * 128 + 128)
                d = [mine[axis] - lanevec[h, axis:axis + 1, lanes] for axis in range(3)]
                squared = d[0] * d[0] + d[1] * d[1] + d[2] * d[2]
                root = lax.rsqrt(jnp.where(squared > 0.5, squared, 1e30))
                inverse = root * root
                prefactor = (0.75 * RADIUS) * root
                iso = prefactor * (1.0 + (2.0 / 3.0 * RADIUS * RADIUS) * inverse)
                along = (prefactor * inverse) * (1.0 - (2.0 * RADIUS * RADIUS) * inverse)
                s = [along * d[axis] for axis in range(3)]
                parts = (s[0] * d[0] + iso, s[0] * d[1], s[0] * d[2], s[1] * d[1] + iso, s[1] * d[2],
                         s[2] * d[2] + iso)
                for k, value in enumerate(parts):
                    high = value.astype(BF16)
                    at = k * BLOCK + tile * 128
                    at = slice(at, at + 128)
                    mob[0, h, rows, at] = high
                    mob[1, h, rows, at] = (value - high.astype(F32)).astype(BF16)

    def arrange(step, h, low):
        base = jnp.where(core == 0, PLANE, h * 8)

        @pl.loop(0, 8)
        def _(s):
            values = [ag[step, base + s, axis] for axis in range(3)]
            if low:
                values = [value - value.astype(BF16).astype(F32) for value in values]
            others = [turn(value) for value in values]
            for j in range(2):
                left, right = (values, others) if j == 0 else (others, values)
                lx, ly, lz = (jnp.where(first, v, 0.0).astype(BF16) for v in left)
                ry, rz = (jnp.where(first, 0.0, v).astype(BF16) for v in right[1:])
                yx = jnp.where(first, left[1], right[0]).astype(BF16)
                for k, half, tile in ((0, 0, lx), (1, 0, yx), (2, 0, lz), (2, 1, lx), (3, 0, ry), (4, 0, rz),
                                      (4, 1, ly), (5, 1, lz)):
                    at = pl.ds(pl.multiple_of(k * BLOCK + s * 64 + j * 32, 32), 32)
                    narrow[int(low), h, at, half * 128:half * 128 + 128] = tile

    def dot(left, right):
        return jnp.dot(left, right, preferred_element_type=F32)

    def halves(i, upper):
        return pl.ds(pl.multiple_of(i * 64 + upper * 32, 32), 32)

    def pack_wide(i):
        low, high = halves(i, 0), halves(i, 1)
        xy_low, xy_high = acc_wide[low, :128], acc_wide[high, :128]
        z_low, z_high = acc_wide[low, 128:], acc_wide[high, 128:]
        return (jnp.where(first, xy_low, turn(xy_high)), jnp.where(first, turn(xy_low), xy_high),
                jnp.where(first, z_low, turn(z_high)))

    def scatter(step, tile):
        chunks = [pack_wide(i) for i in range(4)]
        for i, chunk in enumerate(chunks):
            for axis, value in enumerate(chunk):
                rs_send[step, tile * 4 + i, axis] = value

        @pl.loop(0, 4)
        def _(i):
            n = tile * 4 + 3 - i
            plane, plane_slot = in_plane(n, core)
            line, line_slot = in_line(n, core)
            device = tuple(jnp.where(core == 0, a, b) for a, b in zip(plane, line))
            slot = jnp.where(core == 0, plane_slot, line_slot)

            @pl.when(n > 0)
            def _():
                remote(rs_send.at[step, n], rs.at[step, slot], rs_sent.at[step], rs_recv.at[step], device).start()

            @pl.when(n == 0)
            def _():
                rs[step, 0] = rs_send[step, 0]

    def collect(step):
        @pl.when(core == 0)
        def _():
            wait_recv(rs.at[step, pl.ds(0, PLANE - 1)], rs_recv.at[step])
            for axis in range(3):
                packed[step + 1, axis] = sum((rs[step, s, axis] for s in range(1, PLANE)), rs[step, 0, axis])

        @pl.when(core == 1)
        def _():
            wait_recv(rs.at[step, pl.ds(0, LINE - 1)], rs_recv.at[step])
            for axis in range(3):
                packed[step + 1, axis] = sum((rs[step, s, axis] for s in range(1, LINE)), rs[step, 0, axis])

    front = lax.broadcasted_iota(jnp.int32, (1, 128), 1) < HALF

    def fold(value):
        line = jnp.sum(value, axis=0, keepdims=True)
        return line + turn(line)

    def inner(left, right):
        return fold(sum(left[axis] * right[axis] for axis in range(3)))

    def reduce_plane(k, values):
        for n, value in values:
            red_src[2 * k, :, n * 128:n * 128 + 128] = value

        @pl.loop(1, PLANE)
        def _(n):
            device, slot = in_plane(n, core)
            remote(red_src.at[2 * k], red_one.at[k, slot], red_sem.at[k, 0], red_sem.at[k, 1], device).start()

        red_one[k, 0] = red_src[2 * k]

    def reduce_line(k):
        def send(device, slot):
            remote(red_src.at[2 * k + 1], red_two.at[k, core, slot], red_sem.at[k, 2], red_sem.at[k, 3], device).start()

        wait_recv(red_one.at[k, pl.ds(0, PLANE - 1)], red_sem.at[k, 1])
        red_src[2 * k + 1] = sum((red_one[k, s] for s in range(1, PLANE)), red_one[k, 0])

        @pl.loop(1, LINE)
        def _(n):
            send(*in_line(n, core))
            if k == 1:
                send(*in_line(n, 1 - core))

        if k == 1:
            send(sibling, 0)
        red_two[k, core, 0] = red_src[2 * k + 1]

    def reduced(k, c):
        return sum((red_two[k, c, s] for s in range(1, LINE)), red_two[k, c, 0])

    @pl.loop(0, 4)
    def _(t):
        build(t)

    @pl.loop(0, ITERS)
    def _(step):
        pl.when(core == 0)(lambda: wait_line(step))
        pl.when(core == 1)(lambda: wait_plane(step))

        @pl.loop(0, 1 + core)
        def _(h):
            arrange(step, h, False)
            pl.when(step == 0)(lambda: arrange(step, h, True))

        @pl.loop(0, 4)
        def _(t):
            tile, h, w, rows = places(t)
            more = (core == 1) & (lax.rem(t, 2) == 1) & (step < 2)
            acc_wide[...] = jnp.where(more, acc_wide[...], 0.0) + dot(mob[0, h, rows, :], narrow[0, w])

            @pl.loop(0, jnp.where(step == 0, 2, 0))
            def _(which):
                acc_wide[...] += dot(mob[1 - which, h, rows, :], narrow[which, w])

            @pl.when((step < 2) & ((core == 0) | (lax.rem(t, 2) == 1)))
            def _():
                scatter(step, tile)

            @pl.when(step == 2)
            def _():
                pl.when((t == 0) & (core == 0))(lambda: wait_plane(2))
                pl.when((t == 0) & (core == 1))(lambda: wait_line(2))
                at = jnp.where(core == 0, 0, PLANE) + tile * 4
                total = part[...]
                for i in range(4):
                    for axis, value in enumerate(pack_wide(i)):
                        total = total + value * ag[2, at + i, axis]
                part[...] = total

        @pl.when(step == 1)
        def _():
            reduce_line(0)

        @pl.when(step < 2)
        def _():
            collect(step)

            @pl.when(step == 1)
            def _():
                wait_recv(red_two.at[0, 0, pl.ds(0, LINE - 1)], red_sem.at[0, 3])
                total = reduced(0, core)
                moments[0] = jnp.broadcast_to(total[:, 128:256] / total[:, 0:128], (32, 128))
                a1 = moments[0]
                for axis in range(3):
                    y1 = packed[1, axis]
                    packed[2, axis] = packed[2, axis] - a1 * y1
                    first_dir[axis] = y1 - a1 * packed[0, axis]

            gather(step + 1)

        @pl.when(step == 0)
        def _():
            reduce_plane(0, ((0, inner(packed.at[0], packed.at[0])), (1, inner(packed.at[0], packed.at[1]))))

        @pl.when(step == 1)
        def _():
            remote(first_dir, mate.at[0], mate_sem.at[2], mate_sem.at[3], sibling).start()
            remote(packed.at[2], mate.at[1], mate_sem.at[2], mate_sem.at[3], sibling).start()
            early = (red_src[0][:, 0:128], red_src[0][:, 128:256], inner(first_dir, first_dir),
                     inner(first_dir, packed.at[2]), inner(packed.at[2], packed.at[2]))
            for n, value in enumerate(early):
                red_src[2, :, n * 128:n * 128 + 128] = value

    reduce_plane(1, ((5, fold(part[...])),))
    reduce_line(1)
    wait_recv(red_one.at[1, pl.ds(0, 2 * LINE - 1)], red_sem.at[1, 3])
    low, high = reduced(1, 0), reduced(1, 1)
    for k in range(6):
        at = slice(k * 128, k * 128 + 128)
        moments[k + 1, 0:8] = jnp.broadcast_to(jnp.where(front, low[:, at], high[:, at]), (8, 128))
    moments[7, 0:8] = jnp.zeros((8, 128), F32)
    moments[8, 0:8] = jnp.ones((8, 128), F32)
    m0, m1, e1, f1, g, third, zero, one = (moments[k, 0:8] for k in range(1, 9))

    a1, a2, bb2 = m1 / m0, f1 / e1, e1 / m0
    e2 = g - a2 * f1 - bb2 * e1
    bb3 = e2 / e1
    a3 = (third - a2 * g - bb2 * (f1 + a1 * e1)) / e2 - a2
    d1, d2, d3 = 1.0 + a1, 1.0 + a2, 1.0 + a3
    scale = (d1 + d2 + d3) / ITERS
    current = (d1 / scale, jnp.sqrt(bb2) / scale, zero, d2 / scale, jnp.sqrt(bb3) / scale, d3 / scale)
    partner = (one, zero, zero, one, zero, one)

    def inverse_three(m):
        c00, c01, c02 = m[3] * m[5] - m[4] * m[4], m[2] * m[4] - m[1] * m[5], m[1] * m[4] - m[2] * m[3]
        c11, c12, c22 = m[0] * m[5] - m[2] * m[2], m[1] * m[2] - m[0] * m[4], m[0] * m[3] - m[1] * m[1]
        over = 1.0 / (m[0] * c00 + m[1] * c01 + m[2] * c02)
        return tuple(c * over for c in (c00, c01, c02, c11, c12, c22))

    def newton(_, state):
        now, other = state
        return (tuple(0.5 * (u + v) for u, v in zip(now, inverse_three(other))),
                tuple(0.5 * (u + v) for u, v in zip(other, inverse_three(now))))

    current, partner = lax.fori_loop(0, 20, newton, (current, partner))
    size = jnp.sqrt(scale)
    beta = jnp.sqrt(m0)
    r1, r2, r3 = (current[k] * size for k in range(3))
    f2, f3 = beta * r2 / jnp.sqrt(e1), beta * r3 / jnp.sqrt(e2)
    wait_recv(mate, mate_sem.at[3])
    c0, c1, c2 = (jnp.concatenate([c, c, c, c], axis=0) for c in (r1 - f3 * bb2, f2 - f3 * a2, f3))
    for axis in range(3):
        out_ref[axis] = (c0 * z_ref[axis] + c1 * jnp.where(keep, first_dir[axis], turn(mate[0, axis]))
                         + c2 * jnp.where(keep, packed[2, axis], turn(mate[1, axis])))

    wait_send(posrow.at[0], pos_sem.at[0])
    wait_send(z_mate, mate_sem.at[0])
    wait_send(mate, mate_sem.at[2])
    wait_send(posbuf.at[pl.ds(0, 22)], pos_sem.at[2])
    wait_send(ag.at[2, pl.ds(0, PLANE + LINE - 2)], ag_send.at[2])
    for k, count in enumerate((LINE - 1, 2 * LINE - 1)):
        wait_send(red_one.at[k, pl.ds(0, PLANE - 1)], red_sem.at[k, 0])
        wait_send(red_one.at[k, pl.ds(0, count)], red_sem.at[k, 2])
    for step in range(2):
        @pl.when(core == 0)
        def _(step=step):
            wait_send(ag.at[step, pl.ds(0, LINE - 1)], ag_send.at[step])
            wait_send(rs_send.at[step, pl.ds(0, PLANE - 1)], rs_sent.at[step])

        @pl.when(core == 1)
        def _(step=step):
            wait_send(ag.at[step, pl.ds(0, PLANE - 1)], ag_send.at[step])
            wait_send(rs_send.at[step, pl.ds(0, LINE - 1)], rs_sent.at[step])


def shards(positions, start_vector):
    chunk = (3, 32, 128)
    return pl.pallas_call(
        kernel,
        out_shape=jax.ShapeDtypeStruct(start_vector.shape, F32),
        in_specs=[pl.BlockSpec(memory_space=pltpu.VMEM)] * 2,
        out_specs=pl.BlockSpec(memory_space=pltpu.VMEM),
        scratch_shapes=[
            pltpu.VMEM((2, 1, 128), F32),
            pltpu.VMEM((PLANE + LINE, 1, 256), F32),
            pltpu.VMEM((2, 3, BLOCK, 128), F32),
            pltpu.VMEM((2, 8, BLOCK), F32),
            pltpu.VMEM((2, 2, BLOCK, 6 * BLOCK), BF16),
            pltpu.VMEM((2, 2, 6 * BLOCK, 256), BF16),
            pltpu.VMEM((3, PLANE + LINE) + chunk, F32),
            pltpu.VMEM((2, PLANE) + chunk, F32),
            pltpu.VMEM((2, PLANE) + chunk, F32),
            pltpu.VMEM((3,) + chunk, F32),
            pltpu.VMEM(chunk, F32),
            pltpu.VMEM((2,) + chunk, F32),
            pltpu.VMEM((256, 256), F32),
            pltpu.VMEM((32, 128), F32),
            pltpu.VMEM((4, 1, WIDTH), F32),
            pltpu.VMEM((2, PLANE, 1, WIDTH), F32),
            pltpu.VMEM((2, 2, LINE, 1, WIDTH), F32),
            pltpu.VMEM((9, 32, 128), F32),
            pltpu.VMEM((8, 128), F32),
            pltpu.VMEM(chunk, F32),
            pltpu.SemaphoreType.DMA((4,)),
            pltpu.SemaphoreType.DMA((4,)),
            pltpu.SemaphoreType.DMA((3, 2)),
            pltpu.SemaphoreType.DMA((3,)),
            pltpu.SemaphoreType.DMA((2,)),
            pltpu.SemaphoreType.DMA((2,)),
            pltpu.SemaphoreType.DMA((2, 4)),
        ],
        compiler_params=pltpu.CompilerParams(
            collective_id=0, has_side_effects=True, vmem_limit_bytes=40 * 1024 * 1024),
    )(positions, start_vector)


def solution(mesh):
    in_specs = (P(None, ("row", "col")), P(None, ("row", "col"), None))
    out_specs = P(None, ("row", "col"), None)
    return jax.shard_map(shards, mesh=mesh, in_specs=in_specs, out_specs=out_specs, check_vma=False)
```

```python
import functools

import jax
import jax.numpy as jnp
from jax import lax
from jax.experimental import pallas as pl
from jax.experimental.pallas import tpu as pltpu
from jax.sharding import PartitionSpec as P

ITERS = 3
RADIUS = 0.4
MESH = pl.DeviceIdType.MESH
F32 = jnp.float32
BF16 = jnp.bfloat16

PLANE, LINE = 16, 8
PLACES = ((0, 0), (2, 0), (0, 2), (2, 2), (0, 1), (3, 0), (1, 1), (1, 3), (3, 2), (2, 1),
          (0, 3), (1, 0), (3, 3), (3, 1), (1, 2), (2, 3))
NEEDED = 10
ORDER = ((0, 1), (0, 3), (1, 0), (3, 0), (2, 0), (0, 2), (1, 1), (3, 3), (1, 3), (3, 1),
         (1, 2), (2, 1), (3, 2), (2, 3), (2, 2))
STEPS = (0, 1, 7, 2, 6, 3, 5, 4)


def seen_in_plane(dx, dy):
    return PLACES.index((-dx % 4, -dy % 4))


def seen_in_line(dz):
    return PLANE + STEPS.index(-dz % 8)


HALF = 64
BLOCK = 512
WIDTH = 768


def kernel(pos_ref, z_ref, out_ref, posrow, posbuf, colbc, lanevec, mob_high, mob_low, wide, narrow, ag, rs, rs_send,
           packed, first_dir, mate, acc, acc_wide, part, red_src, red_one, red_two, moments, flatten,
           z_mate, mate_sem, pos_sem, line_sem, plane_sem, ag_send, rs_recv, rs_sent, red_sem):
    row, col = lax.axis_index("row"), lax.axis_index("col")
    x, core = lax.div(row, 2), lax.rem(row, 2)
    z, y = lax.div(col, 4), lax.rem(col, 4)

    xs = [lax.rem(x + d, 4) for d in range(4)]
    ys = [lax.rem(y + d, 4) for d in range(4)]
    zs = [lax.rem(z + d, 8) for d in range(8)]

    def plane_at(dx, dy):
        return (xs[dx] * 2 + core, z * 4 + ys[dy])

    far_places, far_steps = PLACES[:0:-1], STEPS[:0:-1]

    def line_at(dz):
        return (row, zs[dz] * 4 + y)

    def line_mate(dz):
        return (x * 2 + 1 - core, zs[dz] * 4 + y)

    sibling = (x * 2 + 1 - core, col)

    def for_each_core(program):
        for c in range(2):
            pl.when(core == c)(functools.partial(program, c))


    def remote(src, dst, send, recv, device):
        return pltpu.make_async_remote_copy(
            src_ref=src, dst_ref=dst, send_sem=send, recv_sem=recv, device_id=device, device_id_type=MESH)

    def wait_recv(ref, sem):
        remote(ref, ref, sem, sem, (row, col)).wait_recv()

    def wait_send(ref, sem):
        remote(ref, ref, sem, sem, (row, col)).wait_send()

    first = lax.broadcasted_iota(jnp.int32, (32, 128), 1) < HALF
    keep = first == (core == 0)

    def turn(value):
        return pltpu.roll(value, HALF, 1)

    barrier = pltpu.get_barrier_semaphore()

    def signal(device):
        pl.semaphore_signal(barrier, inc=1, device_id=device, device_id_type=MESH)

    signal(sibling)
    for dx, dy in far_places:
        signal(plane_at(dx, dy))
    for dz in far_steps:
        signal(line_at(dz))
        signal(line_mate(dz))

    flatten[...] = jnp.zeros_like(flatten)
    flatten[0:3, 0:32] = pos_ref[...].astype(F32)
    rows3 = flatten[...]
    posrow[core] = rows3[0:1] + pltpu.roll(rows3[1:2], 32, 1) + pltpu.roll(rows3[2:3], 64, 1)
    pl.semaphore_wait(barrier, 30)

    remote(posrow.at[core], posrow.at[core], pos_sem.at[0], pos_sem.at[1], sibling).start()
    remote(z_ref, z_mate, mate_sem.at[0], mate_sem.at[1], sibling).start()
    wait_recv(posrow.at[0], pos_sem.at[1])
    both = jnp.concatenate([posrow[0], posrow[1]], axis=1)
    posbuf[0] = both
    posbuf[PLANE] = both
    for n, spot in enumerate(far_places):
        if n < 7:
            remote(posbuf.at[PLANE], posbuf.at[seen_in_line(far_steps[n])], pos_sem.at[2], pos_sem.at[3],
                   line_at(far_steps[n])).start()
        remote(posbuf.at[0], posbuf.at[seen_in_plane(*spot)], pos_sem.at[2], pos_sem.at[3], plane_at(*spot)).start()
    wait_recv(z_mate, mate_sem.at[1])
    for axis in range(3):
        packed[0, axis] = jnp.where(keep, z_ref[axis], turn(z_mate[axis]))

    def gather(c, step):
        def to_line():
            for dz in STEPS[1:]:
                slot = seen_in_line(dz)
                remote(packed.at[step], ag.at[step, slot], ag_send.at[step], line_sem.at[step, (slot - PLANE) // 4],
                       line_at(dz)).start()

        def to_plane(some):
            for spot in ORDER:
                slot = seen_in_plane(*spot)
                if slot < NEEDED or not some:
                    remote(packed.at[step], ag.at[step, slot], ag_send.at[step], plane_sem.at[step, slot // 8],
                           plane_at(*spot)).start()

        if c == 0:
            to_line()
        if step == 2:
            to_plane(True)
        elif c == 1:
            to_plane(False)
        if c == 1 and step == 2:
            to_line()
        ag[step, 0] = packed[step]
        ag[step, PLANE] = packed[step]

    def wait_line(step, part_of):
        wait_recv(ag.at[step, pl.ds(0, 4 if part_of else 3)], line_sem.at[step, part_of])

    def wait_plane(step, part_of, last=False):
        if part_of == 0:
            wait_recv(ag.at[step, pl.ds(0, 7)], plane_sem.at[step, 0])
        else:
            wait_recv(ag.at[step, pl.ds(0, NEEDED - 8 if last else 8)], plane_sem.at[step, 1])

    for_each_core(lambda c: gather(c, 0))
    acc[...] = jnp.zeros_like(acc)
    acc_wide[...] = jnp.zeros_like(acc_wide)
    part[...] = jnp.zeros_like(part)
    ag[2, NEEDED:PLANE] = jnp.zeros((PLANE - NEEDED, 3, 32, 128), F32)
    for k in range(2):
        red_src[2 * k] = jnp.zeros((1, WIDTH), F32)
    narrow[...] = jnp.zeros_like(narrow)
    wait_recv(posbuf.at[pl.ds(0, 22)], pos_sem.at[3])

    lane_of = lax.broadcasted_iota(jnp.int32, (BLOCK, 128), 1)
    bead_of = lax.broadcasted_iota(jnp.int32, (BLOCK, 128), 0) & 31
    entry_of = lax.broadcasted_iota(jnp.int32, (128, BLOCK), 0)
    column_of = lax.broadcasted_iota(jnp.int32, (128, BLOCK), 1) & 31
    owner_of = lax.broadcasted_iota(jnp.int32, (16, BLOCK), 1) >> 5
    source_of = lax.broadcasted_iota(jnp.int32, (16, BLOCK), 0)
    ones = jnp.ones((128, 128), BF16)

    def place(at, d):
        return posbuf[at + d // 2][:, (d % 2) * 128:(d % 2) * 128 + 128]

    @pl.loop(0, 2)
    def _(h):
        rows_at = jnp.where(core == 0, h, 2) * 8
        lanes_at = jnp.where(core == 0, 2, h) * 8
        spread = jnp.concatenate([jnp.broadcast_to(place(rows_at, d), (32, 128)) for d in range(16)], axis=0)
        flat = jnp.concatenate([place(lanes_at, d) for d in range(16)], axis=0).astype(BF16)
        for axis in range(3):
            own = jnp.where(lane_of == axis * 32 + bead_of, spread, 0.0).astype(BF16)
            colbc[h, axis] = jnp.dot(own, ones, preferred_element_type=F32)
            pick = jnp.where(entry_of == axis * 32 + column_of, 1.0, 0.0).astype(BF16)
            moved = jnp.dot(flat, pick, preferred_element_type=F32)
            lanevec[h, axis:axis + 1, :] = jnp.sum(jnp.where(owner_of == source_of, moved, 0.0), axis=0, keepdims=True)

    def tile_of(c, t):
        return (4 - t) % 4 if c == 0 else 1 - t // 2

    def places(c, t):
        tile = tile_of(c, t)
        h, rt = (tile // 2, tile % 2) if c == 0 else (t % 2, tile)
        return h, c * h, rt * 256

    def build(c, t):
        h, _, begin = places(c, t)

        @pl.loop(0, 16, unroll=2)
        def _(r):
            rows = pl.ds(pl.multiple_of(begin + r * 16, 16), 16)
            mine = [colbc[h, axis, rows, :] for axis in range(3)]
            for tile in range(4):
                lanes = slice(tile * 128, tile * 128 + 128)
                d = [mine[axis] - lanevec[h, axis:axis + 1, lanes] for axis in range(3)]
                squared = d[0] * d[0] + d[1] * d[1] + d[2] * d[2]
                root = lax.rsqrt(jnp.where(squared > 0.5, squared, 1e30))
                inverse = root * root
                prefactor = (0.75 * RADIUS) * root
                iso = prefactor * (1.0 + (2.0 / 3.0 * RADIUS * RADIUS) * inverse)
                along = (prefactor * inverse) * (1.0 - (2.0 * RADIUS * RADIUS) * inverse)
                s = [along * d[axis] for axis in range(3)]
                parts = (s[0] * d[0] + iso, s[0] * d[1], s[0] * d[2], s[1] * d[1] + iso, s[1] * d[2],
                         s[2] * d[2] + iso)
                for k, value in enumerate(parts):
                    high = value.astype(BF16)
                    at = (tile // 2) * 1536 + k * 256 + (tile % 2) * 128
                    at = slice(at, at + 128)
                    mob_high[h, rows, at] = high
                    mob_low[h, rows, at] = (value - high.astype(F32)).astype(BF16)

    def widen(c, h):
        base = PLANE if c == 0 else h * 8

        @pl.loop(0, 8, unroll=4)
        def _(s):
            for axis in range(3):
                value = ag[0, base + s, axis]
                other = turn(value)
                for j, both in enumerate((jnp.where(first, value, other), jnp.where(first, other, value))):
                    high = both.astype(BF16).astype(F32)
                    tile = jnp.where(first, high, both - high).astype(BF16)
                    at = pl.ds(pl.multiple_of(s * 64 + j * 32, 32), 32)
                    wide[h, at, axis * 128:axis * 128 + 128] = tile
                    if axis == 0:
                        wide[h, at, 384:512] = tile

    def arrange(step, base, w, quarter, weight):
        @pl.loop(0, 4, unroll=4)
        def _(s):
            values = [ag[step, base + s, axis] * weight for axis in range(3)]
            others = [turn(value) for value in values]
            for j in range(2):
                left, right = (values, others) if j == 0 else (others, values)
                lx, ly, lz = (jnp.where(first, v, 0.0).astype(BF16) for v in left)
                ry, rz = (jnp.where(first, 0.0, v).astype(BF16) for v in right[1:])
                yx = jnp.where(first, left[1], right[0]).astype(BF16)
                for k, half, tile in ((0, 0, lx), (1, 0, yx), (2, 0, lz), (2, 1, lx), (3, 0, ry), (4, 0, rz),
                                      (4, 1, ly), (5, 1, lz)):
                    at = pl.ds(pl.multiple_of(quarter * 1536 + k * 256 + s * 64 + j * 32, 32), 32)
                    narrow[w, at, half * 128:half * 128 + 128] = tile

    def arrange_half(c, step, part_of):
        if c == 0:
            wait_line(step, part_of)
            arrange(step, PLANE + 4 * part_of, 0, part_of, 1.0)
        else:
            wait_plane(step, part_of, step == 2)
            for quarter in range(2):
                slot = 8 * part_of + 4 * quarter
                if step == 1 or slot < NEEDED:
                    arrange(step, slot, part_of, quarter, 2.0 if step == 2 and slot >= 4 else 1.0)

    def dot(left, right):
        return jnp.dot(left, right, preferred_element_type=F32)

    def product(c, t):
        h, w, begin = places(c, t)
        rows = slice(begin, begin + 256)

        def both(k, lo, hi):
            total = 0.0
            for quarter in range(2):
                at = slice(quarter * 1536 + k * 256, quarter * 1536 + k * 256 + 256)
                right = wide[w, quarter * 256:quarter * 256 + 256, lo:hi]
                total = total + dot(mob_high[h, rows, at], right) + dot(mob_low[h, rows, at], right)
            return total

        xy, yz, zx = both(1, 0, 256), both(4, 128, 384), both(2, 256, 512)
        return (both(0, 0, 128) + xy[:, 128:] + zx[:, :128],
                both(3, 128, 256) + xy[:, :128] + yz[:, 128:],
                both(5, 256, 384) + zx[:, 128:] + yz[:, :128])

    def halves(i, upper):
        return slice(i * 64 + upper * 32, i * 64 + upper * 32 + 32)

    def pack(_, i):
        chunk = []
        for axis in range(3):
            low, high = acc[axis, halves(i, 0), :], acc[axis, halves(i, 1), :]
            chunk.append(jnp.where(first, low + turn(low), high + turn(high)))
        return chunk

    def pack_wide(tile, i):
        low, high = halves(i, 0), halves(i, 1)
        xy_low, xy_high = acc_wide[tile, low, :128], acc_wide[tile, high, :128]
        z_low, z_high = acc_wide[tile, low, 128:], acc_wide[tile, high, 128:]
        return (jnp.where(first, xy_low, turn(xy_high)), jnp.where(first, turn(xy_low), xy_high),
                jnp.where(first, z_low, turn(z_high)))

    def scatter(c, step, t, packer):
        def fill(tile):
            chunks = [packer(tile, i) for i in range(4)]
            for i, chunk in enumerate(chunks):
                for axis, value in enumerate(chunk):
                    rs_send[step, tile * 4 + i, axis] = value

        def send_plane(tile):
            fill(tile)
            for i in (3, 2, 1, 0):
                spot = PLACES[tile * 4 + i]
                if tile * 4 + i:
                    remote(rs_send.at[step, tile * 4 + i], rs.at[step, seen_in_plane(*spot)], rs_sent.at[step],
                           rs_recv.at[step], plane_at(*spot)).start()
                else:
                    rs[step, 0] = rs_send[step, 0]

        def send_line(tile):
            fill(tile)
            for i in (3, 2, 1, 0):
                dz = STEPS[tile * 4 + i]
                if dz:
                    remote(rs_send.at[step, tile * 4 + i], rs.at[step, seen_in_line(dz) - PLANE], rs_sent.at[step],
                           rs_recv.at[step], line_at(dz)).start()
                else:
                    rs[step, 0] = rs_send[step, 0]

        (send_line if c else send_plane)(tile_of(c, t))

    def collect(c, step):
        count = LINE if c else PLANE
        wait_recv(rs.at[step, pl.ds(0, count - 1)], rs_recv.at[step])
        for axis in range(3):
            packed[step + 1, axis] = sum((rs[step, s, axis] for s in range(1, count)), rs[step, 0, axis])

    front = lax.broadcasted_iota(jnp.int32, (1, 128), 1) < HALF

    def fold(value):
        line = jnp.sum(value, axis=0, keepdims=True)
        return line + turn(line)

    def inner(left, right):
        return fold(sum(left[axis] * right[axis] for axis in range(3)))

    def reduce_plane(k, values):
        for n, value in values:
            red_src[2 * k, :, n * 128:n * 128 + 128] = value
        for spot in far_places:
            remote(red_src.at[2 * k], red_one.at[k, seen_in_plane(*spot)], red_sem.at[k, 0], red_sem.at[k, 1], plane_at(*spot)).start()
        red_one[k, 0] = red_src[2 * k]

    def reduce_line(k):
        def send(dz, device):
            slot = seen_in_line(dz) - PLANE
            remote(red_src.at[2 * k + 1], red_two.at[k, core, slot], red_sem.at[k, 2], red_sem.at[k, 3], device).start()

        wait_recv(red_one.at[k, pl.ds(0, PLANE - 1)], red_sem.at[k, 1])
        red_src[2 * k + 1] = sum((red_one[k, s] for s in range(1, PLANE)), red_one[k, 0])
        for dz in far_steps:
            send(dz, line_at(dz))
            if k == 1:
                send(dz, line_mate(dz))
        if k == 1:
            send(0, sibling)
        red_two[k, core, 0] = red_src[2 * k + 1]

    def reduced(k, c):
        return sum((red_two[k, c, s] for s in range(1, LINE)), red_two[k, c, 0])

    def steps(c):
        for t in range(2):
            build(c, t)
        if c == 0:
            wait_line(0, 0)
            wait_line(0, 1)
            widen(c, 0)
        else:
            wait_plane(0, 0)
            wait_plane(0, 1)
            widen(c, 0)
            widen(c, 1)
        for t in range(4):
            if t >= 2:
                build(c, t)
            for axis, value in enumerate(product(c, t)):
                acc[axis] = acc[axis] + value if c == 1 and t % 2 == 1 else value
            if c == 0 or t % 2 == 1:
                scatter(c, 0, t, pack)
        collect(c, 0)
        gather(c, 1)
        reduce_plane(0, ((0, inner(packed.at[0], packed.at[0])), (1, inner(packed.at[0], packed.at[1]))))

        for step in (1, 2):
            for part_of in range(2):
                arrange_half(c, step, part_of)
                for t in range(4):
                    tile = tile_of(c, t)
                    quarter = t % 2 if c else part_of
                    if step == 2 and (tile == 3 if c == 0 else 8 * part_of + 4 * quarter >= NEEDED):
                        skip = True
                    else:
                        skip = False
                        h, rt = (part_of, tile) if c else (tile // 2, tile % 2)
                        inner_at = slice(quarter * 1536, quarter * 1536 + 1536)
                        value = dot(mob_high[h, rt * 256:rt * 256 + 256, inner_at], narrow[h if c else 0, inner_at, :])
                        begin = part_of == 0 and (c == 0 or t % 2 == 0)
                        acc_wide[tile] = value if begin else acc_wide[tile] + value
                    if part_of == 0 or (c == 1 and t % 2 == 0):
                        continue
                    if step == 1:
                        scatter(c, 1, t, pack_wide)
                        continue
                    if t == c:
                        for half in range(2):
                            wait_line(2, half) if c else wait_plane(2, half, True)
                    if c == 0 and skip:
                        continue
                    total = jnp.zeros((32, 128), F32)
                    for i in range(4):
                        for axis, value in enumerate(pack_wide(tile, i)):
                            total = total + value * ag[2, (PLANE if c else 0) + tile * 4 + i, axis]
                    part[...] += total * (2.0 if c == 0 and tile > 0 else 1.0)
            if step == 2:
                break
            reduce_line(0)
            collect(c, 1)
            wait_recv(red_two.at[0, 0, pl.ds(0, LINE - 1)], red_sem.at[0, 3])
            total = reduced(0, c)
            moments[0] = jnp.broadcast_to(total[:, 128:256] / total[:, 0:128], (32, 128))
            a1 = moments[0]
            for axis in range(3):
                y1 = packed[1, axis]
                packed[2, axis] = packed[2, axis] - a1 * y1
                first_dir[axis] = y1 - a1 * packed[0, axis]
            gather(c, 2)
            remote(first_dir, mate.at[0], mate_sem.at[2], mate_sem.at[3], sibling).start()
            remote(packed.at[2], mate.at[1], mate_sem.at[2], mate_sem.at[3], sibling).start()
            early = (red_src[0][:, 0:128], red_src[0][:, 128:256], inner(first_dir, first_dir),
                     inner(first_dir, packed.at[2]), inner(packed.at[2], packed.at[2]))
            for n, value in enumerate(early):
                red_src[2, :, n * 128:n * 128 + 128] = value

    for_each_core(steps)

    reduce_plane(1, ((5, fold(part[...])),))
    reduce_line(1)
    wait_recv(red_one.at[1, pl.ds(0, 2 * LINE - 1)], red_sem.at[1, 3])
    low, high = reduced(1, 0), reduced(1, 1)
    for k in range(6):
        at = slice(k * 128, k * 128 + 128)
        moments[k + 1, 0:8] = jnp.broadcast_to(jnp.where(front, low[:, at], high[:, at]), (8, 128))
    moments[7, 0:8] = jnp.zeros((8, 128), F32)
    moments[8, 0:8] = jnp.ones((8, 128), F32)
    m0, m1, e1, f1, g, third, zero, one = (moments[k, 0:8] for k in range(1, 9))

    a1, a2, bb2 = m1 / m0, f1 / e1, e1 / m0
    e2 = g - a2 * f1 - bb2 * e1
    bb3 = e2 / e1
    a3 = (third - a2 * g - bb2 * (f1 + a1 * e1)) / e2 - a2
    d1, d2, d3 = 1.0 + a1, 1.0 + a2, 1.0 + a3
    scale = (d1 + d2 + d3) / ITERS
    current = (d1 / scale, jnp.sqrt(bb2) / scale, zero, d2 / scale, jnp.sqrt(bb3) / scale, d3 / scale)
    partner = (one, zero, zero, one, zero, one)

    def inverse_three(m):
        c00, c01, c02 = m[3] * m[5] - m[4] * m[4], m[2] * m[4] - m[1] * m[5], m[1] * m[4] - m[2] * m[3]
        c11, c12, c22 = m[0] * m[5] - m[2] * m[2], m[1] * m[2] - m[0] * m[4], m[0] * m[3] - m[1] * m[1]
        over = 1.0 / (m[0] * c00 + m[1] * c01 + m[2] * c02)
        return tuple(c * over for c in (c00, c01, c02, c11, c12, c22))

    def newton(_, state):
        now, other = state
        return (tuple(0.5 * (u + v) for u, v in zip(now, inverse_three(other))),
                tuple(0.5 * (u + v) for u, v in zip(other, inverse_three(now))))

    current, partner = lax.fori_loop(0, 20, newton, (current, partner))
    size = jnp.sqrt(scale)
    beta = jnp.sqrt(m0)
    r1, r2, r3 = (current[k] * size for k in range(3))
    f2, f3 = beta * r2 / jnp.sqrt(e1), beta * r3 / jnp.sqrt(e2)
    wait_recv(mate, mate_sem.at[3])
    c0, c1, c2 = (jnp.concatenate([c, c, c, c], axis=0) for c in (r1 - f3 * bb2, f2 - f3 * a2, f3))
    for axis in range(3):
        out_ref[axis] = (c0 * z_ref[axis] + c1 * jnp.where(keep, first_dir[axis], turn(mate[0, axis]))
                         + c2 * jnp.where(keep, packed[2, axis], turn(mate[1, axis])))

    wait_send(posrow.at[0], pos_sem.at[0])
    wait_send(z_mate, mate_sem.at[0])
    wait_send(mate, mate_sem.at[2])
    wait_send(posbuf.at[pl.ds(0, 22)], pos_sem.at[2])
    wait_send(ag.at[2, pl.ds(0, NEEDED - 1 + LINE - 1)], ag_send.at[2])
    for k, count in enumerate((LINE - 1, 2 * LINE - 1)):
        wait_send(red_one.at[k, pl.ds(0, PLANE - 1)], red_sem.at[k, 0])
        wait_send(red_one.at[k, pl.ds(0, count)], red_sem.at[k, 2])
    for step in range(2):
        @pl.when(core == 0)
        def _(step=step):
            wait_send(ag.at[step, pl.ds(0, LINE - 1)], ag_send.at[step])
            wait_send(rs_send.at[step, pl.ds(0, PLANE - 1)], rs_sent.at[step])

        @pl.when(core == 1)
        def _(step=step):
            wait_send(ag.at[step, pl.ds(0, PLANE - 1)], ag_send.at[step])
            wait_send(rs_send.at[step, pl.ds(0, LINE - 1)], rs_sent.at[step])


def shards(positions, start_vector):
    chunk = (3, 32, 128)
    return pl.pallas_call(
        kernel,
        out_shape=jax.ShapeDtypeStruct(start_vector.shape, F32),
        in_specs=[pl.BlockSpec(memory_space=pltpu.VMEM)] * 2,
        out_specs=pl.BlockSpec(memory_space=pltpu.VMEM),
        scratch_shapes=[
            pltpu.VMEM((2, 1, 128), F32),
            pltpu.VMEM((PLANE + LINE, 1, 256), F32),
            pltpu.VMEM((2, 3, BLOCK, 128), F32),
            pltpu.VMEM((2, 8, BLOCK), F32),
            pltpu.VMEM((2, BLOCK, 6 * BLOCK), BF16),
            pltpu.VMEM((2, BLOCK, 6 * BLOCK), BF16),
            pltpu.VMEM((2, BLOCK, 512), BF16),
            pltpu.VMEM((2, 6 * BLOCK, 256), BF16),
            pltpu.VMEM((3, PLANE + LINE) + chunk, F32),
            pltpu.VMEM((2, PLANE) + chunk, F32),
            pltpu.VMEM((2, PLANE) + chunk, F32),
            pltpu.VMEM((3,) + chunk, F32),
            pltpu.VMEM(chunk, F32),
            pltpu.VMEM((2,) + chunk, F32),
            pltpu.VMEM((3, 256, 128), F32),
            pltpu.VMEM((4, 256, 256), F32),
            pltpu.VMEM((32, 128), F32),
            pltpu.VMEM((4, 1, WIDTH), F32),
            pltpu.VMEM((2, PLANE, 1, WIDTH), F32),
            pltpu.VMEM((2, 2, LINE, 1, WIDTH), F32),
            pltpu.VMEM((9, 32, 128), F32),
            pltpu.VMEM((8, 128), F32),
            pltpu.VMEM(chunk, F32),
            pltpu.SemaphoreType.DMA((4,)),
            pltpu.SemaphoreType.DMA((4,)),
            pltpu.SemaphoreType.DMA((3, 2)),
            pltpu.SemaphoreType.DMA((3, 2)),
            pltpu.SemaphoreType.DMA((3,)),
            pltpu.SemaphoreType.DMA((2,)),
            pltpu.SemaphoreType.DMA((2,)),
            pltpu.SemaphoreType.DMA((2, 4)),
        ],
        compiler_params=pltpu.CompilerParams(
            collective_id=0, has_side_effects=True, vmem_limit_bytes=40 * 1024 * 1024),
    )(positions, start_vector)


def solution(mesh):
    in_specs = (P(None, ("row", "col")), P(None, ("row", "col"), None))
    out_specs = P(None, ("row", "col"), None)
    return jax.shard_map(shards, mesh=mesh, in_specs=in_specs, out_specs=out_specs, check_vma=False)
```

```python
import functools

import jax
import jax.numpy as jnp
from jax import lax
from jax.experimental import pallas as pl
from jax.experimental.pallas import tpu as pltpu
from jax.sharding import PartitionSpec as P

ITERS = 3
RADIUS = 0.4
MESH = pl.DeviceIdType.MESH
F32 = jnp.float32
BF16 = jnp.bfloat16

PLANE, LINE = 16, 8
PLACES = ((0, 0), (2, 0), (0, 2), (2, 2), (0, 1), (3, 0), (1, 1), (1, 3), (3, 2), (2, 1),
          (0, 3), (1, 0), (3, 3), (3, 1), (1, 2), (2, 3))
NEEDED = 10
ORDER = ((0, 1), (0, 3), (1, 0), (3, 0), (2, 0), (0, 2), (1, 1), (3, 3), (1, 3), (3, 1),
         (1, 2), (2, 1), (3, 2), (2, 3), (2, 2))
STEPS = (0, 1, 7, 2, 6, 3, 5, 4)


def seen_in_plane(dx, dy):
    return PLACES.index((-dx % 4, -dy % 4))


def seen_in_line(dz):
    return PLANE + STEPS.index(-dz % 8)


HALF = 64
BLOCK = 512
WIDTH = 768


def kernel(pos_ref, z_ref, out_ref, posrow, posbuf, colbc, lanevec, mob_high, mob_low, wide, narrow, ag, rs, rs_send,
           packed, first_dir, mate, acc, acc_wide, part, red_src, red_one, red_two, moments, flatten,
           z_mate, mate_sem, pos_sem, line_sem, plane_sem, ag_send, rs_recv, rs_sent, red_sem):
    row, col = lax.axis_index("row"), lax.axis_index("col")
    x, core = lax.div(row, 2), lax.rem(row, 2)
    z, y = lax.div(col, 4), lax.rem(col, 4)

    xs = [lax.rem(x + d, 4) for d in range(4)]
    ys = [lax.rem(y + d, 4) for d in range(4)]
    zs = [lax.rem(z + d, 8) for d in range(8)]

    def plane_at(dx, dy):
        return (xs[dx] * 2 + core, z * 4 + ys[dy])

    far_places, far_steps = PLACES[:0:-1], STEPS[:0:-1]

    def line_at(dz):
        return (row, zs[dz] * 4 + y)

    def line_mate(dz):
        return (x * 2 + 1 - core, zs[dz] * 4 + y)

    sibling = (x * 2 + 1 - core, col)

    def for_each_core(program):
        for c in range(2):
            pl.when(core == c)(functools.partial(program, c))


    def remote(src, dst, send, recv, device):
        return pltpu.make_async_remote_copy(
            src_ref=src, dst_ref=dst, send_sem=send, recv_sem=recv, device_id=device, device_id_type=MESH)

    def wait_recv(ref, sem):
        remote(ref, ref, sem, sem, (row, col)).wait_recv()

    def wait_send(ref, sem):
        remote(ref, ref, sem, sem, (row, col)).wait_send()

    first = lax.broadcasted_iota(jnp.int32, (32, 128), 1) < HALF
    keep = first == (core == 0)

    def turn(value):
        return pltpu.roll(value, HALF, 1)

    barrier = pltpu.get_barrier_semaphore()

    def signal(device):
        pl.semaphore_signal(barrier, inc=1, device_id=device, device_id_type=MESH)

    signal(sibling)
    for dx, dy in far_places:
        signal(plane_at(dx, dy))
    for dz in far_steps:
        signal(line_at(dz))
        signal(line_mate(dz))

    flatten[...] = jnp.zeros_like(flatten)
    flatten[0:3, 0:32] = pos_ref[...].astype(F32)
    rows3 = flatten[...]
    posrow[core] = rows3[0:1] + pltpu.roll(rows3[1:2], 32, 1) + pltpu.roll(rows3[2:3], 64, 1)
    pl.semaphore_wait(barrier, 30)

    remote(posrow.at[core], posrow.at[core], pos_sem.at[0], pos_sem.at[1], sibling).start()
    remote(z_ref, z_mate, mate_sem.at[0], mate_sem.at[1], sibling).start()
    wait_recv(posrow.at[0], pos_sem.at[1])
    both = jnp.concatenate([posrow[0], posrow[1]], axis=1)
    posbuf[0] = both
    posbuf[PLANE] = both
    for n, spot in enumerate(far_places):
        if n < 7:
            remote(posbuf.at[PLANE], posbuf.at[seen_in_line(far_steps[n])], pos_sem.at[2], pos_sem.at[3],
                   line_at(far_steps[n])).start()
        remote(posbuf.at[0], posbuf.at[seen_in_plane(*spot)], pos_sem.at[2], pos_sem.at[3], plane_at(*spot)).start()
    wait_recv(z_mate, mate_sem.at[1])
    for axis in range(3):
        packed[0, axis] = jnp.where(keep, z_ref[axis], turn(z_mate[axis]))

    def gather(c, step):
        def to_line():
            for dz in STEPS[1:]:
                slot = seen_in_line(dz)
                remote(packed.at[step], ag.at[step, slot], ag_send.at[step], line_sem.at[step, (slot - PLANE) // 4],
                       line_at(dz)).start()

        def to_plane(some):
            for spot in ORDER:
                slot = seen_in_plane(*spot)
                if slot < NEEDED or not some:
                    remote(packed.at[step], ag.at[step, slot], ag_send.at[step], plane_sem.at[step, slot // 8],
                           plane_at(*spot)).start()

        if c == 0:
            to_line()
        if step == 2:
            to_plane(True)
        elif c == 1:
            to_plane(False)
        if c == 1 and step == 2:
            to_line()
        ag[step, 0] = packed[step]
        ag[step, PLANE] = packed[step]

    def wait_line(step, part_of):
        wait_recv(ag.at[step, pl.ds(0, 4 if part_of else 3)], line_sem.at[step, part_of])

    def wait_plane(step, part_of, last=False):
        if part_of == 0:
            wait_recv(ag.at[step, pl.ds(0, 7)], plane_sem.at[step, 0])
        else:
            wait_recv(ag.at[step, pl.ds(0, NEEDED - 8 if last else 8)], plane_sem.at[step, 1])

    for_each_core(lambda c: gather(c, 0))
    acc[...] = jnp.zeros_like(acc)
    acc_wide[...] = jnp.zeros_like(acc_wide)
    part[...] = jnp.zeros_like(part)
    ag[2, NEEDED:PLANE] = jnp.zeros((PLANE - NEEDED, 3, 32, 128), F32)
    for k in range(2):
        red_src[2 * k] = jnp.zeros((1, WIDTH), F32)
    narrow[...] = jnp.zeros_like(narrow)
    wait_recv(posbuf.at[pl.ds(0, 22)], pos_sem.at[3])

    lane_of = lax.broadcasted_iota(jnp.int32, (BLOCK, 128), 1)
    bead_of = lax.broadcasted_iota(jnp.int32, (BLOCK, 128), 0) & 31
    entry_of = lax.broadcasted_iota(jnp.int32, (128, BLOCK), 0)
    column_of = lax.broadcasted_iota(jnp.int32, (128, BLOCK), 1) & 31
    owner_of = lax.broadcasted_iota(jnp.int32, (16, BLOCK), 1) >> 5
    source_of = lax.broadcasted_iota(jnp.int32, (16, BLOCK), 0)
    ones = jnp.ones((128, 128), BF16)

    def place(at, d):
        return posbuf[at + d // 2][:, (d % 2) * 128:(d % 2) * 128 + 128]

    @pl.loop(0, 2)
    def _(h):
        rows_at = jnp.where(core == 0, h, 2) * 8
        lanes_at = jnp.where(core == 0, 2, h) * 8
        spread = jnp.concatenate([jnp.broadcast_to(place(rows_at, d), (32, 128)) for d in range(16)], axis=0)
        flat = jnp.concatenate([place(lanes_at, d) for d in range(16)], axis=0).astype(BF16)
        for axis in range(3):
            own = jnp.where(lane_of == axis * 32 + bead_of, spread, 0.0).astype(BF16)
            colbc[h, axis] = jnp.dot(own, ones, preferred_element_type=F32)
            pick = jnp.where(entry_of == axis * 32 + column_of, 1.0, 0.0).astype(BF16)
            moved = jnp.dot(flat, pick, preferred_element_type=F32)
            lanevec[h, axis:axis + 1, :] = jnp.sum(jnp.where(owner_of == source_of, moved, 0.0), axis=0, keepdims=True)

    def tile_of(c, t):
        return (4 - t) % 4 if c == 0 else 1 - t // 2

    def places(c, t):
        tile = tile_of(c, t)
        h, rt = (tile // 2, tile % 2) if c == 0 else (t % 2, tile)
        return h, c * h, rt * 256

    def build(c, t):
        h, _, begin = places(c, t)

        @pl.loop(0, 16, unroll=2)
        def _(r):
            rows = pl.ds(pl.multiple_of(begin + r * 16, 16), 16)
            mine = [colbc[h, axis, rows, :] for axis in range(3)]
            for tile in range(4):
                lanes = slice(tile * 128, tile * 128 + 128)
                d = [mine[axis] - lanevec[h, axis:axis + 1, lanes] for axis in range(3)]
                squared = d[0] * d[0] + d[1] * d[1] + d[2] * d[2]
                root = lax.rsqrt(jnp.where(squared > 0.5, squared, 1e30))
                inverse = root * root
                prefactor = (0.75 * RADIUS) * root
                iso = prefactor * (1.0 + (2.0 / 3.0 * RADIUS * RADIUS) * inverse)
                along = (prefactor * inverse) * (1.0 - (2.0 * RADIUS * RADIUS) * inverse)
                s = [along * d[axis] for axis in range(3)]
                parts = (s[0] * d[0] + iso, s[0] * d[1], s[0] * d[2], s[1] * d[1] + iso, s[1] * d[2],
                         s[2] * d[2] + iso)
                for k, value in enumerate(parts):
                    high = value.astype(BF16)
                    at = (tile // 2) * 1536 + k * 256 + (tile % 2) * 128
                    at = slice(at, at + 128)
                    mob_high[h, rows, at] = high
                    mob_low[h, rows, at] = (value - high.astype(F32)).astype(BF16)

    def widen(c, h):
        base = PLANE if c == 0 else h * 8

        @pl.loop(0, 8, unroll=4)
        def _(s):
            for axis in range(3):
                value = ag[0, base + s, axis]
                other = turn(value)
                for j, both in enumerate((jnp.where(first, value, other), jnp.where(first, other, value))):
                    high = both.astype(BF16).astype(F32)
                    tile = jnp.where(first, high, both - high).astype(BF16)
                    at = pl.ds(pl.multiple_of(s * 64 + j * 32, 32), 32)
                    wide[h, at, axis * 128:axis * 128 + 128] = tile
                    if axis == 0:
                        wide[h, at, 384:512] = tile

    def arrange(step, base, w, quarter, weight):
        @pl.loop(0, 4, unroll=4)
        def _(s):
            values = [ag[step, base + s, axis] * weight for axis in range(3)]
            others = [turn(value) for value in values]
            for j in range(2):
                left, right = (values, others) if j == 0 else (others, values)
                lx, ly, lz = (jnp.where(first, v, 0.0).astype(BF16) for v in left)
                ry, rz = (jnp.where(first, 0.0, v).astype(BF16) for v in right[1:])
                yx = jnp.where(first, left[1], right[0]).astype(BF16)
                for k, half, tile in ((0, 0, lx), (1, 0, yx), (2, 0, lz), (2, 1, lx), (3, 0, ry), (4, 0, rz),
                                      (4, 1, ly), (5, 1, lz)):
                    at = pl.ds(pl.multiple_of(quarter * 1536 + k * 256 + s * 64 + j * 32, 32), 32)
                    narrow[w, at, half * 128:half * 128 + 128] = tile

    def arrange_half(c, step, part_of):
        if c == 0:
            wait_line(step, part_of)
            arrange(step, PLANE + 4 * part_of, 0, part_of, 1.0)
        else:
            wait_plane(step, part_of, step == 2)
            for quarter in range(2):
                slot = 8 * part_of + 4 * quarter
                if step == 1 or slot < NEEDED:
                    arrange(step, slot, part_of, quarter, 2.0 if step == 2 and slot >= 4 else 1.0)

    def dot(left, right):
        return jnp.dot(left, right, preferred_element_type=F32)

    def product(c, t):
        h, w, begin = places(c, t)
        rows = slice(begin, begin + 256)

        def both(k, lo, hi):
            total = 0.0
            for quarter in range(2):
                at = slice(quarter * 1536 + k * 256, quarter * 1536 + k * 256 + 256)
                right = wide[w, quarter * 256:quarter * 256 + 256, lo:hi]
                total = total + dot(mob_high[h, rows, at], right) + dot(mob_low[h, rows, at], right)
            return total

        xy, yz, zx = both(1, 0, 256), both(4, 128, 384), both(2, 256, 512)
        return (both(0, 0, 128) + xy[:, 128:] + zx[:, :128],
                both(3, 128, 256) + xy[:, :128] + yz[:, 128:],
                both(5, 256, 384) + zx[:, 128:] + yz[:, :128])

    def halves(i, upper):
        return slice(i * 64 + upper * 32, i * 64 + upper * 32 + 32)

    def pack(_, i):
        chunk = []
        for axis in range(3):
            low, high = acc[axis, halves(i, 0), :], acc[axis, halves(i, 1), :]
            chunk.append(jnp.where(first, low + turn(low), high + turn(high)))
        return chunk

    def pack_wide(tile, i):
        low, high = halves(i, 0), halves(i, 1)
        xy_low, xy_high = acc_wide[tile, low, :128], acc_wide[tile, high, :128]
        z_low, z_high = acc_wide[tile, low, 128:], acc_wide[tile, high, 128:]
        return (jnp.where(first, xy_low, turn(xy_high)), jnp.where(first, turn(xy_low), xy_high),
                jnp.where(first, z_low, turn(z_high)))

    def scatter(c, step, t, packer):
        def fill(tile):
            chunks = [packer(tile, i) for i in range(4)]
            for i, chunk in enumerate(chunks):
                for axis, value in enumerate(chunk):
                    rs_send[step, tile * 4 + i, axis] = value

        def send_plane(tile):
            fill(tile)
            for i in (3, 2, 1, 0):
                spot = PLACES[tile * 4 + i]
                if tile * 4 + i:
                    remote(rs_send.at[step, tile * 4 + i], rs.at[step, seen_in_plane(*spot)], rs_sent.at[step],
                           rs_recv.at[step], plane_at(*spot)).start()
                else:
                    rs[step, 0] = rs_send[step, 0]

        def send_line(tile):
            fill(tile)
            for i in (3, 2, 1, 0):
                dz = STEPS[tile * 4 + i]
                if dz:
                    remote(rs_send.at[step, tile * 4 + i], rs.at[step, seen_in_line(dz) - PLANE], rs_sent.at[step],
                           rs_recv.at[step], line_at(dz)).start()
                else:
                    rs[step, 0] = rs_send[step, 0]

        (send_line if c else send_plane)(tile_of(c, t))

    def collect(c, step):
        count = LINE if c else PLANE
        wait_recv(rs.at[step, pl.ds(0, count - 1)], rs_recv.at[step])
        for axis in range(3):
            packed[step + 1, axis] = sum((rs[step, s, axis] for s in range(1, count)), rs[step, 0, axis])

    front = lax.broadcasted_iota(jnp.int32, (1, 128), 1) < HALF

    def fold(value):
        line = jnp.sum(value, axis=0, keepdims=True)
        return line + turn(line)

    def inner(left, right):
        return fold(sum(left[axis] * right[axis] for axis in range(3)))

    def reduce_plane(k, values):
        for n, value in values:
            red_src[2 * k, :, n * 128:n * 128 + 128] = value
        for spot in far_places:
            remote(red_src.at[2 * k], red_one.at[k, seen_in_plane(*spot)], red_sem.at[k, 0], red_sem.at[k, 1], plane_at(*spot)).start()
        red_one[k, 0] = red_src[2 * k]

    def reduce_line(k):
        def send(dz, device):
            slot = seen_in_line(dz) - PLANE
            remote(red_src.at[2 * k + 1], red_two.at[k, core, slot], red_sem.at[k, 2], red_sem.at[k, 3], device).start()

        wait_recv(red_one.at[k, pl.ds(0, PLANE - 1)], red_sem.at[k, 1])
        red_src[2 * k + 1] = sum((red_one[k, s] for s in range(1, PLANE)), red_one[k, 0])
        for dz in far_steps:
            send(dz, line_at(dz))
            if k == 1:
                send(dz, line_mate(dz))
        if k == 1:
            send(0, sibling)
        red_two[k, core, 0] = red_src[2 * k + 1]

    def reduced(k, c):
        return sum((red_two[k, c, s] for s in range(1, LINE)), red_two[k, c, 0])

    def steps(c):
        built = 4 if c else 2
        for t in range(built):
            build(c, t)
        if c == 0:
            wait_line(0, 0)
            wait_line(0, 1)
            widen(c, 0)
        else:
            wait_plane(0, 0)
            wait_plane(0, 1)
            widen(c, 0)
            widen(c, 1)
        for t in range(4):
            if t >= built:
                build(c, t)
            for axis, value in enumerate(product(c, t)):
                acc[axis] = acc[axis] + value if c == 1 and t % 2 == 1 else value
            if c == 0 or t % 2 == 1:
                scatter(c, 0, t, pack)
        collect(c, 0)
        gather(c, 1)
        reduce_plane(0, ((0, inner(packed.at[0], packed.at[0])), (1, inner(packed.at[0], packed.at[1]))))

        for step in (1, 2):
            for part_of in range(2):
                arrange_half(c, step, part_of)
                for t in range(4):
                    tile = tile_of(c, t)
                    quarter = t % 2 if c else part_of
                    if step == 2 and (tile == 3 if c == 0 else 8 * part_of + 4 * quarter >= NEEDED):
                        skip = True
                    else:
                        skip = False
                        h, rt = (part_of, tile) if c else (tile // 2, tile % 2)
                        inner_at = slice(quarter * 1536, quarter * 1536 + 1536)
                        value = dot(mob_high[h, rt * 256:rt * 256 + 256, inner_at], narrow[h if c else 0, inner_at, :])
                        begin = part_of == 0 and (c == 0 or t % 2 == 0)
                        acc_wide[tile] = value if begin else acc_wide[tile] + value
                    if part_of == 0 or (c == 1 and t % 2 == 0):
                        continue
                    if step == 1:
                        scatter(c, 1, t, pack_wide)
                        continue
                    if t == c:
                        for half in range(2):
                            wait_line(2, half) if c else wait_plane(2, half, True)
                    if c == 0 and skip:
                        continue
                    total = jnp.zeros((32, 128), F32)
                    for i in range(4):
                        for axis, value in enumerate(pack_wide(tile, i)):
                            total = total + value * ag[2, (PLANE if c else 0) + tile * 4 + i, axis]
                    part[...] += total * (2.0 if c == 0 and tile > 0 else 1.0)
            if step == 2:
                break
            reduce_line(0)
            collect(c, 1)
            wait_recv(red_two.at[0, 0, pl.ds(0, LINE - 1)], red_sem.at[0, 3])
            total = reduced(0, c)
            moments[0] = jnp.broadcast_to(total[:, 128:256] / total[:, 0:128], (32, 128))
            a1 = moments[0]
            for axis in range(3):
                y1 = packed[1, axis]
                packed[2, axis] = packed[2, axis] - a1 * y1
                first_dir[axis] = y1 - a1 * packed[0, axis]
            gather(c, 2)
            remote(first_dir, mate.at[0], mate_sem.at[2], mate_sem.at[3], sibling).start()
            remote(packed.at[2], mate.at[1], mate_sem.at[2], mate_sem.at[3], sibling).start()
            early = (red_src[0][:, 0:128], red_src[0][:, 128:256], inner(first_dir, first_dir),
                     inner(first_dir, packed.at[2]), inner(packed.at[2], packed.at[2]))
            for n, value in enumerate(early):
                red_src[2, :, n * 128:n * 128 + 128] = value

    for_each_core(steps)

    reduce_plane(1, ((5, fold(part[...])),))
    reduce_line(1)
    wait_recv(red_one.at[1, pl.ds(0, 2 * LINE - 1)], red_sem.at[1, 3])
    low, high = reduced(1, 0), reduced(1, 1)
    for k in range(6):
        at = slice(k * 128, k * 128 + 128)
        moments[k + 1, 0:8] = jnp.broadcast_to(jnp.where(front, low[:, at], high[:, at]), (8, 128))
    moments[7, 0:8] = jnp.zeros((8, 128), F32)
    moments[8, 0:8] = jnp.ones((8, 128), F32)
    m0, m1, e1, f1, g, third, zero, one = (moments[k, 0:8] for k in range(1, 9))

    a1, a2, bb2 = m1 / m0, f1 / e1, e1 / m0
    e2 = g - a2 * f1 - bb2 * e1
    bb3 = e2 / e1
    a3 = (third - a2 * g - bb2 * (f1 + a1 * e1)) / e2 - a2
    d1, d2, d3 = 1.0 + a1, 1.0 + a2, 1.0 + a3
    scale = (d1 + d2 + d3) / ITERS
    current = (d1 / scale, jnp.sqrt(bb2) / scale, zero, d2 / scale, jnp.sqrt(bb3) / scale, d3 / scale)
    partner = (one, zero, zero, one, zero, one)

    def inverse_three(m):
        c00, c01, c02 = m[3] * m[5] - m[4] * m[4], m[2] * m[4] - m[1] * m[5], m[1] * m[4] - m[2] * m[3]
        c11, c12, c22 = m[0] * m[5] - m[2] * m[2], m[1] * m[2] - m[0] * m[4], m[0] * m[3] - m[1] * m[1]
        over = 1.0 / (m[0] * c00 + m[1] * c01 + m[2] * c02)
        return tuple(c * over for c in (c00, c01, c02, c11, c12, c22))

    def newton(_, state):
        now, other = state
        return (tuple(0.5 * (u + v) for u, v in zip(now, inverse_three(other))),
                tuple(0.5 * (u + v) for u, v in zip(other, inverse_three(now))))

    current, partner = lax.fori_loop(0, 20, newton, (current, partner))
    size = jnp.sqrt(scale)
    beta = jnp.sqrt(m0)
    r1, r2, r3 = (current[k] * size for k in range(3))
    f2, f3 = beta * r2 / jnp.sqrt(e1), beta * r3 / jnp.sqrt(e2)
    wait_recv(mate, mate_sem.at[3])
    c0, c1, c2 = (jnp.concatenate([c, c, c, c], axis=0) for c in (r1 - f3 * bb2, f2 - f3 * a2, f3))
    for axis in range(3):
        out_ref[axis] = (c0 * z_ref[axis] + c1 * jnp.where(keep, first_dir[axis], turn(mate[0, axis]))
                         + c2 * jnp.where(keep, packed[2, axis], turn(mate[1, axis])))

    wait_send(posrow.at[0], pos_sem.at[0])
    wait_send(z_mate, mate_sem.at[0])
    wait_send(mate, mate_sem.at[2])
    wait_send(posbuf.at[pl.ds(0, 22)], pos_sem.at[2])
    wait_send(ag.at[2, pl.ds(0, NEEDED - 1 + LINE - 1)], ag_send.at[2])
    for k, count in enumerate((LINE - 1, 2 * LINE - 1)):
        wait_send(red_one.at[k, pl.ds(0, PLANE - 1)], red_sem.at[k, 0])
        wait_send(red_one.at[k, pl.ds(0, count)], red_sem.at[k, 2])
    for step in range(2):
        @pl.when(core == 0)
        def _(step=step):
            wait_send(ag.at[step, pl.ds(0, LINE - 1)], ag_send.at[step])
            wait_send(rs_send.at[step, pl.ds(0, PLANE - 1)], rs_sent.at[step])

        @pl.when(core == 1)
        def _(step=step):
            wait_send(ag.at[step, pl.ds(0, PLANE - 1)], ag_send.at[step])
            wait_send(rs_send.at[step, pl.ds(0, LINE - 1)], rs_sent.at[step])


def shards(positions, start_vector):
    chunk = (3, 32, 128)
    return pl.pallas_call(
        kernel,
        out_shape=jax.ShapeDtypeStruct(start_vector.shape, F32),
        in_specs=[pl.BlockSpec(memory_space=pltpu.VMEM)] * 2,
        out_specs=pl.BlockSpec(memory_space=pltpu.VMEM),
        scratch_shapes=[
            pltpu.VMEM((2, 1, 128), F32),
            pltpu.VMEM((PLANE + LINE, 1, 256), F32),
            pltpu.VMEM((2, 3, BLOCK, 128), F32),
            pltpu.VMEM((2, 8, BLOCK), F32),
            pltpu.VMEM((2, BLOCK, 6 * BLOCK), BF16),
            pltpu.VMEM((2, BLOCK, 6 * BLOCK), BF16),
            pltpu.VMEM((2, BLOCK, 512), BF16),
            pltpu.VMEM((2, 6 * BLOCK, 256), BF16),
            pltpu.VMEM((3, PLANE + LINE) + chunk, F32),
            pltpu.VMEM((2, PLANE) + chunk, F32),
            pltpu.VMEM((2, PLANE) + chunk, F32),
            pltpu.VMEM((3,) + chunk, F32),
            pltpu.VMEM(chunk, F32),
            pltpu.VMEM((2,) + chunk, F32),
            pltpu.VMEM((3, 256, 128), F32),
            pltpu.VMEM((4, 256, 256), F32),
            pltpu.VMEM((32, 128), F32),
            pltpu.VMEM((4, 1, WIDTH), F32),
            pltpu.VMEM((2, PLANE, 1, WIDTH), F32),
            pltpu.VMEM((2, 2, LINE, 1, WIDTH), F32),
            pltpu.VMEM((9, 32, 128), F32),
            pltpu.VMEM((8, 128), F32),
            pltpu.VMEM(chunk, F32),
            pltpu.SemaphoreType.DMA((4,)),
            pltpu.SemaphoreType.DMA((4,)),
            pltpu.SemaphoreType.DMA((3, 2)),
            pltpu.SemaphoreType.DMA((3, 2)),
            pltpu.SemaphoreType.DMA((3,)),
            pltpu.SemaphoreType.DMA((2,)),
            pltpu.SemaphoreType.DMA((2,)),
            pltpu.SemaphoreType.DMA((2, 4)),
        ],
        compiler_params=pltpu.CompilerParams(
            collective_id=0, has_side_effects=True, vmem_limit_bytes=40 * 1024 * 1024),
    )(positions, start_vector)


def solution(mesh):
    in_specs = (P(None, ("row", "col")), P(None, ("row", "col"), None))
    out_specs = P(None, ("row", "col"), None)
    return jax.shard_map(shards, mesh=mesh, in_specs=in_specs, out_specs=out_specs, check_vma=False)
```

```python
import functools

import jax
import jax.numpy as jnp
from jax import lax
from jax.experimental import pallas as pl
from jax.experimental.pallas import tpu as pltpu
from jax.sharding import PartitionSpec as P

ITERS = 3
RADIUS = 0.4
MESH = pl.DeviceIdType.MESH
F32 = jnp.float32
BF16 = jnp.bfloat16

PLANE, LINE = 16, 8
PLACES = ((0, 0), (2, 0), (0, 2), (2, 2), (0, 1), (3, 0), (1, 1), (1, 3), (3, 2), (2, 1),
          (0, 3), (1, 0), (3, 3), (3, 1), (1, 2), (2, 3))
NEEDED = 10
ORDER = ((0, 1), (0, 3), (1, 0), (3, 0), (2, 0), (0, 2), (1, 1), (3, 3), (1, 3), (3, 1),
         (1, 2), (2, 1), (3, 2), (2, 3), (2, 2))
STEPS = (0, 1, 7, 2, 6, 3, 5, 4)


def seen_in_plane(dx, dy):
    return PLACES.index((-dx % 4, -dy % 4))


def seen_in_line(dz):
    return PLANE + STEPS.index(-dz % 8)


HALF = 64
BLOCK = 512
WIDTH = 768


def kernel(pos_ref, z_ref, out_ref, posrow, posbuf, colbc, lanevec, mob_high, mob_low, wide, narrow, ag, rs, rs_send,
           packed, first_dir, mate, acc, acc_wide, part, red_src, red_one, red_two, moments, flatten,
           z_mate, halved, ag_first, first_sem, mate_sem, pos_sem, line_sem, plane_sem, ag_send, rs_recv, rs_sent, red_sem):
    row, col = lax.axis_index("row"), lax.axis_index("col")
    x, core = lax.div(row, 2), lax.rem(row, 2)
    z, y = lax.div(col, 4), lax.rem(col, 4)

    xs = [lax.rem(x + d, 4) for d in range(4)]
    ys = [lax.rem(y + d, 4) for d in range(4)]
    zs = [lax.rem(z + d, 8) for d in range(8)]

    def plane_at(dx, dy):
        return (xs[dx] * 2 + core, z * 4 + ys[dy])

    far_places, far_steps = PLACES[:0:-1], STEPS[:0:-1]

    def line_at(dz):
        return (row, zs[dz] * 4 + y)

    def plane_core(spot, c):
        return (xs[spot[0]] * 2 + c, z * 4 + ys[spot[1]])

    def line_core(dz, c):
        return (x * 2 + c, zs[dz] * 4 + y)

    def line_mate(dz):
        return (x * 2 + 1 - core, zs[dz] * 4 + y)

    sibling = (x * 2 + 1 - core, col)

    def for_each_core(program):
        for c in range(2):
            pl.when(core == c)(functools.partial(program, c))


    def remote(src, dst, send, recv, device):
        return pltpu.make_async_remote_copy(
            src_ref=src, dst_ref=dst, send_sem=send, recv_sem=recv, device_id=device, device_id_type=MESH)

    def wait_recv(ref, sem):
        remote(ref, ref, sem, sem, (row, col)).wait_recv()

    def wait_send(ref, sem):
        remote(ref, ref, sem, sem, (row, col)).wait_send()

    first = lax.broadcasted_iota(jnp.int32, (32, 128), 1) < HALF
    keep = first == (core == 0)

    def turn(value):
        return pltpu.roll(value, HALF, 1)

    barrier = pltpu.get_barrier_semaphore()

    def signal(device):
        pl.semaphore_signal(barrier, inc=1, device_id=device, device_id_type=MESH)

    signal(sibling)
    for spot in far_places:
        signal(plane_core(spot, 0))
        signal(plane_core(spot, 1))
    for dz in far_steps:
        signal(line_at(dz))
        signal(line_mate(dz))

    flatten[...] = jnp.zeros_like(flatten)
    flatten[0:3, 0:32] = pos_ref[...].astype(F32)
    rows3 = flatten[...]
    posrow[core] = rows3[0:1] + pltpu.roll(rows3[1:2], 32, 1) + pltpu.roll(rows3[2:3], 64, 1)
    for axis in range(3):
        low, high = z_ref[axis, :16, :], z_ref[axis, 16:, :]
        halved[0, axis] = jnp.where(first[:16], low, turn(high))
        halved[1, axis] = jnp.where(first[:16], turn(low), high)
    pl.semaphore_wait(barrier, 45)

    remote(posrow.at[core], posrow.at[core], pos_sem.at[0], pos_sem.at[1], sibling).start()
    remote(z_ref, z_mate, mate_sem.at[0], mate_sem.at[1], sibling).start()
    wait_recv(posrow.at[0], pos_sem.at[1])
    both = jnp.concatenate([posrow[0], posrow[1]], axis=1)
    posbuf[0] = both
    posbuf[PLANE] = both
    for n, spot in enumerate(far_places):
        if n < 7:
            remote(posbuf.at[PLANE], posbuf.at[seen_in_line(far_steps[n])], pos_sem.at[2], pos_sem.at[3],
                   line_at(far_steps[n])).start()
        remote(posbuf.at[0], posbuf.at[seen_in_plane(*spot)], pos_sem.at[2], pos_sem.at[3], plane_at(*spot)).start()

    for n, spot in enumerate(ORDER):
        if n < LINE - 1:
            dz = STEPS[n + 1]
            remote(halved.at[0], ag_first.at[2 * seen_in_line(dz) + core], first_sem.at[0], first_sem.at[1],
                   line_core(dz, 0)).start()
        remote(halved.at[1], ag_first.at[2 * seen_in_plane(*spot) + core], first_sem.at[0], first_sem.at[1],
               plane_core(spot, 1)).start()
    own_slot = jnp.where(core == 0, 2 * PLANE, 0) + core
    remote(halved.at[1 - core], ag_first.at[jnp.where(core == 0, 0, 2 * PLANE) + core], first_sem.at[0],
           first_sem.at[1], sibling).start()
    ag_first[own_slot] = halved[core]

    def gather(c, step):
        def to_line():
            for dz in STEPS[1:]:
                slot = seen_in_line(dz)
                remote(packed.at[step], ag.at[step, slot], ag_send.at[step], line_sem.at[step, (slot - PLANE) // 4],
                       line_at(dz)).start()

        def to_plane(some):
            for spot in ORDER:
                slot = seen_in_plane(*spot)
                if slot < NEEDED or not some:
                    remote(packed.at[step], ag.at[step, slot], ag_send.at[step], plane_sem.at[step, slot // 8],
                           plane_at(*spot)).start()

        if c == 0:
            to_line()
        if step == 2:
            to_plane(True)
        elif c == 1:
            to_plane(False)
        if c == 1 and step == 2:
            to_line()
        ag[step, 0] = packed[step]
        ag[step, PLANE] = packed[step]

    def wait_line(step, part_of):
        wait_recv(ag.at[step, pl.ds(0, 4 if part_of else 3)], line_sem.at[step, part_of])

    def wait_plane(step, part_of, last=False):
        if part_of == 0:
            wait_recv(ag.at[step, pl.ds(0, 7)], plane_sem.at[step, 0])
        else:
            wait_recv(ag.at[step, pl.ds(0, NEEDED - 8 if last else 8)], plane_sem.at[step, 1])

    acc[...] = jnp.zeros_like(acc)
    acc_wide[...] = jnp.zeros_like(acc_wide)
    part[...] = jnp.zeros_like(part)
    ag[2, NEEDED:PLANE] = jnp.zeros((PLANE - NEEDED, 3, 32, 128), F32)
    for k in range(2):
        red_src[2 * k] = jnp.zeros((1, WIDTH), F32)
    narrow[...] = jnp.zeros_like(narrow)
    wait_recv(posbuf.at[pl.ds(0, 22)], pos_sem.at[3])

    lane_of = lax.broadcasted_iota(jnp.int32, (BLOCK, 128), 1)
    bead_of = lax.broadcasted_iota(jnp.int32, (BLOCK, 128), 0) & 31
    entry_of = lax.broadcasted_iota(jnp.int32, (128, BLOCK), 0)
    column_of = lax.broadcasted_iota(jnp.int32, (128, BLOCK), 1) & 31
    owner_of = lax.broadcasted_iota(jnp.int32, (16, BLOCK), 1) >> 5
    source_of = lax.broadcasted_iota(jnp.int32, (16, BLOCK), 0)
    ones = jnp.ones((128, 128), BF16)

    def place(at, d):
        return posbuf[at + d // 2][:, (d % 2) * 128:(d % 2) * 128 + 128]

    @pl.loop(0, 2)
    def _(h):
        rows_at = jnp.where(core == 0, h, 2) * 8
        lanes_at = jnp.where(core == 0, 2, h) * 8
        spread = jnp.concatenate([jnp.broadcast_to(place(rows_at, d), (32, 128)) for d in range(16)], axis=0)
        flat = jnp.concatenate([place(lanes_at, d) for d in range(16)], axis=0).astype(BF16)
        for axis in range(3):
            own = jnp.where(lane_of == axis * 32 + bead_of, spread, 0.0).astype(BF16)
            colbc[h, axis] = jnp.dot(own, ones, preferred_element_type=F32)
            pick = jnp.where(entry_of == axis * 32 + column_of, 1.0, 0.0).astype(BF16)
            moved = jnp.dot(flat, pick, preferred_element_type=F32)
            lanevec[h, axis:axis + 1, :] = jnp.sum(jnp.where(owner_of == source_of, moved, 0.0), axis=0, keepdims=True)

    def tile_of(c, t):
        return (4 - t) % 4 if c == 0 else 1 - t // 2

    def places(c, t):
        tile = tile_of(c, t)
        h, rt = (tile // 2, tile % 2) if c == 0 else (t % 2, tile)
        return h, c * h, rt * 256

    def build(c, t):
        h, _, begin = places(c, t)

        @pl.loop(0, 16, unroll=2)
        def _(r):
            rows = pl.ds(pl.multiple_of(begin + r * 16, 16), 16)
            mine = [colbc[h, axis, rows, :] for axis in range(3)]
            for tile in range(4):
                lanes = slice(tile * 128, tile * 128 + 128)
                d = [mine[axis] - lanevec[h, axis:axis + 1, lanes] for axis in range(3)]
                squared = d[0] * d[0] + d[1] * d[1] + d[2] * d[2]
                root = lax.rsqrt(jnp.where(squared > 0.5, squared, 1e30))
                inverse = root * root
                prefactor = (0.75 * RADIUS) * root
                iso = prefactor * (1.0 + (2.0 / 3.0 * RADIUS * RADIUS) * inverse)
                along = (prefactor * inverse) * (1.0 - (2.0 * RADIUS * RADIUS) * inverse)
                s = [along * d[axis] for axis in range(3)]
                parts = (s[0] * d[0] + iso, s[0] * d[1], s[0] * d[2], s[1] * d[1] + iso, s[1] * d[2],
                         s[2] * d[2] + iso)
                for k, value in enumerate(parts):
                    high = value.astype(BF16)
                    at = (tile // 2) * 1536 + k * 256 + (tile % 2) * 128
                    at = slice(at, at + 128)
                    mob_high[h, rows, at] = high
                    mob_low[h, rows, at] = (value - high.astype(F32)).astype(BF16)

    def widen(c, h):
        base = 2 * PLANE if c == 0 else h * 16

        @pl.loop(0, 16, unroll=8)
        def _(s):
            for axis in range(3):
                value = ag_first[base + s, axis]
                other = turn(value)
                for j, both in enumerate((jnp.where(first[:16], value, other), jnp.where(first[:16], other, value))):
                    high = both.astype(BF16).astype(F32)
                    tile = jnp.where(first[:16], high, both - high).astype(BF16)
                    at = pl.ds(pl.multiple_of(s * 32 + j * 16, 16), 16)
                    wide[h, at, axis * 128:axis * 128 + 128] = tile
                    if axis == 0:
                        wide[h, at, 384:512] = tile

    def arrange(step, base, w, quarter, weight):
        @pl.loop(0, 4, unroll=4)
        def _(s):
            values = [ag[step, base + s, axis] * weight for axis in range(3)]
            others = [turn(value) for value in values]
            for j in range(2):
                left, right = (values, others) if j == 0 else (others, values)
                lx, ly, lz = (jnp.where(first, v, 0.0).astype(BF16) for v in left)
                ry, rz = (jnp.where(first, 0.0, v).astype(BF16) for v in right[1:])
                yx = jnp.where(first, left[1], right[0]).astype(BF16)
                for k, half, tile in ((0, 0, lx), (1, 0, yx), (2, 0, lz), (2, 1, lx), (3, 0, ry), (4, 0, rz),
                                      (4, 1, ly), (5, 1, lz)):
                    at = pl.ds(pl.multiple_of(quarter * 1536 + k * 256 + s * 64 + j * 32, 32), 32)
                    narrow[w, at, half * 128:half * 128 + 128] = tile

    def arrange_half(c, step, part_of):
        if c == 0:
            wait_line(step, part_of)
            arrange(step, PLANE + 4 * part_of, 0, part_of, 1.0)
        else:
            wait_plane(step, part_of, step == 2)
            for quarter in range(2):
                slot = 8 * part_of + 4 * quarter
                if step == 1 or slot < NEEDED:
                    arrange(step, slot, part_of, quarter, 2.0 if step == 2 and slot >= 4 else 1.0)

    def dot(left, right):
        return jnp.dot(left, right, preferred_element_type=F32)

    def product(c, t):
        h, w, begin = places(c, t)
        rows = slice(begin, begin + 256)

        def both(k, lo, hi):
            total = 0.0
            for quarter in range(2):
                at = slice(quarter * 1536 + k * 256, quarter * 1536 + k * 256 + 256)
                right = wide[w, quarter * 256:quarter * 256 + 256, lo:hi]
                total = total + dot(mob_high[h, rows, at], right) + dot(mob_low[h, rows, at], right)
            return total

        xy, yz, zx = both(1, 0, 256), both(4, 128, 384), both(2, 256, 512)
        return (both(0, 0, 128) + xy[:, 128:] + zx[:, :128],
                both(3, 128, 256) + xy[:, :128] + yz[:, 128:],
                both(5, 256, 384) + zx[:, 128:] + yz[:, :128])

    def halves(i, upper):
        return slice(i * 64 + upper * 32, i * 64 + upper * 32 + 32)

    def pack(_, i):
        chunk = []
        for axis in range(3):
            low, high = acc[axis, halves(i, 0), :], acc[axis, halves(i, 1), :]
            chunk.append(jnp.where(first, low + turn(low), high + turn(high)))
        return chunk

    def pack_wide(tile, i):
        low, high = halves(i, 0), halves(i, 1)
        xy_low, xy_high = acc_wide[tile, low, :128], acc_wide[tile, high, :128]
        z_low, z_high = acc_wide[tile, low, 128:], acc_wide[tile, high, 128:]
        return (jnp.where(first, xy_low, turn(xy_high)), jnp.where(first, turn(xy_low), xy_high),
                jnp.where(first, z_low, turn(z_high)))

    def scatter(c, step, t, packer):
        def fill(tile):
            chunks = [packer(tile, i) for i in range(4)]
            for i, chunk in enumerate(chunks):
                for axis, value in enumerate(chunk):
                    rs_send[step, tile * 4 + i, axis] = value

        def send_plane(tile):
            fill(tile)
            for i in (3, 2, 1, 0):
                spot = PLACES[tile * 4 + i]
                if tile * 4 + i:
                    remote(rs_send.at[step, tile * 4 + i], rs.at[step, seen_in_plane(*spot)], rs_sent.at[step],
                           rs_recv.at[step], plane_at(*spot)).start()
                else:
                    rs[step, 0] = rs_send[step, 0]

        def send_line(tile):
            fill(tile)
            for i in (3, 2, 1, 0):
                dz = STEPS[tile * 4 + i]
                if dz:
                    remote(rs_send.at[step, tile * 4 + i], rs.at[step, seen_in_line(dz) - PLANE], rs_sent.at[step],
                           rs_recv.at[step], line_at(dz)).start()
                else:
                    rs[step, 0] = rs_send[step, 0]

        (send_line if c else send_plane)(tile_of(c, t))

    def collect(c, step):
        count = LINE if c else PLANE
        wait_recv(rs.at[step, pl.ds(0, count - 1)], rs_recv.at[step])
        for axis in range(3):
            packed[step + 1, axis] = sum((rs[step, s, axis] for s in range(1, count)), rs[step, 0, axis])

    front = lax.broadcasted_iota(jnp.int32, (1, 128), 1) < HALF

    def fold(value):
        line = jnp.sum(value, axis=0, keepdims=True)
        return line + turn(line)

    def inner(left, right):
        return fold(sum(left[axis] * right[axis] for axis in range(3)))

    def reduce_plane(k, values):
        for n, value in values:
            red_src[2 * k, :, n * 128:n * 128 + 128] = value
        for spot in far_places:
            remote(red_src.at[2 * k], red_one.at[k, seen_in_plane(*spot)], red_sem.at[k, 0], red_sem.at[k, 1], plane_at(*spot)).start()
        red_one[k, 0] = red_src[2 * k]

    def reduce_line(k):
        def send(dz, device):
            slot = seen_in_line(dz) - PLANE
            remote(red_src.at[2 * k + 1], red_two.at[k, core, slot], red_sem.at[k, 2], red_sem.at[k, 3], device).start()

        wait_recv(red_one.at[k, pl.ds(0, PLANE - 1)], red_sem.at[k, 1])
        red_src[2 * k + 1] = sum((red_one[k, s] for s in range(1, PLANE)), red_one[k, 0])
        for dz in far_steps:
            send(dz, line_at(dz))
            if k == 1:
                send(dz, line_mate(dz))
        if k == 1:
            send(0, sibling)
        red_two[k, core, 0] = red_src[2 * k + 1]

    def reduced(k, c):
        return sum((red_two[k, c, s] for s in range(1, LINE)), red_two[k, c, 0])

    def steps(c):
        built = 4 if c else 2
        for t in range(built):
            build(c, t)
        wait_recv(ag_first.at[pl.ds(0, 2 * PLANE - 1 if c else 2 * LINE - 1)], first_sem.at[1])
        for h in range(1 + c):
            widen(c, h)
        for t in range(4):
            if t >= built:
                build(c, t)
            for axis, value in enumerate(product(c, t)):
                acc[axis] = acc[axis] + value if c == 1 and t % 2 == 1 else value
            if c == 0 or t % 2 == 1:
                scatter(c, 0, t, pack)
        wait_recv(z_mate, mate_sem.at[1])
        for axis in range(3):
            packed[0, axis] = jnp.where(keep, z_ref[axis], turn(z_mate[axis]))
        collect(c, 0)
        gather(c, 1)
        reduce_plane(0, ((0, inner(packed.at[0], packed.at[0])), (1, inner(packed.at[0], packed.at[1]))))

        for step in (1, 2):
            for part_of in range(2):
                arrange_half(c, step, part_of)
                for t in range(4):
                    tile = tile_of(c, t)
                    quarter = t % 2 if c else part_of
                    if step == 2 and (tile == 3 if c == 0 else 8 * part_of + 4 * quarter >= NEEDED):
                        skip = True
                    else:
                        skip = False
                        h, rt = (part_of, tile) if c else (tile // 2, tile % 2)
                        inner_at = slice(quarter * 1536, quarter * 1536 + 1536)
                        value = dot(mob_high[h, rt * 256:rt * 256 + 256, inner_at], narrow[h if c else 0, inner_at, :])
                        begin = part_of == 0 and (c == 0 or t % 2 == 0)
                        acc_wide[tile] = value if begin else acc_wide[tile] + value
                    if part_of == 0 or (c == 1 and t % 2 == 0):
                        continue
                    if step == 1:
                        scatter(c, 1, t, pack_wide)
                        continue
                    if t == c:
                        for half in range(2):
                            wait_line(2, half) if c else wait_plane(2, half, True)
                    if c == 0 and skip:
                        continue
                    total = jnp.zeros((32, 128), F32)
                    for i in range(4):
                        for axis, value in enumerate(pack_wide(tile, i)):
                            total = total + value * ag[2, (PLANE if c else 0) + tile * 4 + i, axis]
                    part[...] += total * (2.0 if c == 0 and tile > 0 else 1.0)
            if step == 2:
                break
            reduce_line(0)
            collect(c, 1)
            wait_recv(red_two.at[0, 0, pl.ds(0, LINE - 1)], red_sem.at[0, 3])
            total = reduced(0, c)
            moments[0] = jnp.broadcast_to(total[:, 128:256] / total[:, 0:128], (32, 128))
            a1 = moments[0]
            for axis in range(3):
                y1 = packed[1, axis]
                packed[2, axis] = packed[2, axis] - a1 * y1
                first_dir[axis] = y1 - a1 * packed[0, axis]
            gather(c, 2)
            remote(first_dir, mate.at[0], mate_sem.at[2], mate_sem.at[3], sibling).start()
            remote(packed.at[2], mate.at[1], mate_sem.at[2], mate_sem.at[3], sibling).start()
            early = (red_src[0][:, 0:128], red_src[0][:, 128:256], inner(first_dir, first_dir),
                     inner(first_dir, packed.at[2]), inner(packed.at[2], packed.at[2]))
            for n, value in enumerate(early):
                red_src[2, :, n * 128:n * 128 + 128] = value

    for_each_core(steps)

    reduce_plane(1, ((5, fold(part[...])),))
    reduce_line(1)
    wait_recv(red_one.at[1, pl.ds(0, 2 * LINE - 1)], red_sem.at[1, 3])
    low, high = reduced(1, 0), reduced(1, 1)
    for k in range(6):
        at = slice(k * 128, k * 128 + 128)
        moments[k + 1, 0:8] = jnp.broadcast_to(jnp.where(front, low[:, at], high[:, at]), (8, 128))
    moments[7, 0:8] = jnp.zeros((8, 128), F32)
    moments[8, 0:8] = jnp.ones((8, 128), F32)
    m0, m1, e1, f1, g, third, zero, one = (moments[k, 0:8] for k in range(1, 9))

    a1, a2, bb2 = m1 / m0, f1 / e1, e1 / m0
    e2 = g - a2 * f1 - bb2 * e1
    bb3 = e2 / e1
    a3 = (third - a2 * g - bb2 * (f1 + a1 * e1)) / e2 - a2
    d1, d2, d3 = 1.0 + a1, 1.0 + a2, 1.0 + a3
    scale = (d1 + d2 + d3) / ITERS
    current = (d1 / scale, jnp.sqrt(bb2) / scale, zero, d2 / scale, jnp.sqrt(bb3) / scale, d3 / scale)
    partner = (one, zero, zero, one, zero, one)

    def inverse_three(m):
        c00, c01, c02 = m[3] * m[5] - m[4] * m[4], m[2] * m[4] - m[1] * m[5], m[1] * m[4] - m[2] * m[3]
        c11, c12, c22 = m[0] * m[5] - m[2] * m[2], m[1] * m[2] - m[0] * m[4], m[0] * m[3] - m[1] * m[1]
        over = 1.0 / (m[0] * c00 + m[1] * c01 + m[2] * c02)
        return tuple(c * over for c in (c00, c01, c02, c11, c12, c22))

    def newton(_, state):
        now, other = state
        return (tuple(0.5 * (u + v) for u, v in zip(now, inverse_three(other))),
                tuple(0.5 * (u + v) for u, v in zip(other, inverse_three(now))))

    current, partner = lax.fori_loop(0, 20, newton, (current, partner))
    size = jnp.sqrt(scale)
    beta = jnp.sqrt(m0)
    r1, r2, r3 = (current[k] * size for k in range(3))
    f2, f3 = beta * r2 / jnp.sqrt(e1), beta * r3 / jnp.sqrt(e2)
    wait_recv(mate, mate_sem.at[3])
    c0, c1, c2 = (jnp.concatenate([c, c, c, c], axis=0) for c in (r1 - f3 * bb2, f2 - f3 * a2, f3))
    for axis in range(3):
        out_ref[axis] = (c0 * z_ref[axis] + c1 * jnp.where(keep, first_dir[axis], turn(mate[0, axis]))
                         + c2 * jnp.where(keep, packed[2, axis], turn(mate[1, axis])))

    wait_send(ag_first.at[pl.ds(0, PLANE + LINE - 1)], first_sem.at[0])
    wait_send(posrow.at[0], pos_sem.at[0])
    wait_send(z_mate, mate_sem.at[0])
    wait_send(mate, mate_sem.at[2])
    wait_send(posbuf.at[pl.ds(0, 22)], pos_sem.at[2])
    wait_send(ag.at[2, pl.ds(0, NEEDED - 1 + LINE - 1)], ag_send.at[2])
    for k, count in enumerate((LINE - 1, 2 * LINE - 1)):
        wait_send(red_one.at[k, pl.ds(0, PLANE - 1)], red_sem.at[k, 0])
        wait_send(red_one.at[k, pl.ds(0, count)], red_sem.at[k, 2])
    for step in range(2):
        @pl.when(core == 0)
        def _(step=step):
            if step == 1:
                wait_send(ag.at[step, pl.ds(0, LINE - 1)], ag_send.at[step])
            wait_send(rs_send.at[step, pl.ds(0, PLANE - 1)], rs_sent.at[step])

        @pl.when(core == 1)
        def _(step=step):
            if step == 1:
                wait_send(ag.at[step, pl.ds(0, PLANE - 1)], ag_send.at[step])
            wait_send(rs_send.at[step, pl.ds(0, LINE - 1)], rs_sent.at[step])


def shards(positions, start_vector):
    chunk = (3, 32, 128)
    return pl.pallas_call(
        kernel,
        out_shape=jax.ShapeDtypeStruct(start_vector.shape, F32),
        in_specs=[pl.BlockSpec(memory_space=pltpu.VMEM)] * 2,
        out_specs=pl.BlockSpec(memory_space=pltpu.VMEM),
        scratch_shapes=[
            pltpu.VMEM((2, 1, 128), F32),
            pltpu.VMEM((PLANE + LINE, 1, 256), F32),
            pltpu.VMEM((2, 3, BLOCK, 128), F32),
            pltpu.VMEM((2, 8, BLOCK), F32),
            pltpu.VMEM((2, BLOCK, 6 * BLOCK), BF16),
            pltpu.VMEM((2, BLOCK, 6 * BLOCK), BF16),
            pltpu.VMEM((2, BLOCK, 512), BF16),
            pltpu.VMEM((2, 6 * BLOCK, 256), BF16),
            pltpu.VMEM((3, PLANE + LINE) + chunk, F32),
            pltpu.VMEM((2, PLANE) + chunk, F32),
            pltpu.VMEM((2, PLANE) + chunk, F32),
            pltpu.VMEM((3,) + chunk, F32),
            pltpu.VMEM(chunk, F32),
            pltpu.VMEM((2,) + chunk, F32),
            pltpu.VMEM((3, 256, 128), F32),
            pltpu.VMEM((4, 256, 256), F32),
            pltpu.VMEM((32, 128), F32),
            pltpu.VMEM((4, 1, WIDTH), F32),
            pltpu.VMEM((2, PLANE, 1, WIDTH), F32),
            pltpu.VMEM((2, 2, LINE, 1, WIDTH), F32),
            pltpu.VMEM((9, 32, 128), F32),
            pltpu.VMEM((8, 128), F32),
            pltpu.VMEM(chunk, F32),
            pltpu.VMEM((2, 3, 16, 128), F32),
            pltpu.VMEM((2 * (PLANE + LINE), 3, 16, 128), F32),
            pltpu.SemaphoreType.DMA((2,)),
            pltpu.SemaphoreType.DMA((4,)),
            pltpu.SemaphoreType.DMA((4,)),
            pltpu.SemaphoreType.DMA((3, 2)),
            pltpu.SemaphoreType.DMA((3, 2)),
            pltpu.SemaphoreType.DMA((3,)),
            pltpu.SemaphoreType.DMA((2,)),
            pltpu.SemaphoreType.DMA((2,)),
            pltpu.SemaphoreType.DMA((2, 4)),
        ],
        compiler_params=pltpu.CompilerParams(
            collective_id=0, has_side_effects=True, vmem_limit_bytes=40 * 1024 * 1024),
    )(positions, start_vector)


def solution(mesh):
    in_specs = (P(None, ("row", "col")), P(None, ("row", "col"), None))
    out_specs = P(None, ("row", "col"), None)
    return jax.shard_map(shards, mesh=mesh, in_specs=in_specs, out_specs=out_specs, check_vma=False)
```

```python
import functools

import jax
import jax.numpy as jnp
from jax import lax
from jax.experimental import pallas as pl
from jax.experimental.pallas import tpu as pltpu
from jax.sharding import PartitionSpec as P

ITERS = 3
RADIUS = 0.4
MESH = pl.DeviceIdType.MESH
F32 = jnp.float32
BF16 = jnp.bfloat16

PLANE, LINE = 16, 8
PLACES = ((0, 0), (2, 0), (0, 2), (2, 2), (0, 1), (3, 0), (1, 1), (1, 3), (3, 2), (2, 1),
          (0, 3), (1, 0), (3, 3), (3, 1), (1, 2), (2, 3))
NEEDED = 10
ORDER = ((0, 1), (0, 3), (1, 0), (3, 0), (2, 0), (0, 2), (1, 1), (3, 3), (1, 3), (3, 1),
         (1, 2), (2, 1), (3, 2), (2, 3), (2, 2))
STEPS = (0, 1, 7, 2, 6, 3, 5, 4)


def seen_in_plane(dx, dy):
    return PLACES.index((-dx % 4, -dy % 4))


def seen_in_line(dz):
    return PLANE + STEPS.index(-dz % 8)


HALF = 64
BLOCK = 512
WIDTH = 768


def kernel(pos_ref, z_ref, out_ref, posrow, posbuf, colbc, lanevec, mob_high, mob_low, wide, narrow, ag, rs, rs_send,
           packed, first_dir, mate, acc, acc_wide, part, red_src, red_one, red_two, moments, flatten,
           z_mate, halved, ag_first, first_sem, mate_sem, pos_sem, line_sem, plane_sem, ag_send, rs_recv, rs_sent, red_sem):
    row, col = lax.axis_index("row"), lax.axis_index("col")
    x, core = lax.div(row, 2), lax.rem(row, 2)
    z, y = lax.div(col, 4), lax.rem(col, 4)

    xs = [lax.rem(x + d, 4) for d in range(4)]
    ys = [lax.rem(y + d, 4) for d in range(4)]
    zs = [lax.rem(z + d, 8) for d in range(8)]

    def plane_at(dx, dy):
        return (xs[dx] * 2 + core, z * 4 + ys[dy])

    far_places, far_steps = PLACES[:0:-1], STEPS[:0:-1]

    def line_at(dz):
        return (row, zs[dz] * 4 + y)

    def plane_core(spot, c):
        return (xs[spot[0]] * 2 + c, z * 4 + ys[spot[1]])

    def line_core(dz, c):
        return (x * 2 + c, zs[dz] * 4 + y)

    def line_mate(dz):
        return (x * 2 + 1 - core, zs[dz] * 4 + y)

    sibling = (x * 2 + 1 - core, col)

    def for_each_core(program):
        for c in range(2):
            pl.when(core == c)(functools.partial(program, c))


    def remote(src, dst, send, recv, device):
        return pltpu.make_async_remote_copy(
            src_ref=src, dst_ref=dst, send_sem=send, recv_sem=recv, device_id=device, device_id_type=MESH)

    def wait_recv(ref, sem):
        remote(ref, ref, sem, sem, (row, col)).wait_recv()

    def wait_send(ref, sem):
        remote(ref, ref, sem, sem, (row, col)).wait_send()

    first = lax.broadcasted_iota(jnp.int32, (32, 128), 1) < HALF
    keep = first == (core == 0)

    def turn(value):
        return pltpu.roll(value, HALF, 1)

    barrier = pltpu.get_barrier_semaphore()

    def signal(device):
        pl.semaphore_signal(barrier, inc=1, device_id=device, device_id_type=MESH)

    signal(sibling)
    for spot in far_places:
        signal(plane_core(spot, 0))
        signal(plane_core(spot, 1))
    for dz in far_steps:
        signal(line_at(dz))
        signal(line_mate(dz))

    flatten[...] = jnp.zeros_like(flatten)
    flatten[0:3, 0:32] = pos_ref[...].astype(F32)
    rows3 = flatten[...]
    posrow[core] = rows3[0:1] + pltpu.roll(rows3[1:2], 32, 1) + pltpu.roll(rows3[2:3], 64, 1)
    for axis in range(3):
        low, high = z_ref[axis, :16, :], z_ref[axis, 16:, :]
        halved[0, axis] = jnp.where(first[:16], low, turn(high))
        halved[1, axis] = jnp.where(first[:16], turn(low), high)
    pl.semaphore_wait(barrier, 45)

    remote(posrow.at[core], posrow.at[core], pos_sem.at[0], pos_sem.at[1], sibling).start()
    remote(z_ref, z_mate, mate_sem.at[0], mate_sem.at[1], sibling).start()
    wait_recv(posrow.at[0], pos_sem.at[1])
    both = jnp.concatenate([posrow[0], posrow[1]], axis=1)
    posbuf[0] = both
    posbuf[PLANE] = both
    for n, spot in enumerate(far_places):
        if n < 7:
            remote(posbuf.at[PLANE], posbuf.at[seen_in_line(far_steps[n])], pos_sem.at[2], pos_sem.at[3],
                   line_at(far_steps[n])).start()
        remote(posbuf.at[0], posbuf.at[seen_in_plane(*spot)], pos_sem.at[2], pos_sem.at[3], plane_at(*spot)).start()

    for n, spot in enumerate(ORDER):
        if n < LINE - 1:
            dz = STEPS[n + 1]
            remote(halved.at[0], ag_first.at[2 * seen_in_line(dz) + core], first_sem.at[0], first_sem.at[1],
                   line_core(dz, 0)).start()
        remote(halved.at[1], ag_first.at[2 * seen_in_plane(*spot) + core], first_sem.at[0], first_sem.at[1],
               plane_core(spot, 1)).start()
    own_slot = jnp.where(core == 0, 2 * PLANE, 0) + core
    remote(halved.at[1 - core], ag_first.at[jnp.where(core == 0, 0, 2 * PLANE) + core], first_sem.at[0],
           first_sem.at[1], sibling).start()
    ag_first[own_slot] = halved[core]

    def gather(c, step):
        def to_line():
            for dz in STEPS[1:]:
                slot = seen_in_line(dz)
                remote(packed.at[step], ag.at[step, slot], ag_send.at[step], line_sem.at[step, (slot - PLANE) // 4],
                       line_at(dz)).start()

        def to_plane(some):
            for spot in ORDER:
                slot = seen_in_plane(*spot)
                if slot < NEEDED or not some:
                    remote(packed.at[step], ag.at[step, slot], ag_send.at[step], plane_sem.at[step, slot // 8],
                           plane_at(*spot)).start()

        if c == 0:
            to_line()
        if step == 2:
            to_plane(True)
        elif c == 1:
            to_plane(False)
        if c == 1 and step == 2:
            to_line()
        ag[step, 0] = packed[step]
        ag[step, PLANE] = packed[step]

    def wait_line(step, part_of):
        wait_recv(ag.at[step, pl.ds(0, 4 if part_of else 3)], line_sem.at[step, part_of])

    def wait_plane(step, part_of, last=False):
        if part_of == 0:
            wait_recv(ag.at[step, pl.ds(0, 7)], plane_sem.at[step, 0])
        else:
            wait_recv(ag.at[step, pl.ds(0, NEEDED - 8 if last else 8)], plane_sem.at[step, 1])

    acc[...] = jnp.zeros_like(acc)
    acc_wide[...] = jnp.zeros_like(acc_wide)
    part[...] = jnp.zeros_like(part)
    ag[2, NEEDED:PLANE] = jnp.zeros((PLANE - NEEDED, 3, 32, 128), F32)
    for k in range(2):
        red_src[2 * k] = jnp.zeros((1, WIDTH), F32)
    narrow[...] = jnp.zeros_like(narrow)
    wait_recv(posbuf.at[pl.ds(0, 22)], pos_sem.at[3])

    lane_of = lax.broadcasted_iota(jnp.int32, (BLOCK, 128), 1)
    bead_of = lax.broadcasted_iota(jnp.int32, (BLOCK, 128), 0) & 31
    entry_of = lax.broadcasted_iota(jnp.int32, (128, BLOCK), 0)
    column_of = lax.broadcasted_iota(jnp.int32, (128, BLOCK), 1) & 31
    owner_of = lax.broadcasted_iota(jnp.int32, (16, BLOCK), 1) >> 5
    source_of = lax.broadcasted_iota(jnp.int32, (16, BLOCK), 0)
    ones = jnp.ones((128, 128), BF16)

    def place(at, d):
        return posbuf[at + d // 2][:, (d % 2) * 128:(d % 2) * 128 + 128]

    @pl.loop(0, 2)
    def _(h):
        rows_at = jnp.where(core == 0, h, 2) * 8
        lanes_at = jnp.where(core == 0, 2, h) * 8
        spread = jnp.concatenate([jnp.broadcast_to(place(rows_at, d), (32, 128)) for d in range(16)], axis=0)
        flat = jnp.concatenate([place(lanes_at, d) for d in range(16)], axis=0).astype(BF16)
        for axis in range(3):
            own = jnp.where(lane_of == axis * 32 + bead_of, spread, 0.0).astype(BF16)
            colbc[h, axis] = jnp.dot(own, ones, preferred_element_type=F32)
            pick = jnp.where(entry_of == axis * 32 + column_of, 1.0, 0.0).astype(BF16)
            moved = jnp.dot(flat, pick, preferred_element_type=F32)
            lanevec[h, axis:axis + 1, :] = jnp.sum(jnp.where(owner_of == source_of, moved, 0.0), axis=0, keepdims=True)

    def tile_of(c, t):
        return (4 - t) % 4 if c == 0 else 1 - t // 2

    def places(c, t):
        tile = tile_of(c, t)
        h, rt = (tile // 2, tile % 2) if c == 0 else (t % 2, tile)
        return h, c * h, rt * 256

    def build(c, t):
        h, _, begin = places(c, t)

        @pl.loop(0, 16, unroll=4)
        def _(r):
            rows = pl.ds(pl.multiple_of(begin + r * 16, 16), 16)
            mine = [colbc[h, axis, rows, :] for axis in range(3)]
            for tile in range(4):
                lanes = slice(tile * 128, tile * 128 + 128)
                d = [mine[axis] - lanevec[h, axis:axis + 1, lanes] for axis in range(3)]
                squared = d[0] * d[0] + d[1] * d[1] + d[2] * d[2]
                root = lax.rsqrt(jnp.where(squared > 0.5, squared, 1e30))
                inverse = root * root
                prefactor = (0.75 * RADIUS) * root
                iso = prefactor * (1.0 + (2.0 / 3.0 * RADIUS * RADIUS) * inverse)
                along = (prefactor * inverse) * (1.0 - (2.0 * RADIUS * RADIUS) * inverse)
                s = [along * d[axis] for axis in range(3)]
                parts = (s[0] * d[0] + iso, s[0] * d[1], s[0] * d[2], s[1] * d[1] + iso, s[1] * d[2],
                         s[2] * d[2] + iso)
                for k, value in enumerate(parts):
                    high = value.astype(BF16)
                    at = (tile // 2) * 1536 + k * 256 + (tile % 2) * 128
                    at = slice(at, at + 128)
                    mob_high[h, rows, at] = high
                    mob_low[h, rows, at] = (value - high.astype(F32)).astype(BF16)

    def widen(c, h):
        base = 2 * PLANE if c == 0 else h * 16

        @pl.loop(0, 16, unroll=8)
        def _(s):
            for axis in range(3):
                value = ag_first[base + s, axis]
                other = turn(value)
                for j, both in enumerate((jnp.where(first[:16], value, other), jnp.where(first[:16], other, value))):
                    high = both.astype(BF16).astype(F32)
                    tile = jnp.where(first[:16], high, both - high).astype(BF16)
                    at = pl.ds(pl.multiple_of(s * 32 + j * 16, 16), 16)
                    wide[h, at, axis * 128:axis * 128 + 128] = tile
                    if axis == 0:
                        wide[h, at, 384:512] = tile

    def arrange(step, base, w, quarter, weight):
        @pl.loop(0, 4, unroll=4)
        def _(s):
            values = [ag[step, base + s, axis] * weight for axis in range(3)]
            others = [turn(value) for value in values]
            for j in range(2):
                left, right = (values, others) if j == 0 else (others, values)
                lx, ly, lz = (jnp.where(first, v, 0.0).astype(BF16) for v in left)
                ry, rz = (jnp.where(first, 0.0, v).astype(BF16) for v in right[1:])
                yx = jnp.where(first, left[1], right[0]).astype(BF16)
                for k, half, tile in ((0, 0, lx), (1, 0, yx), (2, 0, lz), (2, 1, lx), (3, 0, ry), (4, 0, rz),
                                      (4, 1, ly), (5, 1, lz)):
                    at = pl.ds(pl.multiple_of(quarter * 1536 + k * 256 + s * 64 + j * 32, 32), 32)
                    narrow[w, at, half * 128:half * 128 + 128] = tile

    def arrange_half(c, step, part_of):
        if c == 0:
            wait_line(step, part_of)
            arrange(step, PLANE + 4 * part_of, 0, part_of, 1.0)
        else:
            wait_plane(step, part_of, step == 2)
            for quarter in range(2):
                slot = 8 * part_of + 4 * quarter
                if step == 1 or slot < NEEDED:
                    arrange(step, slot, part_of, quarter, 2.0 if step == 2 and slot >= 4 else 1.0)

    def dot(left, right):
        return jnp.dot(left, right, preferred_element_type=F32)

    def product(c, t):
        h, w, begin = places(c, t)
        rows = slice(begin, begin + 256)

        def both(k, lo, hi):
            total = 0.0
            for quarter in range(2):
                at = slice(quarter * 1536 + k * 256, quarter * 1536 + k * 256 + 256)
                right = wide[w, quarter * 256:quarter * 256 + 256, lo:hi]
                total = total + dot(mob_high[h, rows, at], right) + dot(mob_low[h, rows, at], right)
            return total

        xy, yz, zx = both(1, 0, 256), both(4, 128, 384), both(2, 256, 512)
        return (both(0, 0, 128) + xy[:, 128:] + zx[:, :128],
                both(3, 128, 256) + xy[:, :128] + yz[:, 128:],
                both(5, 256, 384) + zx[:, 128:] + yz[:, :128])

    def halves(i, upper):
        return slice(i * 64 + upper * 32, i * 64 + upper * 32 + 32)

    def pack(_, i):
        chunk = []
        for axis in range(3):
            low, high = acc[axis, halves(i, 0), :], acc[axis, halves(i, 1), :]
            chunk.append(jnp.where(first, low + turn(low), high + turn(high)))
        return chunk

    def pack_wide(tile, i):
        low, high = halves(i, 0), halves(i, 1)
        xy_low, xy_high = acc_wide[tile, low, :128], acc_wide[tile, high, :128]
        z_low, z_high = acc_wide[tile, low, 128:], acc_wide[tile, high, 128:]
        return (jnp.where(first, xy_low, turn(xy_high)), jnp.where(first, turn(xy_low), xy_high),
                jnp.where(first, z_low, turn(z_high)))

    def scatter(c, step, t, packer):
        def fill(tile):
            chunks = [packer(tile, i) for i in range(4)]
            for i, chunk in enumerate(chunks):
                for axis, value in enumerate(chunk):
                    rs_send[step, tile * 4 + i, axis] = value

        def send_plane(tile):
            fill(tile)
            for i in (3, 2, 1, 0):
                spot = PLACES[tile * 4 + i]
                if tile * 4 + i:
                    remote(rs_send.at[step, tile * 4 + i], rs.at[step, seen_in_plane(*spot)], rs_sent.at[step],
                           rs_recv.at[step], plane_at(*spot)).start()
                else:
                    rs[step, 0] = rs_send[step, 0]

        def send_line(tile):
            fill(tile)
            for i in (3, 2, 1, 0):
                dz = STEPS[tile * 4 + i]
                if dz:
                    remote(rs_send.at[step, tile * 4 + i], rs.at[step, seen_in_line(dz) - PLANE], rs_sent.at[step],
                           rs_recv.at[step], line_at(dz)).start()
                else:
                    rs[step, 0] = rs_send[step, 0]

        (send_line if c else send_plane)(tile_of(c, t))

    def collect(c, step):
        count = LINE if c else PLANE
        wait_recv(rs.at[step, pl.ds(0, count - 1)], rs_recv.at[step])
        for axis in range(3):
            packed[step + 1, axis] = sum((rs[step, s, axis] for s in range(1, count)), rs[step, 0, axis])

    front = lax.broadcasted_iota(jnp.int32, (1, 128), 1) < HALF

    def fold(value):
        line = jnp.sum(value, axis=0, keepdims=True)
        return line + turn(line)

    def inner(left, right):
        return fold(sum(left[axis] * right[axis] for axis in range(3)))

    def reduce_plane(k, values):
        for n, value in values:
            red_src[2 * k, :, n * 128:n * 128 + 128] = value
        for spot in far_places:
            remote(red_src.at[2 * k], red_one.at[k, seen_in_plane(*spot)], red_sem.at[k, 0], red_sem.at[k, 1], plane_at(*spot)).start()
        red_one[k, 0] = red_src[2 * k]

    def reduce_line(k):
        def send(dz, device):
            slot = seen_in_line(dz) - PLANE
            remote(red_src.at[2 * k + 1], red_two.at[k, core, slot], red_sem.at[k, 2], red_sem.at[k, 3], device).start()

        wait_recv(red_one.at[k, pl.ds(0, PLANE - 1)], red_sem.at[k, 1])
        red_src[2 * k + 1] = sum((red_one[k, s] for s in range(1, PLANE)), red_one[k, 0])
        for dz in far_steps:
            send(dz, line_at(dz))
            if k == 1:
                send(dz, line_mate(dz))
        if k == 1:
            send(0, sibling)
        red_two[k, core, 0] = red_src[2 * k + 1]

    def reduced(k, c):
        return sum((red_two[k, c, s] for s in range(1, LINE)), red_two[k, c, 0])

    def steps(c):
        for t in range(4):
            build(c, t)
        wait_recv(ag_first.at[pl.ds(0, 2 * PLANE - 1 if c else 2 * LINE - 1)], first_sem.at[1])
        for h in range(1 + c):
            widen(c, h)
        for t in range(4):
            for axis, value in enumerate(product(c, t)):
                acc[axis] = acc[axis] + value if c == 1 and t % 2 == 1 else value
            if c == 0 or t % 2 == 1:
                scatter(c, 0, t, pack)
        wait_recv(z_mate, mate_sem.at[1])
        for axis in range(3):
            packed[0, axis] = jnp.where(keep, z_ref[axis], turn(z_mate[axis]))
        collect(c, 0)
        gather(c, 1)
        reduce_plane(0, ((0, inner(packed.at[0], packed.at[0])), (1, inner(packed.at[0], packed.at[1]))))

        for step in (1, 2):
            for part_of in range(2):
                arrange_half(c, step, part_of)
                for t in range(4):
                    tile = tile_of(c, t)
                    quarter = t % 2 if c else part_of
                    if step == 2 and (tile == 3 if c == 0 else 8 * part_of + 4 * quarter >= NEEDED):
                        skip = True
                    else:
                        skip = False
                        h, rt = (part_of, tile) if c else (tile // 2, tile % 2)
                        inner_at = slice(quarter * 1536, quarter * 1536 + 1536)
                        value = dot(mob_high[h, rt * 256:rt * 256 + 256, inner_at], narrow[h if c else 0, inner_at, :])
                        begin = part_of == 0 and (c == 0 or t % 2 == 0)
                        acc_wide[tile] = value if begin else acc_wide[tile] + value
                    if part_of == 0 or (c == 1 and t % 2 == 0):
                        continue
                    if step == 1:
                        scatter(c, 1, t, pack_wide)
                        continue
                    if t == c:
                        for half in range(2):
                            wait_line(2, half) if c else wait_plane(2, half, True)
                    if c == 0 and skip:
                        continue
                    total = jnp.zeros((32, 128), F32)
                    for i in range(4):
                        for axis, value in enumerate(pack_wide(tile, i)):
                            total = total + value * ag[2, (PLANE if c else 0) + tile * 4 + i, axis]
                    part[...] += total * (2.0 if c == 0 and tile > 0 else 1.0)
            if step == 2:
                break
            reduce_line(0)
            collect(c, 1)
            wait_recv(red_two.at[0, 0, pl.ds(0, LINE - 1)], red_sem.at[0, 3])
            total = reduced(0, c)
            moments[0] = jnp.broadcast_to(total[:, 128:256] / total[:, 0:128], (32, 128))
            a1 = moments[0]
            for axis in range(3):
                y1 = packed[1, axis]
                packed[2, axis] = packed[2, axis] - a1 * y1
                first_dir[axis] = y1 - a1 * packed[0, axis]
            gather(c, 2)
            remote(first_dir, mate.at[0], mate_sem.at[2], mate_sem.at[3], sibling).start()
            remote(packed.at[2], mate.at[1], mate_sem.at[2], mate_sem.at[3], sibling).start()
            early = (red_src[0][:, 0:128], red_src[0][:, 128:256], inner(first_dir, first_dir),
                     inner(first_dir, packed.at[2]), inner(packed.at[2], packed.at[2]))
            for n, value in enumerate(early):
                red_src[2, :, n * 128:n * 128 + 128] = value

    for_each_core(steps)

    reduce_plane(1, ((5, fold(part[...])),))
    reduce_line(1)
    wait_recv(red_one.at[1, pl.ds(0, 2 * LINE - 1)], red_sem.at[1, 3])
    low, high = reduced(1, 0), reduced(1, 1)
    for k in range(6):
        at = slice(k * 128, k * 128 + 128)
        moments[k + 1, 0:8] = jnp.broadcast_to(jnp.where(front, low[:, at], high[:, at]), (8, 128))
    moments[7, 0:8] = jnp.zeros((8, 128), F32)
    moments[8, 0:8] = jnp.ones((8, 128), F32)
    m0, m1, e1, f1, g, third, zero, one = (moments[k, 0:8] for k in range(1, 9))

    a1, a2, bb2 = m1 / m0, f1 / e1, e1 / m0
    e2 = g - a2 * f1 - bb2 * e1
    bb3 = e2 / e1
    a3 = (third - a2 * g - bb2 * (f1 + a1 * e1)) / e2 - a2
    d1, d2, d3 = 1.0 + a1, 1.0 + a2, 1.0 + a3
    scale = (d1 + d2 + d3) / ITERS
    current = (d1 / scale, jnp.sqrt(bb2) / scale, zero, d2 / scale, jnp.sqrt(bb3) / scale, d3 / scale)
    partner = (one, zero, zero, one, zero, one)

    def inverse_three(m):
        c00, c01, c02 = m[3] * m[5] - m[4] * m[4], m[2] * m[4] - m[1] * m[5], m[1] * m[4] - m[2] * m[3]
        c11, c12, c22 = m[0] * m[5] - m[2] * m[2], m[1] * m[2] - m[0] * m[4], m[0] * m[3] - m[1] * m[1]
        over = 1.0 / (m[0] * c00 + m[1] * c01 + m[2] * c02)
        return tuple(c * over for c in (c00, c01, c02, c11, c12, c22))

    def newton(_, state):
        now, other = state
        return (tuple(0.5 * (u + v) for u, v in zip(now, inverse_three(other))),
                tuple(0.5 * (u + v) for u, v in zip(other, inverse_three(now))))

    current, partner = lax.fori_loop(0, 20, newton, (current, partner))
    size = jnp.sqrt(scale)
    beta = jnp.sqrt(m0)
    r1, r2, r3 = (current[k] * size for k in range(3))
    f2, f3 = beta * r2 / jnp.sqrt(e1), beta * r3 / jnp.sqrt(e2)
    wait_recv(mate, mate_sem.at[3])
    c0, c1, c2 = (jnp.concatenate([c, c, c, c], axis=0) for c in (r1 - f3 * bb2, f2 - f3 * a2, f3))
    for axis in range(3):
        out_ref[axis] = (c0 * z_ref[axis] + c1 * jnp.where(keep, first_dir[axis], turn(mate[0, axis]))
                         + c2 * jnp.where(keep, packed[2, axis], turn(mate[1, axis])))

    wait_send(ag_first.at[pl.ds(0, PLANE + LINE - 1)], first_sem.at[0])
    wait_send(posrow.at[0], pos_sem.at[0])
    wait_send(z_mate, mate_sem.at[0])
    wait_send(mate, mate_sem.at[2])
    wait_send(posbuf.at[pl.ds(0, 22)], pos_sem.at[2])
    wait_send(ag.at[2, pl.ds(0, NEEDED - 1 + LINE - 1)], ag_send.at[2])
    for k, count in enumerate((LINE - 1, 2 * LINE - 1)):
        wait_send(red_one.at[k, pl.ds(0, PLANE - 1)], red_sem.at[k, 0])
        wait_send(red_one.at[k, pl.ds(0, count)], red_sem.at[k, 2])
    for step in range(2):
        @pl.when(core == 0)
        def _(step=step):
            if step == 1:
                wait_send(ag.at[step, pl.ds(0, LINE - 1)], ag_send.at[step])
            wait_send(rs_send.at[step, pl.ds(0, PLANE - 1)], rs_sent.at[step])

        @pl.when(core == 1)
        def _(step=step):
            if step == 1:
                wait_send(ag.at[step, pl.ds(0, PLANE - 1)], ag_send.at[step])
            wait_send(rs_send.at[step, pl.ds(0, LINE - 1)], rs_sent.at[step])


def shards(positions, start_vector):
    chunk = (3, 32, 128)
    return pl.pallas_call(
        kernel,
        out_shape=jax.ShapeDtypeStruct(start_vector.shape, F32),
        in_specs=[pl.BlockSpec(memory_space=pltpu.VMEM)] * 2,
        out_specs=pl.BlockSpec(memory_space=pltpu.VMEM),
        scratch_shapes=[
            pltpu.VMEM((2, 1, 128), F32),
            pltpu.VMEM((PLANE + LINE, 1, 256), F32),
            pltpu.VMEM((2, 3, BLOCK, 128), F32),
            pltpu.VMEM((2, 8, BLOCK), F32),
            pltpu.VMEM((2, BLOCK, 6 * BLOCK), BF16),
            pltpu.VMEM((2, BLOCK, 6 * BLOCK), BF16),
            pltpu.VMEM((2, BLOCK, 512), BF16),
            pltpu.VMEM((2, 6 * BLOCK, 256), BF16),
            pltpu.VMEM((3, PLANE + LINE) + chunk, F32),
            pltpu.VMEM((2, PLANE) + chunk, F32),
            pltpu.VMEM((2, PLANE) + chunk, F32),
            pltpu.VMEM((3,) + chunk, F32),
            pltpu.VMEM(chunk, F32),
            pltpu.VMEM((2,) + chunk, F32),
            pltpu.VMEM((3, 256, 128), F32),
            pltpu.VMEM((4, 256, 256), F32),
            pltpu.VMEM((32, 128), F32),
            pltpu.VMEM((4, 1, WIDTH), F32),
            pltpu.VMEM((2, PLANE, 1, WIDTH), F32),
            pltpu.VMEM((2, 2, LINE, 1, WIDTH), F32),
            pltpu.VMEM((9, 32, 128), F32),
            pltpu.VMEM((8, 128), F32),
            pltpu.VMEM(chunk, F32),
            pltpu.VMEM((2, 3, 16, 128), F32),
            pltpu.VMEM((2 * (PLANE + LINE), 3, 16, 128), F32),
            pltpu.SemaphoreType.DMA((2,)),
            pltpu.SemaphoreType.DMA((4,)),
            pltpu.SemaphoreType.DMA((4,)),
            pltpu.SemaphoreType.DMA((3, 2)),
            pltpu.SemaphoreType.DMA((3, 2)),
            pltpu.SemaphoreType.DMA((3,)),
            pltpu.SemaphoreType.DMA((2,)),
            pltpu.SemaphoreType.DMA((2,)),
            pltpu.SemaphoreType.DMA((2, 4)),
        ],
        compiler_params=pltpu.CompilerParams(
            collective_id=0, has_side_effects=True, vmem_limit_bytes=40 * 1024 * 1024),
    )(positions, start_vector)


def solution(mesh):
    in_specs = (P(None, ("row", "col")), P(None, ("row", "col"), None))
    out_specs = P(None, ("row", "col"), None)
    return jax.shard_map(shards, mesh=mesh, in_specs=in_specs, out_specs=out_specs, check_vma=False)
```

```python
import functools

import jax
import jax.numpy as jnp
from jax import lax
from jax.experimental import pallas as pl
from jax.experimental.pallas import tpu as pltpu
from jax.sharding import PartitionSpec as P

ITERS = 3
RADIUS = 0.4
MESH = pl.DeviceIdType.MESH
F32 = jnp.float32
BF16 = jnp.bfloat16

PLANE, LINE = 16, 8
PLACES = ((0, 0), (2, 0), (0, 2), (2, 2), (0, 1), (3, 0), (1, 1), (1, 3), (3, 2), (2, 1),
          (0, 3), (1, 0), (3, 3), (3, 1), (1, 2), (2, 3))
NEEDED = 10
ORDER = ((0, 1), (0, 3), (1, 0), (3, 0), (2, 0), (0, 2), (1, 1), (3, 3), (1, 3), (3, 1),
         (1, 2), (2, 1), (3, 2), (2, 3), (2, 2))
STEPS = (0, 1, 7, 2, 6, 3, 5, 4)


def seen_in_plane(dx, dy):
    return PLACES.index((-dx % 4, -dy % 4))


def seen_in_line(dz):
    return PLANE + STEPS.index(-dz % 8)


HALF = 64
BLOCK = 512
WIDTH = 768


def kernel(pos_ref, z_ref, out_ref, posrow, posbuf, colbc, lanevec, mob_high, mob_low, wide, narrow, ag, rs, rs_send,
           packed, first_dir, mate, acc, acc_wide, part, red_src, red_one, red_two, moments, flatten,
           z_mate, mate_sem, pos_sem, line_sem, plane_sem, ag_send, rs_recv, rs_sent, red_sem):
    row, col = lax.axis_index("row"), lax.axis_index("col")
    x, core = lax.div(row, 2), lax.rem(row, 2)
    z, y = lax.div(col, 4), lax.rem(col, 4)

    xs = [lax.rem(x + d, 4) for d in range(4)]
    ys = [lax.rem(y + d, 4) for d in range(4)]
    zs = [lax.rem(z + d, 8) for d in range(8)]

    def plane_at(dx, dy):
        return (xs[dx] * 2 + core, z * 4 + ys[dy])

    far_places = sorted(PLACES[1:], key=lambda spot: -min(spot[0], 4 - spot[0]) - min(spot[1], 4 - spot[1]))
    far_steps = STEPS[:0:-1]

    def line_at(dz):
        return (row, zs[dz] * 4 + y)

    def line_mate(dz):
        return (x * 2 + 1 - core, zs[dz] * 4 + y)

    sibling = (x * 2 + 1 - core, col)

    def for_each_core(program):
        for c in range(2):
            pl.when(core == c)(functools.partial(program, c))


    def remote(src, dst, send, recv, device):
        return pltpu.make_async_remote_copy(
            src_ref=src, dst_ref=dst, send_sem=send, recv_sem=recv, device_id=device, device_id_type=MESH)

    def wait_recv(ref, sem):
        remote(ref, ref, sem, sem, (row, col)).wait_recv()

    def wait_send(ref, sem):
        remote(ref, ref, sem, sem, (row, col)).wait_send()

    first = lax.broadcasted_iota(jnp.int32, (32, 128), 1) < HALF
    keep = first == (core == 0)

    def turn(value):
        return pltpu.roll(value, HALF, 1)

    barrier = pltpu.get_barrier_semaphore()

    def signal(device):
        pl.semaphore_signal(barrier, inc=1, device_id=device, device_id_type=MESH)

    signal(sibling)
    for dx, dy in far_places:
        signal(plane_at(dx, dy))
    for dz in far_steps:
        signal(line_at(dz))
        signal(line_mate(dz))

    flatten[...] = jnp.zeros_like(flatten)
    flatten[0:3, 0:32] = pos_ref[...].astype(F32)
    rows3 = flatten[...]
    posrow[core] = rows3[0:1] + pltpu.roll(rows3[1:2], 32, 1) + pltpu.roll(rows3[2:3], 64, 1)
    pl.semaphore_wait(barrier, 30)

    remote(posrow.at[core], posrow.at[core], pos_sem.at[0], pos_sem.at[1], sibling).start()
    remote(z_ref, z_mate, mate_sem.at[0], mate_sem.at[1], sibling).start()
    wait_recv(posrow.at[0], pos_sem.at[1])
    both = jnp.concatenate([posrow[0], posrow[1]], axis=1)
    posbuf[0] = both
    posbuf[PLANE] = both
    for n, spot in enumerate(far_places):
        if n < 7:
            remote(posbuf.at[PLANE], posbuf.at[seen_in_line(far_steps[n])], pos_sem.at[2], pos_sem.at[3],
                   line_at(far_steps[n])).start()
        remote(posbuf.at[0], posbuf.at[seen_in_plane(*spot)], pos_sem.at[2], pos_sem.at[3], plane_at(*spot)).start()
    wait_recv(z_mate, mate_sem.at[1])
    for axis in range(3):
        packed[0, axis] = jnp.where(keep, z_ref[axis], turn(z_mate[axis]))

    def gather(c, step):
        def to_line():
            for dz in STEPS[1:]:
                slot = seen_in_line(dz)
                remote(packed.at[step], ag.at[step, slot], ag_send.at[step], line_sem.at[step, (slot - PLANE) // 4],
                       line_at(dz)).start()

        def to_plane(some):
            for spot in ORDER:
                slot = seen_in_plane(*spot)
                if slot < NEEDED or not some:
                    remote(packed.at[step], ag.at[step, slot], ag_send.at[step], plane_sem.at[step, slot // 8],
                           plane_at(*spot)).start()

        if c == 0:
            to_line()
        if step == 2:
            to_plane(True)
        elif c == 1:
            to_plane(False)
        if c == 1 and step == 2:
            to_line()
        ag[step, 0] = packed[step]
        ag[step, PLANE] = packed[step]

    def wait_line(step, part_of):
        wait_recv(ag.at[step, pl.ds(0, 4 if part_of else 3)], line_sem.at[step, part_of])

    def wait_plane(step, part_of, last=False):
        if part_of == 0:
            wait_recv(ag.at[step, pl.ds(0, 7)], plane_sem.at[step, 0])
        else:
            wait_recv(ag.at[step, pl.ds(0, NEEDED - 8 if last else 8)], plane_sem.at[step, 1])

    for_each_core(lambda c: gather(c, 0))
    acc[...] = jnp.zeros_like(acc)
    acc_wide[...] = jnp.zeros_like(acc_wide)
    part[...] = jnp.zeros_like(part)
    ag[2, NEEDED:PLANE] = jnp.zeros((PLANE - NEEDED, 3, 32, 128), F32)
    for k in range(2):
        red_src[2 * k] = jnp.zeros((1, WIDTH), F32)
    narrow[...] = jnp.zeros_like(narrow)
    wait_recv(posbuf.at[pl.ds(0, 22)], pos_sem.at[3])

    lane_of = lax.broadcasted_iota(jnp.int32, (BLOCK, 128), 1)
    bead_of = lax.broadcasted_iota(jnp.int32, (BLOCK, 128), 0) & 31
    entry_of = lax.broadcasted_iota(jnp.int32, (128, BLOCK), 0)
    column_of = lax.broadcasted_iota(jnp.int32, (128, BLOCK), 1) & 31
    owner_of = lax.broadcasted_iota(jnp.int32, (16, BLOCK), 1) >> 5
    source_of = lax.broadcasted_iota(jnp.int32, (16, BLOCK), 0)
    ones = jnp.ones((128, 128), BF16)

    def place(at, d):
        return posbuf[at + d // 2][:, (d % 2) * 128:(d % 2) * 128 + 128]

    @pl.loop(0, 2)
    def _(h):
        rows_at = jnp.where(core == 0, h, 2) * 8
        lanes_at = jnp.where(core == 0, 2, h) * 8
        spread = jnp.concatenate([jnp.broadcast_to(place(rows_at, d), (32, 128)) for d in range(16)], axis=0)
        flat = jnp.concatenate([place(lanes_at, d) for d in range(16)], axis=0).astype(BF16)
        for axis in range(3):
            own = jnp.where(lane_of == axis * 32 + bead_of, spread, 0.0).astype(BF16)
            colbc[h, axis] = jnp.dot(own, ones, preferred_element_type=F32)
            pick = jnp.where(entry_of == axis * 32 + column_of, 1.0, 0.0).astype(BF16)
            moved = jnp.dot(flat, pick, preferred_element_type=F32)
            lanevec[h, axis:axis + 1, :] = jnp.sum(jnp.where(owner_of == source_of, moved, 0.0), axis=0, keepdims=True)

    def tile_of(c, t):
        return (4 - t) % 4 if c == 0 else 1 - t // 2

    def places(c, t):
        tile = tile_of(c, t)
        h, rt = (tile // 2, tile % 2) if c == 0 else (t % 2, tile)
        return h, c * h, rt * 256

    def build(c, t):
        h, _, begin = places(c, t)

        @pl.loop(0, 16, unroll=2)
        def _(r):
            rows = pl.ds(pl.multiple_of(begin + r * 16, 16), 16)
            mine = [colbc[h, axis, rows, :] for axis in range(3)]
            for tile in range(4):
                lanes = slice(tile * 128, tile * 128 + 128)
                d = [mine[axis] - lanevec[h, axis:axis + 1, lanes] for axis in range(3)]
                squared = d[0] * d[0] + d[1] * d[1] + d[2] * d[2]
                root = lax.rsqrt(jnp.where(squared > 0.5, squared, 1e30))
                inverse = root * root
                prefactor = (0.75 * RADIUS) * root
                iso = prefactor * (1.0 + (2.0 / 3.0 * RADIUS * RADIUS) * inverse)
                along = (prefactor * inverse) * (1.0 - (2.0 * RADIUS * RADIUS) * inverse)
                s = [along * d[axis] for axis in range(3)]
                parts = (s[0] * d[0] + iso, s[0] * d[1], s[0] * d[2], s[1] * d[1] + iso, s[1] * d[2],
                         s[2] * d[2] + iso)
                for k, value in enumerate(parts):
                    high = value.astype(BF16)
                    at = (tile // 2) * 1536 + k * 256 + (tile % 2) * 128
                    at = slice(at, at + 128)
                    mob_high[h, rows, at] = high
                    mob_low[h, rows, at] = (value - high.astype(F32)).astype(BF16)

    def widen(c, h):
        base = PLANE if c == 0 else h * 8

        @pl.loop(0, 8, unroll=4)
        def _(s):
            for axis in range(3):
                value = ag[0, base + s, axis]
                other = turn(value)
                for j, both in enumerate((jnp.where(first, value, other), jnp.where(first, other, value))):
                    high = both.astype(BF16).astype(F32)
                    tile = jnp.where(first, high, both - high).astype(BF16)
                    at = pl.ds(pl.multiple_of(s * 64 + j * 32, 32), 32)
                    wide[h, at, axis * 128:axis * 128 + 128] = tile
                    if axis == 0:
                        wide[h, at, 384:512] = tile

    def arrange(step, base, w, quarter, weight):
        @pl.loop(0, 4, unroll=4)
        def _(s):
            values = [ag[step, base + s, axis] * weight for axis in range(3)]
            others = [turn(value) for value in values]
            for j in range(2):
                left, right = (values, others) if j == 0 else (others, values)
                lx, ly, lz = (jnp.where(first, v, 0.0).astype(BF16) for v in left)
                ry, rz = (jnp.where(first, 0.0, v).astype(BF16) for v in right[1:])
                yx = jnp.where(first, left[1], right[0]).astype(BF16)
                for k, half, tile in ((0, 0, lx), (1, 0, yx), (2, 0, lz), (2, 1, lx), (3, 0, ry), (4, 0, rz),
                                      (4, 1, ly), (5, 1, lz)):
                    at = pl.ds(pl.multiple_of(quarter * 1536 + k * 256 + s * 64 + j * 32, 32), 32)
                    narrow[w, at, half * 128:half * 128 + 128] = tile

    def arrange_half(c, step, part_of):
        if c == 0:
            wait_line(step, part_of)
            arrange(step, PLANE + 4 * part_of, 0, part_of, 1.0)
        else:
            wait_plane(step, part_of, step == 2)
            for quarter in range(2):
                slot = 8 * part_of + 4 * quarter
                if step == 1 or slot < NEEDED:
                    arrange(step, slot, part_of, quarter, 2.0 if step == 2 and slot >= 4 else 1.0)

    def dot(left, right):
        return jnp.dot(left, right, preferred_element_type=F32)

    def product(c, t):
        h, w, begin = places(c, t)
        rows = slice(begin, begin + 256)

        def both(k, lo, hi):
            total = 0.0
            for quarter in range(2):
                at = slice(quarter * 1536 + k * 256, quarter * 1536 + k * 256 + 256)
                right = wide[w, quarter * 256:quarter * 256 + 256, lo:hi]
                total = total + dot(mob_high[h, rows, at], right) + dot(mob_low[h, rows, at], right)
            return total

        xy, yz, zx = both(1, 0, 256), both(4, 128, 384), both(2, 256, 512)
        return (both(0, 0, 128) + xy[:, 128:] + zx[:, :128],
                both(3, 128, 256) + xy[:, :128] + yz[:, 128:],
                both(5, 256, 384) + zx[:, 128:] + yz[:, :128])

    def halves(i, upper):
        return slice(i * 64 + upper * 32, i * 64 + upper * 32 + 32)

    def pack(_, i):
        chunk = []
        for axis in range(3):
            low, high = acc[axis, halves(i, 0), :], acc[axis, halves(i, 1), :]
            chunk.append(jnp.where(first, low + turn(low), high + turn(high)))
        return chunk

    def pack_wide(tile, i):
        low, high = halves(i, 0), halves(i, 1)
        xy_low, xy_high = acc_wide[tile, low, :128], acc_wide[tile, high, :128]
        z_low, z_high = acc_wide[tile, low, 128:], acc_wide[tile, high, 128:]
        return (jnp.where(first, xy_low, turn(xy_high)), jnp.where(first, turn(xy_low), xy_high),
                jnp.where(first, z_low, turn(z_high)))

    def scatter(c, step, t, packer):
        def fill(tile):
            chunks = [packer(tile, i) for i in range(4)]
            for i, chunk in enumerate(chunks):
                for axis, value in enumerate(chunk):
                    rs_send[step, tile * 4 + i, axis] = value

        def send_plane(tile):
            fill(tile)
            for i in (3, 2, 1, 0):
                spot = PLACES[tile * 4 + i]
                if tile * 4 + i:
                    remote(rs_send.at[step, tile * 4 + i], rs.at[step, seen_in_plane(*spot)], rs_sent.at[step],
                           rs_recv.at[step], plane_at(*spot)).start()
                else:
                    rs[step, 0] = rs_send[step, 0]

        def send_line(tile):
            fill(tile)
            for i in (3, 2, 1, 0):
                dz = STEPS[tile * 4 + i]
                if dz:
                    remote(rs_send.at[step, tile * 4 + i], rs.at[step, seen_in_line(dz) - PLANE], rs_sent.at[step],
                           rs_recv.at[step], line_at(dz)).start()
                else:
                    rs[step, 0] = rs_send[step, 0]

        (send_line if c else send_plane)(tile_of(c, t))

    def collect(c, step):
        count = LINE if c else PLANE
        wait_recv(rs.at[step, pl.ds(0, count - 1)], rs_recv.at[step])
        for axis in range(3):
            packed[step + 1, axis] = sum((rs[step, s, axis] for s in range(1, count)), rs[step, 0, axis])

    front = lax.broadcasted_iota(jnp.int32, (1, 128), 1) < HALF

    def fold(value):
        line = jnp.sum(value, axis=0, keepdims=True)
        return line + turn(line)

    def inner(left, right):
        return fold(sum(left[axis] * right[axis] for axis in range(3)))

    def reduce_plane(k, values):
        for n, value in values:
            red_src[2 * k, :, n * 128:n * 128 + 128] = value
        for spot in far_places:
            remote(red_src.at[2 * k], red_one.at[k, seen_in_plane(*spot)], red_sem.at[k, 0], red_sem.at[k, 1], plane_at(*spot)).start()
        red_one[k, 0] = red_src[2 * k]

    def reduce_line(k):
        def send(dz, device):
            slot = seen_in_line(dz) - PLANE
            remote(red_src.at[2 * k + 1], red_two.at[k, core, slot], red_sem.at[k, 2], red_sem.at[k, 3], device).start()

        wait_recv(red_one.at[k, pl.ds(0, PLANE - 1)], red_sem.at[k, 1])
        red_src[2 * k + 1] = sum((red_one[k, s] for s in range(1, PLANE)), red_one[k, 0])
        for dz in far_steps:
            send(dz, line_at(dz))
            if k == 1:
                send(dz, line_mate(dz))
        if k == 1:
            send(0, sibling)
        red_two[k, core, 0] = red_src[2 * k + 1]

    def reduced(k, c):
        return sum((red_two[k, c, s] for s in range(1, LINE)), red_two[k, c, 0])

    def steps(c):
        built = 4 if c else 2
        for t in range(built):
            build(c, t)
        if c == 0:
            wait_line(0, 0)
            wait_line(0, 1)
            widen(c, 0)
        else:
            wait_plane(0, 0)
            wait_plane(0, 1)
            widen(c, 0)
            widen(c, 1)
        for t in range(4):
            if t >= built:
                build(c, t)
            for axis, value in enumerate(product(c, t)):
                acc[axis] = acc[axis] + value if c == 1 and t % 2 == 1 else value
            if c == 0 or t % 2 == 1:
                scatter(c, 0, t, pack)
        collect(c, 0)
        gather(c, 1)
        reduce_plane(0, ((0, inner(packed.at[0], packed.at[0])), (1, inner(packed.at[0], packed.at[1]))))

        for step in (1, 2):
            for part_of in range(2):
                arrange_half(c, step, part_of)
                for t in range(4):
                    tile = tile_of(c, t)
                    quarter = t % 2 if c else part_of
                    if step == 2 and (tile == 3 if c == 0 else 8 * part_of + 4 * quarter >= NEEDED):
                        skip = True
                    else:
                        skip = False
                        h, rt = (part_of, tile) if c else (tile // 2, tile % 2)
                        inner_at = slice(quarter * 1536, quarter * 1536 + 1536)
                        value = dot(mob_high[h, rt * 256:rt * 256 + 256, inner_at], narrow[h if c else 0, inner_at, :])
                        begin = part_of == 0 and (c == 0 or t % 2 == 0)
                        acc_wide[tile] = value if begin else acc_wide[tile] + value
                    if part_of == 0 or (c == 1 and t % 2 == 0):
                        continue
                    if step == 1:
                        scatter(c, 1, t, pack_wide)
                        continue
                    if t == c:
                        for half in range(2):
                            wait_line(2, half) if c else wait_plane(2, half, True)
                    if c == 0 and skip:
                        continue
                    total = jnp.zeros((32, 128), F32)
                    for i in range(4):
                        for axis, value in enumerate(pack_wide(tile, i)):
                            total = total + value * ag[2, (PLANE if c else 0) + tile * 4 + i, axis]
                    part[...] += total * (2.0 if c == 0 and tile > 0 else 1.0)
            if step == 2:
                break
            reduce_line(0)
            collect(c, 1)
            wait_recv(red_two.at[0, 0, pl.ds(0, LINE - 1)], red_sem.at[0, 3])
            total = reduced(0, c)
            moments[0] = jnp.broadcast_to(total[:, 128:256] / total[:, 0:128], (32, 128))
            a1 = moments[0]
            for axis in range(3):
                y1 = packed[1, axis]
                packed[2, axis] = packed[2, axis] - a1 * y1
                first_dir[axis] = y1 - a1 * packed[0, axis]
            gather(c, 2)
            remote(first_dir, mate.at[0], mate_sem.at[2], mate_sem.at[3], sibling).start()
            remote(packed.at[2], mate.at[1], mate_sem.at[2], mate_sem.at[3], sibling).start()
            early = (red_src[0][:, 0:128], red_src[0][:, 128:256], inner(first_dir, first_dir),
                     inner(first_dir, packed.at[2]), inner(packed.at[2], packed.at[2]))
            for n, value in enumerate(early):
                red_src[2, :, n * 128:n * 128 + 128] = value

    for_each_core(steps)

    reduce_plane(1, ((5, fold(part[...])),))
    reduce_line(1)
    wait_recv(red_one.at[1, pl.ds(0, 2 * LINE - 1)], red_sem.at[1, 3])
    low, high = reduced(1, 0), reduced(1, 1)
    for k in range(6):
        at = slice(k * 128, k * 128 + 128)
        moments[k + 1, 0:8] = jnp.broadcast_to(jnp.where(front, low[:, at], high[:, at]), (8, 128))
    moments[7, 0:8] = jnp.zeros((8, 128), F32)
    moments[8, 0:8] = jnp.ones((8, 128), F32)
    m0, m1, e1, f1, g, third, zero, one = (moments[k, 0:8] for k in range(1, 9))

    a1, a2, bb2 = m1 / m0, f1 / e1, e1 / m0
    e2 = g - a2 * f1 - bb2 * e1
    bb3 = e2 / e1
    a3 = (third - a2 * g - bb2 * (f1 + a1 * e1)) / e2 - a2
    d1, d2, d3 = 1.0 + a1, 1.0 + a2, 1.0 + a3
    scale = (d1 + d2 + d3) / ITERS
    current = (d1 / scale, jnp.sqrt(bb2) / scale, zero, d2 / scale, jnp.sqrt(bb3) / scale, d3 / scale)
    partner = (one, zero, zero, one, zero, one)

    def inverse_three(m):
        c00, c01, c02 = m[3] * m[5] - m[4] * m[4], m[2] * m[4] - m[1] * m[5], m[1] * m[4] - m[2] * m[3]
        c11, c12, c22 = m[0] * m[5] - m[2] * m[2], m[1] * m[2] - m[0] * m[4], m[0] * m[3] - m[1] * m[1]
        over = 1.0 / (m[0] * c00 + m[1] * c01 + m[2] * c02)
        return tuple(c * over for c in (c00, c01, c02, c11, c12, c22))

    def newton(_, state):
        now, other = state
        return (tuple(0.5 * (u + v) for u, v in zip(now, inverse_three(other))),
                tuple(0.5 * (u + v) for u, v in zip(other, inverse_three(now))))

    current, partner = lax.fori_loop(0, 20, newton, (current, partner), unroll=4)
    size = jnp.sqrt(scale)
    beta = jnp.sqrt(m0)
    r1, r2, r3 = (current[k] * size for k in range(3))
    f2, f3 = beta * r2 / jnp.sqrt(e1), beta * r3 / jnp.sqrt(e2)
    wait_recv(mate, mate_sem.at[3])
    c0, c1, c2 = (jnp.concatenate([c, c, c, c], axis=0) for c in (r1 - f3 * bb2, f2 - f3 * a2, f3))
    for axis in range(3):
        out_ref[axis] = (c0 * z_ref[axis] + c1 * jnp.where(keep, first_dir[axis], turn(mate[0, axis]))
                         + c2 * jnp.where(keep, packed[2, axis], turn(mate[1, axis])))

    wait_send(posrow.at[0], pos_sem.at[0])
    wait_send(z_mate, mate_sem.at[0])
    wait_send(mate, mate_sem.at[2])
    wait_send(posbuf.at[pl.ds(0, 22)], pos_sem.at[2])
    wait_send(ag.at[2, pl.ds(0, NEEDED - 1 + LINE - 1)], ag_send.at[2])
    for k, count in enumerate((LINE - 1, 2 * LINE - 1)):
        wait_send(red_one.at[k, pl.ds(0, PLANE - 1)], red_sem.at[k, 0])
        wait_send(red_one.at[k, pl.ds(0, count)], red_sem.at[k, 2])
    for step in range(2):
        @pl.when(core == 0)
        def _(step=step):
            wait_send(ag.at[step, pl.ds(0, LINE - 1)], ag_send.at[step])
            wait_send(rs_send.at[step, pl.ds(0, PLANE - 1)], rs_sent.at[step])

        @pl.when(core == 1)
        def _(step=step):
            wait_send(ag.at[step, pl.ds(0, PLANE - 1)], ag_send.at[step])
            wait_send(rs_send.at[step, pl.ds(0, LINE - 1)], rs_sent.at[step])


def shards(positions, start_vector):
    chunk = (3, 32, 128)
    return pl.pallas_call(
        kernel,
        out_shape=jax.ShapeDtypeStruct(start_vector.shape, F32),
        in_specs=[pl.BlockSpec(memory_space=pltpu.VMEM)] * 2,
        out_specs=pl.BlockSpec(memory_space=pltpu.VMEM),
        scratch_shapes=[
            pltpu.VMEM((2, 1, 128), F32),
            pltpu.VMEM((PLANE + LINE, 1, 256), F32),
            pltpu.VMEM((2, 3, BLOCK, 128), F32),
            pltpu.VMEM((2, 8, BLOCK), F32),
            pltpu.VMEM((2, BLOCK, 6 * BLOCK), BF16),
            pltpu.VMEM((2, BLOCK, 6 * BLOCK), BF16),
            pltpu.VMEM((2, BLOCK, 512), BF16),
            pltpu.VMEM((2, 6 * BLOCK, 256), BF16),
            pltpu.VMEM((3, PLANE + LINE) + chunk, F32),
            pltpu.VMEM((2, PLANE) + chunk, F32),
            pltpu.VMEM((2, PLANE) + chunk, F32),
            pltpu.VMEM((3,) + chunk, F32),
            pltpu.VMEM(chunk, F32),
            pltpu.VMEM((2,) + chunk, F32),
            pltpu.VMEM((3, 256, 128), F32),
            pltpu.VMEM((4, 256, 256), F32),
            pltpu.VMEM((32, 128), F32),
            pltpu.VMEM((4, 1, WIDTH), F32),
            pltpu.VMEM((2, PLANE, 1, WIDTH), F32),
            pltpu.VMEM((2, 2, LINE, 1, WIDTH), F32),
            pltpu.VMEM((9, 32, 128), F32),
            pltpu.VMEM((8, 128), F32),
            pltpu.VMEM(chunk, F32),
            pltpu.SemaphoreType.DMA((4,)),
            pltpu.SemaphoreType.DMA((4,)),
            pltpu.SemaphoreType.DMA((3, 2)),
            pltpu.SemaphoreType.DMA((3, 2)),
            pltpu.SemaphoreType.DMA((3,)),
            pltpu.SemaphoreType.DMA((2,)),
            pltpu.SemaphoreType.DMA((2,)),
            pltpu.SemaphoreType.DMA((2, 4)),
        ],
        compiler_params=pltpu.CompilerParams(
            collective_id=0, has_side_effects=True, vmem_limit_bytes=40 * 1024 * 1024),
    )(positions, start_vector)


def solution(mesh):
    in_specs = (P(None, ("row", "col")), P(None, ("row", "col"), None))
    out_specs = P(None, ("row", "col"), None)
    return jax.shard_map(shards, mesh=mesh, in_specs=in_specs, out_specs=out_specs, check_vma=False)
```

```python
import functools

import jax
import jax.numpy as jnp
from jax import lax
from jax.experimental import pallas as pl
from jax.experimental.pallas import tpu as pltpu
from jax.sharding import PartitionSpec as P

ITERS = 3
RADIUS = 0.4
MESH = pl.DeviceIdType.MESH
F32 = jnp.float32
BF16 = jnp.bfloat16

PLANE, LINE = 16, 8
PLACES = ((0, 0), (2, 0), (0, 2), (2, 2), (0, 1), (3, 0), (1, 1), (1, 3), (3, 2), (2, 1),
          (0, 3), (1, 0), (3, 3), (3, 1), (1, 2), (2, 3))
NEEDED = 10
ORDER = ((0, 1), (0, 3), (1, 0), (3, 0), (2, 0), (0, 2), (1, 1), (3, 3), (1, 3), (3, 1),
         (1, 2), (2, 1), (3, 2), (2, 3), (2, 2))
STEPS = (0, 1, 7, 2, 6, 3, 5, 4)


def seen_in_plane(dx, dy):
    return PLACES.index((-dx % 4, -dy % 4))


def seen_in_line(dz):
    return PLANE + STEPS.index(-dz % 8)


HALF = 64
BLOCK = 512
WIDTH = 768


def kernel(pos_ref, z_ref, out_ref, posrow, posbuf, colbc, lanevec, mob_high, mob_low, wide, narrow, ag, rs, rs_send,
           packed, first_dir, mate, acc, acc_wide, part, red_src, red_one, red_two, moments, flatten,
           z_mate, mate_sem, pos_sem, line_sem, plane_sem, ag_send, rs_recv, rs_sent, red_sem):
    row, col = lax.axis_index("row"), lax.axis_index("col")
    x, core = lax.div(row, 2), lax.rem(row, 2)
    z, y = lax.div(col, 4), lax.rem(col, 4)

    xs = [lax.rem(x + d, 4) for d in range(4)]
    ys = [lax.rem(y + d, 4) for d in range(4)]
    zs = [lax.rem(z + d, 8) for d in range(8)]

    def plane_at(dx, dy):
        return (xs[dx] * 2 + core, z * 4 + ys[dy])

    far_places, far_steps = PLACES[:0:-1], STEPS[:0:-1]

    def line_at(dz):
        return (row, zs[dz] * 4 + y)

    def line_mate(dz):
        return (x * 2 + 1 - core, zs[dz] * 4 + y)

    sibling = (x * 2 + 1 - core, col)

    def for_each_core(program):
        for c in range(2):
            pl.when(core == c)(functools.partial(program, c))


    def remote(src, dst, send, recv, device):
        return pltpu.make_async_remote_copy(
            src_ref=src, dst_ref=dst, send_sem=send, recv_sem=recv, device_id=device, device_id_type=MESH)

    def wait_recv(ref, sem):
        remote(ref, ref, sem, sem, (row, col)).wait_recv()

    def wait_send(ref, sem):
        remote(ref, ref, sem, sem, (row, col)).wait_send()

    first = lax.broadcasted_iota(jnp.int32, (32, 128), 1) < HALF
    keep = first == (core == 0)

    def turn(value):
        return pltpu.roll(value, HALF, 1)

    barrier = pltpu.get_barrier_semaphore()

    def signal(device):
        pl.semaphore_signal(barrier, inc=1, device_id=device, device_id_type=MESH)

    signal(sibling)
    for dx, dy in far_places:
        signal(plane_at(dx, dy))
    for dz in far_steps:
        signal(line_at(dz))
        signal(line_mate(dz))

    flatten[...] = jnp.zeros_like(flatten)
    flatten[0:3, 0:32] = pos_ref[...].astype(F32)
    rows3 = flatten[...]
    posrow[core] = rows3[0:1] + pltpu.roll(rows3[1:2], 32, 1) + pltpu.roll(rows3[2:3], 64, 1)
    pl.semaphore_wait(barrier, 30)

    remote(posrow.at[core], posrow.at[core], pos_sem.at[0], pos_sem.at[1], sibling).start()
    remote(z_ref, z_mate, mate_sem.at[0], mate_sem.at[1], sibling).start()
    wait_recv(posrow.at[0], pos_sem.at[1])
    both = jnp.concatenate([posrow[0], posrow[1]], axis=1)
    posbuf[0] = both
    posbuf[PLANE] = both
    for n, spot in enumerate(far_places):
        if n < 7:
            remote(posbuf.at[PLANE], posbuf.at[seen_in_line(far_steps[n])], pos_sem.at[2], pos_sem.at[3],
                   line_at(far_steps[n])).start()
        remote(posbuf.at[0], posbuf.at[seen_in_plane(*spot)], pos_sem.at[2], pos_sem.at[3], plane_at(*spot)).start()
    wait_recv(z_mate, mate_sem.at[1])
    for axis in range(3):
        packed[0, axis] = jnp.where(keep, z_ref[axis], turn(z_mate[axis]))

    def gather(c, step):
        def to_line():
            for dz in STEPS[1:]:
                slot = seen_in_line(dz)
                remote(packed.at[step], ag.at[step, slot], ag_send.at[step], line_sem.at[step, (slot - PLANE) // 4],
                       line_at(dz)).start()

        def to_plane(some):
            for spot in ORDER:
                slot = seen_in_plane(*spot)
                if slot < NEEDED or not some:
                    remote(packed.at[step], ag.at[step, slot], ag_send.at[step], plane_sem.at[step, slot // 8],
                           plane_at(*spot)).start()

        if c == 0:
            to_line()
        if step == 2:
            to_plane(True)
        elif c == 1:
            to_plane(False)
        if c == 1 and step == 2:
            to_line()
        ag[step, 0] = packed[step]
        ag[step, PLANE] = packed[step]

    def wait_line(step, part_of):
        wait_recv(ag.at[step, pl.ds(0, 4 if part_of else 3)], line_sem.at[step, part_of])

    def wait_plane(step, part_of, last=False):
        if part_of == 0:
            wait_recv(ag.at[step, pl.ds(0, 7)], plane_sem.at[step, 0])
        else:
            wait_recv(ag.at[step, pl.ds(0, NEEDED - 8 if last else 8)], plane_sem.at[step, 1])

    for_each_core(lambda c: gather(c, 0))
    acc[...] = jnp.zeros_like(acc)
    acc_wide[...] = jnp.zeros_like(acc_wide)
    part[...] = jnp.zeros_like(part)
    ag[2, NEEDED:PLANE] = jnp.zeros((PLANE - NEEDED, 3, 32, 128), F32)
    for k in range(2):
        red_src[2 * k] = jnp.zeros((1, WIDTH), F32)
    narrow[...] = jnp.zeros_like(narrow)
    wait_recv(posbuf.at[pl.ds(0, 22)], pos_sem.at[3])

    lane_of = lax.broadcasted_iota(jnp.int32, (BLOCK, 128), 1)
    bead_of = lax.broadcasted_iota(jnp.int32, (BLOCK, 128), 0) & 31
    entry_of = lax.broadcasted_iota(jnp.int32, (128, BLOCK), 0)
    column_of = lax.broadcasted_iota(jnp.int32, (128, BLOCK), 1) & 31
    owner_of = lax.broadcasted_iota(jnp.int32, (16, BLOCK), 1) >> 5
    source_of = lax.broadcasted_iota(jnp.int32, (16, BLOCK), 0)
    ones = jnp.ones((128, 128), BF16)

    def place(at, d):
        return posbuf[at + d // 2][:, (d % 2) * 128:(d % 2) * 128 + 128]

    @pl.loop(0, 2)
    def _(h):
        rows_at = jnp.where(core == 0, h, 2) * 8
        lanes_at = jnp.where(core == 0, 2, h) * 8
        spread = jnp.concatenate([jnp.broadcast_to(place(rows_at, d), (32, 128)) for d in range(16)], axis=0)
        flat = jnp.concatenate([place(lanes_at, d) for d in range(16)], axis=0).astype(BF16)
        for axis in range(3):
            own = jnp.where(lane_of == axis * 32 + bead_of, spread, 0.0).astype(BF16)
            colbc[h, axis] = jnp.dot(own, ones, preferred_element_type=F32)
            pick = jnp.where(entry_of == axis * 32 + column_of, 1.0, 0.0).astype(BF16)
            moved = jnp.dot(flat, pick, preferred_element_type=F32)
            lanevec[h, axis:axis + 1, :] = jnp.sum(jnp.where(owner_of == source_of, moved, 0.0), axis=0, keepdims=True)

    def tile_of(c, t):
        return (4 - t) % 4 if c == 0 else 1 - t // 2

    def places(c, t):
        tile = tile_of(c, t)
        h, rt = (tile // 2, tile % 2) if c == 0 else (t % 2, tile)
        return h, c * h, rt * 256

    def build(c, t):
        h, _, begin = places(c, t)

        @pl.loop(0, 16, unroll=2)
        def _(r):
            rows = pl.ds(pl.multiple_of(begin + r * 16, 16), 16)
            mine = [colbc[h, axis, rows, :] for axis in range(3)]
            for tile in range(4):
                lanes = slice(tile * 128, tile * 128 + 128)
                d = [mine[axis] - lanevec[h, axis:axis + 1, lanes] for axis in range(3)]
                squared = d[0] * d[0] + d[1] * d[1] + d[2] * d[2]
                root = lax.rsqrt(jnp.where(squared > 0.5, squared, 1e30))
                inverse = root * root
                prefactor = (0.75 * RADIUS) * root
                iso = prefactor * (1.0 + (2.0 / 3.0 * RADIUS * RADIUS) * inverse)
                along = (prefactor * inverse) * (1.0 - (2.0 * RADIUS * RADIUS) * inverse)
                s = [along * d[axis] for axis in range(3)]
                parts = (s[0] * d[0] + iso, s[0] * d[1], s[0] * d[2], s[1] * d[1] + iso, s[1] * d[2],
                         s[2] * d[2] + iso)
                for k, value in enumerate(parts):
                    high = value.astype(BF16)
                    at = (tile // 2) * 1536 + k * 256 + (tile % 2) * 128
                    at = slice(at, at + 128)
                    mob_high[h, rows, at] = high
                    mob_low[h, rows, at] = (value - high.astype(F32)).astype(BF16)

    def widen(c, h):
        base = PLANE if c == 0 else h * 8

        @pl.loop(0, 8, unroll=4)
        def _(s):
            for axis in range(3):
                value = ag[0, base + s, axis]
                other = turn(value)
                for j, both in enumerate((jnp.where(first, value, other), jnp.where(first, other, value))):
                    high = both.astype(BF16).astype(F32)
                    tile = jnp.where(first, high, both - high).astype(BF16)
                    at = pl.ds(pl.multiple_of(s * 64 + j * 32, 32), 32)
                    wide[h, at, axis * 128:axis * 128 + 128] = tile
                    if axis == 0:
                        wide[h, at, 384:512] = tile

    def arrange(step, base, w, quarter, weight):
        @pl.loop(0, 4, unroll=4)
        def _(s):
            values = [ag[step, base + s, axis] * weight for axis in range(3)]
            others = [turn(value) for value in values]
            for j in range(2):
                left, right = (values, others) if j == 0 else (others, values)
                lx, ly, lz = (jnp.where(first, v, 0.0).astype(BF16) for v in left)
                ry, rz = (jnp.where(first, 0.0, v).astype(BF16) for v in right[1:])
                yx = jnp.where(first, left[1], right[0]).astype(BF16)
                for k, half, tile in ((0, 0, lx), (1, 0, yx), (2, 0, lz), (2, 1, lx), (3, 0, ry), (4, 0, rz),
                                      (4, 1, ly), (5, 1, lz)):
                    at = pl.ds(pl.multiple_of(quarter * 1536 + k * 256 + s * 64 + j * 32, 32), 32)
                    narrow[w, at, half * 128:half * 128 + 128] = tile

    def arrange_half(c, step, part_of):
        if c == 0:
            wait_line(step, part_of)
            arrange(step, PLANE + 4 * part_of, 0, part_of, 1.0)
        else:
            wait_plane(step, part_of, step == 2)
            for quarter in range(2):
                slot = 8 * part_of + 4 * quarter
                if step == 1 or slot < NEEDED:
                    arrange(step, slot, part_of, quarter, 2.0 if step == 2 and slot >= 4 else 1.0)

    def dot(left, right):
        return jnp.dot(left, right, preferred_element_type=F32)

    def product(c, t):
        h, w, begin = places(c, t)
        rows = slice(begin, begin + 256)

        def both(k, lo, hi):
            total = 0.0
            for quarter in range(2):
                at = slice(quarter * 1536 + k * 256, quarter * 1536 + k * 256 + 256)
                right = wide[w, quarter * 256:quarter * 256 + 256, lo:hi]
                total = total + dot(mob_high[h, rows, at], right) + dot(mob_low[h, rows, at], right)
            return total

        xy, yz, zx = both(1, 0, 256), both(4, 128, 384), both(2, 256, 512)
        return (both(0, 0, 128) + xy[:, 128:] + zx[:, :128],
                both(3, 128, 256) + xy[:, :128] + yz[:, 128:],
                both(5, 256, 384) + zx[:, 128:] + yz[:, :128])

    def halves(i, upper):
        return slice(i * 64 + upper * 32, i * 64 + upper * 32 + 32)

    def pack(_, i):
        chunk = []
        for axis in range(3):
            low, high = acc[axis, halves(i, 0), :], acc[axis, halves(i, 1), :]
            chunk.append(jnp.where(first, low + turn(low), high + turn(high)))
        return chunk

    def pack_wide(tile, i):
        low, high = halves(i, 0), halves(i, 1)
        xy_low, xy_high = acc_wide[tile, low, :128], acc_wide[tile, high, :128]
        z_low, z_high = acc_wide[tile, low, 128:], acc_wide[tile, high, 128:]
        return (jnp.where(first, xy_low, turn(xy_high)), jnp.where(first, turn(xy_low), xy_high),
                jnp.where(first, z_low, turn(z_high)))

    def scatter(c, step, t, packer):
        def fill(tile):
            chunks = [packer(tile, i) for i in range(4)]
            for i, chunk in enumerate(chunks):
                for axis, value in enumerate(chunk):
                    rs_send[step, tile * 4 + i, axis] = value

        def send_plane(tile):
            fill(tile)
            for i in (3, 2, 1, 0):
                spot = PLACES[tile * 4 + i]
                if tile * 4 + i:
                    remote(rs_send.at[step, tile * 4 + i], rs.at[step, seen_in_plane(*spot)], rs_sent.at[step],
                           rs_recv.at[step], plane_at(*spot)).start()
                else:
                    rs[step, 0] = rs_send[step, 0]

        def send_line(tile):
            fill(tile)
            for i in (3, 2, 1, 0):
                dz = STEPS[tile * 4 + i]
                if dz:
                    remote(rs_send.at[step, tile * 4 + i], rs.at[step, seen_in_line(dz) - PLANE], rs_sent.at[step],
                           rs_recv.at[step], line_at(dz)).start()
                else:
                    rs[step, 0] = rs_send[step, 0]

        (send_line if c else send_plane)(tile_of(c, t))

    def collect(c, step):
        count = LINE if c else PLANE
        wait_recv(rs.at[step, pl.ds(0, count - 1)], rs_recv.at[step])
        for axis in range(3):
            packed[step + 1, axis] = sum((rs[step, s, axis] for s in range(1, count)), rs[step, 0, axis])

    front = lax.broadcasted_iota(jnp.int32, (1, 128), 1) < HALF

    def fold(value):
        line = jnp.sum(value, axis=0, keepdims=True)
        return line + turn(line)

    def inner(left, right):
        return fold(sum(left[axis] * right[axis] for axis in range(3)))

    def reduce_plane(k, values):
        for n, value in values:
            red_src[2 * k, :, n * 128:n * 128 + 128] = value
        for spot in far_places:
            remote(red_src.at[2 * k], red_one.at[k, seen_in_plane(*spot)], red_sem.at[k, 0], red_sem.at[k, 1], plane_at(*spot)).start()
        red_one[k, 0] = red_src[2 * k]

    def reduce_line(k):
        def send(dz, device):
            slot = seen_in_line(dz) - PLANE
            remote(red_src.at[2 * k + 1], red_two.at[k, core, slot], red_sem.at[k, 2], red_sem.at[k, 3], device).start()

        wait_recv(red_one.at[k, pl.ds(0, PLANE - 1)], red_sem.at[k, 1])
        red_src[2 * k + 1] = sum((red_one[k, s] for s in range(1, PLANE)), red_one[k, 0])
        for dz in far_steps:
            send(dz, line_at(dz))
            if k == 1:
                send(dz, line_mate(dz))
        if k == 1:
            send(0, sibling)
        red_two[k, core, 0] = red_src[2 * k + 1]

    def reduced(k, c):
        return sum((red_two[k, c, s] for s in range(1, LINE)), red_two[k, c, 0])

    def steps(c):
        built = 4 if c else 2
        for t in range(built):
            build(c, t)
        if c == 0:
            wait_line(0, 0)
            wait_line(0, 1)
            widen(c, 0)
        else:
            wait_plane(0, 0)
            wait_plane(0, 1)
            widen(c, 0)
            widen(c, 1)
        for t in range(4):
            if t >= built:
                build(c, t)
            for axis, value in enumerate(product(c, t)):
                acc[axis] = acc[axis] + value if c == 1 and t % 2 == 1 else value
            if c == 0 or t % 2 == 1:
                scatter(c, 0, t, pack)
        collect(c, 0)
        gather(c, 1)
        reduce_plane(0, ((0, inner(packed.at[0], packed.at[0])), (1, inner(packed.at[0], packed.at[1]))))

        for step in (1, 2):
            for part_of in range(2):
                arrange_half(c, step, part_of)
                for t in range(4):
                    tile = tile_of(c, t)
                    if c == 1 and t % 2 == 0:
                        continue
                    skip = c == 0 and step == 2 and tile == 3
                    if not skip:
                        if c == 0:
                            h, rt, w, inner_at = tile // 2, tile % 2, 0, slice(part_of * 1536, part_of * 1536 + 1536)
                        else:
                            h, rt, w, inner_at = part_of, tile, part_of, slice(0, 1536 * (2 - part_of * (step - 1)))
                        value = dot(mob_high[h, rt * 256:rt * 256 + 256, inner_at], narrow[w, inner_at, :])
                        acc_wide[tile] = acc_wide[tile] + value if part_of else value
                    if part_of == 0:
                        continue
                    if step == 1:
                        scatter(c, 1, t, pack_wide)
                        continue
                    if t == c:
                        for half in range(2):
                            wait_line(2, half) if c else wait_plane(2, half, True)
                    if c == 0 and skip:
                        continue
                    total = jnp.zeros((32, 128), F32)
                    for i in range(4):
                        for axis, value in enumerate(pack_wide(tile, i)):
                            total = total + value * ag[2, (PLANE if c else 0) + tile * 4 + i, axis]
                    part[...] += total * (2.0 if c == 0 and tile > 0 else 1.0)
            if step == 2:
                break
            reduce_line(0)
            collect(c, 1)
            wait_recv(red_two.at[0, 0, pl.ds(0, LINE - 1)], red_sem.at[0, 3])
            total = reduced(0, c)
            moments[0] = jnp.broadcast_to(total[:, 128:256] / total[:, 0:128], (32, 128))
            a1 = moments[0]
            for axis in range(3):
                y1 = packed[1, axis]
                packed[2, axis] = packed[2, axis] - a1 * y1
                first_dir[axis] = y1 - a1 * packed[0, axis]
            gather(c, 2)
            remote(first_dir, mate.at[0], mate_sem.at[2], mate_sem.at[3], sibling).start()
            remote(packed.at[2], mate.at[1], mate_sem.at[2], mate_sem.at[3], sibling).start()
            early = (red_src[0][:, 0:128], red_src[0][:, 128:256], inner(first_dir, first_dir),
                     inner(first_dir, packed.at[2]), inner(packed.at[2], packed.at[2]))
            for n, value in enumerate(early):
                red_src[2, :, n * 128:n * 128 + 128] = value

    for_each_core(steps)

    reduce_plane(1, ((5, fold(part[...])),))
    reduce_line(1)
    wait_recv(red_one.at[1, pl.ds(0, 2 * LINE - 1)], red_sem.at[1, 3])
    low, high = reduced(1, 0), reduced(1, 1)
    for k in range(6):
        at = slice(k * 128, k * 128 + 128)
        moments[k + 1, 0:8] = jnp.broadcast_to(jnp.where(front, low[:, at], high[:, at]), (8, 128))
    moments[7, 0:8] = jnp.zeros((8, 128), F32)
    moments[8, 0:8] = jnp.ones((8, 128), F32)
    m0, m1, e1, f1, g, third, zero, one = (moments[k, 0:8] for k in range(1, 9))

    a1, a2, bb2 = m1 / m0, f1 / e1, e1 / m0
    e2 = g - a2 * f1 - bb2 * e1
    bb3 = e2 / e1
    a3 = (third - a2 * g - bb2 * (f1 + a1 * e1)) / e2 - a2
    d1, d2, d3 = 1.0 + a1, 1.0 + a2, 1.0 + a3
    scale = (d1 + d2 + d3) / ITERS
    current = (d1 / scale, jnp.sqrt(bb2) / scale, zero, d2 / scale, jnp.sqrt(bb3) / scale, d3 / scale)
    partner = (one, zero, zero, one, zero, one)

    def inverse_three(m):
        c00, c01, c02 = m[3] * m[5] - m[4] * m[4], m[2] * m[4] - m[1] * m[5], m[1] * m[4] - m[2] * m[3]
        c11, c12, c22 = m[0] * m[5] - m[2] * m[2], m[1] * m[2] - m[0] * m[4], m[0] * m[3] - m[1] * m[1]
        over = 1.0 / (m[0] * c00 + m[1] * c01 + m[2] * c02)
        return tuple(c * over for c in (c00, c01, c02, c11, c12, c22))

    def newton(_, state):
        now, other = state
        return (tuple(0.5 * (u + v) for u, v in zip(now, inverse_three(other))),
                tuple(0.5 * (u + v) for u, v in zip(other, inverse_three(now))))

    current, partner = lax.fori_loop(0, 20, newton, (current, partner))
    size = jnp.sqrt(scale)
    beta = jnp.sqrt(m0)
    r1, r2, r3 = (current[k] * size for k in range(3))
    f2, f3 = beta * r2 / jnp.sqrt(e1), beta * r3 / jnp.sqrt(e2)
    wait_recv(mate, mate_sem.at[3])
    c0, c1, c2 = (jnp.concatenate([c, c, c, c], axis=0) for c in (r1 - f3 * bb2, f2 - f3 * a2, f3))
    for axis in range(3):
        out_ref[axis] = (c0 * z_ref[axis] + c1 * jnp.where(keep, first_dir[axis], turn(mate[0, axis]))
                         + c2 * jnp.where(keep, packed[2, axis], turn(mate[1, axis])))

    wait_send(posrow.at[0], pos_sem.at[0])
    wait_send(z_mate, mate_sem.at[0])
    wait_send(mate, mate_sem.at[2])
    wait_send(posbuf.at[pl.ds(0, 22)], pos_sem.at[2])
    wait_send(ag.at[2, pl.ds(0, NEEDED - 1 + LINE - 1)], ag_send.at[2])
    for k, count in enumerate((LINE - 1, 2 * LINE - 1)):
        wait_send(red_one.at[k, pl.ds(0, PLANE - 1)], red_sem.at[k, 0])
        wait_send(red_one.at[k, pl.ds(0, count)], red_sem.at[k, 2])
    for step in range(2):
        @pl.when(core == 0)
        def _(step=step):
            wait_send(ag.at[step, pl.ds(0, LINE - 1)], ag_send.at[step])
            wait_send(rs_send.at[step, pl.ds(0, PLANE - 1)], rs_sent.at[step])

        @pl.when(core == 1)
        def _(step=step):
            wait_send(ag.at[step, pl.ds(0, PLANE - 1)], ag_send.at[step])
            wait_send(rs_send.at[step, pl.ds(0, LINE - 1)], rs_sent.at[step])


def shards(positions, start_vector):
    chunk = (3, 32, 128)
    return pl.pallas_call(
        kernel,
        out_shape=jax.ShapeDtypeStruct(start_vector.shape, F32),
        in_specs=[pl.BlockSpec(memory_space=pltpu.VMEM)] * 2,
        out_specs=pl.BlockSpec(memory_space=pltpu.VMEM),
        scratch_shapes=[
            pltpu.VMEM((2, 1, 128), F32),
            pltpu.VMEM((PLANE + LINE, 1, 256), F32),
            pltpu.VMEM((2, 3, BLOCK, 128), F32),
            pltpu.VMEM((2, 8, BLOCK), F32),
            pltpu.VMEM((2, BLOCK, 6 * BLOCK), BF16),
            pltpu.VMEM((2, BLOCK, 6 * BLOCK), BF16),
            pltpu.VMEM((2, BLOCK, 512), BF16),
            pltpu.VMEM((2, 6 * BLOCK, 256), BF16),
            pltpu.VMEM((3, PLANE + LINE) + chunk, F32),
            pltpu.VMEM((2, PLANE) + chunk, F32),
            pltpu.VMEM((2, PLANE) + chunk, F32),
            pltpu.VMEM((3,) + chunk, F32),
            pltpu.VMEM(chunk, F32),
            pltpu.VMEM((2,) + chunk, F32),
            pltpu.VMEM((3, 256, 128), F32),
            pltpu.VMEM((4, 256, 256), F32),
            pltpu.VMEM((32, 128), F32),
            pltpu.VMEM((4, 1, WIDTH), F32),
            pltpu.VMEM((2, PLANE, 1, WIDTH), F32),
            pltpu.VMEM((2, 2, LINE, 1, WIDTH), F32),
            pltpu.VMEM((9, 32, 128), F32),
            pltpu.VMEM((8, 128), F32),
            pltpu.VMEM(chunk, F32),
            pltpu.SemaphoreType.DMA((4,)),
            pltpu.SemaphoreType.DMA((4,)),
            pltpu.SemaphoreType.DMA((3, 2)),
            pltpu.SemaphoreType.DMA((3, 2)),
            pltpu.SemaphoreType.DMA((3,)),
            pltpu.SemaphoreType.DMA((2,)),
            pltpu.SemaphoreType.DMA((2,)),
            pltpu.SemaphoreType.DMA((2, 4)),
        ],
        compiler_params=pltpu.CompilerParams(
            collective_id=0, has_side_effects=True, vmem_limit_bytes=40 * 1024 * 1024),
    )(positions, start_vector)


def solution(mesh):
    in_specs = (P(None, ("row", "col")), P(None, ("row", "col"), None))
    out_specs = P(None, ("row", "col"), None)
    return jax.shard_map(shards, mesh=mesh, in_specs=in_specs, out_specs=out_specs, check_vma=False)
```

```python
import functools

import jax
import jax.numpy as jnp
from jax import lax
from jax.experimental import pallas as pl
from jax.experimental.pallas import tpu as pltpu
from jax.sharding import PartitionSpec as P

ITERS = 3
RADIUS = 0.4
MESH = pl.DeviceIdType.MESH
F32 = jnp.float32
BF16 = jnp.bfloat16

PLANE, LINE = 16, 8
PLACES = ((0, 0), (2, 0), (0, 2), (2, 2), (0, 1), (3, 0), (1, 1), (1, 3), (3, 2), (2, 1),
          (0, 3), (1, 0), (3, 3), (3, 1), (1, 2), (2, 3))
NEEDED = 10
ORDER = ((0, 1), (0, 3), (1, 0), (3, 0), (2, 0), (0, 2), (1, 1), (3, 3), (1, 3), (3, 1),
         (1, 2), (2, 1), (3, 2), (2, 3), (2, 2))
STEPS = (0, 1, 7, 2, 6, 3, 5, 4)


def seen_in_plane(dx, dy):
    return PLACES.index((-dx % 4, -dy % 4))


def seen_in_line(dz):
    return PLANE + STEPS.index(-dz % 8)


HALF = 64
BLOCK = 512
WIDTH = 768


def kernel(pos_ref, z_ref, out_ref, posrow, posbuf, colbc, lanevec, mob_high, mob_low, wide, narrow, ag, rs, rs_send,
           packed, first_dir, mate, acc, acc_wide, part, red_src, red_one, red_two, moments, flatten,
           z_mate, mate_sem, pos_sem, line_sem, plane_sem, ag_send, rs_recv, rs_sent, red_sem):
    row, col = lax.axis_index("row"), lax.axis_index("col")
    x, core = lax.div(row, 2), lax.rem(row, 2)
    z, y = lax.div(col, 4), lax.rem(col, 4)

    xs = [lax.rem(x + d, 4) for d in range(4)]
    ys = [lax.rem(y + d, 4) for d in range(4)]
    zs = [lax.rem(z + d, 8) for d in range(8)]

    def plane_at(dx, dy):
        return (xs[dx] * 2 + core, z * 4 + ys[dy])

    far_places, far_steps = PLACES[:0:-1], STEPS[:0:-1]

    def line_at(dz):
        return (row, zs[dz] * 4 + y)

    def line_mate(dz):
        return (x * 2 + 1 - core, zs[dz] * 4 + y)

    sibling = (x * 2 + 1 - core, col)

    def for_each_core(program):
        for c in range(2):
            pl.when(core == c)(functools.partial(program, c))


    def remote(src, dst, send, recv, device):
        return pltpu.make_async_remote_copy(
            src_ref=src, dst_ref=dst, send_sem=send, recv_sem=recv, device_id=device, device_id_type=MESH)

    def wait_recv(ref, sem):
        remote(ref, ref, sem, sem, (row, col)).wait_recv()

    def wait_send(ref, sem):
        remote(ref, ref, sem, sem, (row, col)).wait_send()

    first = lax.broadcasted_iota(jnp.int32, (32, 128), 1) < HALF
    keep = first == (core == 0)

    def turn(value):
        return pltpu.roll(value, HALF, 1)

    barrier = pltpu.get_barrier_semaphore()

    def signal(device):
        pl.semaphore_signal(barrier, inc=1, device_id=device, device_id_type=MESH)

    signal(sibling)
    for dx, dy in far_places:
        signal(plane_at(dx, dy))
    for dz in far_steps:
        signal(line_at(dz))
        signal(line_mate(dz))

    flatten[...] = jnp.zeros_like(flatten)
    flatten[0:3, 0:32] = pos_ref[...].astype(F32)
    rows3 = flatten[...]
    posrow[core] = rows3[0:1] + pltpu.roll(rows3[1:2], 32, 1) + pltpu.roll(rows3[2:3], 64, 1)
    pl.semaphore_wait(barrier, 30)

    remote(posrow.at[core], posrow.at[core], pos_sem.at[0], pos_sem.at[1], sibling).start()
    remote(z_ref, z_mate, mate_sem.at[0], mate_sem.at[1], sibling).start()
    wait_recv(posrow.at[0], pos_sem.at[1])
    both = jnp.concatenate([posrow[0], posrow[1]], axis=1)
    posbuf[0] = both
    posbuf[PLANE] = both
    for n, spot in enumerate(far_places):
        if n < 7:
            remote(posbuf.at[PLANE], posbuf.at[seen_in_line(far_steps[n])], pos_sem.at[2], pos_sem.at[3],
                   line_at(far_steps[n])).start()
        remote(posbuf.at[0], posbuf.at[seen_in_plane(*spot)], pos_sem.at[2], pos_sem.at[3], plane_at(*spot)).start()
    wait_recv(z_mate, mate_sem.at[1])
    for axis in range(3):
        packed[0, axis] = jnp.where(keep, z_ref[axis], turn(z_mate[axis]))

    def gather(c, step):
        def to_line():
            for dz in far_steps:
                slot = seen_in_line(dz)
                remote(packed.at[step], ag.at[step, slot], ag_send.at[step], line_sem.at[step, (slot - PLANE) // 4],
                       line_at(dz)).start()

        def to_plane(some):
            for spot in ORDER[::-1]:
                slot = seen_in_plane(*spot)
                if slot < NEEDED or not some:
                    remote(packed.at[step], ag.at[step, slot], ag_send.at[step], plane_sem.at[step, slot // 8],
                           plane_at(*spot)).start()

        if c == 0:
            to_line()
        if step == 2:
            to_plane(True)
        elif c == 1:
            to_plane(False)
        if c == 1 and step == 2:
            to_line()
        ag[step, 0] = packed[step]
        ag[step, PLANE] = packed[step]

    def wait_line(step, part_of):
        wait_recv(ag.at[step, pl.ds(0, 4 if part_of else 3)], line_sem.at[step, part_of])

    def wait_plane(step, part_of, last=False):
        if part_of == 0:
            wait_recv(ag.at[step, pl.ds(0, 7)], plane_sem.at[step, 0])
        else:
            wait_recv(ag.at[step, pl.ds(0, NEEDED - 8 if last else 8)], plane_sem.at[step, 1])

    for_each_core(lambda c: gather(c, 0))
    acc[...] = jnp.zeros_like(acc)
    acc_wide[...] = jnp.zeros_like(acc_wide)
    part[...] = jnp.zeros_like(part)
    ag[2, NEEDED:PLANE] = jnp.zeros((PLANE - NEEDED, 3, 32, 128), F32)
    for k in range(2):
        red_src[2 * k] = jnp.zeros((1, WIDTH), F32)
    narrow[...] = jnp.zeros_like(narrow)
    wait_recv(posbuf.at[pl.ds(0, 22)], pos_sem.at[3])

    lane_of = lax.broadcasted_iota(jnp.int32, (BLOCK, 128), 1)
    bead_of = lax.broadcasted_iota(jnp.int32, (BLOCK, 128), 0) & 31
    entry_of = lax.broadcasted_iota(jnp.int32, (128, BLOCK), 0)
    column_of = lax.broadcasted_iota(jnp.int32, (128, BLOCK), 1) & 31
    owner_of = lax.broadcasted_iota(jnp.int32, (16, BLOCK), 1) >> 5
    source_of = lax.broadcasted_iota(jnp.int32, (16, BLOCK), 0)
    ones = jnp.ones((128, 128), BF16)

    def place(at, d):
        return posbuf[at + d // 2][:, (d % 2) * 128:(d % 2) * 128 + 128]

    @pl.loop(0, 2)
    def _(h):
        rows_at = jnp.where(core == 0, h, 2) * 8
        lanes_at = jnp.where(core == 0, 2, h) * 8
        spread = jnp.concatenate([jnp.broadcast_to(place(rows_at, d), (32, 128)) for d in range(16)], axis=0)
        flat = jnp.concatenate([place(lanes_at, d) for d in range(16)], axis=0).astype(BF16)
        for axis in range(3):
            own = jnp.where(lane_of == axis * 32 + bead_of, spread, 0.0).astype(BF16)
            colbc[h, axis] = jnp.dot(own, ones, preferred_element_type=F32)
            pick = jnp.where(entry_of == axis * 32 + column_of, 1.0, 0.0).astype(BF16)
            moved = jnp.dot(flat, pick, preferred_element_type=F32)
            lanevec[h, axis:axis + 1, :] = jnp.sum(jnp.where(owner_of == source_of, moved, 0.0), axis=0, keepdims=True)

    def tile_of(c, t):
        return (4 - t) % 4 if c == 0 else 1 - t // 2

    def places(c, t):
        tile = tile_of(c, t)
        h, rt = (tile // 2, tile % 2) if c == 0 else (t % 2, tile)
        return h, c * h, rt * 256

    def build(c, t):
        h, _, begin = places(c, t)

        @pl.loop(0, 16, unroll=2)
        def _(r):
            rows = pl.ds(pl.multiple_of(begin + r * 16, 16), 16)
            mine = [colbc[h, axis, rows, :] for axis in range(3)]
            for tile in range(4):
                lanes = slice(tile * 128, tile * 128 + 128)
                d = [mine[axis] - lanevec[h, axis:axis + 1, lanes] for axis in range(3)]
                squared = d[0] * d[0] + d[1] * d[1] + d[2] * d[2]
                root = lax.rsqrt(jnp.where(squared > 0.5, squared, 1e30))
                inverse = root * root
                prefactor = (0.75 * RADIUS) * root
                iso = prefactor * (1.0 + (2.0 / 3.0 * RADIUS * RADIUS) * inverse)
                along = (prefactor * inverse) * (1.0 - (2.0 * RADIUS * RADIUS) * inverse)
                s = [along * d[axis] for axis in range(3)]
                parts = (s[0] * d[0] + iso, s[0] * d[1], s[0] * d[2], s[1] * d[1] + iso, s[1] * d[2],
                         s[2] * d[2] + iso)
                for k, value in enumerate(parts):
                    high = value.astype(BF16)
                    at = (tile // 2) * 1536 + k * 256 + (tile % 2) * 128
                    at = slice(at, at + 128)
                    mob_high[h, rows, at] = high
                    mob_low[h, rows, at] = (value - high.astype(F32)).astype(BF16)

    def widen(c, h):
        base = PLANE if c == 0 else h * 8

        @pl.loop(0, 8, unroll=4)
        def _(s):
            for axis in range(3):
                value = ag[0, base + s, axis]
                other = turn(value)
                for j, both in enumerate((jnp.where(first, value, other), jnp.where(first, other, value))):
                    high = both.astype(BF16).astype(F32)
                    tile = jnp.where(first, high, both - high).astype(BF16)
                    at = pl.ds(pl.multiple_of(s * 64 + j * 32, 32), 32)
                    wide[h, at, axis * 128:axis * 128 + 128] = tile
                    if axis == 0:
                        wide[h, at, 384:512] = tile

    def arrange(step, base, w, quarter, weight):
        @pl.loop(0, 4, unroll=4)
        def _(s):
            values = [ag[step, base + s, axis] * weight for axis in range(3)]
            others = [turn(value) for value in values]
            for j in range(2):
                left, right = (values, others) if j == 0 else (others, values)
                lx, ly, lz = (jnp.where(first, v, 0.0).astype(BF16) for v in left)
                ry, rz = (jnp.where(first, 0.0, v).astype(BF16) for v in right[1:])
                yx = jnp.where(first, left[1], right[0]).astype(BF16)
                for k, half, tile in ((0, 0, lx), (1, 0, yx), (2, 0, lz), (2, 1, lx), (3, 0, ry), (4, 0, rz),
                                      (4, 1, ly), (5, 1, lz)):
                    at = pl.ds(pl.multiple_of(quarter * 1536 + k * 256 + s * 64 + j * 32, 32), 32)
                    narrow[w, at, half * 128:half * 128 + 128] = tile

    def arrange_half(c, step, part_of):
        if c == 0:
            wait_line(step, part_of)
            arrange(step, PLANE + 4 * part_of, 0, part_of, 1.0)
        else:
            wait_plane(step, part_of, step == 2)
            for quarter in range(2):
                slot = 8 * part_of + 4 * quarter
                if step == 1 or slot < NEEDED:
                    arrange(step, slot, part_of, quarter, 2.0 if step == 2 and slot >= 4 else 1.0)

    def dot(left, right):
        return jnp.dot(left, right, preferred_element_type=F32)

    def product(c, t):
        h, w, begin = places(c, t)
        rows = slice(begin, begin + 256)

        def both(k, lo, hi):
            total = 0.0
            for quarter in range(2):
                at = slice(quarter * 1536 + k * 256, quarter * 1536 + k * 256 + 256)
                right = wide[w, quarter * 256:quarter * 256 + 256, lo:hi]
                total = total + dot(mob_high[h, rows, at], right) + dot(mob_low[h, rows, at], right)
            return total

        xy, yz, zx = both(1, 0, 256), both(4, 128, 384), both(2, 256, 512)
        return (both(0, 0, 128) + xy[:, 128:] + zx[:, :128],
                both(3, 128, 256) + xy[:, :128] + yz[:, 128:],
                both(5, 256, 384) + zx[:, 128:] + yz[:, :128])

    def halves(i, upper):
        return slice(i * 64 + upper * 32, i * 64 + upper * 32 + 32)

    def pack(_, i):
        chunk = []
        for axis in range(3):
            low, high = acc[axis, halves(i, 0), :], acc[axis, halves(i, 1), :]
            chunk.append(jnp.where(first, low + turn(low), high + turn(high)))
        return chunk

    def pack_wide(tile, i):
        low, high = halves(i, 0), halves(i, 1)
        xy_low, xy_high = acc_wide[tile, low, :128], acc_wide[tile, high, :128]
        z_low, z_high = acc_wide[tile, low, 128:], acc_wide[tile, high, 128:]
        return (jnp.where(first, xy_low, turn(xy_high)), jnp.where(first, turn(xy_low), xy_high),
                jnp.where(first, z_low, turn(z_high)))

    def scatter(c, step, t, packer):
        def fill(tile):
            chunks = [packer(tile, i) for i in range(4)]
            for i, chunk in enumerate(chunks):
                for axis, value in enumerate(chunk):
                    rs_send[step, tile * 4 + i, axis] = value

        def send_plane(tile):
            fill(tile)
            for i in (3, 2, 1, 0):
                spot = PLACES[tile * 4 + i]
                if tile * 4 + i:
                    remote(rs_send.at[step, tile * 4 + i], rs.at[step, seen_in_plane(*spot)], rs_sent.at[step],
                           rs_recv.at[step], plane_at(*spot)).start()
                else:
                    rs[step, 0] = rs_send[step, 0]

        def send_line(tile):
            fill(tile)
            for i in (3, 2, 1, 0):
                dz = STEPS[tile * 4 + i]
                if dz:
                    remote(rs_send.at[step, tile * 4 + i], rs.at[step, seen_in_line(dz) - PLANE], rs_sent.at[step],
                           rs_recv.at[step], line_at(dz)).start()
                else:
                    rs[step, 0] = rs_send[step, 0]

        (send_line if c else send_plane)(tile_of(c, t))

    def collect(c, step):
        count = LINE if c else PLANE
        wait_recv(rs.at[step, pl.ds(0, count - 1)], rs_recv.at[step])
        for axis in range(3):
            packed[step + 1, axis] = sum((rs[step, s, axis] for s in range(1, count)), rs[step, 0, axis])

    front = lax.broadcasted_iota(jnp.int32, (1, 128), 1) < HALF

    def fold(value):
        line = jnp.sum(value, axis=0, keepdims=True)
        return line + turn(line)

    def inner(left, right):
        return fold(sum(left[axis] * right[axis] for axis in range(3)))

    def reduce_plane(k, values):
        for n, value in values:
            red_src[2 * k, :, n * 128:n * 128 + 128] = value
        for spot in far_places:
            remote(red_src.at[2 * k], red_one.at[k, seen_in_plane(*spot)], red_sem.at[k, 0], red_sem.at[k, 1], plane_at(*spot)).start()
        red_one[k, 0] = red_src[2 * k]

    def reduce_line(k):
        def send(dz, device):
            slot = seen_in_line(dz) - PLANE
            remote(red_src.at[2 * k + 1], red_two.at[k, core, slot], red_sem.at[k, 2], red_sem.at[k, 3], device).start()

        wait_recv(red_one.at[k, pl.ds(0, PLANE - 1)], red_sem.at[k, 1])
        red_src[2 * k + 1] = sum((red_one[k, s] for s in range(1, PLANE)), red_one[k, 0])
        for dz in far_steps:
            send(dz, line_at(dz))
            if k == 1:
                send(dz, line_mate(dz))
        if k == 1:
            send(0, sibling)
        red_two[k, core, 0] = red_src[2 * k + 1]

    def reduced(k, c):
        return sum((red_two[k, c, s] for s in range(1, LINE)), red_two[k, c, 0])

    def steps(c):
        built = 4 if c else 2
        for t in range(built):
            build(c, t)
        if c == 0:
            wait_line(0, 0)
            wait_line(0, 1)
            widen(c, 0)
        else:
            wait_plane(0, 0)
            wait_plane(0, 1)
            widen(c, 0)
            widen(c, 1)
        for t in range(4):
            if t >= built:
                build(c, t)
            for axis, value in enumerate(product(c, t)):
                acc[axis] = acc[axis] + value if c == 1 and t % 2 == 1 else value
            if c == 0 or t % 2 == 1:
                scatter(c, 0, t, pack)
        collect(c, 0)
        gather(c, 1)
        reduce_plane(0, ((0, inner(packed.at[0], packed.at[0])), (1, inner(packed.at[0], packed.at[1]))))

        for step in (1, 2):
            for part_of in range(2):
                arrange_half(c, step, part_of)
                for t in range(4):
                    tile = tile_of(c, t)
                    if c == 1 and t % 2 == 0:
                        continue
                    skip = c == 0 and step == 2 and tile == 3
                    if not skip:
                        if c == 0:
                            h, rt, w, inner_at = tile // 2, tile % 2, 0, slice(part_of * 1536, part_of * 1536 + 1536)
                        else:
                            h, rt, w, inner_at = part_of, tile, part_of, slice(0, 1536 * (2 - part_of * (step - 1)))
                        value = dot(mob_high[h, rt * 256:rt * 256 + 256, inner_at], narrow[w, inner_at, :])
                        acc_wide[tile] = acc_wide[tile] + value if part_of else value
                    if part_of == 0:
                        continue
                    if step == 1:
                        scatter(c, 1, t, pack_wide)
                        continue
                    if t == c:
                        for half in range(2):
                            wait_line(2, half) if c else wait_plane(2, half, True)
                    if c == 0 and skip:
                        continue
                    total = jnp.zeros((32, 128), F32)
                    for i in range(4):
                        for axis, value in enumerate(pack_wide(tile, i)):
                            total = total + value * ag[2, (PLANE if c else 0) + tile * 4 + i, axis]
                    part[...] += total * (2.0 if c == 0 and tile > 0 else 1.0)
            if step == 2:
                break
            reduce_line(0)
            collect(c, 1)
            wait_recv(red_two.at[0, 0, pl.ds(0, LINE - 1)], red_sem.at[0, 3])
            total = reduced(0, c)
            moments[0] = jnp.broadcast_to(total[:, 128:256] / total[:, 0:128], (32, 128))
            a1 = moments[0]
            for axis in range(3):
                y1 = packed[1, axis]
                packed[2, axis] = packed[2, axis] - a1 * y1
                first_dir[axis] = y1 - a1 * packed[0, axis]
            gather(c, 2)
            remote(first_dir, mate.at[0], mate_sem.at[2], mate_sem.at[3], sibling).start()
            remote(packed.at[2], mate.at[1], mate_sem.at[2], mate_sem.at[3], sibling).start()
            early = (red_src[0][:, 0:128], red_src[0][:, 128:256], inner(first_dir, first_dir),
                     inner(first_dir, packed.at[2]), inner(packed.at[2], packed.at[2]))
            for n, value in enumerate(early):
                red_src[2, :, n * 128:n * 128 + 128] = value

    for_each_core(steps)

    reduce_plane(1, ((5, fold(part[...])),))
    reduce_line(1)
    wait_recv(red_one.at[1, pl.ds(0, 2 * LINE - 1)], red_sem.at[1, 3])
    low, high = reduced(1, 0), reduced(1, 1)
    for k in range(6):
        at = slice(k * 128, k * 128 + 128)
        moments[k + 1, 0:8] = jnp.broadcast_to(jnp.where(front, low[:, at], high[:, at]), (8, 128))
    moments[7, 0:8] = jnp.zeros((8, 128), F32)
    moments[8, 0:8] = jnp.ones((8, 128), F32)
    m0, m1, e1, f1, g, third, zero, one = (moments[k, 0:8] for k in range(1, 9))

    a1, a2, bb2 = m1 / m0, f1 / e1, e1 / m0
    e2 = g - a2 * f1 - bb2 * e1
    bb3 = e2 / e1
    a3 = (third - a2 * g - bb2 * (f1 + a1 * e1)) / e2 - a2
    d1, d2, d3 = 1.0 + a1, 1.0 + a2, 1.0 + a3
    scale = (d1 + d2 + d3) / ITERS
    current = (d1 / scale, jnp.sqrt(bb2) / scale, zero, d2 / scale, jnp.sqrt(bb3) / scale, d3 / scale)
    partner = (one, zero, zero, one, zero, one)

    def inverse_three(m):
        c00, c01, c02 = m[3] * m[5] - m[4] * m[4], m[2] * m[4] - m[1] * m[5], m[1] * m[4] - m[2] * m[3]
        c11, c12, c22 = m[0] * m[5] - m[2] * m[2], m[1] * m[2] - m[0] * m[4], m[0] * m[3] - m[1] * m[1]
        over = 1.0 / (m[0] * c00 + m[1] * c01 + m[2] * c02)
        return tuple(c * over for c in (c00, c01, c02, c11, c12, c22))

    def newton(_, state):
        now, other = state
        return (tuple(0.5 * (u + v) for u, v in zip(now, inverse_three(other))),
                tuple(0.5 * (u + v) for u, v in zip(other, inverse_three(now))))

    current, partner = lax.fori_loop(0, 20, newton, (current, partner))
    size = jnp.sqrt(scale)
    beta = jnp.sqrt(m0)
    r1, r2, r3 = (current[k] * size for k in range(3))
    f2, f3 = beta * r2 / jnp.sqrt(e1), beta * r3 / jnp.sqrt(e2)
    wait_recv(mate, mate_sem.at[3])
    c0, c1, c2 = (jnp.concatenate([c, c, c, c], axis=0) for c in (r1 - f3 * bb2, f2 - f3 * a2, f3))
    for axis in range(3):
        out_ref[axis] = (c0 * z_ref[axis] + c1 * jnp.where(keep, first_dir[axis], turn(mate[0, axis]))
                         + c2 * jnp.where(keep, packed[2, axis], turn(mate[1, axis])))

    wait_send(posrow.at[0], pos_sem.at[0])
    wait_send(z_mate, mate_sem.at[0])
    wait_send(mate, mate_sem.at[2])
    wait_send(posbuf.at[pl.ds(0, 22)], pos_sem.at[2])
    wait_send(ag.at[2, pl.ds(0, NEEDED - 1 + LINE - 1)], ag_send.at[2])
    for k, count in enumerate((LINE - 1, 2 * LINE - 1)):
        wait_send(red_one.at[k, pl.ds(0, PLANE - 1)], red_sem.at[k, 0])
        wait_send(red_one.at[k, pl.ds(0, count)], red_sem.at[k, 2])
    for step in range(2):
        @pl.when(core == 0)
        def _(step=step):
            wait_send(ag.at[step, pl.ds(0, LINE - 1)], ag_send.at[step])
            wait_send(rs_send.at[step, pl.ds(0, PLANE - 1)], rs_sent.at[step])

        @pl.when(core == 1)
        def _(step=step):
            wait_send(ag.at[step, pl.ds(0, PLANE - 1)], ag_send.at[step])
            wait_send(rs_send.at[step, pl.ds(0, LINE - 1)], rs_sent.at[step])


def shards(positions, start_vector):
    chunk = (3, 32, 128)
    return pl.pallas_call(
        kernel,
        out_shape=jax.ShapeDtypeStruct(start_vector.shape, F32),
        in_specs=[pl.BlockSpec(memory_space=pltpu.VMEM)] * 2,
        out_specs=pl.BlockSpec(memory_space=pltpu.VMEM),
        scratch_shapes=[
            pltpu.VMEM((2, 1, 128), F32),
            pltpu.VMEM((PLANE + LINE, 1, 256), F32),
            pltpu.VMEM((2, 3, BLOCK, 128), F32),
            pltpu.VMEM((2, 8, BLOCK), F32),
            pltpu.VMEM((2, BLOCK, 6 * BLOCK), BF16),
            pltpu.VMEM((2, BLOCK, 6 * BLOCK), BF16),
            pltpu.VMEM((2, BLOCK, 512), BF16),
            pltpu.VMEM((2, 6 * BLOCK, 256), BF16),
            pltpu.VMEM((3, PLANE + LINE) + chunk, F32),
            pltpu.VMEM((2, PLANE) + chunk, F32),
            pltpu.VMEM((2, PLANE) + chunk, F32),
            pltpu.VMEM((3,) + chunk, F32),
            pltpu.VMEM(chunk, F32),
            pltpu.VMEM((2,) + chunk, F32),
            pltpu.VMEM((3, 256, 128), F32),
            pltpu.VMEM((4, 256, 256), F32),
            pltpu.VMEM((32, 128), F32),
            pltpu.VMEM((4, 1, WIDTH), F32),
            pltpu.VMEM((2, PLANE, 1, WIDTH), F32),
            pltpu.VMEM((2, 2, LINE, 1, WIDTH), F32),
            pltpu.VMEM((9, 32, 128), F32),
            pltpu.VMEM((8, 128), F32),
            pltpu.VMEM(chunk, F32),
            pltpu.SemaphoreType.DMA((4,)),
            pltpu.SemaphoreType.DMA((4,)),
            pltpu.SemaphoreType.DMA((3, 2)),
            pltpu.SemaphoreType.DMA((3, 2)),
            pltpu.SemaphoreType.DMA((3,)),
            pltpu.SemaphoreType.DMA((2,)),
            pltpu.SemaphoreType.DMA((2,)),
            pltpu.SemaphoreType.DMA((2, 4)),
        ],
        compiler_params=pltpu.CompilerParams(
            collective_id=0, has_side_effects=True, vmem_limit_bytes=40 * 1024 * 1024),
    )(positions, start_vector)


def solution(mesh):
    in_specs = (P(None, ("row", "col")), P(None, ("row", "col"), None))
    out_specs = P(None, ("row", "col"), None)
    return jax.shard_map(shards, mesh=mesh, in_specs=in_specs, out_specs=out_specs, check_vma=False)
```

```python
import functools

import jax
import jax.numpy as jnp
from jax import lax
from jax.experimental import pallas as pl
from jax.experimental.pallas import tpu as pltpu
from jax.sharding import PartitionSpec as P

ITERS = 3
RADIUS = 0.4
MESH = pl.DeviceIdType.MESH
F32 = jnp.float32
BF16 = jnp.bfloat16

PLANE, LINE = 16, 8
PLACES = ((0, 0), (2, 0), (0, 2), (2, 2), (0, 1), (3, 0), (1, 1), (1, 3), (3, 2), (2, 1),
          (0, 3), (1, 0), (3, 3), (3, 1), (1, 2), (2, 3))
NEEDED = 10
ORDER = ((0, 1), (0, 3), (1, 0), (3, 0), (2, 0), (0, 2), (1, 1), (3, 3), (1, 3), (3, 1),
         (1, 2), (2, 1), (3, 2), (2, 3), (2, 2))
STEPS = (0, 1, 7, 2, 6, 3, 5, 4)


def seen_in_plane(dx, dy):
    return PLACES.index((-dx % 4, -dy % 4))


def seen_in_line(dz):
    return PLANE + STEPS.index(-dz % 8)


HALF = 64
BLOCK = 512
WIDTH = 768


def kernel(pos_ref, z_ref, out_ref, posrow, posbuf, colbc, lanevec, mob_high, mob_low, wide, narrow, ag, rs, rs_send,
           packed, first_dir, mate, acc, acc_wide, part, red_src, red_one, red_two, moments, flatten,
           z_mate, mate_sem, pos_sem, line_sem, plane_sem, ag_send, rs_recv, rs_sent, red_sem):
    row, col = lax.axis_index("row"), lax.axis_index("col")
    x, core = lax.div(row, 2), lax.rem(row, 2)
    z, y = lax.div(col, 4), lax.rem(col, 4)

    xs = [lax.rem(x + d, 4) for d in range(4)]
    ys = [lax.rem(y + d, 4) for d in range(4)]
    zs = [lax.rem(z + d, 8) for d in range(8)]

    def plane_at(dx, dy):
        return (xs[dx] * 2 + core, z * 4 + ys[dy])

    far_places, far_steps = PLACES[:0:-1], STEPS[:0:-1]

    def line_at(dz):
        return (row, zs[dz] * 4 + y)

    def line_mate(dz):
        return (x * 2 + 1 - core, zs[dz] * 4 + y)

    sibling = (x * 2 + 1 - core, col)

    def for_each_core(program):
        for c in range(2):
            pl.when(core == c)(functools.partial(program, c))


    def remote(src, dst, send, recv, device):
        return pltpu.make_async_remote_copy(
            src_ref=src, dst_ref=dst, send_sem=send, recv_sem=recv, device_id=device, device_id_type=MESH)

    def wait_recv(ref, sem):
        remote(ref, ref, sem, sem, (row, col)).wait_recv()

    def wait_send(ref, sem):
        remote(ref, ref, sem, sem, (row, col)).wait_send()

    first = lax.broadcasted_iota(jnp.int32, (32, 128), 1) < HALF
    keep = first == (core == 0)

    def turn(value):
        return pltpu.roll(value, HALF, 1)

    barrier = pltpu.get_barrier_semaphore()

    def signal(device):
        pl.semaphore_signal(barrier, inc=1, device_id=device, device_id_type=MESH)

    signal(sibling)
    for dx, dy in far_places:
        signal(plane_at(dx, dy))
    for dz in far_steps:
        signal(line_at(dz))
        signal(line_mate(dz))

    flatten[...] = jnp.zeros_like(flatten)
    flatten[0:3, 0:32] = pos_ref[...].astype(F32)
    rows3 = flatten[...]
    posrow[core] = rows3[0:1] + pltpu.roll(rows3[1:2], 32, 1) + pltpu.roll(rows3[2:3], 64, 1)
    pl.semaphore_wait(barrier, 30)

    remote(posrow.at[core], posrow.at[core], pos_sem.at[0], pos_sem.at[1], sibling).start()
    remote(z_ref, z_mate, mate_sem.at[0], mate_sem.at[1], sibling).start()
    wait_recv(posrow.at[0], pos_sem.at[1])
    both = jnp.concatenate([posrow[0], posrow[1]], axis=1)
    posbuf[0] = both
    posbuf[PLANE] = both
    for n, spot in enumerate(far_places):
        if n < 7:
            remote(posbuf.at[PLANE], posbuf.at[seen_in_line(far_steps[n])], pos_sem.at[2], pos_sem.at[3],
                   line_at(far_steps[n])).start()
        remote(posbuf.at[0], posbuf.at[seen_in_plane(*spot)], pos_sem.at[2], pos_sem.at[3], plane_at(*spot)).start()
    wait_recv(z_mate, mate_sem.at[1])
    for axis in range(3):
        packed[0, axis] = jnp.where(keep, z_ref[axis], turn(z_mate[axis]))

    def gather(c, step):
        def to_line():
            for dz in STEPS[1:]:
                slot = seen_in_line(dz)
                remote(packed.at[step], ag.at[step, slot], ag_send.at[step], line_sem.at[step, (slot - PLANE) // 4],
                       line_at(dz)).start()

        def to_plane(some):
            for spot in sorted(ORDER, key=lambda spot: seen_in_plane(*spot) // 8):
                slot = seen_in_plane(*spot)
                if slot < NEEDED or not some:
                    remote(packed.at[step], ag.at[step, slot], ag_send.at[step], plane_sem.at[step, slot // 8],
                           plane_at(*spot)).start()

        if c == 0:
            to_line()
        if step == 2:
            to_plane(True)
        elif c == 1:
            to_plane(False)
        if c == 1 and step == 2:
            to_line()
        ag[step, 0] = packed[step]
        ag[step, PLANE] = packed[step]

    def wait_line(step, part_of):
        wait_recv(ag.at[step, pl.ds(0, 4 if part_of else 3)], line_sem.at[step, part_of])

    def wait_plane(step, part_of, last=False):
        if part_of == 0:
            wait_recv(ag.at[step, pl.ds(0, 7)], plane_sem.at[step, 0])
        else:
            wait_recv(ag.at[step, pl.ds(0, NEEDED - 8 if last else 8)], plane_sem.at[step, 1])

    for_each_core(lambda c: gather(c, 0))
    acc[...] = jnp.zeros_like(acc)
    acc_wide[...] = jnp.zeros_like(acc_wide)
    part[...] = jnp.zeros_like(part)
    ag[2, NEEDED:PLANE] = jnp.zeros((PLANE - NEEDED, 3, 32, 128), F32)
    for k in range(2):
        red_src[2 * k] = jnp.zeros((1, WIDTH), F32)
    narrow[...] = jnp.zeros_like(narrow)
    wait_recv(posbuf.at[pl.ds(0, 22)], pos_sem.at[3])

    lane_of = lax.broadcasted_iota(jnp.int32, (BLOCK, 128), 1)
    bead_of = lax.broadcasted_iota(jnp.int32, (BLOCK, 128), 0) & 31
    entry_of = lax.broadcasted_iota(jnp.int32, (128, BLOCK), 0)
    column_of = lax.broadcasted_iota(jnp.int32, (128, BLOCK), 1) & 31
    owner_of = lax.broadcasted_iota(jnp.int32, (16, BLOCK), 1) >> 5
    source_of = lax.broadcasted_iota(jnp.int32, (16, BLOCK), 0)
    ones = jnp.ones((128, 128), BF16)

    def place(at, d):
        return posbuf[at + d // 2][:, (d % 2) * 128:(d % 2) * 128 + 128]

    @pl.loop(0, 2)
    def _(h):
        rows_at = jnp.where(core == 0, h, 2) * 8
        lanes_at = jnp.where(core == 0, 2, h) * 8
        spread = jnp.concatenate([jnp.broadcast_to(place(rows_at, d), (32, 128)) for d in range(16)], axis=0)
        flat = jnp.concatenate([place(lanes_at, d) for d in range(16)], axis=0).astype(BF16)
        for axis in range(3):
            own = jnp.where(lane_of == axis * 32 + bead_of, spread, 0.0).astype(BF16)
            colbc[h, axis] = jnp.dot(own, ones, preferred_element_type=F32)
            pick = jnp.where(entry_of == axis * 32 + column_of, 1.0, 0.0).astype(BF16)
            moved = jnp.dot(flat, pick, preferred_element_type=F32)
            lanevec[h, axis:axis + 1, :] = jnp.sum(jnp.where(owner_of == source_of, moved, 0.0), axis=0, keepdims=True)

    def tile_of(c, t):
        return (4 - t) % 4 if c == 0 else 1 - t // 2

    def places(c, t):
        tile = tile_of(c, t)
        h, rt = (tile // 2, tile % 2) if c == 0 else (t % 2, tile)
        return h, c * h, rt * 256

    def build(c, t):
        h, _, begin = places(c, t)

        @pl.loop(0, 16, unroll=2)
        def _(r):
            rows = pl.ds(pl.multiple_of(begin + r * 16, 16), 16)
            mine = [colbc[h, axis, rows, :] for axis in range(3)]
            for tile in range(4):
                lanes = slice(tile * 128, tile * 128 + 128)
                d = [mine[axis] - lanevec[h, axis:axis + 1, lanes] for axis in range(3)]
                squared = d[0] * d[0] + d[1] * d[1] + d[2] * d[2]
                root = lax.rsqrt(jnp.where(squared > 0.5, squared, 1e30))
                inverse = root * root
                prefactor = (0.75 * RADIUS) * root
                iso = prefactor * (1.0 + (2.0 / 3.0 * RADIUS * RADIUS) * inverse)
                along = (prefactor * inverse) * (1.0 - (2.0 * RADIUS * RADIUS) * inverse)
                s = [along * d[axis] for axis in range(3)]
                parts = (s[0] * d[0] + iso, s[0] * d[1], s[0] * d[2], s[1] * d[1] + iso, s[1] * d[2],
                         s[2] * d[2] + iso)
                for k, value in enumerate(parts):
                    high = value.astype(BF16)
                    at = (tile // 2) * 1536 + k * 256 + (tile % 2) * 128
                    at = slice(at, at + 128)
                    mob_high[h, rows, at] = high
                    mob_low[h, rows, at] = (value - high.astype(F32)).astype(BF16)

    def widen(c, h):
        base = PLANE if c == 0 else h * 8

        @pl.loop(0, 8, unroll=4)
        def _(s):
            for axis in range(3):
                value = ag[0, base + s, axis]
                other = turn(value)
                for j, both in enumerate((jnp.where(first, value, other), jnp.where(first, other, value))):
                    high = both.astype(BF16).astype(F32)
                    tile = jnp.where(first, high, both - high).astype(BF16)
                    at = pl.ds(pl.multiple_of(s * 64 + j * 32, 32), 32)
                    wide[h, at, axis * 128:axis * 128 + 128] = tile
                    if axis == 0:
                        wide[h, at, 384:512] = tile

    def arrange(step, base, w, quarter, weight):
        @pl.loop(0, 4, unroll=4)
        def _(s):
            values = [ag[step, base + s, axis] * weight for axis in range(3)]
            others = [turn(value) for value in values]
            for j in range(2):
                left, right = (values, others) if j == 0 else (others, values)
                lx, ly, lz = (jnp.where(first, v, 0.0).astype(BF16) for v in left)
                ry, rz = (jnp.where(first, 0.0, v).astype(BF16) for v in right[1:])
                yx = jnp.where(first, left[1], right[0]).astype(BF16)
                for k, half, tile in ((0, 0, lx), (1, 0, yx), (2, 0, lz), (2, 1, lx), (3, 0, ry), (4, 0, rz),
                                      (4, 1, ly), (5, 1, lz)):
                    at = pl.ds(pl.multiple_of(quarter * 1536 + k * 256 + s * 64 + j * 32, 32), 32)
                    narrow[w, at, half * 128:half * 128 + 128] = tile

    def arrange_half(c, step, part_of):
        if c == 0:
            wait_line(step, part_of)
            arrange(step, PLANE + 4 * part_of, 0, part_of, 1.0)
        else:
            wait_plane(step, part_of, step == 2)
            for quarter in range(2):
                slot = 8 * part_of + 4 * quarter
                if step == 1 or slot < NEEDED:
                    arrange(step, slot, part_of, quarter, 2.0 if step == 2 and slot >= 4 else 1.0)

    def dot(left, right):
        return jnp.dot(left, right, preferred_element_type=F32)

    def product(c, t):
        h, w, begin = places(c, t)
        rows = slice(begin, begin + 256)

        def both(k, lo, hi):
            total = 0.0
            for quarter in range(2):
                at = slice(quarter * 1536 + k * 256, quarter * 1536 + k * 256 + 256)
                right = wide[w, quarter * 256:quarter * 256 + 256, lo:hi]
                total = total + dot(mob_high[h, rows, at], right) + dot(mob_low[h, rows, at], right)
            return total

        xy, yz, zx = both(1, 0, 256), both(4, 128, 384), both(2, 256, 512)
        return (both(0, 0, 128) + xy[:, 128:] + zx[:, :128],
                both(3, 128, 256) + xy[:, :128] + yz[:, 128:],
                both(5, 256, 384) + zx[:, 128:] + yz[:, :128])

    def halves(i, upper):
        return slice(i * 64 + upper * 32, i * 64 + upper * 32 + 32)

    def pack(_, i):
        chunk = []
        for axis in range(3):
            low, high = acc[axis, halves(i, 0), :], acc[axis, halves(i, 1), :]
            chunk.append(jnp.where(first, low + turn(low), high + turn(high)))
        return chunk

    def pack_wide(tile, i):
        low, high = halves(i, 0), halves(i, 1)
        xy_low, xy_high = acc_wide[tile, low, :128], acc_wide[tile, high, :128]
        z_low, z_high = acc_wide[tile, low, 128:], acc_wide[tile, high, 128:]
        return (jnp.where(first, xy_low, turn(xy_high)), jnp.where(first, turn(xy_low), xy_high),
                jnp.where(first, z_low, turn(z_high)))

    def scatter(c, step, t, packer):
        def fill(tile):
            chunks = [packer(tile, i) for i in range(4)]
            for i, chunk in enumerate(chunks):
                for axis, value in enumerate(chunk):
                    rs_send[step, tile * 4 + i, axis] = value

        def send_plane(tile):
            fill(tile)
            for i in (3, 2, 1, 0):
                spot = PLACES[tile * 4 + i]
                if tile * 4 + i:
                    remote(rs_send.at[step, tile * 4 + i], rs.at[step, seen_in_plane(*spot)], rs_sent.at[step],
                           rs_recv.at[step], plane_at(*spot)).start()
                else:
                    rs[step, 0] = rs_send[step, 0]

        def send_line(tile):
            fill(tile)
            for i in (3, 2, 1, 0):
                dz = STEPS[tile * 4 + i]
                if dz:
                    remote(rs_send.at[step, tile * 4 + i], rs.at[step, seen_in_line(dz) - PLANE], rs_sent.at[step],
                           rs_recv.at[step], line_at(dz)).start()
                else:
                    rs[step, 0] = rs_send[step, 0]

        (send_line if c else send_plane)(tile_of(c, t))

    def collect(c, step):
        count = LINE if c else PLANE
        wait_recv(rs.at[step, pl.ds(0, count - 1)], rs_recv.at[step])
        for axis in range(3):
            packed[step + 1, axis] = sum((rs[step, s, axis] for s in range(1, count)), rs[step, 0, axis])

    front = lax.broadcasted_iota(jnp.int32, (1, 128), 1) < HALF

    def fold(value):
        line = jnp.sum(value, axis=0, keepdims=True)
        return line + turn(line)

    def inner(left, right):
        return fold(sum(left[axis] * right[axis] for axis in range(3)))

    def reduce_plane(k, values):
        for n, value in values:
            red_src[2 * k, :, n * 128:n * 128 + 128] = value
        for spot in far_places:
            remote(red_src.at[2 * k], red_one.at[k, seen_in_plane(*spot)], red_sem.at[k, 0], red_sem.at[k, 1], plane_at(*spot)).start()
        red_one[k, 0] = red_src[2 * k]

    def reduce_line(k):
        def send(dz, device):
            slot = seen_in_line(dz) - PLANE
            remote(red_src.at[2 * k + 1], red_two.at[k, core, slot], red_sem.at[k, 2], red_sem.at[k, 3], device).start()

        wait_recv(red_one.at[k, pl.ds(0, PLANE - 1)], red_sem.at[k, 1])
        red_src[2 * k + 1] = sum((red_one[k, s] for s in range(1, PLANE)), red_one[k, 0])
        for dz in far_steps:
            send(dz, line_at(dz))
            if k == 1:
                send(dz, line_mate(dz))
        if k == 1:
            send(0, sibling)
        red_two[k, core, 0] = red_src[2 * k + 1]

    def reduced(k, c):
        return sum((red_two[k, c, s] for s in range(1, LINE)), red_two[k, c, 0])

    def steps(c):
        built = 4 if c else 2
        for t in range(built):
            build(c, t)
        if c == 0:
            wait_line(0, 0)
            wait_line(0, 1)
            widen(c, 0)
        else:
            wait_plane(0, 0)
            wait_plane(0, 1)
            widen(c, 0)
            widen(c, 1)
        for t in range(4):
            if t >= built:
                build(c, t)
            for axis, value in enumerate(product(c, t)):
                acc[axis] = acc[axis] + value if c == 1 and t % 2 == 1 else value
            if c == 0 or t % 2 == 1:
                scatter(c, 0, t, pack)
        collect(c, 0)
        gather(c, 1)
        reduce_plane(0, ((0, inner(packed.at[0], packed.at[0])), (1, inner(packed.at[0], packed.at[1]))))

        for step in (1, 2):
            for part_of in range(2):
                arrange_half(c, step, part_of)
                for t in range(4):
                    tile = tile_of(c, t)
                    if c == 1 and t % 2 == 0:
                        continue
                    skip = c == 0 and step == 2 and tile == 3
                    if not skip:
                        if c == 0:
                            h, rt, w, inner_at = tile // 2, tile % 2, 0, slice(part_of * 1536, part_of * 1536 + 1536)
                        else:
                            h, rt, w, inner_at = part_of, tile, part_of, slice(0, 1536 * (2 - part_of * (step - 1)))
                        value = dot(mob_high[h, rt * 256:rt * 256 + 256, inner_at], narrow[w, inner_at, :])
                        acc_wide[tile] = acc_wide[tile] + value if part_of else value
                    if part_of == 0:
                        continue
                    if step == 1:
                        scatter(c, 1, t, pack_wide)
                        continue
                    if t == c:
                        for half in range(2):
                            wait_line(2, half) if c else wait_plane(2, half, True)
                    if c == 0 and skip:
                        continue
                    total = jnp.zeros((32, 128), F32)
                    for i in range(4):
                        for axis, value in enumerate(pack_wide(tile, i)):
                            total = total + value * ag[2, (PLANE if c else 0) + tile * 4 + i, axis]
                    part[...] += total * (2.0 if c == 0 and tile > 0 else 1.0)
            if step == 2:
                break
            reduce_line(0)
            collect(c, 1)
            wait_recv(red_two.at[0, 0, pl.ds(0, LINE - 1)], red_sem.at[0, 3])
            total = reduced(0, c)
            moments[0] = jnp.broadcast_to(total[:, 128:256] / total[:, 0:128], (32, 128))
            a1 = moments[0]
            for axis in range(3):
                y1 = packed[1, axis]
                packed[2, axis] = packed[2, axis] - a1 * y1
                first_dir[axis] = y1 - a1 * packed[0, axis]
            gather(c, 2)
            remote(first_dir, mate.at[0], mate_sem.at[2], mate_sem.at[3], sibling).start()
            remote(packed.at[2], mate.at[1], mate_sem.at[2], mate_sem.at[3], sibling).start()
            early = (red_src[0][:, 0:128], red_src[0][:, 128:256], inner(first_dir, first_dir),
                     inner(first_dir, packed.at[2]), inner(packed.at[2], packed.at[2]))
            for n, value in enumerate(early):
                red_src[2, :, n * 128:n * 128 + 128] = value

    for_each_core(steps)

    reduce_plane(1, ((5, fold(part[...])),))
    reduce_line(1)
    wait_recv(red_one.at[1, pl.ds(0, 2 * LINE - 1)], red_sem.at[1, 3])
    low, high = reduced(1, 0), reduced(1, 1)
    for k in range(6):
        at = slice(k * 128, k * 128 + 128)
        moments[k + 1, 0:8] = jnp.broadcast_to(jnp.where(front, low[:, at], high[:, at]), (8, 128))
    moments[7, 0:8] = jnp.zeros((8, 128), F32)
    moments[8, 0:8] = jnp.ones((8, 128), F32)
    m0, m1, e1, f1, g, third, zero, one = (moments[k, 0:8] for k in range(1, 9))

    a1, a2, bb2 = m1 / m0, f1 / e1, e1 / m0
    e2 = g - a2 * f1 - bb2 * e1
    bb3 = e2 / e1
    a3 = (third - a2 * g - bb2 * (f1 + a1 * e1)) / e2 - a2
    d1, d2, d3 = 1.0 + a1, 1.0 + a2, 1.0 + a3
    scale = (d1 + d2 + d3) / ITERS
    current = (d1 / scale, jnp.sqrt(bb2) / scale, zero, d2 / scale, jnp.sqrt(bb3) / scale, d3 / scale)
    partner = (one, zero, zero, one, zero, one)

    def inverse_three(m):
        c00, c01, c02 = m[3] * m[5] - m[4] * m[4], m[2] * m[4] - m[1] * m[5], m[1] * m[4] - m[2] * m[3]
        c11, c12, c22 = m[0] * m[5] - m[2] * m[2], m[1] * m[2] - m[0] * m[4], m[0] * m[3] - m[1] * m[1]
        over = 1.0 / (m[0] * c00 + m[1] * c01 + m[2] * c02)
        return tuple(c * over for c in (c00, c01, c02, c11, c12, c22))

    def newton(_, state):
        now, other = state
        return (tuple(0.5 * (u + v) for u, v in zip(now, inverse_three(other))),
                tuple(0.5 * (u + v) for u, v in zip(other, inverse_three(now))))

    current, partner = lax.fori_loop(0, 20, newton, (current, partner))
    size = jnp.sqrt(scale)
    beta = jnp.sqrt(m0)
    r1, r2, r3 = (current[k] * size for k in range(3))
    f2, f3 = beta * r2 / jnp.sqrt(e1), beta * r3 / jnp.sqrt(e2)
    wait_recv(mate, mate_sem.at[3])
    c0, c1, c2 = (jnp.concatenate([c, c, c, c], axis=0) for c in (r1 - f3 * bb2, f2 - f3 * a2, f3))
    for axis in range(3):
        out_ref[axis] = (c0 * z_ref[axis] + c1 * jnp.where(keep, first_dir[axis], turn(mate[0, axis]))
                         + c2 * jnp.where(keep, packed[2, axis], turn(mate[1, axis])))

    wait_send(posrow.at[0], pos_sem.at[0])
    wait_send(z_mate, mate_sem.at[0])
    wait_send(mate, mate_sem.at[2])
    wait_send(posbuf.at[pl.ds(0, 22)], pos_sem.at[2])
    wait_send(ag.at[2, pl.ds(0, NEEDED - 1 + LINE - 1)], ag_send.at[2])
    for k, count in enumerate((LINE - 1, 2 * LINE - 1)):
        wait_send(red_one.at[k, pl.ds(0, PLANE - 1)], red_sem.at[k, 0])
        wait_send(red_one.at[k, pl.ds(0, count)], red_sem.at[k, 2])
    for step in range(2):
        @pl.when(core == 0)
        def _(step=step):
            wait_send(ag.at[step, pl.ds(0, LINE - 1)], ag_send.at[step])
            wait_send(rs_send.at[step, pl.ds(0, PLANE - 1)], rs_sent.at[step])

        @pl.when(core == 1)
        def _(step=step):
            wait_send(ag.at[step, pl.ds(0, PLANE - 1)], ag_send.at[step])
            wait_send(rs_send.at[step, pl.ds(0, LINE - 1)], rs_sent.at[step])


def shards(positions, start_vector):
    chunk = (3, 32, 128)
    return pl.pallas_call(
        kernel,
        out_shape=jax.ShapeDtypeStruct(start_vector.shape, F32),
        in_specs=[pl.BlockSpec(memory_space=pltpu.VMEM)] * 2,
        out_specs=pl.BlockSpec(memory_space=pltpu.VMEM),
        scratch_shapes=[
            pltpu.VMEM((2, 1, 128), F32),
            pltpu.VMEM((PLANE + LINE, 1, 256), F32),
            pltpu.VMEM((2, 3, BLOCK, 128), F32),
            pltpu.VMEM((2, 8, BLOCK), F32),
            pltpu.VMEM((2, BLOCK, 6 * BLOCK), BF16),
            pltpu.VMEM((2, BLOCK, 6 * BLOCK), BF16),
            pltpu.VMEM((2, BLOCK, 512), BF16),
            pltpu.VMEM((2, 6 * BLOCK, 256), BF16),
            pltpu.VMEM((3, PLANE + LINE) + chunk, F32),
            pltpu.VMEM((2, PLANE) + chunk, F32),
            pltpu.VMEM((2, PLANE) + chunk, F32),
            pltpu.VMEM((3,) + chunk, F32),
            pltpu.VMEM(chunk, F32),
            pltpu.VMEM((2,) + chunk, F32),
            pltpu.VMEM((3, 256, 128), F32),
            pltpu.VMEM((4, 256, 256), F32),
            pltpu.VMEM((32, 128), F32),
            pltpu.VMEM((4, 1, WIDTH), F32),
            pltpu.VMEM((2, PLANE, 1, WIDTH), F32),
            pltpu.VMEM((2, 2, LINE, 1, WIDTH), F32),
            pltpu.VMEM((9, 32, 128), F32),
            pltpu.VMEM((8, 128), F32),
            pltpu.VMEM(chunk, F32),
            pltpu.SemaphoreType.DMA((4,)),
            pltpu.SemaphoreType.DMA((4,)),
            pltpu.SemaphoreType.DMA((3, 2)),
            pltpu.SemaphoreType.DMA((3, 2)),
            pltpu.SemaphoreType.DMA((3,)),
            pltpu.SemaphoreType.DMA((2,)),
            pltpu.SemaphoreType.DMA((2,)),
            pltpu.SemaphoreType.DMA((2, 4)),
        ],
        compiler_params=pltpu.CompilerParams(
            collective_id=0, has_side_effects=True, vmem_limit_bytes=40 * 1024 * 1024),
    )(positions, start_vector)


def solution(mesh):
    in_specs = (P(None, ("row", "col")), P(None, ("row", "col"), None))
    out_specs = P(None, ("row", "col"), None)
    return jax.shard_map(shards, mesh=mesh, in_specs=in_specs, out_specs=out_specs, check_vma=False)
```
